32 devices in a mesh: dp: 4 (over y, core), seq: 8 (over z, x).
Axes of the slice: x: 2, y: 2, z: 4, core: 2. Of those that a mesh axis runs over, the one named last changes fastest.
Arguments:
- inputs: float32 [12, 2048, 768], P('dp', 'seq'), may hold values from -6 to 6
- lengths: int32 [12], P('dp'), may hold values from 512 to 2048, as said below
- norm_attn: float32 [768], replicated, may hold values from 0.25 to 1.75
- w_query: bfloat16 [768, 768], replicated, may hold values from -0.0546875 to 0.0546875
- w_key: bfloat16 [768, 768], replicated, may hold values from -0.21875 to 0.21875
- w_value: bfloat16 [768, 768], replicated, may hold values from -0.21875 to 0.21875
- w_out: bfloat16 [768, 768], replicated, may hold values from -1.75 to 1.75
- norm_ffn: float32 [768], replicated, may hold values from 0.25 to 1.75
- w_gate: bfloat16 [768, 2048], replicated, may hold values from -0.21875 to 0.21875
- w_up: bfloat16 [768, 2048], replicated, may hold values from -0.21875 to 0.21875
- w_down: bfloat16 [2048, 768], replicated, may hold values from -0.125 to 0.125
- bucket_bias: float32 [32, 12], replicated, may hold values from -4 to 4
- cotangent: float32 [12, 2048, 768], P('dp', 'seq'), may hold values from -6 to 6
Outputs:
- output: float32 [12, 2048, 768], P('dp', 'seq')
- grad_input: float32 [12, 2048, 768], P('dp', 'seq')
- grad_norm_attn: float32 [768], P('dp')
- grad_norm_ffn: float32 [768], P('dp')
- grad_query: float32 [768, 768], P('dp')
- grad_key: float32 [768, 768], P('dp')
- grad_value: float32 [768, 768], P('dp')
- grad_out: float32 [768, 768], P('dp')
- grad_gate: float32 [768, 2048], P('dp')
- grad_up: float32 [768, 2048], P('dp')
- grad_down: float32 [2048, 768], P('dp')
- grad_table: float32 [32, 12], P('dp')
The draws below stay inside these ranges and needn't reach their ends.
Inputs may be any that keep to these rules, and one draw needn't show every extreme that they name: `lengths`: of the 3 sequences of each index of dp, one has all 2048 positions valid.
All inputs are finite; a program needn't handle non-finite values.
Results may differ from the reference program's by a relative error of at most 0.024.
Values may be sent and summed in bfloat16 or wider, within the bound.
A program may use at most 384 MiB of HBM per device.

```python
import math
import jax
import jax.numpy as jnp
from jax import lax

D = 768
H = 12
DH = 64
FF = 2048
NB = 32
SEQS_DEV = 3
LEN = 2048
SEQS = 12


def draw_lengths(key, part):
    key = jax.random.fold_in(key, 11)
    pick_key, other_key = jax.random.split(key)
    groups = SEQS // SEQS_DEV
    full = jax.random.randint(pick_key, (groups, 1), 0, SEQS_DEV)
    other = jax.random.randint(other_key, (groups, SEQS_DEV), LEN // 4, LEN + 1)
    slots = jnp.arange(SEQS_DEV, dtype=jnp.int32)[None, :]
    return jnp.where(slots == full, LEN, other).reshape(SEQS).astype(jnp.int32)


def steps_of(rng, shape, cuts, least, largest):
    level, own = 1.0, jax.random.fold_in(rng, 6)
    for axis_at, blocks in cuts:
        steps = jnp.exp(jax.random.uniform(jax.random.fold_in(own, axis_at), (blocks,), jnp.float32, least / len(cuts), largest / len(cuts)))
        level = level * jnp.repeat(steps, shape[axis_at] // blocks).reshape([-1 if axis == axis_at else 1 for axis in range(len(shape))])
    return level


def scatter_about(rng, dims, scale, reach, pieces=(), held_as=jnp.bfloat16):
    array = scale * jax.random.normal(rng, dims, jnp.float32)
    if pieces:
        array = array * steps_of(rng, dims, pieces, -0.22, 0.18)
    return jnp.clip(array, -reach, reach).astype(held_as)


def setup_inputs(seed: int = 0) -> dict:
    key_list = jax.random.split(jax.random.key(seed), 14)
    return {
        "inputs": scatter_about(key_list[0], (SEQS, LEN, D), 1.0, 6.0, ((0, 4), (1, 8)), jnp.float32),
        "lengths": draw_lengths(jax.random.fold_in(key_list[13], 71), 0),
        "norm_attn": jnp.clip(1.0 + 0.15 * jax.random.normal(key_list[2], (D,), jnp.float32), 0.25, 1.75),
        "w_query": scatter_about(key_list[3], (D, D), (16 * D) ** -0.5, 0.0546875),
        "w_key": scatter_about(key_list[4], (D, D), D ** -0.5, 0.21875),
        "w_value": scatter_about(key_list[5], (D, D), D ** -0.5, 0.21875),
        "w_out": scatter_about(key_list[6], (D, D), (max(D // 64, 2)) ** -0.5, 1.75),
        "norm_ffn": jnp.clip(1.0 + 0.15 * jax.random.normal(key_list[7], (D,), jnp.float32), 0.25, 1.75),
        "w_gate": scatter_about(key_list[8], (D, FF), D ** -0.5, 0.21875),
        "w_up": scatter_about(key_list[9], (D, FF), D ** -0.5, 0.21875),
        "w_down": scatter_about(key_list[10], (FF, D), FF ** -0.5, 0.125),
        "bucket_bias": scatter_about(key_list[11], (NB, H), 1.0, 4.0, (), jnp.float32),
        "cotangent": scatter_about(key_list[12], (SEQS, LEN, D), 1.0, 6.0, ((0, 4), (1, 8)), jnp.float32),
    }


epsilon = 1e-06
limits = (1, 2, 3, 4, 5, 6, 7, 8, 12, 16, 23, 32, 46, 64, 91)
highest = lax.Precision.HIGHEST

@jax.custom_vjp
def low(v):
    return lax.optimization_barrier(v.astype(jnp.bfloat16)).astype(jnp.float32)

@jax.custom_vjp
def low_back(v):
    return v

def low_keep(v):
    return (low(v), None)

def low_pass(kept, grad):
    return (grad,)

def back_keep(v):
    return (v, None)

def back_low(kept, grad):
    return (low(grad),)
low.defvjp(low_keep, low_pass)
low_back.defvjp(back_keep, back_low)

def bucket_of(relative):
    distance = jnp.abs(relative)
    count = sum(((distance >= limit).astype(jnp.int32) for limit in limits))
    return count + (relative > 0).astype(jnp.int32) * (NB // 2)

def scale_norm(values, gain):
    return values * lax.rsqrt(lax.optimization_barrier(jnp.mean(values * values, axis=-1, keepdims=True)) + epsilon) * gain

def project(left, weight):
    return jnp.einsum('bsd,de->bse', left, weight, precision=highest)

def attend_block(query_block, keys, values, table, length, start):
    height = query_block.shape[0]
    positions = jnp.arange(LEN, dtype=jnp.int32)
    relative = positions[None, :] - (start + jnp.arange(height, dtype=jnp.int32))[:, None]
    bias = jnp.take(table, bucket_of(relative), axis=0)
    logits = jnp.einsum('qhd,khd->hqk', query_block, keys, precision=highest) + jnp.transpose(bias, (2, 0, 1))
    logits = low_back(logits)
    valid = (positions < length)[None, None, :]
    masked = jnp.where(valid, logits, -1e+30)
    shifted = masked - lax.optimization_barrier(jnp.max(masked, axis=-1, keepdims=True))
    expo = jnp.where(valid, jnp.exp(shifted), 0.0)
    weights = low(expo / lax.optimization_barrier(jnp.sum(expo, axis=-1, keepdims=True)))
    return jnp.einsum('hqk,khd->qhd', weights, values, precision=highest)

def sequence_attention(queries, keys, values, table, length):
    height = math.gcd(LEN, 512)
    blocks = queries.reshape(LEN // height, height, H, DH)
    starts = jnp.arange(LEN // height, dtype=jnp.int32) * height
    checked = jax.checkpoint(attend_block)

    def one_block(item):
        return checked(item[0], keys, values, table, length, item[1])
    return lax.map(one_block, (blocks, starts)).reshape(LEN, H * DH)

def layer(inputs, norm_attn, w_query, w_key, w_value, w_out, norm_ffn, w_gate, w_up, w_down, table, lengths):
    normed = low(scale_norm(inputs, norm_attn))
    queries = low(low_back(project(normed, w_query)))
    keys = low(low_back(project(normed, w_key)))
    values = low(low_back(project(normed, w_value)))

    def one_sequence(item):
        return sequence_attention(item[0], item[1], item[2], table, item[3])
    split = (SEQS, LEN, H, DH)
    attended = lax.map(one_sequence, (queries.reshape(split), keys.reshape(split), values.reshape(split), lengths))
    attended = low(low_back(attended))
    mixed = inputs + low_back(project(attended, w_out))
    normed_ffn = low(scale_norm(mixed, norm_ffn))
    gate = low_back(project(normed_ffn, w_gate))
    upward = low_back(project(normed_ffn, w_up))
    hidden = low(jax.nn.gelu(gate, approximate=True) * upward)
    return mixed + low_back(project(hidden, w_down))

def reference(inputs, lengths, norm_attn, w_query, w_key, w_value, w_out, norm_ffn, w_gate, w_up, w_down, bucket_bias, cotangent):

    def forward(inputs, norm_attn, w_query, w_key, w_value, w_out, norm_ffn, w_gate, w_up, w_down, table):
        return layer(inputs, norm_attn, w_query, w_key, w_value, w_out, norm_ffn, w_gate, w_up, w_down, table, lengths)
    result, backward = jax.vjp(forward, inputs, norm_attn, w_query.astype(jnp.float32), w_key.astype(jnp.float32), w_value.astype(jnp.float32), w_out.astype(jnp.float32), norm_ffn, w_gate.astype(jnp.float32), w_up.astype(jnp.float32), w_down.astype(jnp.float32), bucket_bias)
    grads = backward(cotangent)
    return (result, grads[0], grads[1], grads[6], grads[2], grads[3], grads[4], grads[5], grads[7], grads[8], grads[9], grads[10])
```

```python
import functools

import jax
import jax.numpy as jnp
from jax import lax
from jax.experimental import pallas as pl
from jax.experimental.pallas import tpu as pltpu
from jax.sharding import PartitionSpec as P

H = 12
DH = 64
NB = 32
OUTER = 4
HEADS = H // OUTER
HW = HEADS * DH
BLK = 256
AUG = DH + 16
SPAN = 4 * BLK
LOG2E = 1.4426950408889634
LN2 = 0.6931471805599453
F32 = jnp.float32
BF16 = jnp.bfloat16
NT = (((1,), (1,)), ((), ()))
VMEM_BYTES = 48 << 20

epsilon = 1e-06
limits = (1, 2, 3, 4, 5, 6, 7, 8, 12, 16, 23, 32, 46, 64, 91)
highest = lax.Precision.HIGHEST


def bucket_of(relative):
    distance = jnp.abs(relative)
    count = sum(((distance >= limit).astype(jnp.int32) for limit in limits))
    return count + (relative > 0).astype(jnp.int32) * (NB // 2)


def scale_norm(values, gain):
    return values * lax.rsqrt(jnp.mean(values * values, axis=-1, keepdims=True) + epsilon) * gain


def gating(gate, upward):
    return jax.nn.gelu(gate, approximate=True) * upward


def params():
    return pltpu.CompilerParams(vmem_limit_bytes=VMEM_BYTES)


def smem():
    return pl.BlockSpec(memory_space=pltpu.SMEM)


def whole():
    return pl.BlockSpec(memory_space=pltpu.VMEM)


def split3(v):
    a = v.astype(BF16)
    r = v - a.astype(F32)
    b = r.astype(BF16)
    c = (r - b.astype(F32)).astype(BF16)
    return a.astype(F32), b.astype(F32), c.astype(F32)


def tail(width, values):
    row = lax.broadcasted_iota(jnp.int32, (16, width), 0)
    out = jnp.zeros((16, width), F32)
    for i, v in enumerate(values):
        out = jnp.where(row == i, v, out)
    return out


def tiles_kernel(line_ref, out_ref):
    out_ref[0, 0] = jnp.zeros((BLK, BLK), F32)
    out_ref[0, 4] = jnp.zeros((BLK, BLK), F32)
    line = jnp.broadcast_to(line_ref[0], (BLK, SPAN))
    for off in (-1, 0, 1):
        shift = (off * BLK - (2 * BLK - 1)) % SPAN
        rolled = pltpu.roll(line, shift, 1, stride=1, stride_axis=0)
        out_ref[0, off + 2] = rolled[:, :BLK]


def bias_tiles(lines):
    heads = lines.shape[0]
    return pl.pallas_call(
        tiles_kernel,
        grid=(heads,),
        in_specs=[pl.BlockSpec((1, 1, SPAN), lambda h: (h, 0, 0))],
        out_specs=pl.BlockSpec((1, 5, BLK, BLK), lambda h: (h, 0, 0, 0)),
        out_shape=jax.ShapeDtypeStruct((heads, 5, BLK, BLK), F32),
        compiler_params=params(),
        name="bias_tiles",
    )(lines)


def diagonals_kernel(*refs):
    near, out_ref = refs[:-1], refs[-1]
    row = lax.broadcasted_iota(jnp.int32, (BLK, BLK), 0)
    col = lax.broadcasted_iota(jnp.int32, (BLK, BLK), 1)
    flip = (row + col == BLK - 1).astype(F32)
    total = jnp.zeros((1, SPAN), F32)
    for off in (-1, 0, 1):
        tile = sum(r[0, off + 1] for r in near)
        flipped = jnp.dot(flip, tile, preferred_element_type=F32, precision=highest)
        padded = jnp.concatenate([flipped, jnp.zeros((BLK, SPAN - BLK), F32)], axis=1)
        rolled = pltpu.roll(padded, (BLK - off * BLK) % SPAN, 1, stride=1, stride_axis=0)
        total = total + jnp.sum(rolled, axis=0, keepdims=True)
    out_ref[0] = total


def diagonal_sums(nears):
    heads = nears[0].shape[0]
    return pl.pallas_call(
        diagonals_kernel,
        grid=(heads,),
        in_specs=[pl.BlockSpec((1, 3, BLK, BLK), lambda h: (h, 0, 0, 0)) for _ in nears],
        out_specs=pl.BlockSpec((1, 1, SPAN), lambda h: (h, 0, 0)),
        out_shape=jax.ShapeDtypeStruct((heads, 1, SPAN), F32),
        compiler_params=params(),
        name="diagonal_sums",
    )(*nears)


def project_kernel(z_ref, x_ref, gain_ref, wq_ref, wk_ref, wv_ref, normed_ref, *rest):
    outs, held = rest[: 2 * OUTER], rest[2 * OUTER]
    values = x_ref[...]
    scale = lax.rsqrt(jnp.mean(values * values, axis=-1, keepdims=True) + epsilon)
    normed = (values * scale * gain_ref[...]).astype(BF16)
    normed_ref[...] = normed
    for i, (w_ref, factor) in enumerate(((wq_ref, LOG2E), (wk_ref, 1.0), (wv_ref, 1.0))):
        rows = jnp.dot(normed, w_ref[...], preferred_element_type=F32) * factor
        held[i] = rows.T.astype(BF16)
    for d in range(OUTER):
        group = lax.rem(z_ref[0] + d, OUTER)
        rows = pl.ds(pl.multiple_of(group * HW, HW), HW)
        outs[d][...] = held[0, rows]
        outs[OUTER + d][:HW] = held[1, rows]
        outs[OUTER + d][HW:] = held[2, rows]


def project(z, values, gain, wq, wk, wv):
    height, width = values.shape
    shapes = [jax.ShapeDtypeStruct((height, width), BF16)]
    shapes += [jax.ShapeDtypeStruct((HW, height), BF16)] * OUTER
    shapes += [jax.ShapeDtypeStruct((2 * HW, height), BF16)] * OUTER
    out = pl.pallas_call(
        project_kernel,
        in_specs=[smem()] + [whole()] * 5,
        out_specs=[whole()] * len(shapes),
        out_shape=shapes,
        scratch_shapes=[pltpu.VMEM((3, width, height), BF16)],
        compiler_params=params(),
        cost_estimate=pl.CostEstimate(flops=6 * height * width * width, bytes_accessed=6 << 20, transcendentals=0),
        name="project",
    )(z, values, gain.reshape(1, -1), wq, wk, wv)
    return out[0], out[1 : 1 + OUTER], out[1 + OUTER :]


def far_case(n, j, kb):
    if kb < n * j - 1:
        return 0
    if kb > n * j + n:
        return 2
    return None


def near_case(n, j, kb, x):
    off = kb - (n * j + x)
    return jnp.clip(off + 2, 0, 4), jnp.where(off <= -2, 0, jnp.where(off >= 2, 2, 1))


GROUP_F = 4
GROUP_B = 2


def forward_kernel(n, place_ref, len_ref, far_ref, *refs):
    q_refs, refs = refs[:OUTER], refs[OUTER:]
    k_refs, refs = refs[: n * OUTER], refs[n * OUTER :]
    v_refs, refs = refs[: n * OUTER], refs[n * OUTER :]
    tile_ref, refs = refs[0], refs[1:]
    o_refs, refs = refs[:OUTER], refs[OUTER:]
    lse_ref, ka, qa, va, acc, best = refs
    nk = OUTER * n
    head = pl.program_id(0)
    z, x = place_ref[0], place_ref[1]
    length = len_ref[place_ref[2]]
    left, right = far_ref[head, 0], far_ref[head, 1]
    one = jnp.ones((1, BLK), F32)
    lane = lax.broadcasted_iota(jnp.int32, (1, BLK), 1)
    vtail = tail(BLK, (one,)).astype(BF16)
    kmax = jnp.zeros((1, BLK), F32)
    for s in range(n):
        col = lax.rem(x + s, n)
        for d in range(OUTER):
            kb = n * lax.rem(z + d, OUTER) + col
            keys = k_refs[s * OUTER + d][...]
            keys32 = keys.astype(F32)
            kmax = jnp.maximum(kmax, jnp.sum(keys32 * keys32, axis=0, keepdims=True))
            mask = jnp.where(kb * BLK + lane < length, 0.0, -1e30)
            ka[kb] = jnp.concatenate([keys, tail(BLK, (one, one, one, mask)).astype(BF16)], axis=0).T
            va[kb, :DH] = v_refs[s * OUTER + d][...]
            va[kb, DH:] = vtail
    tails = [tail(BLK, split3(jnp.zeros((1, BLK), F32) + c) + (one,)).astype(BF16) for c in (left, 0.0, right)]
    qmax = jnp.zeros((1, BLK), F32)
    for d in range(OUTER):
        j = lax.rem(z + d, OUTER)
        queries = q_refs[d][...]
        queries32 = queries.astype(F32)
        qmax = jnp.maximum(qmax, jnp.sum(queries32 * queries32, axis=0, keepdims=True))
        for v in range(3):
            qa[v, j, :DH] = queries
            qa[v, j, DH:] = tails[v]
    bound = jnp.sqrt(jnp.max(qmax) * jnp.max(kmax)) * 1.01 + far_ref[head, 2]
    safe = bound <= 90.0
    acc[...] = jnp.zeros_like(acc)

    def scores(kb, j):
        case = far_case(n, j, kb)
        if case is not None:
            return jnp.dot(ka[kb], qa[case, j], preferred_element_type=F32)
        tile, case = near_case(n, j, kb, x)
        return jnp.dot(ka[kb], qa[case, j], preferred_element_type=F32) + tile_ref[0, tile]

    @pl.when(safe)
    def _():
        for g in range(0, nk, GROUP_F):

            @pl.when(g * BLK < length)
            def _():
                for j in range(OUTER):
                    add = acc[j]
                    for kb in range(g, g + GROUP_F):
                        p = jnp.exp2(scores(kb, j)).astype(BF16)
                        add = add + jnp.dot(va[kb], p, preferred_element_type=F32)
                    acc[j] = add

        best[...] = jnp.zeros_like(best)

    @pl.when(jnp.logical_not(safe))
    def _():
        best[...] = jnp.full(best.shape, -1e30, F32)
        for kb in range(nk):

            @pl.when(kb * BLK < length)
            def _():
                for j in range(OUTER):
                    s = scores(kb, j)
                    old = best[j]
                    new = jnp.maximum(old, jnp.max(s, axis=0, keepdims=True))
                    p = jnp.exp2(s - new).astype(BF16)
                    acc[j] = acc[j] * jnp.exp2(old - new) + jnp.dot(va[kb], p, preferred_element_type=F32)
                    best[j] = new

    for d in range(OUTER):
        j = lax.rem(z + d, OUTER)
        total = acc[j, DH : DH + 1, :]
        o_refs[d][...] = (acc[j, :DH, :] / total).astype(BF16)
        lse_ref[0, d] = best[j] + jnp.log2(total)


def backward_kernel(n, place_ref, len_ref, far_ref, *refs):
    q_refs, refs = refs[:OUTER], refs[OUTER:]
    k_refs, refs = refs[: n * OUTER], refs[n * OUTER :]
    v_refs, refs = refs[: n * OUTER], refs[n * OUTER :]
    tile_ref, refs = refs[0], refs[1:]
    o_refs, refs = refs[:OUTER], refs[OUTER:]
    do_refs, refs = refs[:OUTER], refs[OUTER:]
    lse_ref, refs = refs[0], refs[1:]
    dq_refs, refs = refs[:OUTER], refs[OUTER:]
    dk_refs, refs = refs[: n * OUTER], refs[n * OUTER :]
    dv_refs, refs = refs[: n * OUTER], refs[n * OUTER :]
    near_ref, far_sum_ref, ka, kt, va, qa, qt, da, acc, near, dk_all, dv_all = refs
    nk = OUTER * n
    head = pl.program_id(0)
    z, x = place_ref[0], place_ref[1]
    length = len_ref[place_ref[2]]
    left, right = far_ref[head, 0], far_ref[head, 1]
    one = jnp.ones((1, BLK), F32)
    lane = lax.broadcasted_iota(jnp.int32, (1, BLK), 1)
    ones3 = tail(BLK, (one, one, one)).astype(BF16)
    for s in range(n):
        col = lax.rem(x + s, n)
        for d in range(OUTER):
            kb = n * lax.rem(z + d, OUTER) + col
            keys = k_refs[s * OUTER + d][...]
            mask = jnp.where(kb * BLK + lane < length, 0.0, -1e30)
            ka[kb] = jnp.concatenate([keys, tail(BLK, (one, one, one, mask)).astype(BF16)], axis=0).T
            kt[kb] = keys
            va[kb] = jnp.concatenate([v_refs[s * OUTER + d][...], ones3], axis=0).T
    for d in range(OUTER):
        j = lax.rem(z + d, OUTER)
        lse = lse_ref[0, d]
        for v, c in enumerate((left, 0.0, right)):
            qa[v, j, :DH] = q_refs[d][...]
            qa[v, j, DH:] = tail(BLK, split3(c - lse) + (one,)).astype(BF16)
        qt[j] = q_refs[d][...]
        grads = do_refs[d][...]
        delta = jnp.sum(grads.astype(F32) * o_refs[d][...].astype(F32), axis=0, keepdims=True)
        da[j, :DH] = grads
        da[j, DH:] = tail(BLK, split3(-delta)).astype(BF16)
    acc[...] = jnp.zeros_like(acc)
    near[...] = jnp.zeros_like(near)
    row16 = lax.broadcasted_iota(jnp.int32, (16, BLK), 0)
    marks = [jnp.where(row16 == r, 1.0, 0.0).astype(BF16) for r in range(2)]

    for g in range(0, nk, GROUP_B):

        @pl.when(g * BLK < length)
        def _():
            dvs = {kb: jnp.zeros((DH, BLK), F32) for kb in range(g, g + GROUP_B)}
            dks = {kb: jnp.zeros((DH, BLK), F32) for kb in range(g, g + GROUP_B)}
            for j in range(OUTER):
                add = acc[j]
                for kb in range(g, g + GROUP_B):
                    case = far_case(n, j, kb)
                    if case is not None:
                        p = jnp.exp2(jnp.dot(ka[kb], qa[case, j], preferred_element_type=F32))
                        mark = marks[case // 2]
                    else:
                        tile, case = near_case(n, j, kb, x)
                        s = jnp.dot(ka[kb], qa[case, j], preferred_element_type=F32)
                        p = jnp.exp2(s + tile_ref[0, tile])
                        want = jnp.where(case == 1, 2, case // 2)
                        mark = jnp.where(row16 == want, 1.0, 0.0).astype(BF16)
                    ds = p * jnp.dot(va[kb], da[j], preferred_element_type=F32)
                    if far_case(n, j, kb) is None:
                        near[tile] += ds
                    p16, ds16 = p.astype(BF16), ds.astype(BF16)
                    lhs = jnp.concatenate([kt[kb], mark], axis=0)
                    add = add + jnp.dot(lhs, ds16, preferred_element_type=F32)
                    dvs[kb] += lax.dot_general(da[j, :DH], p16, NT, preferred_element_type=F32)
                    dks[kb] += lax.dot_general(qt[j], ds16, NT, preferred_element_type=F32)
                acc[j] = add
            for kb in range(g, g + GROUP_B):
                dk_all[kb] = dks[kb] * LN2
                dv_all[kb] = dvs[kb]

        @pl.when(g * BLK >= length)
        def _():
            for kb in range(g, g + GROUP_B):
                dk_all[kb] = jnp.zeros((DH, BLK), F32)
                dv_all[kb] = jnp.zeros((DH, BLK), F32)

    far = jnp.zeros((8, BLK), F32)
    for d in range(OUTER):
        j = lax.rem(z + d, OUTER)
        dq_refs[d][...] = acc[j, :DH, :].astype(BF16)
        far = far + acc[j, DH : DH + 8, :]
    far_sum_ref[0] = far
    for s in range(n):
        col = lax.rem(x + s, n)
        for d in range(OUTER):
            kb = n * lax.rem(z + d, OUTER) + col
            i = s * OUTER + d
            dk_refs[i][...] = dk_all[kb].astype(dk_refs[i].dtype)
            dv_refs[i][...] = dv_all[kb].astype(dv_refs[i].dtype)
    for i in range(3):
        near_ref[0, i] = near[i + 1]


def rows_block(base):
    return pl.BlockSpec((DH, BLK), lambda h: (base + h, 0))


def per_head(shape):
    return pl.BlockSpec((1,) + shape, lambda h: (h,) + (0,) * len(shape))


def attention_inputs(n, place, lengths, far, queries, pairs, tiles):
    specs = [smem()] * 3 + [rows_block(0)] * OUTER + [rows_block(0)] * (n * OUTER)
    specs += [rows_block(HEADS)] * (n * OUTER) + [per_head((5, BLK, BLK))]
    return specs, [place, lengths, far, *queries, *pairs, *pairs, tiles]


def attention_forward(n, place, lengths, far, queries, pairs, tiles):
    nk = n * OUTER
    specs, args = attention_inputs(n, place, lengths, far, queries, pairs, tiles)
    out = pl.pallas_call(
        functools.partial(forward_kernel, n),
        grid=(HEADS,),
        in_specs=specs,
        out_specs=[rows_block(0)] * OUTER + [per_head((OUTER, 1, BLK))],
        out_shape=[jax.ShapeDtypeStruct((HW, BLK), BF16)] * OUTER
        + [jax.ShapeDtypeStruct((HEADS, OUTER, 1, BLK), F32)],
        scratch_shapes=[
            pltpu.VMEM((nk, BLK, AUG), BF16),
            pltpu.VMEM((3, OUTER, AUG, BLK), BF16),
            pltpu.VMEM((nk, AUG, BLK), BF16),
            pltpu.VMEM((OUTER, AUG, BLK), F32),
            pltpu.VMEM((OUTER, 1, BLK), F32),
        ],
        compiler_params=params(),
        cost_estimate=pl.CostEstimate(flops=15 * 10**9, bytes_accessed=6 << 20, transcendentals=0),
        name="attention_forward",
    )(*args)
    return out[:OUTER], out[OUTER]


def attention_backward(n, place, lengths, far, queries, pairs, tiles, outs, douts, lse):
    nk = n * OUTER
    specs, args = attention_inputs(n, place, lengths, far, queries, pairs, tiles)
    specs += [rows_block(0)] * (2 * OUTER) + [per_head((OUTER, 1, BLK))]
    args += [*outs, *douts, lse]
    kinds = [F32] * OUTER + [BF16] * (nk - OUTER)
    out = pl.pallas_call(
        functools.partial(backward_kernel, n),
        grid=(HEADS,),
        in_specs=specs,
        out_specs=[rows_block(0)] * (OUTER + 2 * nk) + [per_head((3, BLK, BLK)), per_head((8, BLK))],
        out_shape=[jax.ShapeDtypeStruct((HW, BLK), BF16)] * OUTER
        + [jax.ShapeDtypeStruct((HW, BLK), kind) for kind in kinds + kinds]
        + [jax.ShapeDtypeStruct((HEADS, 3, BLK, BLK), F32), jax.ShapeDtypeStruct((HEADS, 8, BLK), F32)],
        scratch_shapes=[
            pltpu.VMEM((nk, BLK, AUG), BF16),
            pltpu.VMEM((nk, DH, BLK), BF16),
            pltpu.VMEM((nk, BLK, AUG), BF16),
            pltpu.VMEM((3, OUTER, AUG, BLK), BF16),
            pltpu.VMEM((OUTER, DH, BLK), BF16),
            pltpu.VMEM((OUTER, AUG, BLK), BF16),
            pltpu.VMEM((OUTER, AUG, BLK), F32),
            pltpu.VMEM((5, BLK, BLK), F32),
            pltpu.VMEM((nk, DH, BLK), F32),
            pltpu.VMEM((nk, DH, BLK), F32),
        ],
        compiler_params=params(),
        cost_estimate=pl.CostEstimate(flops=35 * 10**9, bytes_accessed=12 << 20, transcendentals=0),
        name="attention_backward",
    )(*args)
    dq = out[:OUTER]
    dk = out[OUTER : OUTER + nk]
    dv = out[OUTER + nk : OUTER + 2 * nk]
    return dq, dk, dv, out[-2], out[-1]


class Places:
    def __init__(self, mesh):
        self.dp = mesh.shape["dp"]
        self.seq = mesh.shape["seq"]
        self.inner = self.seq // OUTER
        self.cores = 2
        self.groups = self.dp // self.cores

    def shift_outer(self, value, d):
        n = self.inner
        pairs = [(o * n + i, (o + d) % OUTER * n + i) for o in range(OUTER) for i in range(n)]
        return lax.ppermute(value, "seq", pairs)

    def shift_inner(self, value, d):
        n = self.inner
        pairs = [(o * n + i, o * n + (i + d) % n) for o in range(OUTER) for i in range(n)]
        return lax.ppermute(value, "seq", pairs)

    def shift_core(self, value, d):
        c = self.cores
        pairs = [(g * c + i, g * c + (i + d) % c) for g in range(self.groups) for i in range(c)]
        return lax.ppermute(value, "dp", pairs)

    def shift_group(self, value, d):
        c, g = self.cores, self.groups
        pairs = [(o * c + i, (o + d) % g * c + i) for o in range(g) for i in range(c)]
        return lax.ppermute(value, "dp", pairs)


def scatter_sum(pieces, at, size, axis, shift):
    total = pieces(at).astype(F32)
    for d in range(1, size):
        part = pieces(lax.rem(at + d, size))
        total = total + shift(part, d).astype(F32)
    return total


def pick(value, index, axis):
    return lax.dynamic_index_in_dim(value, index, axis, keepdims=False)


def reduce_grad(places, grad, kind):
    rows, columns = grad.shape
    c, g, n = places.cores, places.groups, places.inner
    share = rows // places.dp
    dp, seq = lax.axis_index("dp"), lax.axis_index("seq")
    parts = grad.astype(kind).reshape(g, c, share, columns)
    held = scatter_sum(lambda i: pick(parts, i, 1), lax.rem(dp, c), c, 1, places.shift_core).astype(kind)
    held = scatter_sum(lambda i: pick(held, i, 0), dp // c, g, 0, places.shift_group).astype(kind)
    wide = columns // n
    slabs = held.reshape(share, n, wide)
    held = scatter_sum(lambda i: pick(slabs, i, 1), lax.rem(seq, n), n, 1, places.shift_inner).astype(kind)
    lines = held.reshape(OUTER, share // OUTER, wide)
    z, x = seq // n, lax.rem(seq, n)
    held = scatter_sum(lambda i: pick(lines, i, 0), z, OUTER, 0, places.shift_outer).astype(kind)
    full = jnp.zeros((OUTER, share // OUTER, wide), kind)
    full = lax.dynamic_update_index_in_dim(full, held, z, 0)
    for d in range(1, OUTER):
        full = lax.dynamic_update_index_in_dim(full, places.shift_outer(held, d), lax.rem(z + OUTER - d, OUTER), 0)
    full = full.reshape(share, wide)
    result = jnp.zeros((share, n, wide), kind)
    result = lax.dynamic_update_index_in_dim(result, full, x, 1)
    for d in range(1, n):
        result = lax.dynamic_update_index_in_dim(result, places.shift_inner(full, d), lax.rem(x + n - d, n), 1)
    return result.reshape(share, columns).astype(F32)


def ordered(parts, start):
    both = jnp.concatenate(list(parts) + list(parts), axis=0)
    size = parts[0].shape[0]
    return lax.dynamic_slice_in_dim(both, lax.rem(OUTER - start, OUTER) * size, OUTER * size, 0)


def shards(
    places,
    inputs,
    lengths,
    norm_attn,
    w_query,
    w_key,
    w_value,
    w_out,
    norm_ffn,
    w_gate,
    w_up,
    w_down,
    bucket_bias,
    cotangent,
):
    batch, height, width = inputs.shape
    n = places.inner
    seq = lax.axis_index("seq")
    z, x = seq // n, lax.rem(seq, n)
    z_arg = z.reshape(1).astype(jnp.int32)

    table = lax.dynamic_slice_in_dim(bucket_bias, z * HEADS, HEADS, 1) * LOG2E
    relative = 2 * BLK - 1 - jnp.arange(SPAN, dtype=jnp.int32)
    onehot = (bucket_of(relative)[:, None] == jnp.arange(NB, dtype=jnp.int32)[None, :]).astype(F32)
    lines = jnp.einsum("cn,nh->hc", onehot, table, precision=highest)[:, None, :]
    tiles = bias_tiles(lines)
    far = jnp.stack([table[NB // 2 - 1], table[NB - 1], jnp.max(jnp.abs(table), axis=0)], axis=1)

    normed, query_parts, pair_parts = [], [], []
    for b in range(batch):
        rows, qs, kvs = project(z_arg, inputs[b], norm_attn, w_query, w_key, w_value)
        normed.append(rows)
        own_q, own_kv, other = [qs[0]], [kvs[0]], {}
        for d in range(1, OUTER):
            back = OUTER - d
            own_kv.append(places.shift_outer(kvs[back], back))
            own_q.append(places.shift_outer(qs[back], back))
        pairs = list(own_kv)
        for s in range(1, n):
            pairs += [places.shift_inner(part, n - s) for part in own_kv]
        query_parts.append(own_q)
        pair_parts.append(pairs)
    outs, lses, attended = [], [], []
    places_arg = [jnp.stack([z, x, jnp.int32(b)]).astype(jnp.int32) for b in range(batch)]
    for b in range(batch):
        parts, lse = attention_forward(n, places_arg[b], lengths, far, query_parts[b], pair_parts[b], tiles)
        outs.append(parts)
        lses.append(lse)
        arrived = [parts[0]] + [places.shift_outer(parts[OUTER - d], OUTER - d) for d in range(1, OUTER)]
        attended.append(ordered(arrived, z))
    attended_t = jnp.stack(attended)
    normed = jnp.stack(normed)
    mixed = inputs + jnp.einsum("bes,ed->bsd", attended_t, w_out, preferred_element_type=F32)
    normed_ffn = scale_norm(mixed, norm_ffn).astype(BF16)
    gate = jnp.einsum("bsd,de->bse", normed_ffn, w_gate, preferred_element_type=F32)
    upward = jnp.einsum("bsd,de->bse", normed_ffn, w_up, preferred_element_type=F32)
    hidden = gating(gate, upward).astype(BF16)
    result = mixed + jnp.einsum("bsd,de->bse", hidden, w_down, preferred_element_type=F32)
    grad_out_low = cotangent.astype(BF16)
    grad_down = jnp.einsum("bsd,bse->de", hidden, grad_out_low, preferred_element_type=F32)
    grad_hidden = jnp.einsum("bse,de->bsd", grad_out_low, w_down, preferred_element_type=F32)
    _, gating_back = jax.vjp(gating, gate, upward)
    grad_gate_raw, grad_up_raw = gating_back(grad_hidden)
    grad_gate_low = grad_gate_raw.astype(BF16)
    grad_up_low = grad_up_raw.astype(BF16)
    grad_w_gate = jnp.einsum("bsd,bse->de", normed_ffn, grad_gate_low, preferred_element_type=F32)
    grad_w_up = jnp.einsum("bsd,bse->de", normed_ffn, grad_up_low, preferred_element_type=F32)
    grad_normed_ffn = jnp.einsum("bse,de->bsd", grad_gate_low, w_gate, preferred_element_type=F32) + jnp.einsum(
        "bse,de->bsd", grad_up_low, w_up, preferred_element_type=F32
    )
    _, second_back = jax.vjp(scale_norm, mixed, norm_ffn)
    grad_mixed_norm, grad_norm_ffn = second_back(grad_normed_ffn)
    grad_mixed = cotangent + grad_mixed_norm
    grad_mixed_low = grad_mixed.astype(BF16)
    grad_w_out = jnp.einsum("bes,bsd->ed", attended_t, grad_mixed_low, preferred_element_type=F32)
    grad_attended_t = jnp.einsum("bsd,ed->bes", grad_mixed_low, w_out, preferred_element_type=F32).astype(BF16)

    part_gate = reduce_grad(places, grad_w_gate, BF16)
    part_up = reduce_grad(places, grad_w_up, BF16)
    part_down = reduce_grad(places, grad_down, BF16)
    part_out = reduce_grad(places, grad_w_out, BF16)

    grads_q, grads_k, grads_v, nears, fars = [], [], [], [], []
    for b in range(batch):
        sent = [lax.dynamic_slice_in_dim(grad_attended_t[b], lax.rem(z + d, OUTER) * HW, HW, 0) for d in range(OUTER)]
        douts = [sent[0]] + [places.shift_outer(sent[OUTER - d], OUTER - d) for d in range(1, OUTER)]
        dq, dk, dv, near, far_sum = attention_backward(
            n, places_arg[b], lengths, far, query_parts[b], pair_parts[b], tiles, outs[b], douts, lses[b]
        )
        nears.append(near)
        fars.append(far_sum)
        dk_sum, dv_sum = [], []
        for d in range(OUTER):
            k_total, v_total = dk[d], dv[d]
            for s in range(1, n):
                k_total = k_total + places.shift_inner(dk[s * OUTER + d], s).astype(F32)
                v_total = v_total + places.shift_inner(dv[s * OUTER + d], s).astype(F32)
            dk_sum.append(k_total.astype(BF16))
            dv_sum.append(v_total.astype(BF16))
        for kept, parts in ((grads_q, dq), (grads_k, dk_sum), (grads_v, dv_sum)):
            arrived = [parts[0]] + [places.shift_outer(parts[OUTER - d], OUTER - d) for d in range(1, OUTER)]
            kept.append(ordered(arrived, z))
    grad_q, grad_k, grad_v = jnp.stack(grads_q), jnp.stack(grads_k), jnp.stack(grads_v)
    grad_w_query = jnp.einsum("bsd,bes->de", normed, grad_q, preferred_element_type=F32)
    grad_w_key = jnp.einsum("bsd,bes->de", normed, grad_k, preferred_element_type=F32)
    grad_w_value = jnp.einsum("bsd,bes->de", normed, grad_v, preferred_element_type=F32)
    part_query = reduce_grad(places, grad_w_query, BF16)
    part_key = reduce_grad(places, grad_w_key, BF16)
    part_value = reduce_grad(places, grad_w_value, BF16)
    grad_normed = (
        jnp.einsum("bes,de->bsd", grad_q, w_query, preferred_element_type=F32)
        + jnp.einsum("bes,de->bsd", grad_k, w_key, preferred_element_type=F32)
        + jnp.einsum("bes,de->bsd", grad_v, w_value, preferred_element_type=F32)
    )
    _, first_back = jax.vjp(scale_norm, inputs, norm_attn)
    grad_inputs_norm, grad_norm_attn = first_back(grad_normed)
    grad_inputs = grad_mixed + grad_inputs_norm

    lines_sum = diagonal_sums(nears)[:, 0]
    table_part = jnp.einsum("cn,hc->nh", onehot, lines_sum, precision=highest)
    far_total = sum(jnp.sum(f, axis=-1) for f in fars)
    bucket = jnp.arange(NB, dtype=jnp.int32)[:, None]
    table_part = table_part + jnp.where(bucket == NB // 2 - 1, far_total[:, 0][None, :], 0.0)
    table_part = table_part + jnp.where(bucket == NB - 1, far_total[:, 1][None, :], 0.0)
    grad_table = lax.dynamic_update_slice_in_dim(jnp.zeros((NB, H), F32), table_part, z * HEADS, 1)
    small = jnp.concatenate(
        [
            grad_norm_attn.reshape(places.dp, -1),
            grad_norm_ffn.reshape(places.dp, -1),
            grad_table.reshape(places.dp, -1),
        ],
        axis=1,
    )
    used = small.shape[1]
    small = jnp.pad(small, ((0, 0), (0, 32 * 128 - used))).reshape(places.dp * 32, 128)
    small = reduce_grad(places, small, F32).reshape(-1)
    share = width // places.dp
    return (
        result,
        grad_inputs,
        small[:share],
        small[share : 2 * share],
        part_query,
        part_key,
        part_value,
        part_out,
        part_gate,
        part_up,
        part_down,
        small[2 * share : used].reshape(NB // places.dp, H),
    )


def solution(mesh):
    rows = P("dp", "seq", None)
    share = P("dp", None)
    return jax.shard_map(
        functools.partial(shards, Places(mesh)),
        mesh=mesh,
        in_specs=(rows, P("dp")) + (P(),) * 10 + (rows,),
        out_specs=(rows, rows, P("dp"), P("dp")) + (share,) * 8,
        check_vma=False,
    )
```

```python
import functools

import jax
import jax.numpy as jnp
from jax import lax
from jax.experimental import pallas as pl
from jax.experimental.pallas import tpu as pltpu
from jax.sharding import PartitionSpec as P

H = 12
DH = 64
NB = 32
OUTER = 4
HEADS = H // OUTER
HW = HEADS * DH
BLK = 256
AUG = DH + 16
SPAN = 4 * BLK
LOG2E = 1.4426950408889634
LN2 = 0.6931471805599453
F32 = jnp.float32
BF16 = jnp.bfloat16
NT = (((1,), (1,)), ((), ()))
VMEM_BYTES = 56 << 20
GROUP_B = 2

epsilon = 1e-06
limits = (1, 2, 3, 4, 5, 6, 7, 8, 12, 16, 23, 32, 46, 64, 91)
highest = lax.Precision.HIGHEST


def bucket_of(relative):
    distance = jnp.abs(relative)
    count = sum(((distance >= limit).astype(jnp.int32) for limit in limits))
    return count + (relative > 0).astype(jnp.int32) * (NB // 2)


def scale_norm(values, gain):
    return values * lax.rsqrt(jnp.mean(values * values, axis=-1, keepdims=True) + epsilon) * gain


def gating(gate, upward):
    return jax.nn.gelu(gate, approximate=True) * upward


def params():
    return pltpu.CompilerParams(vmem_limit_bytes=VMEM_BYTES)


def smem():
    return pl.BlockSpec(memory_space=pltpu.SMEM)


def whole():
    return pl.BlockSpec(memory_space=pltpu.VMEM)


def split3(v):
    a = v.astype(BF16)
    r = v - a.astype(F32)
    b = r.astype(BF16)
    c = (r - b.astype(F32)).astype(BF16)
    return a.astype(F32), b.astype(F32), c.astype(F32)


def tail(width, values):
    row = lax.broadcasted_iota(jnp.int32, (16, width), 0)
    out = jnp.zeros((16, width), F32)
    for i, v in enumerate(values):
        out = jnp.where(row == i, v, out)
    return out


def tiles_kernel(line_ref, out_ref):
    out_ref[0, 0] = jnp.zeros((BLK, BLK), F32)
    out_ref[0, 4] = jnp.zeros((BLK, BLK), F32)
    line = jnp.broadcast_to(line_ref[0], (BLK, SPAN))
    for off in (-1, 0, 1):
        shift = (off * BLK - (2 * BLK - 1)) % SPAN
        rolled = pltpu.roll(line, shift, 1, stride=1, stride_axis=0)
        out_ref[0, off + 2] = rolled[:, :BLK]


def bias_tiles(lines):
    heads = lines.shape[0]
    return pl.pallas_call(
        tiles_kernel,
        grid=(heads,),
        in_specs=[pl.BlockSpec((1, 1, SPAN), lambda h: (h, 0, 0))],
        out_specs=pl.BlockSpec((1, 5, BLK, BLK), lambda h: (h, 0, 0, 0)),
        out_shape=jax.ShapeDtypeStruct((heads, 5, BLK, BLK), F32),
        compiler_params=params(),
        name="bias_tiles",
    )(lines)


def diagonals_kernel(near_ref, out_ref):
    row = lax.broadcasted_iota(jnp.int32, (BLK, BLK), 0)
    col = lax.broadcasted_iota(jnp.int32, (BLK, BLK), 1)
    flip = (row + col == BLK - 1).astype(F32)
    total = jnp.zeros((1, SPAN), F32)
    for off in (-1, 0, 1):
        flipped = jnp.dot(flip, near_ref[0, off + 2], preferred_element_type=F32, precision=highest)
        padded = jnp.concatenate([flipped, jnp.zeros((BLK, SPAN - BLK), F32)], axis=1)
        rolled = pltpu.roll(padded, (BLK - off * BLK) % SPAN, 1, stride=1, stride_axis=0)
        total = total + jnp.sum(rolled, axis=0, keepdims=True)
    out_ref[0] = total


def diagonal_sums(near):
    heads = near.shape[0]
    return pl.pallas_call(
        diagonals_kernel,
        grid=(heads,),
        in_specs=[pl.BlockSpec((1, 5, BLK, BLK), lambda h: (h, 0, 0, 0))],
        out_specs=pl.BlockSpec((1, 1, SPAN), lambda h: (h, 0, 0)),
        out_shape=jax.ShapeDtypeStruct((heads, 1, SPAN), F32),
        compiler_params=params(),
        name="diagonal_sums",
    )(near)


def peers(n, z, x):
    return [lax.rem(z + d, OUTER) * n + x for d in range(1, OUTER)] + [z * n + lax.rem(x + s, n) for s in range(1, n)]


def greet(n, z, x):
    barrier = pltpu.get_barrier_semaphore()
    for peer in peers(n, z, x):
        pl.semaphore_signal(barrier, inc=1, device_id={"seq": peer}, device_id_type=pl.DeviceIdType.MESH)
    pl.semaphore_wait(barrier, OUTER - 1 + n - 1)


def remote(src, dst, send, recv, peer):
    return pltpu.make_async_remote_copy(
        src_ref=src,
        dst_ref=dst,
        send_sem=send,
        recv_sem=recv,
        device_id={"seq": peer},
        device_id_type=pl.DeviceIdType.MESH,
    )


def far_case(n, j, kb):
    if kb < n * j - 1:
        return 0
    if kb > n * j + n:
        return 2
    return None


def near_case(n, j, kb, x):
    off = kb - (n * j + x)
    return jnp.clip(off + 2, 0, 4), jnp.where(off <= -2, 0, jnp.where(off >= 2, 2, 1))


def key_rows(keys, kb, length):
    one = jnp.ones((1, BLK), F32)
    lane = lax.broadcasted_iota(jnp.int32, (1, BLK), 1)
    mask = jnp.where(kb * BLK + lane < length, 0.0, -1e30)
    return jnp.concatenate([keys, tail(BLK, (one, one, one, mask)).astype(BF16)], axis=0).T


def forward_kernel(
    n, len_ref, far_ref, tile_ref, x_ref, gain_ref, wq_ref, wk_ref, wv_ref,
    normed_ref, own, pair, att, o_ref, lse_ref,
    send, ka, qa, va,
    z_send, z_recv, x_send, x_recv, o_send, o_recv,
):
    nk = OUTER * n
    batch = x_ref.shape[0]
    units = batch * HEADS
    me = lax.axis_index("seq")
    z, x = lax.div(me, n), lax.rem(me, n)
    greet(n, z, x)

    def z_copy(u, d):
        group = lax.rem(z + d, OUTER)
        return remote(send.at[u, group], own.at[u, z], z_send.at[u, d - 1], z_recv.at[u, d - 1], group * n + x)

    def x_copy(u, s, d):
        group = lax.rem(z + OUTER - d, OUTER)
        rows = pl.ds(DH, 2 * DH)
        peer = z * n + lax.rem(x + s, n)
        return remote(
            own.at[u, group, rows], pair.at[s - 1, u, group], x_send.at[s - 1, u, d], x_recv.at[s - 1, u, d], peer
        )

    def o_copy(u, d):
        group = lax.rem(z + d, OUTER)
        b, h = lax.div(u, HEADS), lax.rem(u, HEADS)
        rows = pl.ds(pl.multiple_of((z * HEADS + h) * DH, DH), DH)
        return remote(o_ref.at[u, group], att.at[b, rows], o_send.at[u, d - 1], o_recv.at[u, d - 1], group * n + x)

    for b in range(batch):
        values = x_ref[b]
        scale = lax.rsqrt(jnp.mean(values * values, axis=-1, keepdims=True) + epsilon)
        normed = (values * scale * gain_ref[...]).astype(BF16)
        normed_ref[b] = normed
        for i, (w_ref, factor) in enumerate(((wq_ref, LOG2E), (wk_ref, 1.0), (wv_ref, 1.0))):
            turned = (jnp.dot(normed, w_ref[...], preferred_element_type=F32) * factor).T.astype(BF16)
            for g in range(OUTER):
                for h in range(HEADS):
                    first = (g * HEADS + h) * DH
                    send[b * HEADS + h, g, i * DH : (i + 1) * DH] = turned[first : first + DH]
        for h in range(HEADS):
            u = b * HEADS + h
            for d in (2, 1, 3):
                z_copy(u, d).start()
            own[u, z] = send[u, z]
            for s in range(1, n):
                x_copy(u, s, 0).start()

    def attend(u):
        b, h = lax.div(u, HEADS), lax.rem(u, HEADS)
        length = len_ref[b]
        left, right = far_ref[h, 0], far_ref[h, 1]
        one = jnp.ones((1, BLK), F32)
        vtail = tail(BLK, (one,)).astype(BF16)
        for s in range(1, n):
            for d in range(OUTER):
                x_copy(u, s, d).wait_recv()
        for s in range(n):
            col = lax.rem(x + s, n)
            for j in range(OUTER):
                kb = n * j + col
                if s == 0:
                    keys, vals = own[u, j, DH : 2 * DH], own[u, j, 2 * DH :]
                else:
                    keys, vals = pair[n - s - 1, u, j, :DH], pair[n - s - 1, u, j, DH:]
                ka[kb] = key_rows(keys, kb, length)
                va[kb, :DH] = vals
                va[kb, DH:] = vtail

        def scores(kb, j):
            case = far_case(n, j, kb)
            if case is not None:
                return jnp.dot(ka[kb], qa[case, j], preferred_element_type=F32)
            tile, case = near_case(n, j, kb, x)
            return jnp.dot(ka[kb], qa[case, j], preferred_element_type=F32) + tile_ref[h, tile]

        for j in range(OUTER):
            for v, c in enumerate((left, 0.0, right)):
                qa[v, j, :DH] = own[u, j, :DH]
                qa[v, j, DH:] = tail(BLK, split3(jnp.zeros((1, BLK), F32) + c) + (one,)).astype(BF16)
        tops = []
        for j in range(OUTER):
            top = jnp.full((8, BLK), -1e30, F32)
            for kb in range(nk):
                top = jnp.maximum(top, jnp.max(scores(kb, j).reshape(BLK // 8, 8, BLK), axis=0))
            top = jnp.max(top, axis=0, keepdims=True)
            tops.append(top)
            for v, c in enumerate((left, 0.0, right)):
                qa[v, j, DH:] = tail(BLK, split3(c - top) + (one,)).astype(BF16)
        for j in range(OUTER):
            total = jnp.zeros((AUG, BLK), F32)
            for kb in range(nk):
                p = jnp.exp2(scores(kb, j)).astype(BF16)
                total = total + jnp.dot(va[kb], p, preferred_element_type=F32)
            weight = total[DH : DH + 1]
            o_ref[u, j] = (total[:DH] / weight).astype(BF16)
            lse_ref[u, j] = tops[j] + jnp.log2(weight)
        rows = pl.ds(pl.multiple_of((z * HEADS + h) * DH, DH), DH)
        att[b, rows] = o_ref[u, z]
        for d in (2, 1, 3):
            o_copy(u, d).start()

    def turn(u, carry):
        @pl.when(u < units)
        def _():
            for d in (1, 3, 2):
                z_copy(u, d).wait_recv()
                for s in range(1, n):
                    x_copy(u, s, d).start()

        @pl.when(u > 0)
        def _():
            attend(u - 1)

        return carry

    lax.fori_loop(0, units + 1, turn, 0)

    def finish(u, carry):
        for d in range(1, OUTER):
            z_copy(u, d).wait_send()
            o_copy(u, d).wait_send()
            o_copy(u, d).wait_recv()
        for s in range(1, n):
            for d in range(OUTER):
                x_copy(u, s, d).wait_send()
        return carry

    lax.fori_loop(0, units, finish, 0)


def attention_forward(n, lengths, far, tiles, inputs, gain, wq, wk, wv):
    batch, height, width = inputs.shape
    units, nk = batch * HEADS, n * OUTER
    dma = pltpu.SemaphoreType.DMA
    return pl.pallas_call(
        functools.partial(forward_kernel, n),
        in_specs=[smem()] * 2 + [whole()] * 6,
        out_specs=[whole()] * 6,
        out_shape=[
            jax.ShapeDtypeStruct((batch, height, width), BF16),
            jax.ShapeDtypeStruct((units, OUTER, 3 * DH, BLK), BF16),
            jax.ShapeDtypeStruct((n - 1, units, OUTER, 2 * DH, BLK), BF16),
            jax.ShapeDtypeStruct((batch, width, height), BF16),
            jax.ShapeDtypeStruct((units, OUTER, DH, BLK), BF16),
            jax.ShapeDtypeStruct((units, OUTER, 1, BLK), F32),
        ],
        scratch_shapes=[
            pltpu.VMEM((units, OUTER, 3 * DH, BLK), BF16),
            pltpu.VMEM((nk, BLK, AUG), BF16),
            pltpu.VMEM((3, OUTER, AUG, BLK), BF16),
            pltpu.VMEM((nk, AUG, BLK), BF16),
            dma((units, OUTER - 1)),
            dma((units, OUTER - 1)),
            dma((n - 1, units, OUTER)),
            dma((n - 1, units, OUTER)),
            dma((units, OUTER - 1)),
            dma((units, OUTER - 1)),
        ],
        compiler_params=pltpu.CompilerParams(
            vmem_limit_bytes=VMEM_BYTES, collective_id=0, has_side_effects=True
        ),
        cost_estimate=pl.CostEstimate(flops=45 * 10**9, bytes_accessed=24 << 20, transcendentals=0),
        name="attention_forward",
    )(lengths, far, tiles, inputs, gain.reshape(1, -1), wq, wk, wv)


def backward_kernel(
    n, len_ref, far_ref, tile_ref, own, pair, o_ref, lse_ref, dout,
    grads, near, far_sum,
    do_land, x_out, x_land, z_out, kept,
    ka, kt, va, qa, da, dk_all, dv_all,
    d_send, d_recv, x_send, x_recv, z_send, z_recv,
):
    nk = OUTER * n
    batch = dout.shape[0]
    units = batch * HEADS
    me = lax.axis_index("seq")
    z, x = lax.div(me, n), lax.rem(me, n)
    greet(n, z, x)

    def head_rows(group, h):
        return pl.ds(pl.multiple_of((group * HEADS + h) * DH, DH), DH)

    def d_copy(u, d):
        group = lax.rem(z + d, OUTER)
        b, h = lax.div(u, HEADS), lax.rem(u, HEADS)
        return remote(
            dout.at[b, head_rows(group, h)], do_land.at[u, z], d_send.at[u, d - 1], d_recv.at[u, d - 1], group * n + x
        )

    def x_copy(u, s):
        peer = z * n + lax.rem(x + s, n)
        return remote(x_out.at[s - 1, u], x_land.at[s - 1, u], x_send.at[s - 1, u], x_recv.at[s - 1, u], peer)

    def z_copy(u, d, i):
        group = lax.rem(z + d, OUTER)
        b, h = lax.div(u, HEADS), lax.rem(u, HEADS)
        return remote(
            z_out.at[u, group, pl.ds(i * DH, DH)],
            grads.at[i, b, head_rows(z, h)],
            z_send.at[u, d - 1, i],
            z_recv.at[u, d - 1, i],
            group * n + x,
        )

    def begin(u, carry):
        for d in (2, 1, 3):
            d_copy(u, d).start()
        do_land[u, z] = dout[lax.div(u, HEADS), head_rows(z, lax.rem(u, HEADS))]
        return carry

    lax.fori_loop(0, units, begin, 0)
    near[...] = jnp.zeros_like(near)
    far_sum[...] = jnp.zeros_like(far_sum)
    one = jnp.ones((1, BLK), F32)
    ones3 = tail(BLK, (one, one, one)).astype(BF16)
    row16 = lax.broadcasted_iota(jnp.int32, (16, BLK), 0)
    marks = [jnp.where(row16 == r, 1.0, 0.0).astype(BF16) for r in range(2)]

    def work(u):
        b, h = lax.div(u, HEADS), lax.rem(u, HEADS)
        length = len_ref[b]
        left, right = far_ref[h, 0], far_ref[h, 1]
        for s in range(n):
            col = lax.rem(x + s, n)
            for j in range(OUTER):
                kb = n * j + col
                if s == 0:
                    keys, vals = own[u, j, DH : 2 * DH], own[u, j, 2 * DH :]
                else:
                    keys, vals = pair[n - s - 1, u, j, :DH], pair[n - s - 1, u, j, DH:]
                ka[kb] = key_rows(keys, kb, length)
                kt[kb] = keys
                va[kb] = jnp.concatenate([vals, ones3], axis=0).T
        for d in range(1, OUTER):
            d_copy(u, d).wait_recv()
        for j in range(OUTER):
            lse = lse_ref[u, j]
            for v, c in enumerate((left, 0.0, right)):
                qa[v, j, :DH] = own[u, j, :DH]
                qa[v, j, DH:] = tail(BLK, split3(c - lse) + (one,)).astype(BF16)
            arrived = do_land[u, j]
            delta = jnp.sum(arrived.astype(F32) * o_ref[u, j].astype(F32), axis=0, keepdims=True)
            da[j, :DH] = arrived
            da[j, DH:] = tail(BLK, split3(-delta)).astype(BF16)
        dqs = [jnp.zeros((AUG, BLK), F32) for _ in range(OUTER)]
        for g in range(0, nk, GROUP_B):
            dvs = {kb: jnp.zeros((DH, BLK), F32) for kb in range(g, g + GROUP_B)}
            dks = {kb: jnp.zeros((DH, BLK), F32) for kb in range(g, g + GROUP_B)}
            for j in range(OUTER):
                for kb in range(g, g + GROUP_B):
                    case = far_case(n, j, kb)
                    if case is not None:
                        p = jnp.exp2(jnp.dot(ka[kb], qa[case, j], preferred_element_type=F32))
                        mark = marks[case // 2]
                    else:
                        tile, case = near_case(n, j, kb, x)
                        s = jnp.dot(ka[kb], qa[case, j], preferred_element_type=F32)
                        p = jnp.exp2(s + tile_ref[h, tile])
                        want = jnp.where(case == 1, 2, lax.div(case, 2))
                        mark = jnp.where(row16 == want, 1.0, 0.0).astype(BF16)
                    ds = p * jnp.dot(va[kb], da[j], preferred_element_type=F32)
                    if far_case(n, j, kb) is None:
                        near[h, tile] += ds
                    p16, ds16 = p.astype(BF16), ds.astype(BF16)
                    lhs = jnp.concatenate([kt[kb], mark], axis=0)
                    dqs[j] = dqs[j] + jnp.dot(lhs, ds16, preferred_element_type=F32)
                    dvs[kb] += lax.dot_general(da[j, :DH], p16, NT, preferred_element_type=F32)
                    dks[kb] += lax.dot_general(qa[0, j, :DH], ds16, NT, preferred_element_type=F32)
            for kb in range(g, g + GROUP_B):
                dk_all[kb] = dks[kb] * LN2
                dv_all[kb] = dvs[kb]
        far = jnp.zeros((8, BLK), F32)
        for j in range(OUTER):
            z_out[u, j, :DH] = dqs[j][:DH].astype(BF16)
            far = far + dqs[j][DH : DH + 8]
        far_sum[h] += far
        parity = lax.rem(u, 2)
        for j in range(OUTER):
            kept[parity, j, :DH] = dk_all[n * j + x]
            kept[parity, j, DH:] = dv_all[n * j + x]
            for s in range(1, n):
                kb = n * j + lax.rem(x + s, n)
                x_out[s - 1, u, j, :DH] = dk_all[kb].astype(BF16)
                x_out[s - 1, u, j, DH:] = dv_all[kb].astype(BF16)
        for s in range(1, n):
            x_copy(u, s).start()

    def hand_over(u):
        b, h = lax.div(u, HEADS), lax.rem(u, HEADS)
        parity = lax.rem(u, 2)
        for s in range(1, n):
            x_copy(u, s).wait_recv()
        for j in range(OUTER):
            total = kept[parity, j]
            for s in range(1, n):
                total = total + x_land[s - 1, u, j].astype(F32)
            z_out[u, j, DH:] = total.astype(BF16)
        for i in range(3):
            grads[i, b, head_rows(z, h)] = z_out[u, z, i * DH : (i + 1) * DH]
            for d in (2, 1, 3):
                z_copy(u, d, i).start()

    def turn(u, carry):
        @pl.when(u < units)
        def _():
            work(u)

        @pl.when(u > 0)
        def _():
            hand_over(u - 1)

        return carry

    lax.fori_loop(0, units + 1, turn, 0)

    def finish(u, carry):
        for d in range(1, OUTER):
            d_copy(u, d).wait_send()
            for i in range(3):
                z_copy(u, d, i).wait_send()
                z_copy(u, d, i).wait_recv()
        for s in range(1, n):
            x_copy(u, s).wait_send()
        return carry

    lax.fori_loop(0, units, finish, 0)


def attention_backward(n, lengths, far, tiles, own, pair, out, lse, dout):
    batch, width, height = dout.shape
    units, nk = batch * HEADS, n * OUTER
    dma = pltpu.SemaphoreType.DMA
    return pl.pallas_call(
        functools.partial(backward_kernel, n),
        in_specs=[smem()] * 2 + [whole()] * 6,
        out_specs=[whole()] * 3,
        out_shape=[
            jax.ShapeDtypeStruct((3, batch, width, height), BF16),
            jax.ShapeDtypeStruct((HEADS, 5, BLK, BLK), F32),
            jax.ShapeDtypeStruct((HEADS, 8, BLK), F32),
        ],
        scratch_shapes=[
            pltpu.VMEM((units, OUTER, DH, BLK), BF16),
            pltpu.VMEM((n - 1, units, OUTER, 2 * DH, BLK), BF16),
            pltpu.VMEM((n - 1, units, OUTER, 2 * DH, BLK), BF16),
            pltpu.VMEM((units, OUTER, 3 * DH, BLK), BF16),
            pltpu.VMEM((2, OUTER, 2 * DH, BLK), F32),
            pltpu.VMEM((nk, BLK, AUG), BF16),
            pltpu.VMEM((nk, DH, BLK), BF16),
            pltpu.VMEM((nk, BLK, AUG), BF16),
            pltpu.VMEM((3, OUTER, AUG, BLK), BF16),
            pltpu.VMEM((OUTER, AUG, BLK), BF16),
            pltpu.VMEM((nk, DH, BLK), F32),
            pltpu.VMEM((nk, DH, BLK), F32),
            dma((units, OUTER - 1)),
            dma((units, OUTER - 1)),
            dma((n - 1, units)),
            dma((n - 1, units)),
            dma((units, OUTER - 1, 3)),
            dma((units, OUTER - 1, 3)),
        ],
        compiler_params=pltpu.CompilerParams(
            vmem_limit_bytes=VMEM_BYTES, collective_id=1, has_side_effects=True
        ),
        cost_estimate=pl.CostEstimate(flops=110 * 10**9, bytes_accessed=24 << 20, transcendentals=0),
        name="attention_backward",
    )(lengths, far, tiles, own, pair, out, lse, dout)


class Places:
    def __init__(self, mesh):
        self.dp = mesh.shape["dp"]
        self.seq = mesh.shape["seq"]
        self.inner = self.seq // OUTER
        self.cores = 2
        self.groups = self.dp // self.cores

    def shift_outer(self, value, d):
        n = self.inner
        pairs = [(o * n + i, (o + d) % OUTER * n + i) for o in range(OUTER) for i in range(n)]
        return lax.ppermute(value, "seq", pairs)

    def shift_inner(self, value, d):
        n = self.inner
        pairs = [(o * n + i, o * n + (i + d) % n) for o in range(OUTER) for i in range(n)]
        return lax.ppermute(value, "seq", pairs)

    def shift_core(self, value, d):
        c = self.cores
        pairs = [(g * c + i, g * c + (i + d) % c) for g in range(self.groups) for i in range(c)]
        return lax.ppermute(value, "dp", pairs)

    def shift_group(self, value, d):
        c, g = self.cores, self.groups
        pairs = [(o * c + i, (o + d) % g * c + i) for o in range(g) for i in range(c)]
        return lax.ppermute(value, "dp", pairs)


def scatter_sum(pieces, at, size, axis, shift):
    total = pieces(at).astype(F32)
    for d in range(1, size):
        part = pieces(lax.rem(at + d, size))
        total = total + shift(part, d).astype(F32)
    return total


def pick(value, index, axis):
    return lax.dynamic_index_in_dim(value, index, axis, keepdims=False)


def reduce_grad(places, grad, kind):
    rows, columns = grad.shape
    c, g, n = places.cores, places.groups, places.inner
    share = rows // places.dp
    dp, seq = lax.axis_index("dp"), lax.axis_index("seq")
    parts = grad.astype(kind).reshape(g, c, share, columns)
    held = scatter_sum(lambda i: pick(parts, i, 1), lax.rem(dp, c), c, 1, places.shift_core).astype(kind)
    held = scatter_sum(lambda i: pick(held, i, 0), dp // c, g, 0, places.shift_group).astype(kind)
    wide = columns // n
    slabs = held.reshape(share, n, wide)
    held = scatter_sum(lambda i: pick(slabs, i, 1), lax.rem(seq, n), n, 1, places.shift_inner).astype(kind)
    lines = held.reshape(OUTER, share // OUTER, wide)
    z, x = seq // n, lax.rem(seq, n)
    held = scatter_sum(lambda i: pick(lines, i, 0), z, OUTER, 0, places.shift_outer).astype(kind)
    full = jnp.zeros((OUTER, share // OUTER, wide), kind)
    full = lax.dynamic_update_index_in_dim(full, held, z, 0)
    for d in range(1, OUTER):
        full = lax.dynamic_update_index_in_dim(full, places.shift_outer(held, d), lax.rem(z + OUTER - d, OUTER), 0)
    full = full.reshape(share, wide)
    result = jnp.zeros((share, n, wide), kind)
    result = lax.dynamic_update_index_in_dim(result, full, x, 1)
    for d in range(1, n):
        result = lax.dynamic_update_index_in_dim(result, places.shift_inner(full, d), lax.rem(x + n - d, n), 1)
    return result.reshape(share, columns).astype(F32)


def shards(
    places,
    inputs,
    lengths,
    norm_attn,
    w_query,
    w_key,
    w_value,
    w_out,
    norm_ffn,
    w_gate,
    w_up,
    w_down,
    bucket_bias,
    cotangent,
):
    batch, height, width = inputs.shape
    n = places.inner
    seq = lax.axis_index("seq")
    z, x = seq // n, lax.rem(seq, n)

    table = lax.dynamic_slice_in_dim(bucket_bias, z * HEADS, HEADS, 1) * LOG2E
    relative = 2 * BLK - 1 - jnp.arange(SPAN, dtype=jnp.int32)
    onehot = (bucket_of(relative)[:, None] == jnp.arange(NB, dtype=jnp.int32)[None, :]).astype(F32)
    lines = jnp.einsum("cn,nh->hc", onehot, table, precision=highest)[:, None, :]
    tiles = bias_tiles(lines)
    far = jnp.stack([table[NB // 2 - 1], table[NB - 1], jnp.max(jnp.abs(table), axis=0)], axis=1)

    normed, own, pair, attended_t, out, lse = attention_forward(
        n, lengths, far, tiles, inputs, norm_attn, w_query, w_key, w_value
    )
    mixed = inputs + jnp.einsum("bes,ed->bsd", attended_t, w_out, preferred_element_type=F32)
    normed_ffn = scale_norm(mixed, norm_ffn).astype(BF16)
    gate = jnp.einsum("bsd,de->bse", normed_ffn, w_gate, preferred_element_type=F32)
    upward = jnp.einsum("bsd,de->bse", normed_ffn, w_up, preferred_element_type=F32)
    hidden = gating(gate, upward).astype(BF16)
    result = mixed + jnp.einsum("bsd,de->bse", hidden, w_down, preferred_element_type=F32)
    grad_out_low = cotangent.astype(BF16)
    grad_down = jnp.einsum("bsd,bse->de", hidden, grad_out_low, preferred_element_type=F32)
    grad_hidden = jnp.einsum("bse,de->bsd", grad_out_low, w_down, preferred_element_type=F32)
    _, gating_back = jax.vjp(gating, gate, upward)
    grad_gate_raw, grad_up_raw = gating_back(grad_hidden)
    grad_gate_low = grad_gate_raw.astype(BF16)
    grad_up_low = grad_up_raw.astype(BF16)
    grad_w_gate = jnp.einsum("bsd,bse->de", normed_ffn, grad_gate_low, preferred_element_type=F32)
    grad_w_up = jnp.einsum("bsd,bse->de", normed_ffn, grad_up_low, preferred_element_type=F32)
    grad_normed_ffn = jnp.einsum("bse,de->bsd", grad_gate_low, w_gate, preferred_element_type=F32) + jnp.einsum(
        "bse,de->bsd", grad_up_low, w_up, preferred_element_type=F32
    )
    _, second_back = jax.vjp(scale_norm, mixed, norm_ffn)
    grad_mixed_norm, grad_norm_ffn = second_back(grad_normed_ffn)
    grad_mixed = cotangent + grad_mixed_norm
    grad_mixed_low = grad_mixed.astype(BF16)
    grad_w_out = jnp.einsum("bes,bsd->ed", attended_t, grad_mixed_low, preferred_element_type=F32)
    grad_attended_t = jnp.einsum("bsd,ed->bes", grad_mixed_low, w_out, preferred_element_type=F32).astype(BF16)

    part_gate = reduce_grad(places, grad_w_gate, BF16)
    part_up = reduce_grad(places, grad_w_up, BF16)
    part_down = reduce_grad(places, grad_down, BF16)
    part_out = reduce_grad(places, grad_w_out, BF16)

    grads, near, far_sum = attention_backward(n, lengths, far, tiles, own, pair, out, lse, grad_attended_t)
    grad_q, grad_k, grad_v = grads[0], grads[1], grads[2]
    grad_w_query = jnp.einsum("bsd,bes->de", normed, grad_q, preferred_element_type=F32)
    grad_w_key = jnp.einsum("bsd,bes->de", normed, grad_k, preferred_element_type=F32)
    grad_w_value = jnp.einsum("bsd,bes->de", normed, grad_v, preferred_element_type=F32)
    part_query = reduce_grad(places, grad_w_query, BF16)
    part_key = reduce_grad(places, grad_w_key, BF16)
    part_value = reduce_grad(places, grad_w_value, BF16)
    grad_normed = (
        jnp.einsum("bes,de->bsd", grad_q, w_query, preferred_element_type=F32)
        + jnp.einsum("bes,de->bsd", grad_k, w_key, preferred_element_type=F32)
        + jnp.einsum("bes,de->bsd", grad_v, w_value, preferred_element_type=F32)
    )
    _, first_back = jax.vjp(scale_norm, inputs, norm_attn)
    grad_inputs_norm, grad_norm_attn = first_back(grad_normed)
    grad_inputs = grad_mixed + grad_inputs_norm

    lines_sum = diagonal_sums(near)[:, 0]
    table_part = jnp.einsum("cn,hc->nh", onehot, lines_sum, precision=highest)
    far_total = jnp.sum(far_sum, axis=-1)
    bucket = jnp.arange(NB, dtype=jnp.int32)[:, None]
    table_part = table_part + jnp.where(bucket == NB // 2 - 1, far_total[:, 0][None, :], 0.0)
    table_part = table_part + jnp.where(bucket == NB - 1, far_total[:, 1][None, :], 0.0)
    grad_table = lax.dynamic_update_slice_in_dim(jnp.zeros((NB, H), F32), table_part, z * HEADS, 1)
    small = jnp.concatenate(
        [
            grad_norm_attn.reshape(places.dp, -1),
            grad_norm_ffn.reshape(places.dp, -1),
            grad_table.reshape(places.dp, -1),
        ],
        axis=1,
    )
    used = small.shape[1]
    small = jnp.pad(small, ((0, 0), (0, 32 * 128 - used))).reshape(places.dp * 32, 128)
    small = reduce_grad(places, small, F32).reshape(-1)
    share = width // places.dp
    return (
        result,
        grad_inputs,
        small[:share],
        small[share : 2 * share],
        part_query,
        part_key,
        part_value,
        part_out,
        part_gate,
        part_up,
        part_down,
        small[2 * share : used].reshape(NB // places.dp, H),
    )


def solution(mesh):
    rows = P("dp", "seq", None)
    share = P("dp", None)
    return jax.shard_map(
        functools.partial(shards, Places(mesh)),
        mesh=mesh,
        in_specs=(rows, P("dp")) + (P(),) * 10 + (rows,),
        out_specs=(rows, rows, P("dp"), P("dp")) + (share,) * 8,
        check_vma=False,
    )
```

```python
import functools

import jax
import jax.numpy as jnp
from jax import lax
from jax.experimental import pallas as pl
from jax.experimental.pallas import tpu as pltpu
from jax.sharding import PartitionSpec as P

H = 12
DH = 64
NB = 32
OUTER = 4
HEADS = H // OUTER
HW = HEADS * DH
BLK = 256
AUG = DH + 16
SPAN = 4 * BLK
LANES = 256
LOG2E = 1.4426950408889634
LN2 = 0.6931471805599453
F32 = jnp.float32
BF16 = jnp.bfloat16
NT = (((1,), (1,)), ((), ()))
VMEM_BYTES = 56 << 20
GROUP_B = 2

epsilon = 1e-06
limits = (1, 2, 3, 4, 5, 6, 7, 8, 12, 16, 23, 32, 46, 64, 91)
highest = lax.Precision.HIGHEST


def bucket_of(relative):
    distance = jnp.abs(relative)
    count = sum(((distance >= limit).astype(jnp.int32) for limit in limits))
    return count + (relative > 0).astype(jnp.int32) * (NB // 2)


def scale_norm(values, gain):
    return values * lax.rsqrt(jnp.mean(values * values, axis=-1, keepdims=True) + epsilon) * gain


def gating(gate, upward):
    return jax.nn.gelu(gate, approximate=True) * upward


def params():
    return pltpu.CompilerParams(vmem_limit_bytes=VMEM_BYTES)


def smem():
    return pl.BlockSpec(memory_space=pltpu.SMEM)


def whole():
    return pl.BlockSpec(memory_space=pltpu.VMEM)


def split3(v):
    a = v.astype(BF16)
    r = v - a.astype(F32)
    b = r.astype(BF16)
    c = (r - b.astype(F32)).astype(BF16)
    return a.astype(F32), b.astype(F32), c.astype(F32)


def tail(width, values):
    row = lax.broadcasted_iota(jnp.int32, (16, width), 0)
    out = jnp.zeros((16, width), F32)
    for i, v in enumerate(values):
        out = jnp.where(row == i, v, out)
    return out


def tiles_kernel(line_ref, out_ref):
    out_ref[0, 0] = jnp.zeros((BLK, BLK), F32)
    out_ref[0, 4] = jnp.zeros((BLK, BLK), F32)
    line = jnp.broadcast_to(line_ref[0], (BLK, SPAN))
    for off in (-1, 0, 1):
        shift = (off * BLK - (2 * BLK - 1)) % SPAN
        rolled = pltpu.roll(line, shift, 1, stride=1, stride_axis=0)
        out_ref[0, off + 2] = rolled[:, :BLK]


def bias_tiles(lines):
    heads = lines.shape[0]
    return pl.pallas_call(
        tiles_kernel,
        grid=(heads,),
        in_specs=[pl.BlockSpec((1, 1, SPAN), lambda h: (h, 0, 0))],
        out_specs=pl.BlockSpec((1, 5, BLK, BLK), lambda h: (h, 0, 0, 0)),
        out_shape=jax.ShapeDtypeStruct((heads, 5, BLK, BLK), F32),
        compiler_params=params(),
        name="bias_tiles",
    )(lines)


def diagonals_kernel(near_ref, out_ref):
    row = lax.broadcasted_iota(jnp.int32, (BLK, BLK), 0)
    col = lax.broadcasted_iota(jnp.int32, (BLK, BLK), 1)
    flip = (row + col == BLK - 1).astype(F32)
    total = jnp.zeros((1, SPAN), F32)
    for off in (-1, 0, 1):
        flipped = jnp.dot(flip, near_ref[0, off + 2], preferred_element_type=F32, precision=highest)
        padded = jnp.concatenate([flipped, jnp.zeros((BLK, SPAN - BLK), F32)], axis=1)
        rolled = pltpu.roll(padded, (BLK - off * BLK) % SPAN, 1, stride=1, stride_axis=0)
        total = total + jnp.sum(rolled, axis=0, keepdims=True)
    out_ref[0] = total


def diagonal_sums(near):
    heads = near.shape[0]
    return pl.pallas_call(
        diagonals_kernel,
        grid=(heads,),
        in_specs=[pl.BlockSpec((1, 5, BLK, BLK), lambda h: (h, 0, 0, 0))],
        out_specs=pl.BlockSpec((1, 1, SPAN), lambda h: (h, 0, 0)),
        out_shape=jax.ShapeDtypeStruct((heads, 1, SPAN), F32),
        compiler_params=params(),
        name="diagonal_sums",
    )(near)


def peers(n, z, x):
    return [lax.rem(z + d, OUTER) * n + x for d in range(1, OUTER)] + [z * n + lax.rem(x + s, n) for s in range(1, n)]


def greet(n, z, x):
    barrier = pltpu.get_barrier_semaphore()
    for peer in peers(n, z, x):
        pl.semaphore_signal(barrier, inc=1, device_id={"seq": peer}, device_id_type=pl.DeviceIdType.MESH)
    pl.semaphore_wait(barrier, OUTER - 1 + n - 1)


def remote(src, dst, send, recv, peer):
    return pltpu.make_async_remote_copy(
        src_ref=src,
        dst_ref=dst,
        send_sem=send,
        recv_sem=recv,
        device_id={"seq": peer},
        device_id_type=pl.DeviceIdType.MESH,
    )


def far_case(n, j, kb):
    if kb < n * j - 1:
        return 0
    if kb > n * j + n:
        return 2
    return None


def near_case(n, j, kb, x):
    off = kb - (n * j + x)
    return jnp.clip(off + 2, 0, 4), jnp.where(off <= -2, 0, jnp.where(off >= 2, 2, 1))


def key_rows(keys, kb, length):
    one = jnp.ones((1, BLK), F32)
    lane = lax.broadcasted_iota(jnp.int32, (1, BLK), 1)
    mask = jnp.where(kb * BLK + lane < length, 0.0, -1e30)
    return jnp.concatenate([keys, tail(BLK, (one, one, one, mask)).astype(BF16)], axis=0).T


def forward_kernel(
    n, len_ref, far_ref, tile_ref, x_ref, gain_ref, wq_ref, wk_ref, wv_ref,
    normed_ref, own, pair, att, o_ref, lse_ref,
    send, ka, qa, va,
    z_send, z_recv, x_send, x_recv, o_send, o_recv,
):
    nk = OUTER * n
    batch = x_ref.shape[0]
    units = batch * HEADS
    me = lax.axis_index("seq")
    z, x = lax.div(me, n), lax.rem(me, n)
    greet(n, z, x)

    def z_copy(u, d):
        group = lax.rem(z + d, OUTER)
        return remote(send.at[u, group], own.at[u, z], z_send.at[u, d - 1], z_recv.at[u, d - 1], group * n + x)

    def x_copy(u, s, d):
        group = lax.rem(z + OUTER - d, OUTER)
        rows = pl.ds(DH, 2 * DH)
        peer = z * n + lax.rem(x + s, n)
        return remote(
            own.at[u, group, rows], pair.at[s - 1, u, group], x_send.at[s - 1, u, d], x_recv.at[s - 1, u, d], peer
        )

    def o_copy(u, d):
        group = lax.rem(z + d, OUTER)
        b, h = lax.div(u, HEADS), lax.rem(u, HEADS)
        rows = pl.ds(pl.multiple_of((z * HEADS + h) * DH, DH), DH)
        return remote(o_ref.at[u, group], att.at[b, rows], o_send.at[u, d - 1], o_recv.at[u, d - 1], group * n + x)

    for b in range(batch):
        values = x_ref[b]
        scale = lax.rsqrt(jnp.mean(values * values, axis=-1, keepdims=True) + epsilon)
        normed = (values * scale * gain_ref[...]).astype(BF16)
        normed_ref[b] = normed
        for i, (w_ref, factor) in enumerate(((wq_ref, LOG2E), (wk_ref, 1.0), (wv_ref, 1.0))):
            turned = (jnp.dot(normed, w_ref[...], preferred_element_type=F32) * factor).T.astype(BF16)
            for g in range(OUTER):
                for h in range(HEADS):
                    first = (g * HEADS + h) * DH
                    send[b * HEADS + h, g, i * DH : (i + 1) * DH] = turned[first : first + DH]
        for h in range(HEADS):
            u = b * HEADS + h
            for d in (2, 1, 3):
                z_copy(u, d).start()
            own[u, z] = send[u, z]
            for s in range(1, n):
                x_copy(u, s, 0).start()

    def attend(u):
        b, h = lax.div(u, HEADS), lax.rem(u, HEADS)
        length = len_ref[b]
        left, right = far_ref[h, 0], far_ref[h, 1]
        one = jnp.ones((1, BLK), F32)
        vtail = tail(BLK, (one,)).astype(BF16)
        for s in range(1, n):
            for d in range(OUTER):
                x_copy(u, s, d).wait_recv()
        for s in range(n):
            col = lax.rem(x + s, n)
            for j in range(OUTER):
                kb = n * j + col
                if s == 0:
                    keys, vals = own[u, j, DH : 2 * DH], own[u, j, 2 * DH :]
                else:
                    keys, vals = pair[n - s - 1, u, j, :DH], pair[n - s - 1, u, j, DH:]
                ka[kb] = key_rows(keys, kb, length)
                va[kb, :DH] = vals
                va[kb, DH:] = vtail

        def scores(kb, j):
            case = far_case(n, j, kb)
            if case is not None:
                return jnp.dot(ka[kb], qa[case, j], preferred_element_type=F32)
            tile, case = near_case(n, j, kb, x)
            return jnp.dot(ka[kb], qa[case, j], preferred_element_type=F32) + tile_ref[h, tile]

        for j in range(OUTER):
            for v, c in enumerate((left, 0.0, right)):
                qa[v, j, :DH] = own[u, j, :DH]
                qa[v, j, DH:] = tail(BLK, split3(jnp.zeros((1, BLK), F32) + c) + (one,)).astype(BF16)
        tops = []
        for j in range(OUTER):
            top = jnp.full((8, BLK), -1e30, F32)
            for kb in range(nk):
                top = jnp.maximum(top, jnp.max(scores(kb, j).reshape(BLK // 8, 8, BLK), axis=0))
            top = jnp.max(top, axis=0, keepdims=True)
            tops.append(top)
            for v, c in enumerate((left, 0.0, right)):
                qa[v, j, DH:] = tail(BLK, split3(c - top) + (one,)).astype(BF16)
        for j in range(OUTER):
            total = jnp.zeros((AUG, BLK), F32)
            for kb in range(nk):
                p = jnp.exp2(scores(kb, j)).astype(BF16)
                total = total + jnp.dot(va[kb], p, preferred_element_type=F32)
            weight = total[DH : DH + 1]
            o_ref[u, j] = (total[:DH] / weight).astype(BF16)
            lse_ref[u, j] = tops[j] + jnp.log2(weight)
        rows = pl.ds(pl.multiple_of((z * HEADS + h) * DH, DH), DH)
        att[b, rows] = o_ref[u, z]
        for d in (2, 1, 3):
            o_copy(u, d).start()

    def turn(u, carry):
        @pl.when(u < units)
        def _():
            for d in (1, 3, 2):
                z_copy(u, d).wait_recv()
                for s in range(1, n):
                    x_copy(u, s, d).start()

        @pl.when(u > 0)
        def _():
            attend(u - 1)

        return carry

    lax.fori_loop(0, units + 1, turn, 0)

    def finish(u, carry):
        for d in range(1, OUTER):
            z_copy(u, d).wait_send()
            o_copy(u, d).wait_send()
            o_copy(u, d).wait_recv()
        for s in range(1, n):
            for d in range(OUTER):
                x_copy(u, s, d).wait_send()
        return carry

    lax.fori_loop(0, units, finish, 0)


def attention_forward(n, lengths, far, tiles, inputs, gain, wq, wk, wv):
    batch, height, width = inputs.shape
    units, nk = batch * HEADS, n * OUTER
    dma = pltpu.SemaphoreType.DMA
    return pl.pallas_call(
        functools.partial(forward_kernel, n),
        in_specs=[smem()] * 2 + [whole()] * 6,
        out_specs=[whole()] * 6,
        out_shape=[
            jax.ShapeDtypeStruct((batch, height, width), BF16),
            jax.ShapeDtypeStruct((units, OUTER, 3 * DH, BLK), BF16),
            jax.ShapeDtypeStruct((n - 1, units, OUTER, 2 * DH, BLK), BF16),
            jax.ShapeDtypeStruct((batch, width, height), BF16),
            jax.ShapeDtypeStruct((units, OUTER, DH, BLK), BF16),
            jax.ShapeDtypeStruct((units, OUTER, 1, BLK), F32),
        ],
        scratch_shapes=[
            pltpu.VMEM((units, OUTER, 3 * DH, BLK), BF16),
            pltpu.VMEM((nk, BLK, AUG), BF16),
            pltpu.VMEM((3, OUTER, AUG, BLK), BF16),
            pltpu.VMEM((nk, AUG, BLK), BF16),
            dma((units, OUTER - 1)),
            dma((units, OUTER - 1)),
            dma((n - 1, units, OUTER)),
            dma((n - 1, units, OUTER)),
            dma((units, OUTER - 1)),
            dma((units, OUTER - 1)),
        ],
        compiler_params=pltpu.CompilerParams(
            vmem_limit_bytes=VMEM_BYTES, collective_id=0, has_side_effects=True
        ),
        cost_estimate=pl.CostEstimate(flops=45 * 10**9, bytes_accessed=24 << 20, transcendentals=0),
        name="attention_forward",
    )(lengths, far, tiles, inputs, gain.reshape(1, -1), wq, wk, wv)


def backward_kernel(
    n, len_ref, far_ref, tile_ref, own, pair, o_ref, lse_ref, dout,
    grads, near, far_sum,
    do_land, x_out, x_land, z_out, kept,
    ka, kt, va, qa, da, dk_all, dv_all,
    d_send, d_recv, x_send, x_recv, z_send, z_recv,
):
    nk = OUTER * n
    batch = dout.shape[0]
    units = batch * HEADS
    me = lax.axis_index("seq")
    z, x = lax.div(me, n), lax.rem(me, n)
    greet(n, z, x)

    def head_rows(group, h):
        return pl.ds(pl.multiple_of((group * HEADS + h) * DH, DH), DH)

    def d_copy(u, d):
        group = lax.rem(z + d, OUTER)
        b, h = lax.div(u, HEADS), lax.rem(u, HEADS)
        return remote(
            dout.at[b, head_rows(group, h)], do_land.at[u, z], d_send.at[u, d - 1], d_recv.at[u, d - 1], group * n + x
        )

    def x_copy(u, s):
        peer = z * n + lax.rem(x + s, n)
        return remote(x_out.at[s - 1, u], x_land.at[s - 1, u], x_send.at[s - 1, u], x_recv.at[s - 1, u], peer)

    def z_copy(u, d, i):
        group = lax.rem(z + d, OUTER)
        b, h = lax.div(u, HEADS), lax.rem(u, HEADS)
        return remote(
            z_out.at[u, group, pl.ds(i * DH, DH)],
            grads.at[i, b, head_rows(z, h)],
            z_send.at[u, d - 1, i],
            z_recv.at[u, d - 1, i],
            group * n + x,
        )

    def begin(u, carry):
        for d in (2, 1, 3):
            d_copy(u, d).start()
        do_land[u, z] = dout[lax.div(u, HEADS), head_rows(z, lax.rem(u, HEADS))]
        return carry

    lax.fori_loop(0, units, begin, 0)
    near[...] = jnp.zeros_like(near)
    far_sum[...] = jnp.zeros_like(far_sum)
    one = jnp.ones((1, BLK), F32)
    ones3 = tail(BLK, (one, one, one)).astype(BF16)
    row16 = lax.broadcasted_iota(jnp.int32, (16, BLK), 0)
    marks = [jnp.where(row16 == r, 1.0, 0.0).astype(BF16) for r in range(2)]

    def work(u):
        b, h = lax.div(u, HEADS), lax.rem(u, HEADS)
        length = len_ref[b]
        left, right = far_ref[h, 0], far_ref[h, 1]
        for s in range(n):
            col = lax.rem(x + s, n)
            for j in range(OUTER):
                kb = n * j + col
                if s == 0:
                    keys, vals = own[u, j, DH : 2 * DH], own[u, j, 2 * DH :]
                else:
                    keys, vals = pair[n - s - 1, u, j, :DH], pair[n - s - 1, u, j, DH:]
                ka[kb] = key_rows(keys, kb, length)
                kt[kb] = keys
                va[kb] = jnp.concatenate([vals, ones3], axis=0).T
        for d in range(1, OUTER):
            d_copy(u, d).wait_recv()
        for j in range(OUTER):
            lse = lse_ref[u, j]
            for v, c in enumerate((left, 0.0, right)):
                qa[v, j, :DH] = own[u, j, :DH]
                qa[v, j, DH:] = tail(BLK, split3(c - lse) + (one,)).astype(BF16)
            arrived = do_land[u, j]
            delta = jnp.sum(arrived.astype(F32) * o_ref[u, j].astype(F32), axis=0, keepdims=True)
            da[j, :DH] = arrived
            da[j, DH:] = tail(BLK, split3(-delta)).astype(BF16)
        dqs = [jnp.zeros((AUG, BLK), F32) for _ in range(OUTER)]
        for g in range(0, nk, GROUP_B):
            dvs = {kb: jnp.zeros((DH, BLK), F32) for kb in range(g, g + GROUP_B)}
            dks = {kb: jnp.zeros((DH, BLK), F32) for kb in range(g, g + GROUP_B)}
            for j in range(OUTER):
                for kb in range(g, g + GROUP_B):
                    case = far_case(n, j, kb)
                    if case is not None:
                        p = jnp.exp2(jnp.dot(ka[kb], qa[case, j], preferred_element_type=F32))
                        mark = marks[case // 2]
                    else:
                        tile, case = near_case(n, j, kb, x)
                        s = jnp.dot(ka[kb], qa[case, j], preferred_element_type=F32)
                        p = jnp.exp2(s + tile_ref[h, tile])
                        want = jnp.where(case == 1, 2, lax.div(case, 2))
                        mark = jnp.where(row16 == want, 1.0, 0.0).astype(BF16)
                    ds = p * jnp.dot(va[kb], da[j], preferred_element_type=F32)
                    if far_case(n, j, kb) is None:
                        near[h, tile] += ds
                    p16, ds16 = p.astype(BF16), ds.astype(BF16)
                    lhs = jnp.concatenate([kt[kb], mark], axis=0)
                    dqs[j] = dqs[j] + jnp.dot(lhs, ds16, preferred_element_type=F32)
                    dvs[kb] += lax.dot_general(da[j, :DH], p16, NT, preferred_element_type=F32)
                    dks[kb] += lax.dot_general(qa[0, j, :DH], ds16, NT, preferred_element_type=F32)
            for kb in range(g, g + GROUP_B):
                dk_all[kb] = dks[kb] * LN2
                dv_all[kb] = dvs[kb]
        far = jnp.zeros((8, BLK), F32)
        for j in range(OUTER):
            z_out[u, j, :DH] = dqs[j][:DH].astype(BF16)
            far = far + dqs[j][DH : DH + 8]
        far_sum[h] += far
        parity = lax.rem(u, 2)
        for j in range(OUTER):
            kept[parity, j, :DH] = dk_all[n * j + x]
            kept[parity, j, DH:] = dv_all[n * j + x]
            for s in range(1, n):
                kb = n * j + lax.rem(x + s, n)
                x_out[s - 1, u, j, :DH] = dk_all[kb].astype(BF16)
                x_out[s - 1, u, j, DH:] = dv_all[kb].astype(BF16)
        for s in range(1, n):
            x_copy(u, s).start()

    def hand_over(u):
        b, h = lax.div(u, HEADS), lax.rem(u, HEADS)
        parity = lax.rem(u, 2)
        for s in range(1, n):
            x_copy(u, s).wait_recv()
        for j in range(OUTER):
            total = kept[parity, j]
            for s in range(1, n):
                total = total + x_land[s - 1, u, j].astype(F32)
            z_out[u, j, DH:] = total.astype(BF16)
        for i in range(3):
            grads[i, b, head_rows(z, h)] = z_out[u, z, i * DH : (i + 1) * DH]
            for d in (2, 1, 3):
                z_copy(u, d, i).start()

    def turn(u, carry):
        @pl.when(u < units)
        def _():
            work(u)

        @pl.when(u > 0)
        def _():
            hand_over(u - 1)

        return carry

    lax.fori_loop(0, units + 1, turn, 0)

    def finish(u, carry):
        for d in range(1, OUTER):
            d_copy(u, d).wait_send()
            for i in range(3):
                z_copy(u, d, i).wait_send()
                z_copy(u, d, i).wait_recv()
        for s in range(1, n):
            x_copy(u, s).wait_send()
        return carry

    lax.fori_loop(0, units, finish, 0)


def attention_backward(n, lengths, far, tiles, own, pair, out, lse, dout):
    batch, width, height = dout.shape
    units, nk = batch * HEADS, n * OUTER
    dma = pltpu.SemaphoreType.DMA
    return pl.pallas_call(
        functools.partial(backward_kernel, n),
        in_specs=[smem()] * 2 + [whole()] * 6,
        out_specs=[whole()] * 3,
        out_shape=[
            jax.ShapeDtypeStruct((3, batch, width, height), BF16),
            jax.ShapeDtypeStruct((HEADS, 5, BLK, BLK), F32),
            jax.ShapeDtypeStruct((HEADS, 8, BLK), F32),
        ],
        scratch_shapes=[
            pltpu.VMEM((units, OUTER, DH, BLK), BF16),
            pltpu.VMEM((n - 1, units, OUTER, 2 * DH, BLK), BF16),
            pltpu.VMEM((n - 1, units, OUTER, 2 * DH, BLK), BF16),
            pltpu.VMEM((units, OUTER, 3 * DH, BLK), BF16),
            pltpu.VMEM((2, OUTER, 2 * DH, BLK), F32),
            pltpu.VMEM((nk, BLK, AUG), BF16),
            pltpu.VMEM((nk, DH, BLK), BF16),
            pltpu.VMEM((nk, BLK, AUG), BF16),
            pltpu.VMEM((3, OUTER, AUG, BLK), BF16),
            pltpu.VMEM((OUTER, AUG, BLK), BF16),
            pltpu.VMEM((nk, DH, BLK), F32),
            pltpu.VMEM((nk, DH, BLK), F32),
            dma((units, OUTER - 1)),
            dma((units, OUTER - 1)),
            dma((n - 1, units)),
            dma((n - 1, units)),
            dma((units, OUTER - 1, 3)),
            dma((units, OUTER - 1, 3)),
        ],
        compiler_params=pltpu.CompilerParams(
            vmem_limit_bytes=VMEM_BYTES, collective_id=1, has_side_effects=True
        ),
        cost_estimate=pl.CostEstimate(flops=110 * 10**9, bytes_accessed=24 << 20, transcendentals=0),
        name="attention_backward",
    )(lengths, far, tiles, own, pair, out, lse, dout)


def rows_of(shape, dp):
    return shape[0] // dp * (shape[1] // LANES)


class Places:
    def __init__(self, mesh):
        self.dp = mesh.shape["dp"]
        self.groups = self.dp // 2
        self.inner = mesh.shape["seq"] // OUTER


class Sum:
    def __init__(self, places, shapes):
        self.p = places
        self.shapes = shapes
        self.grain = places.inner * OUTER * 16
        used = sum(rows_of(s, places.dp) for s in shapes)
        self.total = -(-used // (2 * self.grain)) * 2 * self.grain
        half = self.total // 2
        self.lines = [(0, half, True), (half, half, False)]
        self.starts = []
        at = 0
        for s in shapes:
            self.starts.append(at)
            at += rows_of(s, places.dp)
        self.used = at

    def scratch(self):
        p, dma = self.p, pltpu.SemaphoreType.DMA
        g, n, half = p.groups, p.inner, self.total // 2
        out = [pltpu.VMEM((2, g, s[0] // p.dp, s[1]), BF16) for s in self.shapes]
        out += [
            pltpu.VMEM((g, self.total, LANES), BF16),
            pltpu.VMEM((g - 1, half, LANES), BF16),
            pltpu.VMEM((g - 1, half // n, LANES), BF16),
            pltpu.VMEM((n - 1, half // n, LANES), BF16),
            pltpu.VMEM((n - 1, g, half // n, LANES), BF16),
            pltpu.VMEM((2, OUTER - 1, half // n // OUTER, LANES), BF16),
            dma((len(self.shapes), g, 3)),
            dma((2, g - 1, 2)),
            dma((2, n - 1, g, 2)),
            dma((2, OUTER - 1, 2)),
            dma((2, OUTER - 1, 2)),
            dma((2, OUTER, n - 1, 2)),
        ]
        return out

    def bind(self, grads, full, refs):
        count = len(self.shapes)
        self.grads, self.full = grads, full
        self.land = refs[:count]
        (self.held, self.y_first, self.y_second, self.x_second, self.x_first, self.z_land,
         self.c_sem, self.y_sem, self.x_sem, self.z_sem, self.az_sem, self.ax_sem) = refs[count:]
        dp, seq = lax.axis_index("dp"), lax.axis_index("seq")
        n = self.p.inner
        self.core, self.group = lax.rem(dp, 2), lax.div(dp, 2)
        self.z, self.x = lax.div(seq, n), lax.rem(seq, n)
        return self

    def copy(self, src, dst, sems, **peer):
        return pltpu.make_async_remote_copy(
            src_ref=src, dst_ref=dst, send_sem=sems[0], recv_sem=sems[1],
            device_id=peer, device_id_type=pl.DeviceIdType.MESH,
        )

    def core_copies(self):
        out = []
        for m, shape in enumerate(self.shapes):
            share = shape[0] // self.p.dp
            for g in range(self.p.groups):
                first = pl.multiple_of((g * 2 + 1 - self.core) * share, 16)
                sems = self.c_sem.at[m, g, 0], self.c_sem.at[m, g, 1]
                peer = self.group * 2 + 1 - self.core
                out.append(self.copy(self.grads[m].at[pl.ds(first, share)], self.land[m].at[0, g], sems, dp=peer))
        return out

    def own_copies(self):
        out = []
        for m, shape in enumerate(self.shapes):
            share = shape[0] // self.p.dp
            for g in range(self.p.groups):
                first = pl.multiple_of((g * 2 + self.core) * share, 16)
                out.append(
                    pltpu.make_async_copy(
                        self.grads[m].at[pl.ds(first, share)], self.land[m].at[1, g], self.c_sem.at[m, g, 2]
                    )
                )
        return out

    def part(self, line, x):
        first, rows, _ = self.lines[line]
        size = rows // self.p.inner
        return pl.ds(pl.multiple_of(first + x * size, 16), size)

    def quarter(self, line, x, z):
        first, rows, _ = self.lines[line]
        size = rows // self.p.inner
        small = size // OUTER
        return pl.ds(pl.multiple_of(first + x * size + z * small, 16), small)

    def y_copies(self, line):
        first, rows, y_first = self.lines[line]
        out = []
        for t in range(1, self.p.groups):
            other = lax.rem(self.group + t, self.p.groups)
            where = pl.ds(first, rows) if y_first else self.part(line, self.x)
            land = self.y_first if y_first else self.y_second
            sems = self.y_sem.at[line, t - 1, 0], self.y_sem.at[line, t - 1, 1]
            out.append(self.copy(self.held.at[other, where], land.at[t - 1], sems, dp=other * 2 + self.core))
        return out

    def x_copies(self, line):
        first, rows, y_first = self.lines[line]
        n, out = self.p.inner, []
        for s in range(1, n):
            other = lax.rem(self.x + s, n)
            where = self.part(line, other)
            for g in range(1 if y_first else self.p.groups):
                sems = self.x_sem.at[line, s - 1, g, 0], self.x_sem.at[line, s - 1, g, 1]
                if y_first:
                    src, dst = self.held.at[self.group, where], self.x_second.at[s - 1]
                else:
                    src, dst = self.held.at[g, where], self.x_first.at[s - 1, g]
                out.append(self.copy(src, dst, sems, seq=self.z * n + other))
        return out

    def z_copies(self, line):
        out = []
        for d in (2, 1, 3):
            other = lax.rem(self.z + d, OUTER)
            sems = self.z_sem.at[line, d - 1, 0], self.z_sem.at[line, d - 1, 1]
            src = self.held.at[self.group, self.quarter(line, self.x, other)]
            out.append(self.copy(src, self.z_land.at[line, d - 1], sems, seq=other * self.p.inner + self.x))
        return out

    def az_copies(self, line, steps=(1, 2, 3)):
        out = []
        for d in steps:
            other = lax.rem(self.z + d, OUTER)
            sems = self.az_sem.at[line, d - 1, 0], self.az_sem.at[line, d - 1, 1]
            where = self.quarter(line, self.x, self.z)
            out.append(self.copy(self.full.at[where], self.full.at[where], sems, seq=other * self.p.inner + self.x))
        return out

    def ax_copies(self, line, d):
        n, out = self.p.inner, []
        where = self.quarter(line, self.x, lax.rem(self.z + OUTER - d, OUTER))
        for s in range(1, n):
            other = lax.rem(self.x + s, n)
            sems = self.ax_sem.at[line, d, s - 1, 0], self.ax_sem.at[line, d, s - 1, 1]
            out.append(self.copy(self.full.at[where], self.full.at[where], sems, seq=self.z * n + other))
        return out


    def step_core(self):
        for c in self.core_copies() + self.own_copies():
            c.start()

    def step_first(self):
        for c in self.core_copies():
            c.wait_recv()
        for c in self.own_copies():
            c.wait()
        for m, shape in enumerate(self.shapes):
            share = shape[0] // self.p.dp
            for g in range(self.p.groups):
                for block in range(shape[1] // LANES):
                    columns = slice(block * LANES, (block + 1) * LANES)
                    first = self.starts[m] + block * share
                    total = self.land[m][0, g, :, columns].astype(F32) + self.land[m][1, g, :, columns].astype(F32)
                    self.held[g, first : first + share] = total.astype(BF16)
        if self.used < self.total:
            blank = jnp.zeros((self.p.groups, self.total - self.used, LANES), BF16)
            self.held[:, self.used :] = blank
        for c in self.y_copies(0) + self.x_copies(1):
            c.start()

    def add(self, g, where, arrived):
        total = self.held[g, where].astype(F32)
        for a in arrived:
            total = total + a.astype(F32)
        self.held[g, where] = total.astype(BF16)

    def step_second(self):
        for c in self.y_copies(0) + self.x_copies(1):
            c.wait_recv()
        first, rows, _ = self.lines[0]
        self.add(self.group, pl.ds(first, rows), [self.y_first[t] for t in range(self.p.groups - 1)])
        for g in range(self.p.groups):
            self.add(g, self.part(1, self.x), [self.x_first[s, g] for s in range(self.p.inner - 1)])
        for c in self.x_copies(0) + self.y_copies(1):
            c.start()

    def step_z(self):
        for c in self.x_copies(0) + self.y_copies(1):
            c.wait_recv()
        self.add(self.group, self.part(0, self.x), [self.x_second[s] for s in range(self.p.inner - 1)])
        self.add(self.group, self.part(1, self.x), [self.y_second[t] for t in range(self.p.groups - 1)])
        for line in range(2):
            for c in self.z_copies(line):
                c.start()

    def step_gather(self):
        for line in range(2):
            for c in self.z_copies(line):
                c.wait_recv()
            where = self.quarter(line, self.x, self.z)
            total = self.held[self.group, where].astype(F32)
            for d in range(OUTER - 1):
                total = total + self.z_land[line, d].astype(F32)
            self.full[where] = total.astype(BF16)
            for c in self.az_copies(line) + self.ax_copies(line, 0):
                c.start()

    def step_forward(self):
        for d in (1, 3, 2):
            for line in range(2):
                self.az_copies(line, (d,))[0].wait_recv()
                for c in self.ax_copies(line, d):
                    c.start()

    def step_end(self):
        for line in range(2):
            for d in range(OUTER):
                for c in self.ax_copies(line, d):
                    c.wait()
            for c in self.az_copies(line) + self.z_copies(line) + self.y_copies(line) + self.x_copies(line):
                c.wait_send()
        for c in self.core_copies():
            c.wait_send()

    def unpack(self, outs):
        for m, shape in enumerate(self.shapes):
            share = shape[0] // self.p.dp
            for block in range(shape[1] // LANES):
                first = self.starts[m] + block * share
                outs[m][:, block * LANES : (block + 1) * LANES] = self.full[first : first + share].astype(F32)

    def greet(self):
        p = self.p
        barrier = pltpu.get_barrier_semaphore()
        mesh = pl.DeviceIdType.MESH
        pl.semaphore_signal(barrier, inc=1, device_id={"dp": self.group * 2 + 1 - self.core}, device_id_type=mesh)
        for t in range(1, p.groups):
            other = lax.rem(self.group + t, p.groups) * 2 + self.core
            pl.semaphore_signal(barrier, inc=1, device_id={"dp": other}, device_id_type=mesh)
        for peer in peers(p.inner, self.z, self.x):
            pl.semaphore_signal(barrier, inc=1, device_id={"seq": peer}, device_id_type=mesh)
        pl.semaphore_wait(barrier, 1 + p.groups - 1 + OUTER - 1 + p.inner - 1)


def sum_kernel(job, *refs):
    count = len(job.shapes)
    grads, outs, refs = refs[:count], refs[count : 2 * count], refs[2 * count :]
    job.bind(grads, refs[0], refs[1:])
    job.greet()
    job.step_core()
    job.step_first()
    job.step_second()
    job.step_z()
    job.step_gather()
    job.step_forward()
    job.step_end()
    job.unpack(outs)


def sum_grads(places, grads, collective_id):
    job = Sum(places, [g.shape for g in grads])
    count = len(grads)
    return pl.pallas_call(
        functools.partial(sum_kernel, job),
        in_specs=[pl.BlockSpec(memory_space=pl.ANY)] * count,
        out_specs=[whole()] * count,
        out_shape=[jax.ShapeDtypeStruct((g.shape[0] // places.dp, g.shape[1]), F32) for g in grads],
        scratch_shapes=[pltpu.VMEM((job.total, LANES), BF16)] + job.scratch(),
        compiler_params=pltpu.CompilerParams(
            vmem_limit_bytes=VMEM_BYTES, collective_id=collective_id, has_side_effects=True
        ),
        name="sum_grads",
    )(*grads)


def shards(
    places,
    inputs,
    lengths,
    norm_attn,
    w_query,
    w_key,
    w_value,
    w_out,
    norm_ffn,
    w_gate,
    w_up,
    w_down,
    bucket_bias,
    cotangent,
):
    batch, height, width = inputs.shape
    n = places.inner
    seq = lax.axis_index("seq")
    z, x = seq // n, lax.rem(seq, n)

    table = lax.dynamic_slice_in_dim(bucket_bias, z * HEADS, HEADS, 1) * LOG2E
    relative = 2 * BLK - 1 - jnp.arange(SPAN, dtype=jnp.int32)
    onehot = (bucket_of(relative)[:, None] == jnp.arange(NB, dtype=jnp.int32)[None, :]).astype(F32)
    lines = jnp.einsum("cn,nh->hc", onehot, table, precision=highest)[:, None, :]
    tiles = bias_tiles(lines)
    far = jnp.stack([table[NB // 2 - 1], table[NB - 1], jnp.max(jnp.abs(table), axis=0)], axis=1)

    normed, own, pair, attended_t, out, lse = attention_forward(
        n, lengths, far, tiles, inputs, norm_attn, w_query, w_key, w_value
    )
    mixed = inputs + jnp.einsum("bes,ed->bsd", attended_t, w_out, preferred_element_type=F32)
    normed_ffn = scale_norm(mixed, norm_ffn).astype(BF16)
    gate = jnp.einsum("bsd,de->bse", normed_ffn, w_gate, preferred_element_type=F32)
    upward = jnp.einsum("bsd,de->bse", normed_ffn, w_up, preferred_element_type=F32)
    hidden = gating(gate, upward).astype(BF16)
    result = mixed + jnp.einsum("bsd,de->bse", hidden, w_down, preferred_element_type=F32)
    grad_out_low = cotangent.astype(BF16)
    grad_down = jnp.einsum("bsd,bse->de", hidden, grad_out_low, preferred_element_type=F32)
    grad_hidden = jnp.einsum("bse,de->bsd", grad_out_low, w_down, preferred_element_type=F32)
    _, gating_back = jax.vjp(gating, gate, upward)
    grad_gate_raw, grad_up_raw = gating_back(grad_hidden)
    grad_gate_low = grad_gate_raw.astype(BF16)
    grad_up_low = grad_up_raw.astype(BF16)
    grad_w_gate = jnp.einsum("bsd,bse->de", normed_ffn, grad_gate_low, preferred_element_type=F32)
    grad_w_up = jnp.einsum("bsd,bse->de", normed_ffn, grad_up_low, preferred_element_type=F32)
    grad_normed_ffn = jnp.einsum("bse,de->bsd", grad_gate_low, w_gate, preferred_element_type=F32) + jnp.einsum(
        "bse,de->bsd", grad_up_low, w_up, preferred_element_type=F32
    )
    _, second_back = jax.vjp(scale_norm, mixed, norm_ffn)
    grad_mixed_norm, grad_norm_ffn = second_back(grad_normed_ffn)
    grad_mixed = cotangent + grad_mixed_norm
    grad_mixed_low = grad_mixed.astype(BF16)
    grad_w_out = jnp.einsum("bes,bsd->ed", attended_t, grad_mixed_low, preferred_element_type=F32)
    grad_attended_t = jnp.einsum("bsd,ed->bes", grad_mixed_low, w_out, preferred_element_type=F32).astype(BF16)

    grads, near, far_sum = attention_backward(n, lengths, far, tiles, own, pair, out, lse, grad_attended_t)
    grad_q, grad_k, grad_v = grads[0], grads[1], grads[2]
    grad_w_query = jnp.einsum("bsd,bes->de", normed, grad_q, preferred_element_type=F32)
    grad_w_key = jnp.einsum("bsd,bes->de", normed, grad_k, preferred_element_type=F32)
    grad_w_value = jnp.einsum("bsd,bes->de", normed, grad_v, preferred_element_type=F32)
    grad_normed = (
        jnp.einsum("bes,de->bsd", grad_q, w_query, preferred_element_type=F32)
        + jnp.einsum("bes,de->bsd", grad_k, w_key, preferred_element_type=F32)
        + jnp.einsum("bes,de->bsd", grad_v, w_value, preferred_element_type=F32)
    )
    _, first_back = jax.vjp(scale_norm, inputs, norm_attn)
    grad_inputs_norm, grad_norm_attn = first_back(grad_normed)
    grad_inputs = grad_mixed + grad_inputs_norm

    lines_sum = diagonal_sums(near)[:, 0]
    table_part = jnp.einsum("cn,hc->nh", onehot, lines_sum, precision=highest)
    far_total = jnp.sum(far_sum, axis=-1)
    bucket = jnp.arange(NB, dtype=jnp.int32)[:, None]
    table_part = table_part + jnp.where(bucket == NB // 2 - 1, far_total[:, 0][None, :], 0.0)
    table_part = table_part + jnp.where(bucket == NB - 1, far_total[:, 1][None, :], 0.0)
    grad_table = lax.dynamic_update_slice_in_dim(jnp.zeros((NB, H), F32), table_part, z * HEADS, 1)
    small = jnp.concatenate(
        [
            grad_norm_attn.reshape(places.dp, -1),
            grad_norm_ffn.reshape(places.dp, -1),
            grad_table.reshape(places.dp, -1),
        ],
        axis=1,
    )
    used = small.shape[1]
    small = jnp.pad(small, ((0, 0), (0, 16 * LANES - used))).reshape(places.dp * 16, LANES)
    wide = [g.astype(BF16) for g in (grad_w_query, grad_w_key, grad_w_value, grad_w_out, grad_w_gate, grad_w_up, grad_down, small)]
    part_query, part_key, part_value, part_out, part_gate, part_up, part_down, small = sum_grads(places, wide, 2)
    small = small.reshape(-1)
    share = width // places.dp
    return (
        result,
        grad_inputs,
        small[:share],
        small[share : 2 * share],
        part_query,
        part_key,
        part_value,
        part_out,
        part_gate,
        part_up,
        part_down,
        small[2 * share : used].reshape(NB // places.dp, H),
    )


def solution(mesh):
    rows = P("dp", "seq", None)
    share = P("dp", None)
    return jax.shard_map(
        functools.partial(shards, Places(mesh)),
        mesh=mesh,
        in_specs=(rows, P("dp")) + (P(),) * 10 + (rows,),
        out_specs=(rows, rows, P("dp"), P("dp")) + (share,) * 8,
        check_vma=False,
    )
```

```python
import functools

import jax
import jax.numpy as jnp
import numpy as np
from jax import lax
from jax.experimental import pallas as pl
from jax.experimental.pallas import tpu as pltpu
from jax.sharding import PartitionSpec as P

H = 12
DH = 64
NB = 32
OUTER = 4
HEADS = H // OUTER
HW = HEADS * DH
BLK = 256
AUG = DH + 16
SPAN = 4 * BLK
LANES = 256
LOG2E = 1.4426950408889634
LN2 = 0.6931471805599453
F32 = jnp.float32
BF16 = jnp.bfloat16
NT = (((1,), (1,)), ((), ()))
VMEM_BYTES = 62 << 20
GROUP = 8
TILES = 4

epsilon = 1e-06
limits = (1, 2, 3, 4, 5, 6, 7, 8, 12, 16, 23, 32, 46, 64, 91)
highest = lax.Precision.HIGHEST


def bucket_lines():
    relative = 2 * BLK - 1 - np.arange(SPAN)
    count = sum((np.abs(relative) >= limit).astype(np.int32) for limit in limits)
    bucket = count + (relative > 0).astype(np.int32) * (NB // 2)
    return (bucket[None, :] == np.arange(NB)[:, None]).astype(np.float32)


ONEHOT = bucket_lines()


def params():
    return pltpu.CompilerParams(vmem_limit_bytes=VMEM_BYTES)


def smem():
    return pl.BlockSpec(memory_space=pltpu.SMEM)


def anywhere():
    return pl.BlockSpec(memory_space=pl.ANY)


def whole():
    return pl.BlockSpec(memory_space=pltpu.VMEM)


def split3(v):
    a = v.astype(BF16)
    r = v - a.astype(F32)
    b = r.astype(BF16)
    c = (r - b.astype(F32)).astype(BF16)
    return a.astype(F32), b.astype(F32), c.astype(F32)


def tail(width, values):
    row = lax.broadcasted_iota(jnp.int32, (16, width), 0)
    out = jnp.zeros((16, width), F32)
    for i, v in enumerate(values):
        out = jnp.where(row == i, v, out)
    return out


def peers(n, z, x):
    return [lax.rem(z + d, OUTER) * n + x for d in range(1, OUTER)] + [z * n + lax.rem(x + s, n) for s in range(1, n)]


class Places:
    def __init__(self, mesh):
        self.dp = mesh.shape["dp"]
        self.groups = self.dp // 2
        self.inner = mesh.shape["seq"] // OUTER


def remote(src, dst, sems, **peer):
    return pltpu.make_async_remote_copy(
        src_ref=src,
        dst_ref=dst,
        send_sem=sems[0],
        recv_sem=sems[1],
        device_id=peer,
        device_id_type=pl.DeviceIdType.MESH,
    )


class Rows:
    def __init__(self, places, shapes):
        self.p = places
        self.shapes = shapes
        grain = places.inner * OUTER * 16
        self.blocks = []
        at = 0
        for m, (rows, columns) in enumerate(shapes):
            share = rows // places.dp
            for block in range(columns // LANES):
                self.blocks.append((m, block, at, share))
                at += share
        self.used = at
        self.total = -(-at // (2 * grain)) * 2 * grain
        self.half = self.total // 2
        self.size = self.half // places.inner
        self.small = self.size // OUTER

    def part(self, line, x):
        return pl.ds(pl.multiple_of(line * self.half + x * self.size, 16), self.size)

    def quarter(self, line, x, z):
        return pl.ds(pl.multiple_of(line * self.half + x * self.size + z * self.small, 16), self.small)


def add_to(ref, arrived):
    if len(arrived) == 1:
        ref[...] = ref[...] + arrived[0]
        return
    total = ref[...].astype(F32)
    for a in arrived:
        total = total + a.astype(F32)
    ref[...] = total.astype(BF16)


class Scatter:
    def __init__(self, rows, y_first):
        self.rows = rows
        self.y_first = y_first

    def scratch(self):
        r, p, dma = self.rows, self.rows.p, pltpu.SemaphoreType.DMA
        g, n = p.groups, p.inner
        out = [pltpu.VMEM((g, r.total, LANES), BF16), pltpu.VMEM((g, r.total, LANES), BF16)]
        for y_first in self.y_first:
            out.append(pltpu.VMEM((g - 1, r.half if y_first else r.size, LANES), BF16))
            out.append(pltpu.VMEM((n - 1, 1 if y_first else g, r.size, LANES), BF16))
        return out + [dma((len(r.blocks), g, 3)), dma((2, g - 1, 2)), dma((2, n - 1, g, 2))]

    count = 9

    def bind(self, grads, refs):
        self.grads = grads
        self.held, self.land, self.c_sem, self.y_sem, self.x_sem = refs[0], refs[1], refs[6], refs[7], refs[8]
        self.y_land, self.x_land = (refs[2], refs[4]), (refs[3], refs[5])
        dp, seq = lax.axis_index("dp"), lax.axis_index("seq")
        n = self.rows.p.inner
        self.core, self.group = lax.rem(dp, 2), lax.div(dp, 2)
        self.z, self.x = lax.div(seq, n), lax.rem(seq, n)

    def source(self, i, g, core):
        m, block, at, share = self.rows.blocks[i]
        first = pl.multiple_of((g * 2 + core) * share, 16)
        return self.grads[m].at[pl.ds(first, share), pl.ds(block * LANES, LANES)], pl.ds(at, share)

    def picked(self, chosen):
        return [i for i, b in enumerate(self.rows.blocks) if chosen is None or b[0] in chosen]

    def core_copies(self, chosen=None):
        for i in self.picked(chosen):
            for g in range(self.rows.p.groups):
                src, where = self.source(i, g, 1 - self.core)
                sems = self.c_sem.at[i, g, 0], self.c_sem.at[i, g, 1]
                yield remote(src, self.land.at[g, where], sems, dp=self.group * 2 + 1 - self.core)

    def own_copies(self, chosen=None):
        for i in self.picked(chosen):
            for g in range(self.rows.p.groups):
                src, where = self.source(i, g, self.core)
                yield pltpu.make_async_copy(src, self.held.at[g, where], self.c_sem.at[i, g, 2])

    def y_copies(self, line):
        r = self.rows
        for t in range(1, r.p.groups):
            other = lax.rem(self.group + t, r.p.groups)
            where = pl.ds(line * r.half, r.half) if self.y_first[line] else r.part(line, self.x)
            sems = self.y_sem.at[line, t - 1, 0], self.y_sem.at[line, t - 1, 1]
            yield remote(self.held.at[other, where], self.y_land[line].at[t - 1], sems, dp=other * 2 + self.core)

    def x_copies(self, line):
        r = self.rows
        n = r.p.inner
        for s in range(1, n):
            other = lax.rem(self.x + s, n)
            where = r.part(line, other)
            for g in range(1 if self.y_first[line] else r.p.groups):
                sems = self.x_sem.at[line, s - 1, g, 0], self.x_sem.at[line, s - 1, g, 1]
                src = self.held.at[self.group if self.y_first[line] else g, where]
                yield remote(src, self.x_land[line].at[s - 1, g], sems, seq=self.z * n + other)

    def hop(self, line, which):
        return self.y_copies(line) if (which == 0) == self.y_first[line] else self.x_copies(line)


    def step_core(self, chosen=None):
        for c in self.core_copies(chosen):
            c.start()
        for c in self.own_copies(chosen):
            c.start()

    def step_first(self):
        r = self.rows
        for c in self.core_copies():
            c.wait_recv()
        for c in self.own_copies():
            c.wait()
        for line in range(2):
            for g in range(r.p.groups):
                first, last = line * r.half, min((line + 1) * r.half, r.used)
                where = pl.ds(first, last - first)
                add_to(self.held.at[g, where], [self.land[g, where]])
                if last < (line + 1) * r.half:
                    self.held[g, last : (line + 1) * r.half] = jnp.zeros(((line + 1) * r.half - last, LANES), BF16)
            for c in self.hop(line, 0):
                c.start()

    def step_second(self, line):
        r = self.rows
        for c in self.hop(line, 0):
            c.wait_recv()
        if self.y_first[line]:
            arrived = [self.y_land[line][t] for t in range(r.p.groups - 1)]
            add_to(self.held.at[self.group, pl.ds(line * r.half, r.half)], arrived)
        else:
            for g in range(r.p.groups):
                arrived = [self.x_land[line][s, g] for s in range(r.p.inner - 1)]
                add_to(self.held.at[g, r.part(line, self.x)], arrived)
        for c in self.hop(line, 1):
            c.start()

    def step_third(self, line):
        r = self.rows
        for c in self.hop(line, 1):
            c.wait_recv()
        if self.y_first[line]:
            arrived = [self.x_land[line][s, 0] for s in range(r.p.inner - 1)]
        else:
            arrived = [self.y_land[line][t] for t in range(r.p.groups - 1)]
        add_to(self.held.at[self.group, r.part(line, self.x)], arrived)

    def part(self, line):
        return self.held.at[self.group, self.rows.part(line, self.x)]

    def end(self):
        for c in self.core_copies():
            c.wait_send()
        for line in range(2):
            for which in range(2):
                for c in self.hop(line, which):
                    c.wait_send()


class Spread:
    def __init__(self, rows):
        self.rows = rows

    def scratch(self):
        r, dma = self.rows, pltpu.SemaphoreType.DMA
        return [
            pltpu.VMEM((2, 3, r.small, LANES), BF16),
            dma((2, 3, 2)),
            dma((2, 3, 2)),
            dma((2, OUTER, r.p.inner - 1, 2)),
        ]

    count = 4

    def bind(self, piece, full, refs):
        self.piece, self.full = piece, full
        self.land, self.s_sem, self.g_sem, self.x_sem = refs
        seq = lax.axis_index("seq")
        n = self.rows.p.inner
        self.z, self.x = lax.div(seq, n), lax.rem(seq, n)
        self.near = self.z + 1 - 2 * lax.rem(self.z, 2)
        self.two = lax.rem(self.z + 2, OUTER)
        self.across = lax.rem(self.near + 2, OUTER)

    def copy(self, src, dst, sems, group):
        return remote(src, dst, sems, seq=group * self.rows.p.inner + self.x)

    def sum_copy(self, line, i):
        piece = self.piece(line, (self.near, self.across, self.two)[i])
        sems = self.s_sem.at[line, i, 0], self.s_sem.at[line, i, 1]
        return self.copy(piece, self.land.at[line, i], sems, self.two if i == 2 else self.near)

    def z_copy(self, line, i):
        where = self.rows.quarter(line, self.x, self.two if i == 2 else self.z)
        sems = self.g_sem.at[line, i, 0], self.g_sem.at[line, i, 1]
        return self.copy(self.full.at[where], self.full.at[where], sems, self.two if i == 0 else self.near)

    def x_copies(self, line, c):
        n = self.rows.p.inner
        where = self.rows.quarter(line, self.x, c)
        for s in range(1, n):
            sems = self.x_sem.at[line, c, s - 1, 0], self.x_sem.at[line, c, s - 1, 1]
            yield remote(self.full.at[where], self.full.at[where], sems, seq=self.z * n + lax.rem(self.x + s, n))

    def spread(self, line, c):
        for s in self.x_copies(line, c):
            s.start()

    def step_pair(self, line):
        self.sum_copy(line, 0).start()
        self.sum_copy(line, 1).start()

    def step_two(self, line):
        for i, c in ((0, self.z), (1, self.two)):
            self.sum_copy(line, i).wait_recv()
            add_to(self.piece(line, c), [self.land[line, i]])
        self.sum_copy(line, 2).start()

    def step_back(self, line):
        self.sum_copy(line, 2).wait_recv()
        where = self.rows.quarter(line, self.x, self.z)
        self.full[where] = self.piece(line, self.z)[...] + self.land[line, 2]
        self.z_copy(line, 0).start()
        self.z_copy(line, 1).start()
        self.spread(line, self.z)

    def step_rest(self, line):
        self.z_copy(line, 0).wait_recv()
        self.z_copy(line, 2).start()
        self.spread(line, self.two)
        self.z_copy(line, 1).wait_recv()
        self.spread(line, self.near)

    def step_last(self, line):
        self.z_copy(line, 2).wait_recv()
        self.spread(line, self.across)

    def end(self):
        for line in range(2):
            for c in range(OUTER):
                for s in self.x_copies(line, c):
                    s.wait_send()
                    s.wait_recv()
            for i in range(3):
                self.sum_copy(line, i).wait_send()
                self.z_copy(line, i).wait_send()


def greet_all(places):
    dp, seq = lax.axis_index("dp"), lax.axis_index("seq")
    n = places.inner
    core, group = lax.rem(dp, 2), lax.div(dp, 2)
    barrier = pltpu.get_barrier_semaphore()
    mesh = pl.DeviceIdType.MESH
    pl.semaphore_signal(barrier, inc=1, device_id={"dp": group * 2 + 1 - core}, device_id_type=mesh)
    for t in range(1, places.groups):
        other = lax.rem(group + t, places.groups) * 2 + core
        pl.semaphore_signal(barrier, inc=1, device_id={"dp": other}, device_id_type=mesh)
    for peer in peers(n, lax.div(seq, n), lax.rem(seq, n)):
        pl.semaphore_signal(barrier, inc=1, device_id={"seq": peer}, device_id_type=mesh)
    pl.semaphore_wait(barrier, 1 + places.groups - 1 + OUTER - 1 + n - 1)


SMALL = 16


def last_kernel(early, late, *refs):
    count = 11
    sources, (gain_ref, ffn_ref), refs = refs[:count], refs[count : count + 2], refs[count + 2 :]
    grad_in, full_early, full_late, refs = refs[0], refs[1], refs[2], refs[3:]
    slots, load_sem, refs = refs[:count], refs[count], refs[count + 1 :]
    loads = [pltpu.make_async_copy(src, dst, load_sem.at[i]) for i, (src, dst) in enumerate(zip(sources, slots))]
    for c in loads:
        c.start()
    held, grads, normed_t, wq_ref, wk_ref, wv_ref, x_ref, mixed_ref, near, far_sum, onehot = slots
    gq, gk, gv, small, refs = refs[0], refs[1], refs[2], refs[3], refs[4:]
    p = late.p
    scatter, spread_early, spread_late = Scatter(late, (True, False)), Spread(early), Spread(late)
    scatter.bind((gq, gk, gv, small), refs[: Scatter.count])
    refs = refs[Scatter.count :]

    def early_piece(line, c):
        return held.at[line, pl.ds(pl.multiple_of(c * early.small, 16), early.small)]

    def late_piece(line, c):
        return scatter.held.at[scatter.group, late.quarter(line, scatter.x, c)]

    spread_early.bind(early_piece, full_early, refs[: Spread.count])
    spread_late.bind(late_piece, full_late, refs[Spread.count :])
    greet_all(p)
    loads[0].wait()
    for line in range(2):
        spread_early.step_pair(line)
    for c in loads[1:]:
        c.wait()
    batch, height, width = x_ref.shape
    for i, out in enumerate((gq, gk, gv)):
        total = jnp.zeros((width, width), F32)
        for b in range(batch):
            total = total + lax.dot_general(normed_t[b], grads[i, b], NT, preferred_element_type=F32)
        out[...] = total.astype(BF16)
        scatter.step_core((i,))
    gain = gain_ref[...]
    gain_sum = jnp.zeros((1, width), F32)
    for b in range(batch):
        back = jnp.dot(wq_ref[...], grads[0, b], preferred_element_type=F32)
        back = back + jnp.dot(wk_ref[...], grads[1, b], preferred_element_type=F32)
        back = (back + jnp.dot(wv_ref[...], grads[2, b], preferred_element_type=F32)).T
        values = x_ref[b]
        scale = lax.rsqrt(jnp.mean(values * values, axis=-1, keepdims=True) + epsilon)
        gain_sum = gain_sum + jnp.sum(back * values * scale, axis=0, keepdims=True)
        u = back * gain
        along = jnp.mean(u * values, axis=-1, keepdims=True)
        grad_in[b] = mixed_ref[b] + scale * (u - values * (scale * scale * along))
    row = lax.broadcasted_iota(jnp.int32, (BLK, BLK), 0)
    col = lax.broadcasted_iota(jnp.int32, (BLK, BLK), 1)
    flip = (row + col == BLK - 1).astype(F32)
    bucket = lax.broadcasted_iota(jnp.int32, (NB, 1), 0)
    head_lane = lax.broadcasted_iota(jnp.int32, (NB, LANES), 1)
    table = jnp.zeros((NB, LANES), F32)
    for h in range(HEADS):
        line = jnp.zeros((1, SPAN), F32)
        for off in (-1, 0, 1):
            flipped = jnp.dot(flip, near[h, off + 2], preferred_element_type=F32, precision=highest)
            padded = jnp.concatenate([flipped, jnp.zeros((BLK, SPAN - BLK), F32)], axis=1)
            rolled = pltpu.roll(padded, (BLK - off * BLK) % SPAN, 1, stride=1, stride_axis=0)
            line = line + jnp.sum(rolled, axis=0, keepdims=True)
        column = jnp.sum(onehot[...] * line, axis=1, keepdims=True)
        sides = jnp.sum(far_sum[h], axis=1, keepdims=True)
        column = column + jnp.where(bucket == NB // 2 - 1, sides[0:1], 0.0) + jnp.where(bucket == NB - 1, sides[1:2], 0.0)
        table = jnp.where(head_lane == scatter.z * HEADS + h, column, table)
    share, buckets = width // p.dp, NB // p.dp
    for i in range(p.dp):
        block = [v[:, i * share : (i + 1) * share] for v in (gain_sum, ffn_ref[...])]
        block = [jnp.concatenate([v, jnp.zeros((1, LANES - share), F32)], axis=1) for v in block]
        block += [table[i * buckets : (i + 1) * buckets], jnp.zeros((SMALL - 2 - buckets, LANES), F32)]
        small[i * SMALL : (i + 1) * SMALL] = jnp.concatenate(block, axis=0).astype(BF16)
    scatter.step_core((3,))
    for line in range(2):
        spread_early.step_two(line)
    scatter.step_first()
    for line in range(2):
        spread_early.step_back(line)
    for line in range(2):
        scatter.step_second(line)
    for line in range(2):
        spread_early.step_rest(line)
    for line in range(2):
        scatter.step_third(line)
        spread_late.step_pair(line)
    for line in range(2):
        spread_early.step_last(line)
    for line in range(2):
        spread_late.step_two(line)
    for line in range(2):
        spread_late.step_back(line)
    for line in range(2):
        spread_late.step_rest(line)
    for line in range(2):
        spread_late.step_last(line)
    spread_early.end()
    spread_late.end()
    scatter.end()


def last_grads(early, late, loaded, gain, ffn):
    inputs = loaded[6]
    width = inputs.shape[-1]
    return pl.pallas_call(
        functools.partial(last_kernel, early, late),
        in_specs=[anywhere()] * len(loaded) + [whole()] * 2,
        out_specs=[whole()] * 3,
        out_shape=[jax.ShapeDtypeStruct(inputs.shape, F32)]
        + [jax.ShapeDtypeStruct((r.total, LANES), BF16) for r in (early, late)],
        scratch_shapes=[pltpu.VMEM(v.shape, v.dtype) for v in loaded]
        + [pltpu.SemaphoreType.DMA((len(loaded),))]
        + [pltpu.VMEM((width, width), BF16)] * 3
        + [pltpu.VMEM((late.p.dp * SMALL, LANES), BF16)]
        + Scatter(late, (True, False)).scratch()
        + Spread(early).scratch()
        + Spread(late).scratch(),
        compiler_params=pltpu.CompilerParams(
            vmem_limit_bytes=VMEM_BYTES, collective_id=2, has_side_effects=True
        ),
        name="last_grads",
    )(*loaded, gain.reshape(1, -1), ffn.reshape(1, -1))


def unpack_kernel(all_rows, *refs):
    fulls, outs = refs[: len(all_rows)], list(refs[len(all_rows) :])
    *_, (_, _, first, _) = all_rows[-1].blocks
    share = outs[-3].shape[1]
    buckets, heads = outs[-1].shape
    outs[-3][...] = fulls[-1][first : first + SMALL].astype(F32)[0:1, :share]
    outs[-2][...] = fulls[-1][first : first + SMALL].astype(F32)[1:2, :share]
    outs[-1][...] = fulls[-1][first : first + SMALL].astype(F32)[2 : 2 + buckets, :heads]
    outs = outs[:-3] + [None]
    for rows, full in zip(all_rows, fulls):
        for m, block, at, share in rows.blocks:
            if outs[m] is not None:
                outs[m][:, block * LANES : (block + 1) * LANES] = full[at : at + share].astype(F32)
        outs = outs[len(rows.shapes) :]


def unpack(all_rows, fulls, width):
    dp = all_rows[0].p.dp
    shapes = [(height // dp, columns) for r in all_rows for height, columns in r.shapes][:-1]
    shapes += [(1, width // dp)] * 2 + [(NB // dp, H)]
    return pl.pallas_call(
        functools.partial(unpack_kernel, all_rows),
        in_specs=[whole()] * len(fulls),
        out_specs=[whole()] * len(shapes),
        out_shape=[jax.ShapeDtypeStruct(s, F32) for s in shapes],
        compiler_params=params(),
        name="unpack",
    )(*fulls)


def greet(n, z, x):
    barrier = pltpu.get_barrier_semaphore()
    for peer in peers(n, z, x):
        pl.semaphore_signal(barrier, inc=1, device_id={"seq": peer}, device_id_type=pl.DeviceIdType.MESH)
    pl.semaphore_wait(barrier, OUTER - 1 + n - 1)


def far_case(n, j, kb):
    if kb < n * j - 1:
        return 0
    if kb > n * j + n:
        return 2
    return None


def near_case(n, j, kb, x):
    off = kb - (n * j + x)
    near = jnp.logical_and(off >= -1, off <= 1)
    return jnp.where(near, off + 2, 0), jnp.where(off <= -2, 0, jnp.where(off >= 2, 2, 1))


def key_rows(keys, kb, length):
    one = jnp.ones((1, BLK), F32)
    lane = lax.broadcasted_iota(jnp.int32, (1, BLK), 1)
    mask = jnp.where(kb * BLK + lane < length, 0.0, -1e30)
    return jnp.concatenate([keys, tail(BLK, (one, one, one, mask)).astype(BF16)], axis=0).T


def forward_kernel(
    n, len_ref, table_ref, onehot_ref, x_ref, gain_ref, wq_ref, wk_ref, wv_ref,
    normed_ref, own, pair, att, o_ref, lse_ref, tile_ref, far_ref,
    send, ka, qa, va,
    z_send, z_recv, x_send, x_recv, o_send, o_recv,
):
    nk = OUTER * n
    batch = x_ref.shape[0]
    units = batch * HEADS
    me = lax.axis_index("seq")
    z, x = lax.div(me, n), lax.rem(me, n)
    greet(n, z, x)

    def z_copy(u, d):
        group = lax.rem(z + d, OUTER)
        sems = z_send.at[u, d - 1], z_recv.at[u, d - 1]
        return remote(send.at[u, group], own.at[u, z], sems, seq=group * n + x)

    def x_copy(u, s, d):
        group = lax.rem(z + OUTER - d, OUTER)
        rows = pl.ds(DH, 2 * DH)
        peer = z * n + lax.rem(x + s, n)
        sems = x_send.at[s - 1, u, d], x_recv.at[s - 1, u, d]
        return remote(own.at[u, group, rows], pair.at[s - 1, u, group], sems, seq=peer)

    def o_copy(u, d):
        group = lax.rem(z + d, OUTER)
        b, h = lax.div(u, HEADS), lax.rem(u, HEADS)
        rows = pl.ds(pl.multiple_of((z * HEADS + h) * DH, DH), DH)
        sems = o_send.at[u, d - 1], o_recv.at[u, d - 1]
        return remote(o_ref.at[u, group], att.at[b, rows], sems, seq=group * n + x)

    for b in range(batch):
        values = x_ref[b]
        scale = lax.rsqrt(jnp.mean(values * values, axis=-1, keepdims=True) + epsilon)
        normed = (values * scale * gain_ref[...]).astype(BF16)
        normed_ref[b] = normed.T
        for i, (w_ref, factor) in enumerate(((wq_ref, LOG2E), (wk_ref, 1.0), (wv_ref, 1.0))):
            turned = (jnp.dot(normed, w_ref[...], preferred_element_type=F32) * factor).T.astype(BF16)
            for g in range(OUTER):
                for h in range(HEADS):
                    first = (g * HEADS + h) * DH
                    send[b * HEADS + h, g, i * DH : (i + 1) * DH] = turned[first : first + DH]
        for h in range(HEADS):
            u = b * HEADS + h
            for d in (2, 1, 3):
                z_copy(u, d).start()
            own[u, z] = send[u, z]
            for s in range(1, n):
                x_copy(u, s, 0).start()

    head_lane = lax.broadcasted_iota(jnp.int32, (NB, H), 1)
    for h in range(HEADS):
        chosen = jnp.where(head_lane == z * HEADS + h, table_ref[...], 0.0)
        column = jnp.sum(chosen, axis=1, keepdims=True) * LOG2E
        line = jnp.broadcast_to(jnp.sum(onehot_ref[...] * column, axis=0, keepdims=True), (BLK, SPAN))
        tile_ref[h, 0] = jnp.zeros((BLK, BLK), F32)
        for off in (-1, 0, 1):
            shift = (off * BLK - (2 * BLK - 1)) % SPAN
            tile_ref[h, off + 2] = pltpu.roll(line, shift, 1, stride=1, stride_axis=0)[:, :BLK]
        far_ref[h, 0] = jnp.broadcast_to(column[NB // 2 - 1 : NB // 2], (1, BLK))
        far_ref[h, 1] = jnp.broadcast_to(column[NB - 1 :], (1, BLK))

    def attend(u):
        b, h = lax.div(u, HEADS), lax.rem(u, HEADS)
        length = len_ref[b]
        left, right = far_ref[h, 0], far_ref[h, 1]
        one = jnp.ones((1, BLK), F32)
        vtail = tail(BLK, (one,)).astype(BF16)
        for s in range(1, n):
            for d in range(OUTER):
                x_copy(u, s, d).wait_recv()
        for s in range(n):
            col = lax.rem(x + s, n)
            for j in range(OUTER):
                kb = n * j + col
                if s == 0:
                    keys, vals = own[u, j, DH : 2 * DH], own[u, j, 2 * DH :]
                else:
                    keys, vals = pair[n - s - 1, u, j, :DH], pair[n - s - 1, u, j, DH:]
                ka[kb] = key_rows(keys, kb, length)
                columns = pl.ds(pl.multiple_of(kb * BLK, BLK), BLK)
                va[:DH, columns] = vals
                va[DH:, columns] = vtail

        def scores(kb, j):
            case = far_case(n, j, kb)
            if case is not None:
                return jnp.dot(ka[kb], qa[case, j], preferred_element_type=F32)
            tile, case = near_case(n, j, kb, x)
            return jnp.dot(ka[kb], qa[case, j], preferred_element_type=F32) + tile_ref[h, tile]

        for j in range(OUTER):
            for v, c in enumerate((left, 0.0 * one, right)):
                qa[v, j, :DH] = own[u, j, :DH]
                qa[v, j, DH:] = tail(BLK, split3(c) + (one,)).astype(BF16)
        tops = []
        for j in range(OUTER):
            top = jnp.full((8, BLK), -1e30, F32)
            for kb in range(nk):
                top = jnp.maximum(top, jnp.max(scores(kb, j).reshape(BLK // 8, 8, BLK), axis=0))
            top = jnp.max(top, axis=0, keepdims=True)
            tops.append(top)
            for v, c in enumerate((left, 0.0, right)):
                qa[v, j, DH:] = tail(BLK, split3(c - top) + (one,)).astype(BF16)
        for j in range(OUTER):
            weights = [jnp.exp2(scores(kb, j)).astype(BF16) for kb in range(nk)]
            total = jnp.dot(va[...], jnp.concatenate(weights, axis=0), preferred_element_type=F32)
            weight = total[DH : DH + 1]
            o_ref[u, j] = (total[:DH] / weight).astype(BF16)
            lse_ref[u, j] = tops[j] + jnp.log2(weight)
        rows = pl.ds(pl.multiple_of((z * HEADS + h) * DH, DH), DH)
        att[b, rows] = o_ref[u, z]
        for d in (2, 1, 3):
            o_copy(u, d).start()

    def turn(u, carry):
        @pl.when(u < units)
        def _():
            for d in (1, 3, 2):
                z_copy(u, d).wait_recv()
                for s in range(1, n):
                    x_copy(u, s, d).start()

        @pl.when(u > 0)
        def _():
            attend(u - 1)

        return carry

    lax.fori_loop(0, units + 1, turn, 0)

    def finish(u, carry):
        for d in range(1, OUTER):
            z_copy(u, d).wait_send()
            o_copy(u, d).wait_send()
            o_copy(u, d).wait_recv()
        for s in range(1, n):
            for d in range(OUTER):
                x_copy(u, s, d).wait_send()
        return carry

    lax.fori_loop(0, units, finish, 0)


def attention_forward(n, lengths, table, onehot, inputs, gain, wq, wk, wv):
    batch, height, width = inputs.shape
    units, nk = batch * HEADS, n * OUTER
    dma = pltpu.SemaphoreType.DMA
    return pl.pallas_call(
        functools.partial(forward_kernel, n),
        in_specs=[smem()] + [whole()] * 7,
        out_specs=[whole()] * 8,
        out_shape=[
            jax.ShapeDtypeStruct((batch, width, height), BF16),
            jax.ShapeDtypeStruct((units, OUTER, 3 * DH, BLK), BF16),
            jax.ShapeDtypeStruct((n - 1, units, OUTER, 2 * DH, BLK), BF16),
            jax.ShapeDtypeStruct((batch, width, height), BF16),
            jax.ShapeDtypeStruct((units, OUTER, DH, BLK), BF16),
            jax.ShapeDtypeStruct((units, OUTER, 1, BLK), F32),
            jax.ShapeDtypeStruct((HEADS, TILES, BLK, BLK), F32),
            jax.ShapeDtypeStruct((HEADS, 2, 1, BLK), F32),
        ],
        scratch_shapes=[
            pltpu.VMEM((units, OUTER, 3 * DH, BLK), BF16),
            pltpu.VMEM((nk, BLK, AUG), BF16),
            pltpu.VMEM((3, OUTER, AUG, BLK), BF16),
            pltpu.VMEM((AUG, nk * BLK), BF16),
            dma((units, OUTER - 1)),
            dma((units, OUTER - 1)),
            dma((n - 1, units, OUTER)),
            dma((n - 1, units, OUTER)),
            dma((units, OUTER - 1)),
            dma((units, OUTER - 1)),
        ],
        compiler_params=pltpu.CompilerParams(
            vmem_limit_bytes=VMEM_BYTES, collective_id=0, has_side_effects=True
        ),
        cost_estimate=pl.CostEstimate(flops=45 * 10**9, bytes_accessed=24 << 20, transcendentals=0),
        name="attention_forward",
    )(lengths, table, onehot, inputs, gain.reshape(1, -1), wq, wk, wv)


def backward_kernel(
    n, early, len_ref, far_ref, tile_ref, own, pair, o_ref, lse_ref, dout, *refs
):
    count = len(early.shapes)
    weights, refs = refs[:count], refs[count:]
    (grads, near, far_sum, parts, own_slot, pair_slot, load_sem,
    do_land, x_out, x_land, z_out, kept,
    ka, kt, va, qa, da, dk_all, dv_all,
    d_send, d_recv, x_send, x_recv, z_send, z_recv) = refs[: -Scatter.count]
    scatter = Scatter(early, (True, True))
    scatter.bind(weights, refs[-Scatter.count :])
    nk = OUTER * n
    batch = dout.shape[0]
    units = batch * HEADS
    x_slots, z_slots = staging(n, units)
    me = lax.axis_index("seq")
    z, x = lax.div(me, n), lax.rem(me, n)
    greet_all(early.p)
    scatter.step_core()

    def head_rows(group, h):
        return pl.ds(pl.multiple_of((group * HEADS + h) * DH, DH), DH)

    def d_copy(u, d):
        group = lax.rem(z + d, OUTER)
        b, h = lax.div(u, HEADS), lax.rem(u, HEADS)
        sems = d_send.at[u, d - 1], d_recv.at[u, d - 1]
        return remote(dout.at[b, head_rows(group, h)], do_land.at[u, z], sems, seq=group * n + x)

    def x_copy(u, s):
        peer = z * n + lax.rem(x + s, n)
        sems = x_send.at[s - 1, u], x_recv.at[s - 1, u]
        return remote(x_out.at[s - 1, lax.rem(u, x_slots)], x_land.at[s - 1, u], sems, seq=peer)

    def z_copy(u, d, i):
        group = lax.rem(z + d, OUTER)
        b, h = lax.div(u, HEADS), lax.rem(u, HEADS)
        sems = z_send.at[u, d - 1, i], z_recv.at[u, d - 1, i]
        src, dst = z_out.at[lax.rem(u, z_slots), group, pl.ds(i * DH, DH)], grads.at[i, b, head_rows(z, h)]
        return remote(src, dst, sems, seq=group * n + x)

    def loads(u):
        slot = lax.rem(u, 2)
        yield pltpu.make_async_copy(own.at[u], own_slot.at[slot], load_sem.at[slot, 0])
        for s in range(1, n):
            yield pltpu.make_async_copy(pair.at[s - 1, u], pair_slot.at[slot, s - 1], load_sem.at[slot, s])

    for c in loads(0):
        c.start()

    def begin(u, carry):
        for d in (2, 1, 3):
            d_copy(u, d).start()
        do_land[u, z] = dout[lax.div(u, HEADS), head_rows(z, lax.rem(u, HEADS))]
        return carry

    lax.fori_loop(0, units, begin, 0)
    near[...] = jnp.zeros_like(near)
    far_sum[...] = jnp.zeros_like(far_sum)
    one = jnp.ones((1, BLK), F32)
    ones3 = tail(BLK, (one, one, one)).astype(BF16)
    row16 = lax.broadcasted_iota(jnp.int32, (16, BLK), 0)
    marks = [jnp.where(row16 == r, 1.0, 0.0).astype(BF16) for r in range(2)]

    def work(u):
        b, h = lax.div(u, HEADS), lax.rem(u, HEADS)
        length = len_ref[b]
        left, right = far_ref[h, 0], far_ref[h, 1]
        slot = lax.rem(u, 2)
        for c in loads(u):
            c.wait()

        @pl.when(u + 1 < units)
        def _():
            for c in loads(u + 1):
                c.start()

        for s in range(n):
            col = lax.rem(x + s, n)
            for j in range(OUTER):
                kb = n * j + col
                if s == 0:
                    keys, vals = own_slot[slot, j, DH : 2 * DH], own_slot[slot, j, 2 * DH :]
                else:
                    keys, vals = pair_slot[slot, n - s - 1, j, :DH], pair_slot[slot, n - s - 1, j, DH:]
                ka[kb] = key_rows(keys, kb, length)
                kt[kb] = keys
                va[kb] = jnp.concatenate([vals, ones3], axis=0).T
        for d in range(1, OUTER):
            d_copy(u, d).wait_recv()
        for j in range(OUTER):
            lse = lse_ref[u, j]
            for v, c in enumerate((left, 0.0, right)):
                qa[v, j, :DH] = own_slot[slot, j, :DH]
                qa[v, j, DH:] = tail(BLK, split3(c - lse) + (one,)).astype(BF16)
            arrived = do_land[u, j]
            delta = jnp.sum(arrived.astype(F32) * o_ref[u, j].astype(F32), axis=0, keepdims=True)
            da[j, :DH] = arrived
            da[j, DH:] = tail(BLK, split3(-delta)).astype(BF16)
        dqs = [None] * OUTER
        for g in range(0, nk, GROUP):
            blocks = range(g, g + GROUP)
            ps, dss = {}, {}
            for j in range(OUTER):
                left_side = []
                for kb in blocks:
                    case = far_case(n, j, kb)
                    if case is not None:
                        p = jnp.exp2(jnp.dot(ka[kb], qa[case, j], preferred_element_type=F32))
                        mark = marks[case // 2]
                    else:
                        tile, case = near_case(n, j, kb, x)
                        s = jnp.dot(ka[kb], qa[case, j], preferred_element_type=F32)
                        p = jnp.exp2(s + tile_ref[h, tile])
                        want = jnp.where(case == 1, 2, lax.div(case, 2))
                        mark = jnp.where(row16 == want, 1.0, 0.0).astype(BF16)
                    ds = p * jnp.dot(va[kb], da[j], preferred_element_type=F32)
                    if far_case(n, j, kb) is None:
                        near[h, tile] += ds
                    ps[kb, j], dss[kb, j] = p.astype(BF16), ds.astype(BF16)
                    left_side.append(jnp.concatenate([kt[kb], mark], axis=0))
                right_side = jnp.concatenate([dss[kb, j] for kb in blocks], axis=0)
                dq = jnp.dot(jnp.concatenate(left_side, axis=1), right_side, preferred_element_type=F32)
                dqs[j] = dq if g == 0 else dqs[j] + dq
            for kb in blocks:
                dv, dk = jnp.zeros((DH, BLK), F32), jnp.zeros((DH, BLK), F32)
                for j in range(OUTER):
                    dv = dv + lax.dot_general(da[j, :DH], ps[kb, j], NT, preferred_element_type=F32)
                    dk = dk + lax.dot_general(qa[0, j, :DH], dss[kb, j], NT, preferred_element_type=F32)
                dk_all[kb] = dk * LN2
                dv_all[kb] = dv
        @pl.when(u >= z_slots)
        def _():
            for d in range(1, OUTER):
                for i in range(3):
                    z_copy(u - z_slots, d, i).wait_send()

        @pl.when(u >= x_slots)
        def _():
            for s in range(1, n):
                x_copy(u - x_slots, s).wait_send()

        far = jnp.zeros((8, BLK), F32)
        for j in range(OUTER):
            z_out[lax.rem(u, z_slots), j, :DH] = dqs[j][:DH].astype(BF16)
            far = far + dqs[j][DH : DH + 8]
        far_sum[h] += far
        parity = lax.rem(u, 2)
        for j in range(OUTER):
            kept[parity, j, :DH] = dk_all[n * j + x]
            kept[parity, j, DH:] = dv_all[n * j + x]
            for s in range(1, n):
                kb = n * j + lax.rem(x + s, n)
                x_out[s - 1, lax.rem(u, x_slots), j, :DH] = dk_all[kb].astype(BF16)
                x_out[s - 1, lax.rem(u, x_slots), j, DH:] = dv_all[kb].astype(BF16)
        for s in range(1, n):
            x_copy(u, s).start()

    def hand_over(u):
        b, h = lax.div(u, HEADS), lax.rem(u, HEADS)
        parity = lax.rem(u, 2)
        for s in range(1, n):
            x_copy(u, s).wait_recv()
        for j in range(OUTER):
            total = kept[parity, j]
            for s in range(1, n):
                total = total + x_land[s - 1, u, j].astype(F32)
            z_out[lax.rem(u, z_slots), j, DH:] = total.astype(BF16)
        for i in range(3):
            grads[i, b, head_rows(z, h)] = z_out[lax.rem(u, z_slots), z, i * DH : (i + 1) * DH]
            for d in (2, 1, 3):
                z_copy(u, d, i).start()

    def turn(u, carry):
        @pl.when(u < units)
        def _():
            work(u)

        @pl.when(u > 0)
        def _():
            hand_over(u - 1)

        pl.when(u == 0)(scatter.step_first)
        for line in range(2):
            pl.when(u == 4 + 3 * line)(functools.partial(scatter.step_second, line))

        return carry

    lax.fori_loop(0, units + 1, turn, 0)

    def finish(u, carry):
        for d in range(1, OUTER):
            d_copy(u, d).wait_send()
            for i in range(3):
                z_copy(u, d, i).wait_recv()

                @pl.when(u >= units - z_slots)
                def _():
                    z_copy(u, d, i).wait_send()

        @pl.when(u >= units - x_slots)
        def _():
            for s in range(1, n):
                x_copy(u, s).wait_send()

        return carry

    lax.fori_loop(0, units, finish, 0)
    for line in range(2):
        scatter.step_third(line)
        parts[line] = scatter.part(line)[...]
    scatter.end()


def staging(n, units):
    return (units, units) if n <= 2 else (2, 4)


def attention_backward(n, early, lengths, far, tiles, own, pair, out, lse, dout, weights):
    batch, width, height = dout.shape
    units, nk = batch * HEADS, n * OUTER
    dma = pltpu.SemaphoreType.DMA
    x_slots, z_slots = staging(n, units)
    return pl.pallas_call(
        functools.partial(backward_kernel, n, early),
        in_specs=[smem()] + [whole()] * 2 + [anywhere()] * 2 + [whole()] * 3 + [anywhere()] * len(weights),
        out_specs=[whole()] * 4,
        out_shape=[
            jax.ShapeDtypeStruct((3, batch, width, height), BF16),
            jax.ShapeDtypeStruct((HEADS, TILES, BLK, BLK), F32),
            jax.ShapeDtypeStruct((HEADS, 8, BLK), F32),
            jax.ShapeDtypeStruct((2, early.size, LANES), BF16),
        ],
        scratch_shapes=[
            pltpu.VMEM((2, OUTER, 3 * DH, BLK), BF16),
            pltpu.VMEM((2, n - 1, OUTER, 2 * DH, BLK), BF16),
            dma((2, n)),
            pltpu.VMEM((units, OUTER, DH, BLK), BF16),
            pltpu.VMEM((n - 1, x_slots, OUTER, 2 * DH, BLK), BF16),
            pltpu.VMEM((n - 1, units, OUTER, 2 * DH, BLK), BF16),
            pltpu.VMEM((z_slots, OUTER, 3 * DH, BLK), BF16),
            pltpu.VMEM((2, OUTER, 2 * DH, BLK), F32),
            pltpu.VMEM((nk, BLK, AUG), BF16),
            pltpu.VMEM((nk, DH, BLK), BF16),
            pltpu.VMEM((nk, BLK, AUG), BF16),
            pltpu.VMEM((3, OUTER, AUG, BLK), BF16),
            pltpu.VMEM((OUTER, AUG, BLK), BF16),
            pltpu.VMEM((nk, DH, BLK), F32),
            pltpu.VMEM((nk, DH, BLK), F32),
            dma((units, OUTER - 1)),
            dma((units, OUTER - 1)),
            dma((n - 1, units)),
            dma((n - 1, units)),
            dma((units, OUTER - 1, 3)),
            dma((units, OUTER - 1, 3)),
        ]
        + Scatter(early, (True, True)).scratch(),
        compiler_params=pltpu.CompilerParams(
            vmem_limit_bytes=VMEM_BYTES, collective_id=1, has_side_effects=True
        ),
        cost_estimate=pl.CostEstimate(flops=110 * 10**9, bytes_accessed=24 << 20, transcendentals=0),
        name="attention_backward",
    )(lengths, far, tiles, own, pair, out, lse, dout, *weights)


FF_STEP = 512


def middle_kernel(
    x_ref, att_ref, cot_ref, gain_ref, w_out, w_gate, w_up, w_down,
    result, grad_mixed, dout, d_gain, d_out, d_gate, d_up, d_down,
    wo, wg, wu, wd, att, low, hidden, g_gate, g_up, s_out, s_gate, s_up, s_down, kept, in_sem, out_sem,
):
    tokens, width = x_ref.shape
    batch = att_ref.shape[0]
    ff = w_gate.shape[1]
    loads = [
        pltpu.make_async_copy(src, dst, in_sem.at[i])
        for i, (src, dst) in enumerate(((w_out, wo), (w_gate, wg), (w_up, wu), (w_down, wd)))
    ]
    stores = [
        pltpu.make_async_copy(src, dst, out_sem.at[i])
        for i, (src, dst) in enumerate(((s_out, d_out), (s_gate, d_gate), (s_up, d_up), (s_down, d_down)))
    ]
    for c in loads:
        c.start()
    height = tokens // batch
    for b in range(batch):
        att[b * height : (b + 1) * height] = att_ref[b].T
    low[...] = cot_ref[...].astype(BF16)
    loads[0].wait()
    mixed = x_ref[...] + jnp.dot(att[...], wo[...], preferred_element_type=F32)
    kept[...] = mixed
    result[...] = mixed
    scale = lax.rsqrt(jnp.mean(mixed * mixed, axis=-1, keepdims=True) + epsilon)
    normed = (mixed * scale * gain_ref[...]).astype(BF16)
    att[...] = normed
    for c in loads[1:]:
        c.wait()
    root = 0.7978845608028654
    for at in range(0, ff, FF_STEP):
        part = slice(at, at + FF_STEP)
        gate = jnp.dot(att[...], wg[:, part], preferred_element_type=F32)
        upward = jnp.dot(att[...], wu[:, part], preferred_element_type=F32)
        g_hidden = lax.dot_general(low[...], wd[part], NT, preferred_element_type=F32)
        square = gate * gate
        t = jnp.tanh(root * gate * (1.0 + 0.044715 * square))
        half = 0.5 * (1.0 + t)
        act = gate * half
        slope = half + 0.5 * gate * (1.0 - t * t) * (root * (1.0 + 3.0 * 0.044715 * square))
        hidden[:, part] = (act * upward).astype(BF16)
        g_gate[:, part] = (g_hidden * upward * slope).astype(BF16)
        g_up[:, part] = (g_hidden * act).astype(BF16)
    result[...] += jnp.dot(hidden[...], wd[...], preferred_element_type=F32)
    d_normed = lax.dot_general(g_gate[...], wg[...], NT, preferred_element_type=F32)
    d_normed = d_normed + lax.dot_general(g_up[...], wu[...], NT, preferred_element_type=F32)
    mixed = kept[...]
    scale = lax.rsqrt(jnp.mean(mixed * mixed, axis=-1, keepdims=True) + epsilon)
    d_gain[...] = jnp.sum(d_normed * mixed * scale, axis=0, keepdims=True)
    u = d_normed * gain_ref[...]
    along = jnp.mean(u * mixed, axis=-1, keepdims=True)
    d_mixed = cot_ref[...] + scale * (u - mixed * (scale * scale * along))
    grad_mixed[...] = d_mixed
    d_low = d_mixed.astype(BF16)
    turned = lax.dot_general(wo[...], d_low, NT, preferred_element_type=F32).astype(BF16)
    for b in range(batch):
        dout[b] = turned[:, b * height : (b + 1) * height]
    total = jnp.zeros((width, width), F32)
    for b in range(batch):
        total = total + jnp.dot(att_ref[b], d_low[b * height : (b + 1) * height], preferred_element_type=F32)
    s_out[...] = total.astype(BF16)
    stores[0].start()
    normed_t = att[...].T
    for src, dst, store in ((g_gate, s_gate, stores[1]), (g_up, s_up, stores[2])):
        for at in range(0, ff, FF_STEP):
            part = slice(at, at + FF_STEP)
            dst[:, part] = jnp.dot(normed_t, src[:, part], preferred_element_type=F32).astype(BF16)
        store.start()
    for at in range(0, ff, FF_STEP):
        part = slice(at, at + FF_STEP)
        s_down[part] = jnp.dot(hidden[:, part].T, low[...], preferred_element_type=F32).astype(BF16)
    stores[3].start()
    for c in stores:
        c.wait()


def middle(inputs, att, cotangent, gain, w_out, w_gate, w_up, w_down):
    batch, height, width = inputs.shape
    tokens, ff = batch * height, w_gate.shape[1]
    weights = (w_out, w_gate, w_up, w_down)
    flat = (tokens, width)
    out = pl.pallas_call(
        middle_kernel,
        in_specs=[whole()] * 4 + [anywhere()] * 4,
        out_specs=[whole()] * 4 + [anywhere()] * 4,
        out_shape=[
            jax.ShapeDtypeStruct(flat, F32),
            jax.ShapeDtypeStruct(flat, F32),
            jax.ShapeDtypeStruct((batch, width, height), BF16),
            jax.ShapeDtypeStruct((1, width), F32),
        ]
        + [jax.ShapeDtypeStruct(w.shape, BF16) for w in weights],
        scratch_shapes=[pltpu.VMEM(w.shape, BF16) for w in weights]
        + [pltpu.VMEM(flat, BF16)] * 2
        + [pltpu.VMEM((tokens, ff), BF16)] * 3
        + [pltpu.VMEM(w.shape, BF16) for w in weights]
        + [pltpu.VMEM(flat, F32)]
        + [pltpu.SemaphoreType.DMA((4,))] * 2,
        compiler_params=params(),
        cost_estimate=pl.CostEstimate(flops=25 * 10**9, bytes_accessed=32 << 20, transcendentals=0),
        name="middle",
    )(inputs.reshape(flat), att, cotangent.reshape(flat), gain.reshape(1, -1), *weights)
    return out[0].reshape(inputs.shape), out[1].reshape(inputs.shape), out[2], out[3], out[4:]


def shards(
    places,
    inputs,
    lengths,
    norm_attn,
    w_query,
    w_key,
    w_value,
    w_out,
    norm_ffn,
    w_gate,
    w_up,
    w_down,
    bucket_bias,
    cotangent,
):
    batch, height, width = inputs.shape
    n = places.inner
    onehot = jnp.asarray(ONEHOT)
    normed_t, own, pair, attended_t, out, lse, tiles, far = attention_forward(
        n, lengths, bucket_bias, onehot, inputs, norm_attn, w_query, w_key, w_value
    )
    result, grad_mixed, grad_attended_t, grad_norm_ffn, weights = middle(
        inputs, attended_t, cotangent, norm_ffn, w_out, w_gate, w_up, w_down
    )
    early = Rows(places, [g.shape for g in weights])
    grads, near, far_sum, parts = attention_backward(
        n, early, lengths, far, tiles, own, pair, out, lse, grad_attended_t, weights
    )
    shapes = [w_query.shape, w_key.shape, w_value.shape, (places.dp * SMALL, LANES)]
    late = Rows(places, shapes)
    loaded = (
        parts, grads, normed_t, w_query, w_key, w_value, inputs, grad_mixed, near, far_sum, onehot
    )
    grad_inputs, full_early, full_late = last_grads(early, late, loaded, norm_attn, grad_norm_ffn)
    part_out, part_gate, part_up, part_down, part_query, part_key, part_value, part_attn, part_ffn, part_table = unpack(
        (early, late), (full_early, full_late), width
    )
    return (
        result,
        grad_inputs,
        part_attn.reshape(-1),
        part_ffn.reshape(-1),
        part_query,
        part_key,
        part_value,
        part_out,
        part_gate,
        part_up,
        part_down,
        part_table,
    )


def solution(mesh):
    rows = P("dp", "seq", None)
    share = P("dp", None)
    return jax.shard_map(
        functools.partial(shards, Places(mesh)),
        mesh=mesh,
        in_specs=(rows, P("dp")) + (P(),) * 10 + (rows,),
        out_specs=(rows, rows, P("dp"), P("dp")) + (share,) * 8,
        check_vma=False,
    )
```

```python
import functools

import jax
import jax.numpy as jnp
import numpy as np
from jax import lax
from jax.experimental import pallas as pl
from jax.experimental.pallas import tpu as pltpu
from jax.sharding import PartitionSpec as P

H = 12
DH = 64
NB = 32
OUTER = 4
HEADS = H // OUTER
HW = HEADS * DH
HALF = 2 * HW
BLK = 256
AUG = DH + 16
SPAN = 4 * BLK
LANES = 256
LANE = 128
LOG2E = 1.4426950408889634
LN2 = 0.6931471805599453
F32 = jnp.float32
BF16 = jnp.bfloat16
NT = (((1,), (1,)), ((), ()))
VMEM_BYTES = 62 << 20
GROUP = 8
TILES = 4

epsilon = 1e-06
limits = (1, 2, 3, 4, 5, 6, 7, 8, 12, 16, 23, 32, 46, 64, 91)
highest = lax.Precision.HIGHEST


def bucket_lines():
    relative = 2 * BLK - 1 - np.arange(SPAN)
    count = sum((np.abs(relative) >= limit).astype(np.int32) for limit in limits)
    bucket = count + (relative > 0).astype(np.int32) * (NB // 2)
    return (bucket[None, :] == np.arange(NB)[:, None]).astype(np.float32)


ONEHOT = bucket_lines()


def params():
    return pltpu.CompilerParams(vmem_limit_bytes=VMEM_BYTES)


def smem():
    return pl.BlockSpec(memory_space=pltpu.SMEM)


def anywhere():
    return pl.BlockSpec(memory_space=pl.ANY)


def whole():
    return pl.BlockSpec(memory_space=pltpu.VMEM)


def split3(v):
    a = v.astype(BF16)
    r = v - a.astype(F32)
    b = r.astype(BF16)
    c = (r - b.astype(F32)).astype(BF16)
    return a.astype(F32), b.astype(F32), c.astype(F32)


def tail(width, values):
    row = lax.broadcasted_iota(jnp.int32, (16, width), 0)
    out = jnp.zeros((16, width), F32)
    for i, v in enumerate(values):
        out = jnp.where(row == i, v, out)
    return out


def peers(n, z, x):
    return [lax.rem(z + d, OUTER) * n + x for d in range(1, OUTER)] + [z * n + lax.rem(x + s, n) for s in range(1, n)]


def around(z):
    near = z + 1 - 2 * lax.rem(z, 2)
    return near, lax.rem(z + 2, OUTER), lax.rem(near + 2, OUTER)


class Places:
    def __init__(self, mesh):
        self.dp = mesh.shape["dp"]
        self.groups = self.dp // 2
        self.inner = mesh.shape["seq"] // OUTER


def remote(src, dst, sems, **peer):
    return pltpu.make_async_remote_copy(
        src_ref=src,
        dst_ref=dst,
        send_sem=sems[0],
        recv_sem=sems[1],
        device_id=peer,
        device_id_type=pl.DeviceIdType.MESH,
    )


class Rows:
    def __init__(self, places, shapes, lanes, lines):
        self.p = places
        self.shapes = shapes
        self.lanes = lanes
        self.lines = range(lines)
        grain = places.inner * OUTER * 16
        self.blocks = []
        at = 0
        for m, (rows, columns) in enumerate(shapes):
            share = rows // places.dp
            for block in range(columns // lanes):
                self.blocks.append((m, block, at, share))
                at += share
        self.used = at
        grains = max(-(-at // grain), lines)
        self.total = grains * grain
        cuts = [grains * line // lines * grain for line in range(lines + 1)]
        self.start = cuts[:-1]
        self.span = [b - a for a, b in zip(cuts[:-1], cuts[1:])]
        self.size = [v // places.inner for v in self.span]
        self.small = [v // OUTER for v in self.size]
        self.part_start = [v // places.inner for v in self.start]
        self.part_total = self.total // places.inner

    def line(self, line):
        return pl.ds(self.start[line], self.span[line])

    def part(self, line, x):
        return pl.ds(pl.multiple_of(self.start[line] + x * self.size[line], 16), self.size[line])

    def quarter(self, line, x, z):
        first = self.start[line] + x * self.size[line] + z * self.small[line]
        return pl.ds(pl.multiple_of(first, 16), self.small[line])


def add_to(ref, arrived):
    if len(arrived) == 1:
        ref[...] = ref[...] + arrived[0]
        return
    total = ref[...].astype(F32)
    for a in arrived:
        total = total + a.astype(F32)
    ref[...] = total.astype(BF16)


class Scatter:
    def __init__(self, rows, y_first):
        self.rows = rows
        self.y_first = y_first
        self.count = 5 + 2 * len(rows.lines)

    def scratch(self):
        r, p, dma = self.rows, self.rows.p, pltpu.SemaphoreType.DMA
        g, n, lines = p.groups, p.inner, len(r.lines)
        out = [pltpu.VMEM((g, r.total, r.lanes), BF16), pltpu.VMEM((g, r.total, r.lanes), BF16)]
        for line, y_first in enumerate(self.y_first):
            out.append(pltpu.VMEM((g - 1, r.span[line] if y_first else r.size[line], r.lanes), BF16))
            out.append(pltpu.VMEM((n - 1, 1 if y_first else g, r.size[line], r.lanes), BF16))
        return out + [dma((len(r.blocks), g, 3)), dma((lines, g - 1, 2)), dma((lines, n - 1, g, 2))]

    def bind(self, grads, refs):
        self.grads = grads
        self.held, self.land = refs[:2]
        self.c_sem, self.y_sem, self.x_sem = refs[-3:]
        self.y_land, self.x_land = refs[2:-3:2], refs[3:-3:2]
        dp, seq = lax.axis_index("dp"), lax.axis_index("seq")
        n = self.rows.p.inner
        self.core, self.group = lax.rem(dp, 2), lax.div(dp, 2)
        self.z, self.x = lax.div(seq, n), lax.rem(seq, n)

    def source(self, i, g, core):
        m, block, at, share = self.rows.blocks[i]
        first = pl.multiple_of((g * 2 + core) * share, 16)
        return self.grads[m].at[pl.ds(first, share), pl.ds(block * self.rows.lanes, self.rows.lanes)], pl.ds(at, share)

    def picked(self, chosen):
        return [i for i, b in enumerate(self.rows.blocks) if chosen is None or b[0] in chosen]

    def core_copies(self, chosen=None):
        for i in self.picked(chosen):
            for g in range(self.rows.p.groups):
                src, where = self.source(i, g, 1 - self.core)
                sems = self.c_sem.at[i, g, 0], self.c_sem.at[i, g, 1]
                yield remote(src, self.land.at[g, where], sems, dp=self.group * 2 + 1 - self.core)

    def own_copies(self, chosen=None):
        for i in self.picked(chosen):
            for g in range(self.rows.p.groups):
                src, where = self.source(i, g, self.core)
                yield pltpu.make_async_copy(src, self.held.at[g, where], self.c_sem.at[i, g, 2])

    def y_copies(self, line):
        r = self.rows
        for t in range(1, r.p.groups):
            other = lax.rem(self.group + t, r.p.groups)
            where = r.line(line) if self.y_first[line] else r.part(line, self.x)
            sems = self.y_sem.at[line, t - 1, 0], self.y_sem.at[line, t - 1, 1]
            yield remote(self.held.at[other, where], self.y_land[line].at[t - 1], sems, dp=other * 2 + self.core)

    def x_copies(self, line):
        r = self.rows
        n = r.p.inner
        for s in range(1, n):
            other = lax.rem(self.x + s, n)
            where = r.part(line, other)
            for g in range(1 if self.y_first[line] else r.p.groups):
                sems = self.x_sem.at[line, s - 1, g, 0], self.x_sem.at[line, s - 1, g, 1]
                src = self.held.at[self.group if self.y_first[line] else g, where]
                yield remote(src, self.x_land[line].at[s - 1, g], sems, seq=self.z * n + other)

    def hop(self, line, which):
        return self.y_copies(line) if (which == 0) == self.y_first[line] else self.x_copies(line)


    def step_core(self, chosen=None):
        for c in self.core_copies(chosen):
            c.start()
        for c in self.own_copies(chosen):
            c.start()

    def step_first(self, begin):
        r = self.rows
        for c in self.core_copies():
            c.wait_recv()
        for c in self.own_copies():
            c.wait()
        for line in r.lines:
            end = r.start[line] + r.span[line]
            first, last = r.start[line], min(end, r.used)
            for g in range(r.p.groups):
                where = pl.ds(first, last - first)
                add_to(self.held.at[g, where], [self.land[g, where]])
                if last < end:
                    self.held[g, last:end] = jnp.zeros((end - last, r.lanes), BF16)
            if line in begin:
                self.start_first(line)

    def start_first(self, line):
        for c in self.hop(line, 0):
            c.start()

    def step_second(self, line):
        r = self.rows
        for c in self.hop(line, 0):
            c.wait_recv()
        if self.y_first[line]:
            arrived = [self.y_land[line][t] for t in range(r.p.groups - 1)]
            add_to(self.held.at[self.group, r.line(line)], arrived)
        else:
            for g in range(r.p.groups):
                arrived = [self.x_land[line][s, g] for s in range(r.p.inner - 1)]
                add_to(self.held.at[g, r.part(line, self.x)], arrived)
        for c in self.hop(line, 1):
            c.start()

    def step_third(self, line):
        r = self.rows
        for c in self.hop(line, 1):
            c.wait_recv()
        if self.y_first[line]:
            arrived = [self.x_land[line][s, 0] for s in range(r.p.inner - 1)]
        else:
            arrived = [self.y_land[line][t] for t in range(r.p.groups - 1)]
        add_to(self.held.at[self.group, r.part(line, self.x)], arrived)

    def part(self, line):
        return self.held.at[self.group, self.rows.part(line, self.x)]

    def end(self):
        for c in self.core_copies():
            c.wait_send()
        for line in self.rows.lines:
            for which in range(2):
                for c in self.hop(line, which):
                    c.wait_send()


class Spread:
    def __init__(self, rows, halves=False):
        self.rows = rows
        self.halves = halves

    def scratch(self):
        r, dma = self.rows, pltpu.SemaphoreType.DMA
        lines = len(r.lines)
        land = (lines, 1, max(r.size) // 2, r.lanes) if self.halves else (lines, 3, max(r.small), r.lanes)
        sems = dma((lines, 3, 2))
        return [pltpu.VMEM(land, BF16), sems, sems, dma((lines, OUTER, r.p.inner - 1, 2))]

    count = 4

    def bind(self, piece, target, refs):
        self.piece, self.target = piece, target
        self.land, self.s_sem, self.g_sem, self.x_sem = refs
        seq = lax.axis_index("seq")
        n = self.rows.p.inner
        self.z, self.x = lax.div(seq, n), lax.rem(seq, n)
        self.near, self.two, self.across = around(self.z)

    def copy(self, src, dst, sems, group):
        return remote(src, dst, sems, seq=group * self.rows.p.inner + self.x)

    def sum_copy(self, line, i):
        piece = self.piece(line, (self.near, self.across, self.two)[i])
        sems = self.s_sem.at[line, i, 0], self.s_sem.at[line, i, 1]
        return self.copy(piece, self.landing(line, i), sems, self.two if i == 2 else self.near)

    def landing(self, line, i):
        rows = self.rows.size[line] // 2 if self.halves else self.rows.small[line]
        return self.land.at[line, i, pl.ds(0, rows)]

    def sums(self, line):
        return [self.sum_copy(line, i) for i in range(1 if self.halves else 3)]

    def z_copy(self, line, i):
        where = self.target(line, self.two if i == 2 else self.z)
        sems = self.g_sem.at[line, i, 0], self.g_sem.at[line, i, 1]
        return self.copy(where, where, sems, self.two if i == 0 else self.near)

    def x_copies(self, line, c):
        n = self.rows.p.inner
        where = self.target(line, c)
        for s in range(1, n):
            sems = self.x_sem.at[line, c, s - 1, 0], self.x_sem.at[line, c, s - 1, 1]
            yield remote(where, where, sems, seq=self.z * n + lax.rem(self.x + s, n))

    def spread(self, line, c):
        for s in self.x_copies(line, c):
            s.start()

    def step_pair(self, line):
        self.sum_copy(line, 0).start()
        if not self.halves:
            self.sum_copy(line, 1).start()

    def step_two(self, line):
        for i, c in ((0, self.z), (1, self.two)):
            self.sum_copy(line, i).wait_recv()
            add_to(self.piece(line, c), [self.landing(line, i)[...]])
        self.sum_copy(line, 2).start()

    def step_back(self, line):
        last = 0 if self.halves else 2
        self.sum_copy(line, last).wait_recv()
        self.target(line, self.z)[...] = self.piece(line, self.z)[...] + self.landing(line, last)[...]
        self.z_copy(line, 0).start()
        self.z_copy(line, 1).start()
        self.spread(line, self.z)

    def step_rest(self, line):
        self.z_copy(line, 0).wait_recv()
        self.z_copy(line, 2).start()
        self.spread(line, self.two)
        self.z_copy(line, 1).wait_recv()
        self.spread(line, self.near)

    def step_last(self, line):
        self.z_copy(line, 2).wait_recv()
        self.spread(line, self.across)

    def end(self):
        for line in self.rows.lines:
            for c in range(OUTER):
                for s in self.x_copies(line, c):
                    s.wait_send()
                    s.wait_recv()
            for c in self.sums(line):
                c.wait_send()
            for i in range(3):
                self.z_copy(line, i).wait_send()


def greet_all(places):
    dp, seq = lax.axis_index("dp"), lax.axis_index("seq")
    n = places.inner
    core, group = lax.rem(dp, 2), lax.div(dp, 2)
    barrier = pltpu.get_barrier_semaphore()
    mesh = pl.DeviceIdType.MESH
    pl.semaphore_signal(barrier, inc=1, device_id={"dp": group * 2 + 1 - core}, device_id_type=mesh)
    for t in range(1, places.groups):
        other = lax.rem(group + t, places.groups) * 2 + core
        pl.semaphore_signal(barrier, inc=1, device_id={"dp": other}, device_id_type=mesh)
    for peer in peers(n, lax.div(seq, n), lax.rem(seq, n)):
        pl.semaphore_signal(barrier, inc=1, device_id={"seq": peer}, device_id_type=mesh)
    pl.semaphore_wait(barrier, 1 + places.groups - 1 + OUTER - 1 + n - 1)


SMALL = 16


def last_kernel(early, late, *refs):
    count = 13
    sources, (gain_ref, ffn_ref), refs = refs[:count], refs[count : count + 2], refs[count + 2 :]
    grad_in, full_early, full_late, refs = refs[0], refs[1], refs[2], refs[3:]
    slots, load_sem, refs = refs[:count], refs[count], refs[count + 1 :]
    p = late.p
    scatter, spread_early, spread_late = Scatter(late, (True, False)), Spread(early), Spread(late, True)
    (gq, gk, gv, small, arriving, n_sem), refs = refs[:6], refs[6:]
    scatter.bind((gq, gk, gv, small), refs[: scatter.count])
    refs = refs[scatter.count :]
    z, x = scatter.z, scatter.x
    columns = half_columns(z)
    loads = []
    for i, (src, dst) in enumerate(zip(sources, slots)):
        loads.append(pltpu.make_async_copy(src.at[:, columns] if 3 <= i < 6 else src, dst, load_sem.at[i]))
    for c in loads:
        c.start()
    held, grads, normed_t, wq_ref, wk_ref, wv_ref, x_ref, mixed_ref, near, far_sum, onehot, other, leaving = slots

    def early_piece(line, c):
        first = pl.multiple_of(early.part_start[line] + c * early.small[line], 16)
        return held.at[pl.ds(first, early.small[line])]

    def late_rows(line, c):
        size = late.size[line] // 2
        first = late.start[line] + x * late.size[line] + lax.rem(c, 2) * size
        return pl.ds(pl.multiple_of(first, 16), size)

    spread_early.bind(early_piece, lambda line, c: full_early.at[early.quarter(line, x, c)], refs[: Spread.count])
    spread_late.bind(
        lambda line, c: scatter.held.at[scatter.group, late_rows(line, c)],
        lambda line, c: full_late.at[lax.div(c, 2), late_rows(line, c)],
        refs[Spread.count :],
    )
    two = spread_early.two
    n_copy = remote(leaving, arriving, (n_sem.at[0], n_sem.at[1]), seq=two * p.inner + x)
    greet_all(p)
    loads[0].wait()
    loads[-1].wait()
    n_copy.start()
    for line in early.lines:
        spread_early.step_pair(line)
    for c in loads[1:-1]:
        c.wait()
    batch, height, width = x_ref.shape
    for i, out in enumerate((gq, gk, gv)):
        total = jnp.zeros((width, HALF), F32)
        for b in range(batch):
            for block in range(2):
                total = total + lax.dot_general(normed_t[block, b], grads[i, b, block], NT, preferred_element_type=F32)
        out[...] = total.astype(BF16)
        scatter.step_core((i,))
    gain = gain_ref[...]
    gain_sum = jnp.zeros((1, width), F32)
    for b in range(batch):
        back = jnp.dot(wq_ref[...], grads[0, b, 0], preferred_element_type=F32)
        back = back + jnp.dot(wk_ref[...], grads[1, b, 0], preferred_element_type=F32)
        back = back + jnp.dot(wv_ref[...], grads[2, b, 0], preferred_element_type=F32)
        if b == batch - 1:
            n_copy.wait_recv()
        back = (back + (arriving if b == batch - 1 else other.at[b])[...].astype(F32)).T
        values = x_ref[b]
        scale = lax.rsqrt(jnp.mean(values * values, axis=-1, keepdims=True) + epsilon)
        gain_sum = gain_sum + jnp.sum(back * values * scale, axis=0, keepdims=True)
        u = back * gain
        along = jnp.mean(u * values, axis=-1, keepdims=True)
        grad_in[b] = mixed_ref[b] + scale * (u - values * (scale * scale * along))
    row = lax.broadcasted_iota(jnp.int32, (BLK, BLK), 0)
    col = lax.broadcasted_iota(jnp.int32, (BLK, BLK), 1)
    flip = (row + col == BLK - 1).astype(F32)
    bucket = lax.broadcasted_iota(jnp.int32, (NB, 1), 0)
    head_lane = lax.broadcasted_iota(jnp.int32, (NB, LANE), 1)
    table = jnp.zeros((NB, LANE), F32)
    for h in range(HEADS):
        line = jnp.zeros((1, SPAN), F32)
        for off in (-1, 0, 1):
            flipped = jnp.dot(flip, near[h, off + 2], preferred_element_type=F32, precision=highest)
            padded = jnp.concatenate([flipped, jnp.zeros((BLK, SPAN - BLK), F32)], axis=1)
            rolled = pltpu.roll(padded, (BLK - off * BLK) % SPAN, 1, stride=1, stride_axis=0)
            line = line + jnp.sum(rolled, axis=0, keepdims=True)
        column = jnp.sum(onehot[...] * line, axis=1, keepdims=True)
        sides = jnp.sum(far_sum[h], axis=1, keepdims=True)
        column = column + jnp.where(bucket == NB // 2 - 1, sides[0:1], 0.0) + jnp.where(bucket == NB - 1, sides[1:2], 0.0)
        table = jnp.where(head_lane == z * HEADS + h, column, table)
    share, buckets = width // p.dp, NB // p.dp
    for i in range(p.dp):
        block = []
        for v in (gain_sum, ffn_ref[...]):
            for first, last in gain_rows(share):
                v_row = v[:, i * share + first : i * share + last]
                block.append(jnp.concatenate([v_row, jnp.zeros((1, LANE - (last - first)), F32)], axis=1) if last - first < LANE else v_row)
        block.append(table[i * buckets : (i + 1) * buckets])
        block.append(jnp.zeros((SMALL - 2 * len(gain_rows(share)) - buckets, LANE), F32))
        small[i * SMALL : (i + 1) * SMALL] = jnp.concatenate(block, axis=0).astype(BF16)
    scatter.step_core((3,))
    for line in early.lines:
        spread_early.step_two(line)
    scatter.step_first(late.lines)
    for line in early.lines:
        spread_early.step_back(line)
    for line in late.lines:
        scatter.step_second(line)
    for line in early.lines:
        spread_early.step_rest(line)
    for line in late.lines:
        scatter.step_third(line)
        spread_late.step_pair(line)
    for line in early.lines:
        spread_early.step_last(line)
    for line in late.lines:
        spread_late.step_back(line)
    for line in late.lines:
        spread_late.step_rest(line)
    for line in late.lines:
        spread_late.step_last(line)
    n_copy.wait_send()
    spread_early.end()
    spread_late.end()
    scatter.end()


def gain_rows(share):
    return [(at, min(at + LANE, share)) for at in range(0, share, LANE)]


def half_columns(z):
    return pl.ds(pl.multiple_of(lax.div(z, 2) * HALF, LANE), HALF)


def last_grads(early, late, loaded, gain, ffn):
    inputs = loaded[6]
    width = inputs.shape[-1]
    shapes = [(width, HALF) if 3 <= i < 6 else v.shape for i, v in enumerate(loaded)]
    return pl.pallas_call(
        functools.partial(last_kernel, early, late),
        in_specs=[anywhere()] * len(loaded) + [whole()] * 2,
        out_specs=[whole()] * 3,
        out_shape=[
            jax.ShapeDtypeStruct(inputs.shape, F32),
            jax.ShapeDtypeStruct((early.total, early.lanes), BF16),
            jax.ShapeDtypeStruct((2, late.total, late.lanes), BF16),
        ],
        scratch_shapes=[pltpu.VMEM(shape, v.dtype) for shape, v in zip(shapes, loaded)]
        + [pltpu.SemaphoreType.DMA((len(loaded),))]
        + [pltpu.VMEM((width, HALF), BF16)] * 3
        + [pltpu.VMEM((late.p.dp * SMALL, LANE), BF16)]
        + [pltpu.VMEM(loaded[-1].shape, BF16), pltpu.SemaphoreType.DMA((2,))]
        + Scatter(late, (True, False)).scratch()
        + Spread(early).scratch()
        + Spread(late, True).scratch(),
        compiler_params=pltpu.CompilerParams(
            vmem_limit_bytes=VMEM_BYTES, collective_id=2, has_side_effects=True
        ),
        name="last_grads",
    )(*loaded, gain.reshape(1, -1), ffn.reshape(1, -1))


def unpack_kernel(early, late, full_early, full_late, *outs):
    for m, block, at, share in early.blocks:
        outs[m][:, block * LANES : (block + 1) * LANES] = full_early[at : at + share].astype(F32)
    outs = outs[len(early.shapes) :]
    for m, block, at, share in late.blocks[:-1]:
        for half in range(2):
            first = half * HALF + block * LANE
            outs[m][:, first : first + LANE] = full_late[half, at : at + share].astype(F32)
    *_, (_, _, first, _) = late.blocks
    d_attn, d_ffn, d_table = outs[len(late.shapes) - 1 :]
    small = full_late[0, first : first + SMALL].astype(F32) + full_late[1, first : first + SMALL].astype(F32)
    at = 0
    for out in (d_attn, d_ffn):
        for begin, end in gain_rows(out.shape[1]):
            out[:, begin:end] = small[at : at + 1, : end - begin]
            at += 1
    buckets, heads = d_table.shape
    d_table[...] = small[at : at + buckets, :heads]


def unpack(early, late, full_early, full_late, width):
    dp = early.p.dp
    shapes = [(height // dp, columns) for height, columns in early.shapes]
    shapes += [(width // dp, width)] * 3 + [(1, width // dp)] * 2 + [(NB // dp, H)]
    return pl.pallas_call(
        functools.partial(unpack_kernel, early, late),
        in_specs=[whole()] * 2,
        out_specs=[whole()] * len(shapes),
        out_shape=[jax.ShapeDtypeStruct(s, F32) for s in shapes],
        compiler_params=params(),
        name="unpack",
    )(full_early, full_late)


def greet(n, z, x):
    barrier = pltpu.get_barrier_semaphore()
    for peer in peers(n, z, x):
        pl.semaphore_signal(barrier, inc=1, device_id={"seq": peer}, device_id_type=pl.DeviceIdType.MESH)
    pl.semaphore_wait(barrier, OUTER - 1 + n - 1)


def far_case(n, j, kb):
    if kb < n * j - 1:
        return 0
    if kb > n * j + n:
        return 2
    return None


def near_case(n, j, kb, x):
    off = kb - (n * j + x)
    near = jnp.logical_and(off >= -1, off <= 1)
    return jnp.where(near, off + 2, 0), jnp.where(off <= -2, 0, jnp.where(off >= 2, 2, 1))


def key_rows(keys, kb, length):
    one = jnp.ones((1, BLK), F32)
    lane = lax.broadcasted_iota(jnp.int32, (1, BLK), 1)
    mask = jnp.where(kb * BLK + lane < length, 0.0, -1e30)
    return jnp.concatenate([keys, tail(BLK, (one, one, one, mask)).astype(BF16)], axis=0).T


def forward_kernel(
    n, len_ref, table_ref, onehot_ref, x_ref, gain_ref, wq_ref, wk_ref, wv_ref,
    normed_ref, own, pair, att, o_ref, lse_ref, tile_ref, far_ref,
    here, there, send, ka, qa, va,
    n_send, n_recv, z_send, z_recv, x_send, x_recv, o_send, o_recv,
):
    nk = OUTER * n
    batch = x_ref.shape[0]
    units = batch * HEADS
    me = lax.axis_index("seq")
    z, x = lax.div(me, n), lax.rem(me, n)
    greet(n, z, x)

    near, two, across = around(z)
    groups = (z, two, near, across)
    low = lax.rem(z, 2) == 0
    columns = half_columns(z)

    def n_copy(b):
        return remote(here.at[b], there.at[b], (n_send.at[b], n_recv.at[b]), seq=two * n + x)

    def z_copy(u, i):
        sems = z_send.at[u, i], z_recv.at[u, i]
        return remote(send.at[u, i], own.at[u, groups[i]], sems, seq=near * n + x)

    def x_copy(u, s, i):
        rows = pl.ds(DH, 2 * DH)
        sems = x_send.at[s - 1, u, i], x_recv.at[s - 1, u, i]
        peer = z * n + lax.rem(x + s, n)
        return remote(own.at[u, groups[i], rows], pair.at[s - 1, u, groups[i]], sems, seq=peer)

    def o_copy(u, d):
        group = lax.rem(z + d, OUTER)
        b, h = lax.div(u, HEADS), lax.rem(u, HEADS)
        rows = pl.ds(pl.multiple_of((z * HEADS + h) * DH, DH), DH)
        sems = o_send.at[u, d - 1], o_recv.at[u, d - 1]
        return remote(o_ref.at[u, group], att.at[b, rows], sems, seq=group * n + x)

    for b in range(batch):
        values = x_ref[b]
        scale = lax.rsqrt(jnp.mean(values * values, axis=-1, keepdims=True) + epsilon)
        here[b] = (values * scale * gain_ref[...]).astype(BF16)
        if b == 0:
            n_copy(0).start()

    def project(b, i):
        normed = (here, there)[i][b]
        normed_ref[i, b] = normed.T
        for m, (w_ref, factor) in enumerate(((wq_ref, LOG2E), (wk_ref, 1.0), (wv_ref, 1.0))):
            turned = (jnp.dot(normed, w_ref[:, columns], preferred_element_type=F32) * factor).T.astype(BF16)
            for h in range(HEADS):
                first, second = turned[h * DH : (h + 1) * DH], turned[HW + h * DH : HW + (h + 1) * DH]
                rows = slice(m * DH, (m + 1) * DH)
                own[b * HEADS + h, groups[i], rows] = jnp.where(low, first, second)
                send[b * HEADS + h, i, rows] = jnp.where(low, second, first)
        for h in range(HEADS):
            for s in range(1, n):
                x_copy(b * HEADS + h, s, i).start()

    def start_near(b, i):
        for h in range(HEADS):
            z_copy(b * HEADS + h, i).start()

    for b in range(batch):
        project(b, 0)
        if b == 0:
            start_near(0, 0)

    head_lane = lax.broadcasted_iota(jnp.int32, (NB, H), 1)
    for h in range(HEADS):
        chosen = jnp.where(head_lane == z * HEADS + h, table_ref[...], 0.0)
        column = jnp.sum(chosen, axis=1, keepdims=True) * LOG2E
        line = jnp.broadcast_to(jnp.sum(onehot_ref[...] * column, axis=0, keepdims=True), (BLK, SPAN))
        tile_ref[h, 0] = jnp.zeros((BLK, BLK), F32)
        for off in (-1, 0, 1):
            shift = (off * BLK - (2 * BLK - 1)) % SPAN
            tile_ref[h, off + 2] = pltpu.roll(line, shift, 1, stride=1, stride_axis=0)[:, :BLK]
        far_ref[h, 0] = jnp.broadcast_to(column[NB // 2 - 1 : NB // 2], (1, BLK))
        far_ref[h, 1] = jnp.broadcast_to(column[NB - 1 :], (1, BLK))

    def attend(u):
        b, h = lax.div(u, HEADS), lax.rem(u, HEADS)
        length = len_ref[b]
        left, right = far_ref[h, 0], far_ref[h, 1]
        one = jnp.ones((1, BLK), F32)
        vtail = tail(BLK, (one,)).astype(BF16)
        for s in range(1, n):
            for i in range(OUTER):
                x_copy(u, s, i).wait_recv()
        for s in range(n):
            col = lax.rem(x + s, n)
            for j in range(OUTER):
                kb = n * j + col
                if s == 0:
                    keys, vals = own[u, j, DH : 2 * DH], own[u, j, 2 * DH :]
                else:
                    keys, vals = pair[n - s - 1, u, j, :DH], pair[n - s - 1, u, j, DH:]
                ka[kb] = key_rows(keys, kb, length)
                columns = pl.ds(pl.multiple_of(kb * BLK, BLK), BLK)
                va[:DH, columns] = vals
                va[DH:, columns] = vtail

        def scores(kb, j):
            case = far_case(n, j, kb)
            if case is not None:
                return jnp.dot(ka[kb], qa[case, j], preferred_element_type=F32)
            tile, case = near_case(n, j, kb, x)
            return jnp.dot(ka[kb], qa[case, j], preferred_element_type=F32) + tile_ref[h, tile]

        for j in range(OUTER):
            for v, c in enumerate((left, 0.0 * one, right)):
                qa[v, j, :DH] = own[u, j, :DH]
                qa[v, j, DH:] = tail(BLK, split3(c) + (one,)).astype(BF16)
        tops = []
        for j in range(OUTER):
            top = jnp.full((8, BLK), -1e30, F32)
            for kb in range(nk):
                top = jnp.maximum(top, jnp.max(scores(kb, j).reshape(BLK // 8, 8, BLK), axis=0))
            top = jnp.max(top, axis=0, keepdims=True)
            tops.append(top)
            for v, c in enumerate((left, 0.0, right)):
                qa[v, j, DH:] = tail(BLK, split3(c - top) + (one,)).astype(BF16)
        for j in range(OUTER):
            weights = [jnp.exp2(scores(kb, j)).astype(BF16) for kb in range(nk)]
            total = jnp.dot(va[...], jnp.concatenate(weights, axis=0), preferred_element_type=F32)
            weight = total[DH : DH + 1]
            o_ref[u, j] = (total[:DH] / weight).astype(BF16)
            lse_ref[u, j] = tops[j] + jnp.log2(weight)
        rows = pl.ds(pl.multiple_of((z * HEADS + h) * DH, DH), DH)
        att[b, rows] = o_ref[u, z]
        @pl.when(u >= held_back)
        def _():
            start_o(u)

    held_back = units - HEADS - 1

    def start_o(u):
        for d in (2, 1, 3):
            o_copy(u, d).start()

    def turn(u, carry):
        @pl.when(jnp.logical_and(u < units, lax.rem(u, HEADS) == 0))
        def _():
            b = lax.div(u, HEADS)
            n_copy(b).wait_recv()

            @pl.when(b == batch - 1)
            def _():
                lax.fori_loop(0, held_back, lambda u, c: (start_o(u), c)[1], 0)

            @pl.when(b + 1 < batch)
            def _():
                n_copy(b + 1).start()

            project(b, 1)
            start_near(b, 1)

            @pl.when(b + 1 < batch)
            def _():
                start_near(b + 1, 0)

        @pl.when(u < units)
        def _():
            for i in range(2):
                z_copy(u, i).wait_recv()
                for s in range(1, n):
                    x_copy(u, s, 2 + i).start()

        @pl.when(u > 0)
        def _():
            attend(u - 1)

        return carry

    lax.fori_loop(0, units + 1, turn, 0)

    def finish(u, carry):
        for d in range(1, OUTER):
            o_copy(u, d).wait_send()
            o_copy(u, d).wait_recv()
        for i in range(2):
            z_copy(u, i).wait_send()
        for s in range(1, n):
            for i in range(OUTER):
                x_copy(u, s, i).wait_send()
        return carry

    lax.fori_loop(0, units, finish, 0)
    for b in range(batch):
        n_copy(b).wait_send()


def attention_forward(n, lengths, table, onehot, inputs, gain, wq, wk, wv):
    batch, height, width = inputs.shape
    units, nk = batch * HEADS, n * OUTER
    dma = pltpu.SemaphoreType.DMA
    return pl.pallas_call(
        functools.partial(forward_kernel, n),
        in_specs=[smem()] + [whole()] * 7,
        out_specs=[whole()] * 8,
        out_shape=[
            jax.ShapeDtypeStruct((2, batch, width, height), BF16),
            jax.ShapeDtypeStruct((units, OUTER, 3 * DH, BLK), BF16),
            jax.ShapeDtypeStruct((n - 1, units, OUTER, 2 * DH, BLK), BF16),
            jax.ShapeDtypeStruct((batch, width, height), BF16),
            jax.ShapeDtypeStruct((units, OUTER, DH, BLK), BF16),
            jax.ShapeDtypeStruct((units, OUTER, 1, BLK), F32),
            jax.ShapeDtypeStruct((HEADS, TILES, BLK, BLK), F32),
            jax.ShapeDtypeStruct((HEADS, 2, 1, BLK), F32),
        ],
        scratch_shapes=[
            pltpu.VMEM((batch, height, width), BF16),
            pltpu.VMEM((batch, height, width), BF16),
            pltpu.VMEM((units, 2, 3 * DH, BLK), BF16),
            pltpu.VMEM((nk, BLK, AUG), BF16),
            pltpu.VMEM((3, OUTER, AUG, BLK), BF16),
            pltpu.VMEM((AUG, nk * BLK), BF16),
            dma((batch,)),
            dma((batch,)),
            dma((units, 2)),
            dma((units, 2)),
            dma((n - 1, units, OUTER)),
            dma((n - 1, units, OUTER)),
            dma((units, OUTER - 1)),
            dma((units, OUTER - 1)),
        ],
        compiler_params=pltpu.CompilerParams(
            vmem_limit_bytes=VMEM_BYTES, collective_id=0, has_side_effects=True
        ),
        cost_estimate=pl.CostEstimate(flops=45 * 10**9, bytes_accessed=24 << 20, transcendentals=0),
        name="attention_forward",
    )(lengths, table, onehot, inputs, gain.reshape(1, -1), wq, wk, wv)


def early_scatter(early):
    return Scatter(early, (True,) * len(early.lines))


def backward_kernel(
    n, early, len_ref, far_ref, tile_ref, own, pair, o_ref, lse_ref, dout, *refs
):
    scatter = early_scatter(early)
    count = len(early.shapes)
    weights, refs = refs[:count], refs[count:]
    projections, refs = refs[:3], refs[3:]
    (grads, near, far_sum, parts, other, leaving, w_half, other_out, w_sem, n_send, n_recv, own_slot, pair_slot, load_sem,
    do_land, x_out, x_land, z_out, kept,
    ka, kt, va, qa, da, dk_all, dv_all,
    d_send, d_recv, x_send, x_recv, z_send, z_recv) = refs[: -scatter.count]
    scatter.bind(weights, refs[-scatter.count :])
    nk = OUTER * n
    batch = dout.shape[0]
    units = batch * HEADS
    x_slots, z_slots = staging(n, units)
    me = lax.axis_index("seq")
    z, x = lax.div(me, n), lax.rem(me, n)
    near_z, two, across = around(z)
    low = lax.rem(z, 2) * HW
    greet_all(early.p)
    scatter.step_core()
    columns = half_columns(z)
    w_loads = [pltpu.make_async_copy(w.at[:, columns], w_half.at[m], w_sem.at[m]) for m, w in enumerate(projections)]
    for c in w_loads:
        c.start()

    def head_rows(group, h):
        return pl.ds(pl.multiple_of((group * HEADS + h) * DH, DH), DH)

    def d_copy(u, d):
        group = lax.rem(z + d, OUTER)
        b, h = lax.div(u, HEADS), lax.rem(u, HEADS)
        sems = d_send.at[u, d - 1], d_recv.at[u, d - 1]
        return remote(dout.at[b, head_rows(group, h)], do_land.at[u, z], sems, seq=group * n + x)

    def x_copy(u, s):
        peer = z * n + lax.rem(x + s, n)
        sems = x_send.at[s - 1, u], x_recv.at[s - 1, u]
        return remote(
            x_out.at[s - 1, lax.rem(u, x_slots)], x_land.at[s - 1, lax.rem(u, X_LAND)], sems, seq=peer
        )

    def half_rows(h):
        return pl.ds(pl.multiple_of(low + h * DH, DH), DH)

    def z_copy(u, i, m):
        b, h = lax.div(u, HEADS), lax.rem(u, HEADS)
        sems = z_send.at[u, i, m], z_recv.at[u, i, m]
        src, dst = z_out.at[lax.rem(u, z_slots), i, pl.ds(m * DH, DH)], grads.at[m, b, i, half_rows(h)]
        return remote(src, dst, sems, seq=near_z * n + x)

    def n_copy(b):
        return remote(other_out.at[b], other.at[b], (n_send.at[b], n_recv.at[b]), seq=two * n + x)

    def loads(u):
        slot = lax.rem(u, 2)
        yield pltpu.make_async_copy(own.at[u], own_slot.at[slot], load_sem.at[slot, 0])
        for s in range(1, n):
            yield pltpu.make_async_copy(pair.at[s - 1, u], pair_slot.at[slot, s - 1], load_sem.at[slot, s])

    for c in loads(0):
        c.start()

    def start_d(u):
        for d in (2, 1, 3):
            d_copy(u, d).start()

    start_d(0)
    start_d(1)

    def begin(u, carry):
        do_land[u, z] = dout[lax.div(u, HEADS), head_rows(z, lax.rem(u, HEADS))]
        return carry

    lax.fori_loop(0, units, begin, 0)
    near[...] = jnp.zeros_like(near)
    far_sum[...] = jnp.zeros_like(far_sum)
    one = jnp.ones((1, BLK), F32)
    ones3 = tail(BLK, (one, one, one)).astype(BF16)
    row16 = lax.broadcasted_iota(jnp.int32, (16, BLK), 0)
    marks = [jnp.where(row16 == r, 1.0, 0.0).astype(BF16) for r in range(2)]

    def work(u):
        b, h = lax.div(u, HEADS), lax.rem(u, HEADS)
        length = len_ref[b]
        left, right = far_ref[h, 0], far_ref[h, 1]
        slot = lax.rem(u, 2)
        for c in loads(u):
            c.wait()

        @pl.when(u + 1 < units)
        def _():
            for c in loads(u + 1):
                c.start()

        @pl.when(u + 2 < units)
        def _():
            start_d(u + 2)

        for s in range(n):
            col = lax.rem(x + s, n)
            for j in range(OUTER):
                kb = n * j + col
                if s == 0:
                    keys, vals = own_slot[slot, j, DH : 2 * DH], own_slot[slot, j, 2 * DH :]
                else:
                    keys, vals = pair_slot[slot, n - s - 1, j, :DH], pair_slot[slot, n - s - 1, j, DH:]
                ka[kb] = key_rows(keys, kb, length)
                kt[kb] = keys
                va[kb] = jnp.concatenate([vals, ones3], axis=0).T
        for d in range(1, OUTER):
            d_copy(u, d).wait_recv()
        for j in range(OUTER):
            lse = lse_ref[u, j]
            for v, c in enumerate((left, 0.0, right)):
                qa[v, j, :DH] = own_slot[slot, j, :DH]
                qa[v, j, DH:] = tail(BLK, split3(c - lse) + (one,)).astype(BF16)
            arrived = do_land[u, j]
            delta = jnp.sum(arrived.astype(F32) * o_ref[u, j].astype(F32), axis=0, keepdims=True)
            da[j, :DH] = arrived
            da[j, DH:] = tail(BLK, split3(-delta)).astype(BF16)
        dqs = [None] * OUTER
        for g in range(0, nk, GROUP):
            blocks = range(g, g + GROUP)
            ps, dss = {}, {}
            for j in range(OUTER):
                left_side = []
                for kb in blocks:
                    case = far_case(n, j, kb)
                    if case is not None:
                        p = jnp.exp2(jnp.dot(ka[kb], qa[case, j], preferred_element_type=F32))
                        mark = marks[case // 2]
                    else:
                        tile, case = near_case(n, j, kb, x)
                        s = jnp.dot(ka[kb], qa[case, j], preferred_element_type=F32)
                        p = jnp.exp2(s + tile_ref[h, tile])
                        want = jnp.where(case == 1, 2, lax.div(case, 2))
                        mark = jnp.where(row16 == want, 1.0, 0.0).astype(BF16)
                    ds = p * jnp.dot(va[kb], da[j], preferred_element_type=F32)
                    if far_case(n, j, kb) is None:
                        near[h, tile] += ds
                    ps[kb, j], dss[kb, j] = p.astype(BF16), ds.astype(BF16)
                    left_side.append(jnp.concatenate([kt[kb], mark], axis=0))
                right_side = jnp.concatenate([dss[kb, j] for kb in blocks], axis=0)
                dq = jnp.dot(jnp.concatenate(left_side, axis=1), right_side, preferred_element_type=F32)
                dqs[j] = dq if g == 0 else dqs[j] + dq
            for kb in blocks:
                dv, dk = jnp.zeros((DH, BLK), F32), jnp.zeros((DH, BLK), F32)
                for j in range(OUTER):
                    dv = dv + lax.dot_general(da[j, :DH], ps[kb, j], NT, preferred_element_type=F32)
                    dk = dk + lax.dot_general(qa[0, j, :DH], dss[kb, j], NT, preferred_element_type=F32)
                dk_all[kb] = dk * LN2
                dv_all[kb] = dv
        @pl.when(u >= x_slots)
        def _():
            for s in range(1, n):
                x_copy(u - x_slots, s).wait_send()

        far = jnp.zeros((8, BLK), F32)
        for j in range(OUTER):
            far = far + dqs[j][DH : DH + 8]
        far_sum[h] += far
        parity = lax.rem(u, 2)
        for j in range(OUTER):
            kept[parity, j, :DH] = dqs[j][:DH]
            kept[parity, j, DH : 2 * DH] = dk_all[n * j + x]
            kept[parity, j, 2 * DH :] = dv_all[n * j + x]
            for s in range(1, n):
                kb = n * j + lax.rem(x + s, n)
                x_out[s - 1, lax.rem(u, x_slots), j, :DH] = dk_all[kb].astype(BF16)
                x_out[s - 1, lax.rem(u, x_slots), j, DH:] = dv_all[kb].astype(BF16)
        for s in range(1, n):
            x_copy(u, s).start()

    def hand_over(u):
        b, h = lax.div(u, HEADS), lax.rem(u, HEADS)
        parity = lax.rem(u, 2)
        for s in range(1, n):
            x_copy(u, s).wait_recv()

        @pl.when(u >= z_slots)
        def _():
            for i in range(2):
                for m in range(3):
                    z_copy(u - z_slots, i, m).wait_send()

        for i, (mine, theirs) in enumerate(((z, near_z), (two, across))):
            for j, stays in ((mine, True), (theirs, False)):
                rest = kept[parity, j, DH:]
                for s in range(1, n):
                    rest = rest + x_land[s - 1, lax.rem(u, X_LAND), j].astype(F32)
                total = jnp.concatenate([kept[parity, j, :DH], rest], axis=0).astype(BF16)
                if stays:
                    for m in range(3):
                        grads[m, b, i, half_rows(h)] = total[m * DH : (m + 1) * DH]
                else:
                    z_out[lax.rem(u, z_slots), i] = total
            for m in range(3):
                z_copy(u, i, m).start()

    def combine(b):
        for h in range(HEADS):
            for i in range(2):
                for m in range(3):
                    z_copy(b * HEADS + h, i, m).wait_recv()
        total = jnp.dot(w_half[0], grads[0, b, 1], preferred_element_type=F32)
        total = total + jnp.dot(w_half[1], grads[1, b, 1], preferred_element_type=F32)
        total = total + jnp.dot(w_half[2], grads[2, b, 1], preferred_element_type=F32)
        @pl.when(b < batch - 1)
        def _():
            other_out[b] = total.astype(BF16)
            n_copy(b).start()

        @pl.when(b == batch - 1)
        def _():
            leaving[...] = total.astype(BF16)

    def turn(u, carry):
        @pl.when(u < units)
        def _():
            work(u)

        @pl.when(jnp.logical_and(u > 0, u <= units))
        def _():
            hand_over(u - 1)

        @pl.when(jnp.logical_and(u > HEADS, lax.rem(u - 1, HEADS) == 0))
        def _():
            combine(lax.div(u - 1, HEADS) - 1)

        @pl.when(u == 0)
        def _():
            scatter.step_first((0,))

        for line in early.lines:

            @pl.when(u == 2 * line + 2)
            def _():
                scatter.step_second(line)
                if line + 1 < len(early.lines):
                    scatter.start_first(line + 1)

        return carry

    for c in w_loads:
        c.wait()
    lax.fori_loop(0, units + 2, turn, 0)

    def finish(u, carry):
        for d in range(1, OUTER):
            d_copy(u, d).wait_send()

        @pl.when(u >= units - z_slots)
        def _():
            for i in range(2):
                for m in range(3):
                    z_copy(u, i, m).wait_send()

        @pl.when(u >= units - x_slots)
        def _():
            for s in range(1, n):
                x_copy(u, s).wait_send()

        return carry

    lax.fori_loop(0, units, finish, 0)
    for b in range(batch - 1):
        n_copy(b).wait_send()
        n_copy(b).wait_recv()
    for line in early.lines:
        scatter.step_third(line)
        parts[early.part_start[line] : early.part_start[line] + early.size[line]] = scatter.part(line)[...]
    scatter.end()


def staging(n, units):
    return (units, units) if n <= 2 else (2, 4)


X_LAND = 4


def attention_backward(n, early, lengths, far, tiles, own, pair, out, lse, dout, weights, projections):
    batch, width, height = dout.shape
    units, nk = batch * HEADS, n * OUTER
    dma = pltpu.SemaphoreType.DMA
    x_slots, z_slots = staging(n, units)
    return pl.pallas_call(
        functools.partial(backward_kernel, n, early),
        in_specs=[smem()] + [whole()] * 2 + [anywhere()] * 2 + [whole()] * 3 + [anywhere()] * (len(weights) + 3),
        out_specs=[whole()] * 6,
        out_shape=[
            jax.ShapeDtypeStruct((3, batch, 2, HALF, height), BF16),
            jax.ShapeDtypeStruct((HEADS, TILES, BLK, BLK), F32),
            jax.ShapeDtypeStruct((HEADS, 8, BLK), F32),
            jax.ShapeDtypeStruct((early.part_total, LANES), BF16),
            jax.ShapeDtypeStruct((batch - 1, width, height), BF16),
            jax.ShapeDtypeStruct((width, height), BF16),
        ],
        scratch_shapes=[
            pltpu.VMEM((3, width, HALF), BF16),
            pltpu.VMEM((batch - 1, width, height), BF16),
            dma((3,)),
            dma((batch - 1,)),
            dma((batch - 1,)),
            pltpu.VMEM((2, OUTER, 3 * DH, BLK), BF16),
            pltpu.VMEM((2, n - 1, OUTER, 2 * DH, BLK), BF16),
            dma((2, n)),
            pltpu.VMEM((units, OUTER, DH, BLK), BF16),
            pltpu.VMEM((n - 1, x_slots, OUTER, 2 * DH, BLK), BF16),
            pltpu.VMEM((n - 1, X_LAND, OUTER, 2 * DH, BLK), BF16),
            pltpu.VMEM((z_slots, 2, 3 * DH, BLK), BF16),
            pltpu.VMEM((2, OUTER, 3 * DH, BLK), F32),
            pltpu.VMEM((nk, BLK, AUG), BF16),
            pltpu.VMEM((nk, DH, BLK), BF16),
            pltpu.VMEM((nk, BLK, AUG), BF16),
            pltpu.VMEM((3, OUTER, AUG, BLK), BF16),
            pltpu.VMEM((OUTER, AUG, BLK), BF16),
            pltpu.VMEM((nk, DH, BLK), F32),
            pltpu.VMEM((nk, DH, BLK), F32),
            dma((units, OUTER - 1)),
            dma((units, OUTER - 1)),
            dma((n - 1, units)),
            dma((n - 1, units)),
            dma((units, 2, 3)),
            dma((units, 2, 3)),
        ]
        + early_scatter(early).scratch(),
        compiler_params=pltpu.CompilerParams(
            vmem_limit_bytes=VMEM_BYTES, collective_id=1, has_side_effects=True
        ),
        cost_estimate=pl.CostEstimate(flops=110 * 10**9, bytes_accessed=24 << 20, transcendentals=0),
        name="attention_backward",
    )(lengths, far, tiles, own, pair, out, lse, dout, *weights, *projections)


FF_STEP = 512


def middle_kernel(
    x_ref, att_ref, cot_ref, gain_ref, w_out, w_gate, w_up, w_down,
    result, grad_mixed, dout, d_gain, d_out, d_gate, d_up, d_down,
    wo, wg, wu, wd, att, low, hidden, g_gate, g_up, s_out, s_gate, s_up, s_down, kept, in_sem, out_sem,
):
    tokens, width = x_ref.shape
    batch = att_ref.shape[0]
    ff = w_gate.shape[1]
    loads = [
        pltpu.make_async_copy(src, dst, in_sem.at[i])
        for i, (src, dst) in enumerate(((w_out, wo), (w_gate, wg), (w_up, wu), (w_down, wd)))
    ]
    stores = [
        pltpu.make_async_copy(src, dst, out_sem.at[i])
        for i, (src, dst) in enumerate(((s_out, d_out), (s_gate, d_gate), (s_up, d_up), (s_down, d_down)))
    ]
    for c in loads:
        c.start()
    height = tokens // batch
    for b in range(batch):
        att[b * height : (b + 1) * height] = att_ref[b].T
    low[...] = cot_ref[...].astype(BF16)
    loads[0].wait()
    mixed = x_ref[...] + jnp.dot(att[...], wo[...], preferred_element_type=F32)
    kept[...] = mixed
    result[...] = mixed
    scale = lax.rsqrt(jnp.mean(mixed * mixed, axis=-1, keepdims=True) + epsilon)
    normed = (mixed * scale * gain_ref[...]).astype(BF16)
    att[...] = normed
    for c in loads[1:]:
        c.wait()
    root = 0.7978845608028654
    for at in range(0, ff, FF_STEP):
        part = slice(at, at + FF_STEP)
        gate = jnp.dot(att[...], wg[:, part], preferred_element_type=F32)
        upward = jnp.dot(att[...], wu[:, part], preferred_element_type=F32)
        g_hidden = lax.dot_general(low[...], wd[part], NT, preferred_element_type=F32)
        square = gate * gate
        t = jnp.tanh(root * gate * (1.0 + 0.044715 * square))
        half = 0.5 * (1.0 + t)
        act = gate * half
        slope = half + 0.5 * gate * (1.0 - t * t) * (root * (1.0 + 3.0 * 0.044715 * square))
        hidden[:, part] = (act * upward).astype(BF16)
        g_gate[:, part] = (g_hidden * upward * slope).astype(BF16)
        g_up[:, part] = (g_hidden * act).astype(BF16)
    result[...] += jnp.dot(hidden[...], wd[...], preferred_element_type=F32)
    d_normed = lax.dot_general(g_gate[...], wg[...], NT, preferred_element_type=F32)
    d_normed = d_normed + lax.dot_general(g_up[...], wu[...], NT, preferred_element_type=F32)
    mixed = kept[...]
    scale = lax.rsqrt(jnp.mean(mixed * mixed, axis=-1, keepdims=True) + epsilon)
    d_gain[...] = jnp.sum(d_normed * mixed * scale, axis=0, keepdims=True)
    u = d_normed * gain_ref[...]
    along = jnp.mean(u * mixed, axis=-1, keepdims=True)
    d_mixed = cot_ref[...] + scale * (u - mixed * (scale * scale * along))
    grad_mixed[...] = d_mixed
    d_low = d_mixed.astype(BF16)
    turned = lax.dot_general(wo[...], d_low, NT, preferred_element_type=F32).astype(BF16)
    for b in range(batch):
        dout[b] = turned[:, b * height : (b + 1) * height]
    total = jnp.zeros((width, width), F32)
    for b in range(batch):
        total = total + jnp.dot(att_ref[b], d_low[b * height : (b + 1) * height], preferred_element_type=F32)
    s_out[...] = total.astype(BF16)
    stores[0].start()
    normed_t = att[...].T
    for src, dst, store in ((g_gate, s_gate, stores[1]), (g_up, s_up, stores[2])):
        for at in range(0, ff, FF_STEP):
            part = slice(at, at + FF_STEP)
            dst[:, part] = jnp.dot(normed_t, src[:, part], preferred_element_type=F32).astype(BF16)
        store.start()
    for at in range(0, ff, FF_STEP):
        part = slice(at, at + FF_STEP)
        s_down[part] = jnp.dot(hidden[:, part].T, low[...], preferred_element_type=F32).astype(BF16)
    stores[3].start()
    for c in stores:
        c.wait()


def middle(inputs, att, cotangent, gain, w_out, w_gate, w_up, w_down):
    batch, height, width = inputs.shape
    tokens, ff = batch * height, w_gate.shape[1]
    weights = (w_out, w_gate, w_up, w_down)
    flat = (tokens, width)
    out = pl.pallas_call(
        middle_kernel,
        in_specs=[whole()] * 4 + [anywhere()] * 4,
        out_specs=[whole()] * 4 + [anywhere()] * 4,
        out_shape=[
            jax.ShapeDtypeStruct(flat, F32),
            jax.ShapeDtypeStruct(flat, F32),
            jax.ShapeDtypeStruct((batch, width, height), BF16),
            jax.ShapeDtypeStruct((1, width), F32),
        ]
        + [jax.ShapeDtypeStruct(w.shape, BF16) for w in weights],
        scratch_shapes=[pltpu.VMEM(w.shape, BF16) for w in weights]
        + [pltpu.VMEM(flat, BF16)] * 2
        + [pltpu.VMEM((tokens, ff), BF16)] * 3
        + [pltpu.VMEM(w.shape, BF16) for w in weights]
        + [pltpu.VMEM(flat, F32)]
        + [pltpu.SemaphoreType.DMA((4,))] * 2,
        compiler_params=params(),
        cost_estimate=pl.CostEstimate(flops=25 * 10**9, bytes_accessed=32 << 20, transcendentals=0),
        name="middle",
    )(inputs.reshape(flat), att, cotangent.reshape(flat), gain.reshape(1, -1), *weights)
    return out[0].reshape(inputs.shape), out[1].reshape(inputs.shape), out[2], out[3], out[4:]


def shards(
    places,
    inputs,
    lengths,
    norm_attn,
    w_query,
    w_key,
    w_value,
    w_out,
    norm_ffn,
    w_gate,
    w_up,
    w_down,
    bucket_bias,
    cotangent,
):
    batch, height, width = inputs.shape
    n = places.inner
    onehot = jnp.asarray(ONEHOT)
    normed_t, own, pair, attended_t, out, lse, tiles, far = attention_forward(
        n, lengths, bucket_bias, onehot, inputs, norm_attn, w_query, w_key, w_value
    )
    result, grad_mixed, grad_attended_t, grad_norm_ffn, weights = middle(
        inputs, attended_t, cotangent, norm_ffn, w_out, w_gate, w_up, w_down
    )
    early = Rows(places, [g.shape for g in weights], LANES, 4)
    projections = (w_query, w_key, w_value)
    grads, near, far_sum, parts, other, leaving = attention_backward(
        n, early, lengths, far, tiles, own, pair, out, lse, grad_attended_t, weights, projections
    )
    late = Rows(places, [(width, HALF)] * 3 + [(places.dp * SMALL, LANE)], LANE, 2)
    loaded = (
        parts, grads, normed_t, *projections, inputs, grad_mixed, near, far_sum, onehot, other, leaving
    )
    grad_inputs, full_early, full_late = last_grads(early, late, loaded, norm_attn, grad_norm_ffn)
    part_out, part_gate, part_up, part_down, part_query, part_key, part_value, part_attn, part_ffn, part_table = unpack(
        early, late, full_early, full_late, width
    )
    return (
        result,
        grad_inputs,
        part_attn.reshape(-1),
        part_ffn.reshape(-1),
        part_query,
        part_key,
        part_value,
        part_out,
        part_gate,
        part_up,
        part_down,
        part_table,
    )


def solution(mesh):
    rows = P("dp", "seq", None)
    share = P("dp", None)
    return jax.shard_map(
        functools.partial(shards, Places(mesh)),
        mesh=mesh,
        in_specs=(rows, P("dp")) + (P(),) * 10 + (rows,),
        out_specs=(rows, rows, P("dp"), P("dp")) + (share,) * 8,
        check_vma=False,
    )
```

```python
import functools

import jax
import jax.numpy as jnp
import numpy as np
from jax import lax
from jax.experimental import pallas as pl
from jax.experimental.pallas import tpu as pltpu
from jax.sharding import PartitionSpec as P

H = 12
DH = 64
NB = 32
OUTER = 4
HEADS = H // OUTER
HW = HEADS * DH
HALF = 2 * HW
BLK = 256
AUG = DH + 16
SPAN = 4 * BLK
LANES = 256
LANE = 128
LOG2E = 1.4426950408889634
LN2 = 0.6931471805599453
F32 = jnp.float32
BF16 = jnp.bfloat16
NT = (((1,), (1,)), ((), ()))
VMEM_BYTES = 62 << 20
GROUP = 8
TILES = 4

epsilon = 1e-06
limits = (1, 2, 3, 4, 5, 6, 7, 8, 12, 16, 23, 32, 46, 64, 91)
highest = lax.Precision.HIGHEST


def bucket_lines():
    relative = 2 * BLK - 1 - np.arange(SPAN)
    count = sum((np.abs(relative) >= limit).astype(np.int32) for limit in limits)
    bucket = count + (relative > 0).astype(np.int32) * (NB // 2)
    return (bucket[None, :] == np.arange(NB)[:, None]).astype(np.float32)


ONEHOT = bucket_lines()


def params():
    return pltpu.CompilerParams(vmem_limit_bytes=VMEM_BYTES)


def smem():
    return pl.BlockSpec(memory_space=pltpu.SMEM)


def anywhere():
    return pl.BlockSpec(memory_space=pl.ANY)


def whole():
    return pl.BlockSpec(memory_space=pltpu.VMEM)


def split3(v):
    a = v.astype(BF16)
    r = v - a.astype(F32)
    b = r.astype(BF16)
    c = (r - b.astype(F32)).astype(BF16)
    return a.astype(F32), b.astype(F32), c.astype(F32)


def tail(width, values):
    row = lax.broadcasted_iota(jnp.int32, (16, width), 0)
    out = jnp.zeros((16, width), F32)
    for i, v in enumerate(values):
        out = jnp.where(row == i, v, out)
    return out


def peers(n, z, x):
    return [lax.rem(z + d, OUTER) * n + x for d in range(1, OUTER)] + [z * n + lax.rem(x + s, n) for s in range(1, n)]


def around(z):
    near = z + 1 - 2 * lax.rem(z, 2)
    return near, lax.rem(z + 2, OUTER), lax.rem(near + 2, OUTER)


class Places:
    def __init__(self, mesh):
        self.dp = mesh.shape["dp"]
        self.groups = self.dp // 2
        self.inner = mesh.shape["seq"] // OUTER


def remote(src, dst, sems, **peer):
    return pltpu.make_async_remote_copy(
        src_ref=src,
        dst_ref=dst,
        send_sem=sems[0],
        recv_sem=sems[1],
        device_id=peer,
        device_id_type=pl.DeviceIdType.MESH,
    )


class Rows:
    def __init__(self, places, shapes, lanes, lines):
        self.p = places
        self.shapes = shapes
        self.lanes = lanes
        self.lines = range(lines)
        grain = places.inner * OUTER * 16
        self.blocks = []
        at = 0
        for m, (rows, columns) in enumerate(shapes):
            share = rows // places.dp
            for block in range(columns // lanes):
                self.blocks.append((m, block, at, share))
                at += share
        self.used = at
        grains = max(-(-at // grain), lines)
        self.total = grains * grain
        cuts = [grains * line // lines * grain for line in range(lines + 1)]
        self.start = cuts[:-1]
        self.span = [b - a for a, b in zip(cuts[:-1], cuts[1:])]
        self.size = [v // places.inner for v in self.span]
        self.small = [v // OUTER for v in self.size]
        self.part_start = [v // places.inner for v in self.start]
        self.part_total = self.total // places.inner

    def line(self, line):
        return pl.ds(self.start[line], self.span[line])

    def part(self, line, x):
        return pl.ds(pl.multiple_of(self.start[line] + x * self.size[line], 16), self.size[line])

    def quarter(self, line, x, z):
        first = self.start[line] + x * self.size[line] + z * self.small[line]
        return pl.ds(pl.multiple_of(first, 16), self.small[line])


def add_to(ref, arrived):
    if len(arrived) == 1:
        ref[...] = ref[...] + arrived[0]
        return
    total = ref[...].astype(F32)
    for a in arrived:
        total = total + a.astype(F32)
    ref[...] = total.astype(BF16)


class Scatter:
    def __init__(self, rows, y_first):
        self.rows = rows
        self.y_first = y_first
        self.count = 5 + 2 * len(rows.lines)

    def scratch(self):
        r, p, dma = self.rows, self.rows.p, pltpu.SemaphoreType.DMA
        g, n, lines = p.groups, p.inner, len(r.lines)
        out = [pltpu.VMEM((g, r.total, r.lanes), BF16), pltpu.VMEM((g, r.total, r.lanes), BF16)]
        for line, y_first in enumerate(self.y_first):
            out.append(pltpu.VMEM((g - 1, r.span[line] if y_first else r.size[line], r.lanes), BF16))
            out.append(pltpu.VMEM((n - 1, 1 if y_first else g, r.size[line], r.lanes), BF16))
        return out + [dma((len(r.blocks), g, 3)), dma((lines, g - 1, 2)), dma((lines, n - 1, g, 2))]

    def bind(self, grads, refs):
        self.grads = grads
        self.held, self.land = refs[:2]
        self.c_sem, self.y_sem, self.x_sem = refs[-3:]
        self.y_land, self.x_land = refs[2:-3:2], refs[3:-3:2]
        dp, seq = lax.axis_index("dp"), lax.axis_index("seq")
        n = self.rows.p.inner
        self.core, self.group = lax.rem(dp, 2), lax.div(dp, 2)
        self.z, self.x = lax.div(seq, n), lax.rem(seq, n)

    def source(self, i, g, core):
        m, block, at, share = self.rows.blocks[i]
        first = pl.multiple_of((g * 2 + core) * share, 16)
        return self.grads[m].at[pl.ds(first, share), pl.ds(block * self.rows.lanes, self.rows.lanes)], pl.ds(at, share)

    def picked(self, chosen):
        return [i for i, b in enumerate(self.rows.blocks) if chosen is None or b[0] in chosen]

    def core_copies(self, chosen=None):
        for i in self.picked(chosen):
            for g in range(self.rows.p.groups):
                src, where = self.source(i, g, 1 - self.core)
                sems = self.c_sem.at[i, g, 0], self.c_sem.at[i, g, 1]
                yield remote(src, self.land.at[g, where], sems, dp=self.group * 2 + 1 - self.core)

    def own_copies(self, chosen=None):
        for i in self.picked(chosen):
            for g in range(self.rows.p.groups):
                src, where = self.source(i, g, self.core)
                yield pltpu.make_async_copy(src, self.held.at[g, where], self.c_sem.at[i, g, 2])

    def y_copies(self, line):
        r = self.rows
        for t in range(1, r.p.groups):
            other = lax.rem(self.group + t, r.p.groups)
            where = r.line(line) if self.y_first[line] else r.part(line, self.x)
            sems = self.y_sem.at[line, t - 1, 0], self.y_sem.at[line, t - 1, 1]
            yield remote(self.held.at[other, where], self.y_land[line].at[t - 1], sems, dp=other * 2 + self.core)

    def x_copies(self, line):
        r = self.rows
        n = r.p.inner
        for s in range(1, n):
            other = lax.rem(self.x + s, n)
            where = r.part(line, other)
            for g in range(1 if self.y_first[line] else r.p.groups):
                sems = self.x_sem.at[line, s - 1, g, 0], self.x_sem.at[line, s - 1, g, 1]
                src = self.held.at[self.group if self.y_first[line] else g, where]
                yield remote(src, self.x_land[line].at[s - 1, g], sems, seq=self.z * n + other)

    def hop(self, line, which):
        return self.y_copies(line) if (which == 0) == self.y_first[line] else self.x_copies(line)


    def step_core(self, chosen=None):
        for c in self.core_copies(chosen):
            c.start()
        for c in self.own_copies(chosen):
            c.start()

    def step_first(self, begin):
        r = self.rows
        for c in self.core_copies():
            c.wait_recv()
        for c in self.own_copies():
            c.wait()
        for line in r.lines:
            end = r.start[line] + r.span[line]
            first, last = r.start[line], min(end, r.used)
            for g in range(r.p.groups):
                where = pl.ds(first, last - first)
                add_to(self.held.at[g, where], [self.land[g, where]])
                if last < end:
                    self.held[g, last:end] = jnp.zeros((end - last, r.lanes), BF16)
            if line in begin:
                self.start_first(line)

    def start_first(self, line):
        for c in self.hop(line, 0):
            c.start()

    def step_second(self, line):
        r = self.rows
        for c in self.hop(line, 0):
            c.wait_recv()
        if self.y_first[line]:
            arrived = [self.y_land[line][t] for t in range(r.p.groups - 1)]
            add_to(self.held.at[self.group, r.line(line)], arrived)
        else:
            for g in range(r.p.groups):
                arrived = [self.x_land[line][s, g] for s in range(r.p.inner - 1)]
                add_to(self.held.at[g, r.part(line, self.x)], arrived)
        for c in self.hop(line, 1):
            c.start()

    def step_third(self, line):
        r = self.rows
        for c in self.hop(line, 1):
            c.wait_recv()
        if self.y_first[line]:
            arrived = [self.x_land[line][s, 0] for s in range(r.p.inner - 1)]
        else:
            arrived = [self.y_land[line][t] for t in range(r.p.groups - 1)]
        add_to(self.held.at[self.group, r.part(line, self.x)], arrived)

    def part(self, line):
        return self.held.at[self.group, self.rows.part(line, self.x)]

    def end(self):
        for c in self.core_copies():
            c.wait_send()
        for line in self.rows.lines:
            for which in range(2):
                for c in self.hop(line, which):
                    c.wait_send()


class Spread:
    def __init__(self, rows, halves=False):
        self.rows = rows
        self.halves = halves

    def scratch(self):
        r, dma = self.rows, pltpu.SemaphoreType.DMA
        lines = len(r.lines)
        land = (lines, 1, max(r.size) // 2, r.lanes) if self.halves else (lines, 3, max(r.small), r.lanes)
        sems = dma((lines, 3, 2))
        return [pltpu.VMEM(land, BF16), sems, sems, dma((lines, OUTER, r.p.inner - 1, 2))]

    count = 4

    def bind(self, piece, target, refs):
        self.piece, self.target = piece, target
        self.land, self.s_sem, self.g_sem, self.x_sem = refs
        seq = lax.axis_index("seq")
        n = self.rows.p.inner
        self.z, self.x = lax.div(seq, n), lax.rem(seq, n)
        self.near, self.two, self.across = around(self.z)

    def copy(self, src, dst, sems, group):
        return remote(src, dst, sems, seq=group * self.rows.p.inner + self.x)

    def sum_copy(self, line, i):
        piece = self.piece(line, (self.near, self.across, self.two)[i])
        sems = self.s_sem.at[line, i, 0], self.s_sem.at[line, i, 1]
        return self.copy(piece, self.landing(line, i), sems, self.two if i == 2 else self.near)

    def landing(self, line, i):
        rows = self.rows.size[line] // 2 if self.halves else self.rows.small[line]
        return self.land.at[line, i, pl.ds(0, rows)]

    def sums(self, line):
        return [self.sum_copy(line, i) for i in range(1 if self.halves else 3)]

    def z_copy(self, line, i):
        where = self.target(line, self.two if i == 2 else self.z)
        sems = self.g_sem.at[line, i, 0], self.g_sem.at[line, i, 1]
        return self.copy(where, where, sems, self.two if i == 0 else self.near)

    def x_copies(self, line, c):
        n = self.rows.p.inner
        where = self.target(line, c)
        for s in range(1, n):
            sems = self.x_sem.at[line, c, s - 1, 0], self.x_sem.at[line, c, s - 1, 1]
            yield remote(where, where, sems, seq=self.z * n + lax.rem(self.x + s, n))

    def spread(self, line, c):
        for s in self.x_copies(line, c):
            s.start()

    def step_pair(self, line):
        self.sum_copy(line, 0).start()
        if not self.halves:
            self.sum_copy(line, 1).start()

    def step_two(self, line):
        for i, c in ((0, self.z), (1, self.two)):
            self.sum_copy(line, i).wait_recv()
            add_to(self.piece(line, c), [self.landing(line, i)[...]])
        self.sum_copy(line, 2).start()

    def step_back(self, line):
        last = 0 if self.halves else 2
        self.sum_copy(line, last).wait_recv()
        self.target(line, self.z)[...] = self.piece(line, self.z)[...] + self.landing(line, last)[...]
        self.z_copy(line, 0).start()
        self.z_copy(line, 1).start()
        self.spread(line, self.z)

    def step_rest(self, line):
        self.z_copy(line, 0).wait_recv()
        self.z_copy(line, 2).start()
        self.spread(line, self.two)
        self.z_copy(line, 1).wait_recv()
        self.spread(line, self.near)

    def step_last(self, line):
        self.z_copy(line, 2).wait_recv()
        self.spread(line, self.across)

    def end(self):
        for line in self.rows.lines:
            for c in range(OUTER):
                for s in self.x_copies(line, c):
                    s.wait_send()
                    s.wait_recv()
            for c in self.sums(line):
                c.wait_send()
            for i in range(3):
                self.z_copy(line, i).wait_send()


class Total:
    def __init__(self, places, rows):
        self.p = places
        self.rows = rows
        self.peers = [1, places.groups - 1, places.inner - 1, 1, 1]
        self.hops = range(5)
        self.count = 8

    def scratch(self):
        dma = pltpu.SemaphoreType.DMA
        out = [pltpu.VMEM((len(self.hops) + 1, self.rows, LANE), F32)]
        out += [pltpu.VMEM((k, self.rows, LANE), F32) for k in self.peers]
        return out + [dma((len(self.hops), max(self.peers))) for _ in range(2)]

    def bind(self, refs):
        self.held, self.land, self.sems = refs[0], refs[1:6], refs[6:]
        dp, seq = lax.axis_index("dp"), lax.axis_index("seq")
        n, groups = self.p.inner, self.p.groups
        core, group, z, x = lax.rem(dp, 2), lax.div(dp, 2), lax.div(seq, n), lax.rem(seq, n)
        near, two, _ = around(z)
        self.targets = [
            [{"dp": group * 2 + 1 - core}],
            [{"dp": lax.rem(group + t, groups) * 2 + core} for t in range(1, groups)],
            [{"seq": z * n + lax.rem(x + s, n)} for s in range(1, n)],
            [{"seq": near * n + x}],
            [{"seq": two * n + x}],
        ]

    def copies(self, hop):
        for i, target in enumerate(self.targets[hop]):
            yield remote(self.held.at[hop], self.land[hop].at[i], (self.sems[0].at[hop, i], self.sems[1].at[hop, i]), **target)

    def send(self, hop):
        for c in self.copies(hop):
            c.start()

    def step(self, hop):
        for c in self.copies(hop):
            c.wait_recv()
        total = self.held[hop]
        for i in range(self.peers[hop]):
            total = total + self.land[hop][i]
        self.held[hop + 1] = total
        if hop + 1 < len(self.hops):
            self.send(hop + 1)

    def end(self):
        for hop in self.hops:
            for c in self.copies(hop):
                c.wait_send()


def greet_all(places):
    dp, seq = lax.axis_index("dp"), lax.axis_index("seq")
    n = places.inner
    core, group = lax.rem(dp, 2), lax.div(dp, 2)
    barrier = pltpu.get_barrier_semaphore()
    mesh = pl.DeviceIdType.MESH
    pl.semaphore_signal(barrier, inc=1, device_id={"dp": group * 2 + 1 - core}, device_id_type=mesh)
    for t in range(1, places.groups):
        other = lax.rem(group + t, places.groups) * 2 + core
        pl.semaphore_signal(barrier, inc=1, device_id={"dp": other}, device_id_type=mesh)
    for peer in peers(n, lax.div(seq, n), lax.rem(seq, n)):
        pl.semaphore_signal(barrier, inc=1, device_id={"seq": peer}, device_id_type=mesh)
    pl.semaphore_wait(barrier, 1 + places.groups - 1 + OUTER - 1 + n - 1)


SMALL = 16


def last_kernel(early, late, *refs):
    count = 13
    sources, (gain_ref, ffn_ref), refs = refs[:count], refs[count : count + 2], refs[count + 2 :]
    grad_in, full_early, full_late, small_out, refs = refs[0], refs[1], refs[2], refs[3], refs[4:]
    slots, load_sem, refs = refs[:count], refs[count], refs[count + 1 :]
    p = late.p
    scatter, spread_early, spread_late = Scatter(late, (True, False)), Spread(early), Spread(late, True)
    (gq, gk, gv, arriving, n_sem), refs = refs[:5], refs[5:]
    scatter.bind((gq, gk, gv), refs[: scatter.count])
    refs = refs[scatter.count :]
    z, x = scatter.z, scatter.x
    columns = half_columns(z)
    loads = []
    for i, (src, dst) in enumerate(zip(sources, slots)):
        loads.append(pltpu.make_async_copy(src.at[:, columns] if 3 <= i < 6 else src, dst, load_sem.at[i]))
    for c in loads:
        c.start()
    held, grads, normed_t, wq_ref, wk_ref, wv_ref, x_ref, mixed_ref, near, far_sum, onehot, other, leaving = slots

    def early_piece(line, c):
        first = pl.multiple_of(early.part_start[line] + c * early.small[line], 16)
        return held.at[pl.ds(first, early.small[line])]

    def late_rows(line, c):
        size = late.size[line] // 2
        first = late.start[line] + x * late.size[line] + lax.rem(c, 2) * size
        return pl.ds(pl.multiple_of(first, 16), size)

    spread_early.bind(early_piece, lambda line, c: full_early.at[early.quarter(line, x, c)], refs[: Spread.count])
    spread_late.bind(
        lambda line, c: scatter.held.at[scatter.group, late_rows(line, c)],
        lambda line, c: full_late.at[lax.div(c, 2), late_rows(line, c)],
        refs[Spread.count : 2 * Spread.count],
    )
    total_small = Total(p, p.dp * SMALL)
    total_small.bind(refs[2 * Spread.count :])
    two = spread_early.two
    n_copy = remote(leaving, arriving, (n_sem.at[0], n_sem.at[1]), seq=two * p.inner + x)
    greet_all(p)
    loads[0].wait()
    loads[-1].wait()
    n_copy.start()
    early_lines, late_lines = list(early.lines), list(late.lines)
    for line in early_lines[:2]:
        spread_early.step_pair(line)
    for c in loads[1:-1]:
        c.wait()
    batch, height, width = x_ref.shape

    def weight(i, out):
        total = jnp.zeros((width, HALF), F32)
        for b in range(batch):
            for block in range(2):
                total = total + lax.dot_general(normed_t[block, b], grads[i, b, block], NT, preferred_element_type=F32)
        out[...] = total.astype(BF16)
        scatter.step_core((i,))

    for i, out in enumerate((gq, gk, gv)):
        weight(i, out)
    spread_early.step_two(0)
    spread_early.step_pair(2)
    scatter.step_first(late.lines)
    spread_early.step_two(1)
    spread_early.step_pair(3)
    gain = gain_ref[...].reshape(1, -1)
    gain_sums = []

    def positions(b, arrived):
        back = jnp.dot(wq_ref[...], grads[0, b, 0], preferred_element_type=F32)
        back = back + jnp.dot(wk_ref[...], grads[1, b, 0], preferred_element_type=F32)
        back = back + jnp.dot(wv_ref[...], grads[2, b, 0], preferred_element_type=F32)
        back = (back + arrived[...].astype(F32)).T
        values = x_ref[b]
        scale = lax.rsqrt(jnp.mean(values * values, axis=-1, keepdims=True) + epsilon)
        gain_sums.append(jnp.sum(back * values * scale, axis=0, keepdims=True))
        u = back * gain
        along = jnp.mean(u * values, axis=-1, keepdims=True)
        grad_in[b] = mixed_ref[b] + scale * (u - values * (scale * scale * along))

    positions(0, other.at[0])
    spread_early.step_back(0)
    spread_early.step_two(2)
    for line in late_lines:
        scatter.step_second(line)
    for b in range(1, batch - 1):
        positions(b, other.at[b])
    spread_early.step_back(1)
    spread_early.step_two(3)
    for line in late_lines:
        scatter.step_third(line)
        spread_late.step_pair(line)
    n_copy.wait_recv()
    positions(batch - 1, arriving)
    gain_sum = sum(gain_sums)
    spread_early.step_rest(0)
    spread_early.step_back(2)
    for line in late_lines:
        spread_late.step_back(line)
    row = lax.broadcasted_iota(jnp.int32, (BLK, BLK), 0)
    col = lax.broadcasted_iota(jnp.int32, (BLK, BLK), 1)
    flip = (row + col == BLK - 1).astype(F32)
    bucket = lax.broadcasted_iota(jnp.int32, (NB, 1), 0)
    head_lane = lax.broadcasted_iota(jnp.int32, (NB, LANE), 1)
    table = jnp.zeros((NB, LANE), F32)
    for h in range(HEADS):
        line = jnp.zeros((1, SPAN), F32)
        for off in (-1, 0, 1):
            flipped = jnp.dot(flip, near[h, off + 2], preferred_element_type=F32, precision=highest)
            padded = jnp.concatenate([flipped, jnp.zeros((BLK, SPAN - BLK), F32)], axis=1)
            rolled = pltpu.roll(padded, (BLK - off * BLK) % SPAN, 1, stride=1, stride_axis=0)
            line = line + jnp.sum(rolled, axis=0, keepdims=True)
        column = jnp.sum(onehot[...] * line, axis=1, keepdims=True)
        sides = jnp.sum(far_sum[h], axis=1, keepdims=True)
        column = column + jnp.where(bucket == NB // 2 - 1, sides[0:1], 0.0) + jnp.where(bucket == NB - 1, sides[1:2], 0.0)
        table = jnp.where(head_lane == z * HEADS + h, column, table)
    share, buckets = width // p.dp, NB // p.dp
    for i in range(p.dp):
        block = []
        for v in (gain_sum, ffn_ref[...]):
            for first, last in gain_rows(share):
                v_row = v[:, i * share + first : i * share + last]
                if last - first < LANE:
                    v_row = jnp.concatenate([v_row, jnp.zeros((1, LANE - (last - first)), F32)], axis=1)
                block.append(v_row)
        block.append(table[i * buckets : (i + 1) * buckets])
        block.append(jnp.zeros((SMALL - 2 * len(gain_rows(share)) - buckets, LANE), F32))
        total_small.held[0, i * SMALL : (i + 1) * SMALL] = jnp.concatenate(block, axis=0)
    total_small.send(0)
    spread_early.step_rest(1)
    spread_early.step_back(3)
    spread_early.step_last(0)
    total_small.step(0)
    for line in late_lines:
        spread_late.step_rest(line)
    spread_early.step_rest(2)
    spread_early.step_last(1)
    total_small.step(1)
    for line in late_lines:
        spread_late.step_last(line)
    spread_early.step_rest(3)
    total_small.step(2)
    spread_early.step_last(2)
    total_small.step(3)
    spread_early.step_last(3)
    total_small.step(4)
    mine = pl.ds(pl.multiple_of(lax.axis_index("dp") * SMALL, SMALL), SMALL)
    small_out[...] = total_small.held[len(total_small.hops), mine]
    total_small.end()
    n_copy.wait_send()
    spread_early.end()
    spread_late.end()
    scatter.end()


def gain_rows(share):
    return [(at, min(at + LANE, share)) for at in range(0, share, LANE)]


def half_columns(z):
    return pl.ds(pl.multiple_of(lax.div(z, 2) * HALF, LANE), HALF)


def last_grads(early, late, loaded, gain, ffn):
    inputs = loaded[6]
    width = inputs.shape[-1]
    shapes = [(width, HALF) if 3 <= i < 6 else v.shape for i, v in enumerate(loaded)]
    return pl.pallas_call(
        functools.partial(last_kernel, early, late),
        in_specs=[anywhere()] * len(loaded) + [whole()] * 2,
        out_specs=[whole()] * 4,
        out_shape=[
            jax.ShapeDtypeStruct(inputs.shape, F32),
            jax.ShapeDtypeStruct((early.total, early.lanes), BF16),
            jax.ShapeDtypeStruct((2, late.total, late.lanes), BF16),
            jax.ShapeDtypeStruct((SMALL, LANE), F32),
        ],
        scratch_shapes=[pltpu.VMEM(shape, v.dtype) for shape, v in zip(shapes, loaded)]
        + [pltpu.SemaphoreType.DMA((len(loaded),))]
        + [pltpu.VMEM((width, HALF), BF16)] * 3
        + [pltpu.VMEM(loaded[-1].shape, BF16), pltpu.SemaphoreType.DMA((2,))]
        + Scatter(late, (True, False)).scratch()
        + Spread(early).scratch()
        + Spread(late, True).scratch()
        + Total(late.p, late.p.dp * SMALL).scratch(),
        compiler_params=pltpu.CompilerParams(
            vmem_limit_bytes=VMEM_BYTES, collective_id=2, has_side_effects=True
        ),
        name="last_grads",
    )(*loaded, gain, ffn)


def unpack_kernel(early, late, full_early, full_late, small, *outs):
    for m, block, at, share in early.blocks:
        outs[m][:, block * LANES : (block + 1) * LANES] = full_early[at : at + share].astype(F32)
    outs = outs[len(early.shapes) :]
    for m, block, at, share in late.blocks:
        for half in range(2):
            first = half * HALF + block * LANE
            outs[m][:, first : first + LANE] = full_late[half, at : at + share].astype(F32)
    d_attn, d_ffn, d_table = outs[len(late.shapes) :]
    at = 0
    for out in (d_attn, d_ffn):
        for begin, end in gain_rows(out.shape[1]):
            out[:, begin:end] = small[at : at + 1, : end - begin]
            at += 1
    buckets, heads = d_table.shape
    d_table[...] = small[at : at + buckets, :heads]


def unpack(early, late, full_early, full_late, small, width):
    dp = early.p.dp
    shapes = [(height // dp, columns) for height, columns in early.shapes]
    shapes += [(width // dp, width)] * 3 + [(1, width // dp)] * 2 + [(NB // dp, H)]
    return pl.pallas_call(
        functools.partial(unpack_kernel, early, late),
        in_specs=[whole()] * 3,
        out_specs=[whole()] * len(shapes),
        out_shape=[jax.ShapeDtypeStruct(s, F32) for s in shapes],
        compiler_params=params(),
        name="unpack",
    )(full_early, full_late, small)


def greet(n, z, x):
    barrier = pltpu.get_barrier_semaphore()
    for peer in peers(n, z, x):
        pl.semaphore_signal(barrier, inc=1, device_id={"seq": peer}, device_id_type=pl.DeviceIdType.MESH)
    pl.semaphore_wait(barrier, OUTER - 1 + n - 1)


def far_case(n, j, kb):
    if kb < n * j - 1:
        return 0
    if kb > n * j + n:
        return 2
    return None


def near_case(n, j, kb, x):
    off = kb - (n * j + x)
    near = jnp.logical_and(off >= -1, off <= 1)
    return jnp.where(near, off + 2, 0), jnp.where(off <= -2, 0, jnp.where(off >= 2, 2, 1))


def key_rows(keys, kb, length):
    one = jnp.ones((1, BLK), F32)
    lane = lax.broadcasted_iota(jnp.int32, (1, BLK), 1)
    mask = jnp.where(kb * BLK + lane < length, 0.0, -1e30)
    return jnp.concatenate([keys, tail(BLK, (one, one, one, mask)).astype(BF16)], axis=0).T


def forward_kernel(
    n, len_ref, table_ref, onehot_ref, x_ref, gain_ref, wq_ref, wk_ref, wv_ref,
    normed_ref, own, pair, att, o_ref, lse_ref, tile_ref, far_ref,
    here, there, send, ka, qa, va,
    n_send, n_recv, z_send, z_recv, x_send, x_recv, o_send, o_recv,
):
    nk = OUTER * n
    batch = x_ref.shape[0]
    units = batch * HEADS
    me = lax.axis_index("seq")
    z, x = lax.div(me, n), lax.rem(me, n)
    greet(n, z, x)

    near, two, across = around(z)
    groups = (z, two, near, across)
    low = lax.rem(z, 2) == 0
    columns = half_columns(z)

    def n_copy(b):
        return remote(here.at[b], there.at[b], (n_send.at[b], n_recv.at[b]), seq=two * n + x)

    def z_copy(u, i):
        sems = z_send.at[u, i], z_recv.at[u, i]
        return remote(send.at[u, i], own.at[u, groups[i]], sems, seq=near * n + x)

    def x_copy(u, s, i):
        rows = pl.ds(DH, 2 * DH)
        sems = x_send.at[s - 1, u, i], x_recv.at[s - 1, u, i]
        peer = z * n + lax.rem(x + s, n)
        return remote(own.at[u, groups[i], rows], pair.at[s - 1, u, groups[i]], sems, seq=peer)

    def o_copy(u, d):
        group = lax.rem(z + d, OUTER)
        b, h = lax.div(u, HEADS), lax.rem(u, HEADS)
        rows = pl.ds(pl.multiple_of((z * HEADS + h) * DH, DH), DH)
        sems = o_send.at[u, d - 1], o_recv.at[u, d - 1]
        return remote(o_ref.at[u, group], att.at[b, rows], sems, seq=group * n + x)

    for b in range(batch):
        values = x_ref[b]
        scale = lax.rsqrt(jnp.mean(values * values, axis=-1, keepdims=True) + epsilon)
        here[b] = (values * scale * gain_ref[...].reshape(1, -1)).astype(BF16)
        if b == 0:
            n_copy(0).start()

    def project(b, i):
        normed = (here, there)[i][b]
        normed_ref[i, b] = normed.T
        for m, (w_ref, factor) in enumerate(((wq_ref, LOG2E), (wk_ref, 1.0), (wv_ref, 1.0))):
            turned = (jnp.dot(normed, w_ref[:, columns], preferred_element_type=F32) * factor).T.astype(BF16)
            for h in range(HEADS):
                first, second = turned[h * DH : (h + 1) * DH], turned[HW + h * DH : HW + (h + 1) * DH]
                rows = slice(m * DH, (m + 1) * DH)
                own[b * HEADS + h, groups[i], rows] = jnp.where(low, first, second)
                send[b * HEADS + h, i, rows] = jnp.where(low, second, first)
        for h in range(HEADS):
            for s in range(1, n):
                x_copy(b * HEADS + h, s, i).start()

    def start_near(b, i):
        for h in range(HEADS):
            z_copy(b * HEADS + h, i).start()

    for b in range(batch):
        project(b, 0)
        if b == 0:
            start_near(0, 0)

    table_lane = lax.broadcasted_iota(jnp.int32, (1, NB), 1)
    for h in range(HEADS):
        chosen = table_ref[pl.ds(z * HEADS + h, 1), :] * LOG2E
        padded = jnp.broadcast_to(chosen, (8, NB))
        line = jnp.dot(padded, onehot_ref[...], preferred_element_type=F32, precision=highest)[0:1]
        line = jnp.broadcast_to(line, (BLK, SPAN))
        tile_ref[h, 0] = jnp.zeros((BLK, BLK), F32)
        for off in (-1, 0, 1):
            shift = (off * BLK - (2 * BLK - 1)) % SPAN
            tile_ref[h, off + 2] = pltpu.roll(line, shift, 1, stride=1, stride_axis=0)[:, :BLK]
        for side, bucket in enumerate((NB // 2 - 1, NB - 1)):
            value = jnp.sum(jnp.where(table_lane == bucket, chosen, 0.0), axis=1, keepdims=True)
            far_ref[h, side] = jnp.broadcast_to(value, (1, BLK))

    def attend(u):
        b, h = lax.div(u, HEADS), lax.rem(u, HEADS)
        length = len_ref[b]
        left, right = far_ref[h, 0], far_ref[h, 1]
        one = jnp.ones((1, BLK), F32)
        vtail = tail(BLK, (one,)).astype(BF16)
        for s in range(1, n):
            for i in range(OUTER):
                x_copy(u, s, i).wait_recv()
        for s in range(n):
            col = lax.rem(x + s, n)
            for j in range(OUTER):
                kb = n * j + col
                if s == 0:
                    keys, vals = own[u, j, DH : 2 * DH], own[u, j, 2 * DH :]
                else:
                    keys, vals = pair[n - s - 1, u, j, :DH], pair[n - s - 1, u, j, DH:]
                ka[kb] = key_rows(keys, kb, length)
                columns = pl.ds(pl.multiple_of(kb * BLK, BLK), BLK)
                va[:DH, columns] = vals
                va[DH:, columns] = vtail

        def scores(kb, j):
            case = far_case(n, j, kb)
            if case is not None:
                return jnp.dot(ka[kb], qa[case, j], preferred_element_type=F32)
            tile, case = near_case(n, j, kb, x)
            return jnp.dot(ka[kb], qa[case, j], preferred_element_type=F32) + tile_ref[h, tile]

        for j in range(OUTER):
            for v, c in enumerate((left, 0.0 * one, right)):
                qa[v, j, :DH] = own[u, j, :DH]
                qa[v, j, DH:] = tail(BLK, split3(c) + (one,)).astype(BF16)
        tops = []
        for j in range(OUTER):
            top = jnp.full((8, BLK), -1e30, F32)
            for kb in range(nk):
                top = jnp.maximum(top, jnp.max(scores(kb, j).reshape(BLK // 8, 8, BLK), axis=0))
            top = jnp.max(top, axis=0, keepdims=True)
            tops.append(top)
            for v, c in enumerate((left, 0.0, right)):
                qa[v, j, DH:] = tail(BLK, split3(c - top) + (one,)).astype(BF16)
        for j in range(OUTER):
            weights = [jnp.exp2(scores(kb, j)).astype(BF16) for kb in range(nk)]
            total = jnp.dot(va[...], jnp.concatenate(weights, axis=0), preferred_element_type=F32)
            weight = total[DH : DH + 1]
            o_ref[u, j] = (total[:DH] / weight).astype(BF16)
            lse_ref[u, j] = tops[j] + jnp.log2(weight)
        rows = pl.ds(pl.multiple_of((z * HEADS + h) * DH, DH), DH)
        att[b, rows] = o_ref[u, z]
        @pl.when(u >= held_back)
        def _():
            start_o(u)

    held_back = units - HEADS - 1

    def start_o(u):
        for d in (2, 1, 3):
            o_copy(u, d).start()

    def turn(u, carry):
        @pl.when(jnp.logical_and(u < units, lax.rem(u, HEADS) == 0))
        def _():
            b = lax.div(u, HEADS)
            n_copy(b).wait_recv()

            @pl.when(b == batch - 1)
            def _():
                lax.fori_loop(0, held_back, lambda u, c: (start_o(u), c)[1], 0)

            @pl.when(b + 1 < batch)
            def _():
                n_copy(b + 1).start()

            project(b, 1)
            start_near(b, 1)

            @pl.when(b + 1 < batch)
            def _():
                start_near(b + 1, 0)

        @pl.when(u < units)
        def _():
            for i in range(2):
                z_copy(u, i).wait_recv()
                for s in range(1, n):
                    x_copy(u, s, 2 + i).start()

        @pl.when(u > 0)
        def _():
            attend(u - 1)

        return carry

    lax.fori_loop(0, units + 1, turn, 0)

    def finish(u, carry):
        for d in range(1, OUTER):
            o_copy(u, d).wait_send()
            o_copy(u, d).wait_recv()
        for i in range(2):
            z_copy(u, i).wait_send()
        for s in range(1, n):
            for i in range(OUTER):
                x_copy(u, s, i).wait_send()
        return carry

    lax.fori_loop(0, units, finish, 0)
    for b in range(batch):
        n_copy(b).wait_send()


def attention_forward(n, lengths, table, onehot, inputs, gain, wq, wk, wv):
    batch, height, width = inputs.shape
    units, nk = batch * HEADS, n * OUTER
    dma = pltpu.SemaphoreType.DMA
    return pl.pallas_call(
        functools.partial(forward_kernel, n),
        in_specs=[smem()] + [whole()] * 7,
        out_specs=[whole()] * 8,
        out_shape=[
            jax.ShapeDtypeStruct((2, batch, width, height), BF16),
            jax.ShapeDtypeStruct((units, OUTER, 3 * DH, BLK), BF16),
            jax.ShapeDtypeStruct((n - 1, units, OUTER, 2 * DH, BLK), BF16),
            jax.ShapeDtypeStruct((batch, width, height), BF16),
            jax.ShapeDtypeStruct((units, OUTER, DH, BLK), BF16),
            jax.ShapeDtypeStruct((units, OUTER, 1, BLK), F32),
            jax.ShapeDtypeStruct((HEADS, TILES, BLK, BLK), F32),
            jax.ShapeDtypeStruct((HEADS, 2, 1, BLK), F32),
        ],
        scratch_shapes=[
            pltpu.VMEM((batch, height, width), BF16),
            pltpu.VMEM((batch, height, width), BF16),
            pltpu.VMEM((units, 2, 3 * DH, BLK), BF16),
            pltpu.VMEM((nk, BLK, AUG), BF16),
            pltpu.VMEM((3, OUTER, AUG, BLK), BF16),
            pltpu.VMEM((AUG, nk * BLK), BF16),
            dma((batch,)),
            dma((batch,)),
            dma((units, 2)),
            dma((units, 2)),
            dma((n - 1, units, OUTER)),
            dma((n - 1, units, OUTER)),
            dma((units, OUTER - 1)),
            dma((units, OUTER - 1)),
        ],
        compiler_params=pltpu.CompilerParams(
            vmem_limit_bytes=VMEM_BYTES, collective_id=0, has_side_effects=True
        ),
        cost_estimate=pl.CostEstimate(flops=45 * 10**9, bytes_accessed=24 << 20, transcendentals=0),
        name="attention_forward",
    )(lengths, table, onehot, inputs, gain, wq, wk, wv)


def early_scatter(early):
    return Scatter(early, (True,) * len(early.lines))


def backward_kernel(
    n, early, len_ref, far_ref, tile_ref, own, pair, o_ref, lse_ref, dout, *refs
):
    scatter = early_scatter(early)
    count = len(early.shapes)
    weights, refs = refs[:count], refs[count:]
    projections, refs = refs[:3], refs[3:]
    (grads, near, far_sum, parts, other, leaving, w_half, other_out, w_sem, n_send, n_recv, own_slot, pair_slot, load_sem,
    do_land, x_out, x_land, z_out, kept,
    ka, kt, va, qa, da, dk_all, dv_all,
    d_send, d_recv, x_send, x_recv, z_send, z_recv) = refs[: -scatter.count]
    scatter.bind(weights, refs[-scatter.count :])
    nk = OUTER * n
    batch = dout.shape[0]
    units = batch * HEADS
    x_slots, z_slots = staging(n, units)
    me = lax.axis_index("seq")
    z, x = lax.div(me, n), lax.rem(me, n)
    near_z, two, across = around(z)
    low = lax.rem(z, 2) * HW
    greet_all(early.p)
    scatter.step_core()
    columns = half_columns(z)
    w_loads = [pltpu.make_async_copy(w.at[:, columns], w_half.at[m], w_sem.at[m]) for m, w in enumerate(projections)]
    for c in w_loads:
        c.start()

    def head_rows(group, h):
        return pl.ds(pl.multiple_of((group * HEADS + h) * DH, DH), DH)

    def d_copy(u, d):
        group = lax.rem(z + d, OUTER)
        b, h = lax.div(u, HEADS), lax.rem(u, HEADS)
        sems = d_send.at[u, d - 1], d_recv.at[u, d - 1]
        return remote(dout.at[b, head_rows(group, h)], do_land.at[u, z], sems, seq=group * n + x)

    def x_copy(u, s):
        peer = z * n + lax.rem(x + s, n)
        sems = x_send.at[s - 1, u], x_recv.at[s - 1, u]
        return remote(
            x_out.at[s - 1, lax.rem(u, x_slots)], x_land.at[s - 1, lax.rem(u, X_LAND)], sems, seq=peer
        )

    def half_rows(h):
        return pl.ds(pl.multiple_of(low + h * DH, DH), DH)

    def z_copy(u, i, m):
        b, h = lax.div(u, HEADS), lax.rem(u, HEADS)
        sems = z_send.at[u, i, m], z_recv.at[u, i, m]
        src, dst = z_out.at[lax.rem(u, z_slots), i, pl.ds(m * DH, DH)], grads.at[m, b, i, half_rows(h)]
        return remote(src, dst, sems, seq=near_z * n + x)

    def n_copy(b):
        return remote(other_out.at[b], other.at[b], (n_send.at[b], n_recv.at[b]), seq=two * n + x)

    def loads(u):
        slot = lax.rem(u, 2)
        yield pltpu.make_async_copy(own.at[u], own_slot.at[slot], load_sem.at[slot, 0])
        for s in range(1, n):
            yield pltpu.make_async_copy(pair.at[s - 1, u], pair_slot.at[slot, s - 1], load_sem.at[slot, s])

    for c in loads(0):
        c.start()

    def start_d(u):
        for d in (2, 1, 3):
            d_copy(u, d).start()

    start_d(0)
    start_d(1)

    def begin(u, carry):
        do_land[u, z] = dout[lax.div(u, HEADS), head_rows(z, lax.rem(u, HEADS))]
        return carry

    lax.fori_loop(0, units, begin, 0)
    near[...] = jnp.zeros_like(near)
    far_sum[...] = jnp.zeros_like(far_sum)
    one = jnp.ones((1, BLK), F32)
    ones3 = tail(BLK, (one, one, one)).astype(BF16)
    row16 = lax.broadcasted_iota(jnp.int32, (16, BLK), 0)
    marks = [jnp.where(row16 == r, 1.0, 0.0).astype(BF16) for r in range(2)]

    def work(u):
        b, h = lax.div(u, HEADS), lax.rem(u, HEADS)
        length = len_ref[b]
        left, right = far_ref[h, 0], far_ref[h, 1]
        slot = lax.rem(u, 2)
        for c in loads(u):
            c.wait()

        @pl.when(u + 1 < units)
        def _():
            for c in loads(u + 1):
                c.start()

        @pl.when(u + 2 < units)
        def _():
            start_d(u + 2)

        for s in range(n):
            col = lax.rem(x + s, n)
            for j in range(OUTER):
                kb = n * j + col
                if s == 0:
                    keys, vals = own_slot[slot, j, DH : 2 * DH], own_slot[slot, j, 2 * DH :]
                else:
                    keys, vals = pair_slot[slot, n - s - 1, j, :DH], pair_slot[slot, n - s - 1, j, DH:]
                ka[kb] = key_rows(keys, kb, length)
                kt[kb] = keys
                va[kb] = jnp.concatenate([vals, ones3], axis=0).T
        for d in range(1, OUTER):
            d_copy(u, d).wait_recv()
        for j in range(OUTER):
            lse = lse_ref[u, j]
            for v, c in enumerate((left, 0.0, right)):
                qa[v, j, :DH] = own_slot[slot, j, :DH]
                qa[v, j, DH:] = tail(BLK, split3(c - lse) + (one,)).astype(BF16)
            arrived = do_land[u, j]
            delta = jnp.sum(arrived.astype(F32) * o_ref[u, j].astype(F32), axis=0, keepdims=True)
            da[j, :DH] = arrived
            da[j, DH:] = tail(BLK, split3(-delta)).astype(BF16)
        dqs = [None] * OUTER
        for g in range(0, nk, GROUP):
            blocks = range(g, g + GROUP)
            ps, dss = {}, {}
            for j in range(OUTER):
                left_side = []
                for kb in blocks:
                    case = far_case(n, j, kb)
                    if case is not None:
                        p = jnp.exp2(jnp.dot(ka[kb], qa[case, j], preferred_element_type=F32))
                        mark = marks[case // 2]
                    else:
                        tile, case = near_case(n, j, kb, x)
                        s = jnp.dot(ka[kb], qa[case, j], preferred_element_type=F32)
                        p = jnp.exp2(s + tile_ref[h, tile])
                        want = jnp.where(case == 1, 2, lax.div(case, 2))
                        mark = jnp.where(row16 == want, 1.0, 0.0).astype(BF16)
                    ds = p * jnp.dot(va[kb], da[j], preferred_element_type=F32)
                    if far_case(n, j, kb) is None:
                        near[h, tile] += ds
                    ps[kb, j], dss[kb, j] = p.astype(BF16), ds.astype(BF16)
                    left_side.append(jnp.concatenate([kt[kb], mark], axis=0))
                right_side = jnp.concatenate([dss[kb, j] for kb in blocks], axis=0)
                dq = jnp.dot(jnp.concatenate(left_side, axis=1), right_side, preferred_element_type=F32)
                dqs[j] = dq if g == 0 else dqs[j] + dq
            for kb in blocks:
                dv, dk = jnp.zeros((DH, BLK), F32), jnp.zeros((DH, BLK), F32)
                for j in range(OUTER):
                    dv = dv + lax.dot_general(da[j, :DH], ps[kb, j], NT, preferred_element_type=F32)
                    dk = dk + lax.dot_general(qa[0, j, :DH], dss[kb, j], NT, preferred_element_type=F32)
                dk_all[kb] = dk * LN2
                dv_all[kb] = dv
        @pl.when(u >= x_slots)
        def _():
            for s in range(1, n):
                x_copy(u - x_slots, s).wait_send()

        far = jnp.zeros((8, BLK), F32)
        for j in range(OUTER):
            far = far + dqs[j][DH : DH + 8]
        far_sum[h] += far
        parity = lax.rem(u, 2)
        for j in range(OUTER):
            kept[parity, j, :DH] = dqs[j][:DH]
            kept[parity, j, DH : 2 * DH] = dk_all[n * j + x]
            kept[parity, j, 2 * DH :] = dv_all[n * j + x]
            for s in range(1, n):
                kb = n * j + lax.rem(x + s, n)
                x_out[s - 1, lax.rem(u, x_slots), j, :DH] = dk_all[kb].astype(BF16)
                x_out[s - 1, lax.rem(u, x_slots), j, DH:] = dv_all[kb].astype(BF16)
        for s in range(1, n):
            x_copy(u, s).start()

    def hand_over(u):
        b, h = lax.div(u, HEADS), lax.rem(u, HEADS)
        parity = lax.rem(u, 2)
        for s in range(1, n):
            x_copy(u, s).wait_recv()

        @pl.when(u >= z_slots)
        def _():
            for i in range(2):
                for m in range(3):
                    z_copy(u - z_slots, i, m).wait_send()

        for i, (mine, theirs) in enumerate(((z, near_z), (two, across))):
            for j, stays in ((mine, True), (theirs, False)):
                rest = kept[parity, j, DH:]
                for s in range(1, n):
                    rest = rest + x_land[s - 1, lax.rem(u, X_LAND), j].astype(F32)
                total = jnp.concatenate([kept[parity, j, :DH], rest], axis=0).astype(BF16)
                if stays:
                    for m in range(3):
                        grads[m, b, i, half_rows(h)] = total[m * DH : (m + 1) * DH]
                else:
                    z_out[lax.rem(u, z_slots), i] = total
            for m in range(3):
                z_copy(u, i, m).start()

    def combine(b):
        for h in range(HEADS):
            for i in range(2):
                for m in range(3):
                    z_copy(b * HEADS + h, i, m).wait_recv()
        total = jnp.dot(w_half[0], grads[0, b, 1], preferred_element_type=F32)
        total = total + jnp.dot(w_half[1], grads[1, b, 1], preferred_element_type=F32)
        total = total + jnp.dot(w_half[2], grads[2, b, 1], preferred_element_type=F32)
        @pl.when(b < batch - 1)
        def _():
            other_out[b] = total.astype(BF16)
            n_copy(b).start()

        @pl.when(b == batch - 1)
        def _():
            leaving[...] = total.astype(BF16)

    def turn(u, carry):
        @pl.when(u < units)
        def _():
            work(u)

        @pl.when(jnp.logical_and(u > 0, u <= units))
        def _():
            hand_over(u - 1)

        @pl.when(jnp.logical_and(u > HEADS, lax.rem(u - 1, HEADS) == 0))
        def _():
            combine(lax.div(u - 1, HEADS) - 1)

        @pl.when(u == 0)
        def _():
            scatter.step_first((0,))

        for line in early.lines:

            @pl.when(u == 2 * line + 2)
            def _():
                scatter.step_second(line)
                if line + 1 < len(early.lines):
                    scatter.start_first(line + 1)

        return carry

    for c in w_loads:
        c.wait()
    lax.fori_loop(0, units + 2, turn, 0)

    def finish(u, carry):
        for d in range(1, OUTER):
            d_copy(u, d).wait_send()

        @pl.when(u >= units - z_slots)
        def _():
            for i in range(2):
                for m in range(3):
                    z_copy(u, i, m).wait_send()

        @pl.when(u >= units - x_slots)
        def _():
            for s in range(1, n):
                x_copy(u, s).wait_send()

        return carry

    lax.fori_loop(0, units, finish, 0)
    for b in range(batch - 1):
        n_copy(b).wait_send()
        n_copy(b).wait_recv()
    for line in early.lines:
        scatter.step_third(line)
        parts[early.part_start[line] : early.part_start[line] + early.size[line]] = scatter.part(line)[...]
    scatter.end()


def staging(n, units):
    return (units, units) if n <= 2 else (2, 4)


X_LAND = 4


def attention_backward(n, early, lengths, far, tiles, own, pair, out, lse, dout, weights, projections):
    batch, width, height = dout.shape
    units, nk = batch * HEADS, n * OUTER
    dma = pltpu.SemaphoreType.DMA
    x_slots, z_slots = staging(n, units)
    return pl.pallas_call(
        functools.partial(backward_kernel, n, early),
        in_specs=[smem()] + [whole()] * 2 + [anywhere()] * 2 + [whole()] * 3 + [anywhere()] * (len(weights) + 3),
        out_specs=[whole()] * 6,
        out_shape=[
            jax.ShapeDtypeStruct((3, batch, 2, HALF, height), BF16),
            jax.ShapeDtypeStruct((HEADS, TILES, BLK, BLK), F32),
            jax.ShapeDtypeStruct((HEADS, 8, BLK), F32),
            jax.ShapeDtypeStruct((early.part_total, LANES), BF16),
            jax.ShapeDtypeStruct((batch - 1, width, height), BF16),
            jax.ShapeDtypeStruct((width, height), BF16),
        ],
        scratch_shapes=[
            pltpu.VMEM((3, width, HALF), BF16),
            pltpu.VMEM((batch - 1, width, height), BF16),
            dma((3,)),
            dma((batch - 1,)),
            dma((batch - 1,)),
            pltpu.VMEM((2, OUTER, 3 * DH, BLK), BF16),
            pltpu.VMEM((2, n - 1, OUTER, 2 * DH, BLK), BF16),
            dma((2, n)),
            pltpu.VMEM((units, OUTER, DH, BLK), BF16),
            pltpu.VMEM((n - 1, x_slots, OUTER, 2 * DH, BLK), BF16),
            pltpu.VMEM((n - 1, X_LAND, OUTER, 2 * DH, BLK), BF16),
            pltpu.VMEM((z_slots, 2, 3 * DH, BLK), BF16),
            pltpu.VMEM((2, OUTER, 3 * DH, BLK), F32),
            pltpu.VMEM((nk, BLK, AUG), BF16),
            pltpu.VMEM((nk, DH, BLK), BF16),
            pltpu.VMEM((nk, BLK, AUG), BF16),
            pltpu.VMEM((3, OUTER, AUG, BLK), BF16),
            pltpu.VMEM((OUTER, AUG, BLK), BF16),
            pltpu.VMEM((nk, DH, BLK), F32),
            pltpu.VMEM((nk, DH, BLK), F32),
            dma((units, OUTER - 1)),
            dma((units, OUTER - 1)),
            dma((n - 1, units)),
            dma((n - 1, units)),
            dma((units, 2, 3)),
            dma((units, 2, 3)),
        ]
        + early_scatter(early).scratch(),
        compiler_params=pltpu.CompilerParams(
            vmem_limit_bytes=VMEM_BYTES, collective_id=1, has_side_effects=True
        ),
        cost_estimate=pl.CostEstimate(flops=110 * 10**9, bytes_accessed=24 << 20, transcendentals=0),
        name="attention_backward",
    )(lengths, far, tiles, own, pair, out, lse, dout, *weights, *projections)


FF_STEP = 512


def middle_kernel(
    x_ref, att_ref, cot_ref, gain_ref, w_out, w_gate, w_up, w_down,
    result, grad_mixed, dout, d_gain, d_out, d_gate, d_up, d_down,
    wo, wg, wu, wd, att, low, hidden, g_gate, g_up, s_out, s_gate, s_up, s_down, kept, in_sem, out_sem,
):
    tokens, width = x_ref.shape
    batch = att_ref.shape[0]
    ff = w_gate.shape[1]
    loads = [
        pltpu.make_async_copy(src, dst, in_sem.at[i])
        for i, (src, dst) in enumerate(((w_out, wo), (w_gate, wg), (w_up, wu), (w_down, wd)))
    ]
    stores = [
        pltpu.make_async_copy(src, dst, out_sem.at[i])
        for i, (src, dst) in enumerate(((s_out, d_out), (s_gate, d_gate), (s_up, d_up), (s_down, d_down)))
    ]
    for c in loads:
        c.start()
    height = tokens // batch
    for b in range(batch):
        att[b * height : (b + 1) * height] = att_ref[b].T
    low[...] = cot_ref[...].astype(BF16)
    loads[0].wait()
    mixed = x_ref[...] + jnp.dot(att[...], wo[...], preferred_element_type=F32)
    kept[...] = mixed
    result[...] = mixed
    scale = lax.rsqrt(jnp.mean(mixed * mixed, axis=-1, keepdims=True) + epsilon)
    normed = (mixed * scale * gain_ref[...].reshape(1, -1)).astype(BF16)
    att[...] = normed
    for c in loads[1:]:
        c.wait()
    root = 0.7978845608028654
    for at in range(0, ff, FF_STEP):
        part = slice(at, at + FF_STEP)
        gate = jnp.dot(att[...], wg[:, part], preferred_element_type=F32)
        upward = jnp.dot(att[...], wu[:, part], preferred_element_type=F32)
        g_hidden = lax.dot_general(low[...], wd[part], NT, preferred_element_type=F32)
        square = gate * gate
        t = jnp.tanh(root * gate * (1.0 + 0.044715 * square))
        half = 0.5 * (1.0 + t)
        act = gate * half
        slope = half + 0.5 * gate * (1.0 - t * t) * (root * (1.0 + 3.0 * 0.044715 * square))
        hidden[:, part] = (act * upward).astype(BF16)
        g_gate[:, part] = (g_hidden * upward * slope).astype(BF16)
        g_up[:, part] = (g_hidden * act).astype(BF16)
    result[...] += jnp.dot(hidden[...], wd[...], preferred_element_type=F32)
    d_normed = lax.dot_general(g_gate[...], wg[...], NT, preferred_element_type=F32)
    d_normed = d_normed + lax.dot_general(g_up[...], wu[...], NT, preferred_element_type=F32)
    mixed = kept[...]
    scale = lax.rsqrt(jnp.mean(mixed * mixed, axis=-1, keepdims=True) + epsilon)
    d_gain[...] = jnp.sum(d_normed * mixed * scale, axis=0, keepdims=True)
    u = d_normed * gain_ref[...].reshape(1, -1)
    along = jnp.mean(u * mixed, axis=-1, keepdims=True)
    d_mixed = cot_ref[...] + scale * (u - mixed * (scale * scale * along))
    grad_mixed[...] = d_mixed
    d_low = d_mixed.astype(BF16)
    turned = lax.dot_general(wo[...], d_low, NT, preferred_element_type=F32).astype(BF16)
    for b in range(batch):
        dout[b] = turned[:, b * height : (b + 1) * height]
    total = jnp.zeros((width, width), F32)
    for b in range(batch):
        total = total + jnp.dot(att_ref[b], d_low[b * height : (b + 1) * height], preferred_element_type=F32)
    s_out[...] = total.astype(BF16)
    stores[0].start()
    normed_t = att[...].T
    for src, dst, store in ((g_gate, s_gate, stores[1]), (g_up, s_up, stores[2])):
        for at in range(0, ff, FF_STEP):
            part = slice(at, at + FF_STEP)
            dst[:, part] = jnp.dot(normed_t, src[:, part], preferred_element_type=F32).astype(BF16)
        store.start()
    for at in range(0, ff, FF_STEP):
        part = slice(at, at + FF_STEP)
        s_down[part] = jnp.dot(hidden[:, part].T, low[...], preferred_element_type=F32).astype(BF16)
    stores[3].start()
    for c in stores:
        c.wait()


def middle(inputs, att, cotangent, gain, w_out, w_gate, w_up, w_down):
    batch, height, width = inputs.shape
    tokens, ff = batch * height, w_gate.shape[1]
    weights = (w_out, w_gate, w_up, w_down)
    flat = (tokens, width)
    out = pl.pallas_call(
        middle_kernel,
        in_specs=[whole()] * 4 + [anywhere()] * 4,
        out_specs=[whole()] * 4 + [anywhere()] * 4,
        out_shape=[
            jax.ShapeDtypeStruct(flat, F32),
            jax.ShapeDtypeStruct(flat, F32),
            jax.ShapeDtypeStruct((batch, width, height), BF16),
            jax.ShapeDtypeStruct((1, width), F32),
        ]
        + [jax.ShapeDtypeStruct(w.shape, BF16) for w in weights],
        scratch_shapes=[pltpu.VMEM(w.shape, BF16) for w in weights]
        + [pltpu.VMEM(flat, BF16)] * 2
        + [pltpu.VMEM((tokens, ff), BF16)] * 3
        + [pltpu.VMEM(w.shape, BF16) for w in weights]
        + [pltpu.VMEM(flat, F32)]
        + [pltpu.SemaphoreType.DMA((4,))] * 2,
        compiler_params=params(),
        cost_estimate=pl.CostEstimate(flops=25 * 10**9, bytes_accessed=32 << 20, transcendentals=0),
        name="middle",
    )(inputs.reshape(flat), att, cotangent.reshape(flat), gain, *weights)
    return out[0].reshape(inputs.shape), out[1].reshape(inputs.shape), out[2], out[3], out[4:]


def shards(
    places,
    inputs,
    lengths,
    norm_attn,
    w_query,
    w_key,
    w_value,
    w_out,
    norm_ffn,
    w_gate,
    w_up,
    w_down,
    bucket_bias,
    cotangent,
):
    batch, height, width = inputs.shape
    n = places.inner
    onehot = jnp.asarray(ONEHOT)
    normed_t, own, pair, attended_t, out, lse, tiles, far = attention_forward(
        n, lengths, bucket_bias.T, onehot, inputs, norm_attn, w_query, w_key, w_value
    )
    result, grad_mixed, grad_attended_t, grad_norm_ffn, weights = middle(
        inputs, attended_t, cotangent, norm_ffn, w_out, w_gate, w_up, w_down
    )
    early = Rows(places, [g.shape for g in weights], LANES, 4)
    projections = (w_query, w_key, w_value)
    grads, near, far_sum, parts, other, leaving = attention_backward(
        n, early, lengths, far, tiles, own, pair, out, lse, grad_attended_t, weights, projections
    )
    late = Rows(places, [(width, HALF)] * 3, LANE, 2)
    loaded = (
        parts, grads, normed_t, *projections, inputs, grad_mixed, near, far_sum, onehot, other, leaving
    )
    grad_inputs, full_early, full_late, small = last_grads(early, late, loaded, norm_attn, grad_norm_ffn)
    part_out, part_gate, part_up, part_down, part_query, part_key, part_value, part_attn, part_ffn, part_table = unpack(
        early, late, full_early, full_late, small, width
    )
    return (
        result,
        grad_inputs,
        part_attn.reshape(-1),
        part_ffn.reshape(-1),
        part_query,
        part_key,
        part_value,
        part_out,
        part_gate,
        part_up,
        part_down,
        part_table,
    )


def solution(mesh):
    rows = P("dp", "seq", None)
    share = P("dp", None)
    return jax.shard_map(
        functools.partial(shards, Places(mesh)),
        mesh=mesh,
        in_specs=(rows, P("dp")) + (P(),) * 10 + (rows,),
        out_specs=(rows, rows, P("dp"), P("dp")) + (share,) * 8,
        check_vma=False,
    )
```

```python
import functools

import jax
import jax.numpy as jnp
import numpy as np
from jax import lax
from jax.experimental import pallas as pl
from jax.experimental.pallas import tpu as pltpu
from jax.sharding import PartitionSpec as P

H = 12
DH = 64
NB = 32
OUTER = 4
HEADS = H // OUTER
HW = HEADS * DH
HALF = 2 * HW
BLK = 256
AUG = DH + 16
SPAN = 4 * BLK
LANES = 256
LANE = 128
LOG2E = 1.4426950408889634
LN2 = 0.6931471805599453
F32 = jnp.float32
BF16 = jnp.bfloat16
NT = (((1,), (1,)), ((), ()))
VMEM_BYTES = 62 << 20
GROUP = 8
TILES = 4

epsilon = 1e-06
limits = (1, 2, 3, 4, 5, 6, 7, 8, 12, 16, 23, 32, 46, 64, 91)
highest = lax.Precision.HIGHEST


def bucket_lines():
    relative = 2 * BLK - 1 - np.arange(SPAN)
    count = sum((np.abs(relative) >= limit).astype(np.int32) for limit in limits)
    bucket = count + (relative > 0).astype(np.int32) * (NB // 2)
    return (bucket[None, :] == np.arange(NB)[:, None]).astype(np.float32)


ONEHOT = bucket_lines()


def params():
    return pltpu.CompilerParams(vmem_limit_bytes=VMEM_BYTES)


def smem():
    return pl.BlockSpec(memory_space=pltpu.SMEM)


def anywhere():
    return pl.BlockSpec(memory_space=pl.ANY)


def whole():
    return pl.BlockSpec(memory_space=pltpu.VMEM)


def split3(v):
    a = v.astype(BF16)
    r = v - a.astype(F32)
    b = r.astype(BF16)
    c = (r - b.astype(F32)).astype(BF16)
    return a.astype(F32), b.astype(F32), c.astype(F32)


def tail(width, values):
    row = lax.broadcasted_iota(jnp.int32, (16, width), 0)
    out = jnp.zeros((16, width), F32)
    for i, v in enumerate(values):
        out = jnp.where(row == i, v, out)
    return out


def peers(n, z, x):
    return [lax.rem(z + d, OUTER) * n + x for d in range(1, OUTER)] + [z * n + lax.rem(x + s, n) for s in range(1, n)]


def around(z):
    near = z + 1 - 2 * lax.rem(z, 2)
    return near, lax.rem(z + 2, OUTER), lax.rem(near + 2, OUTER)


class Places:
    def __init__(self, mesh):
        self.dp = mesh.shape["dp"]
        self.groups = self.dp // 2
        self.inner = mesh.shape["seq"] // OUTER


def remote(src, dst, sems, **peer):
    return pltpu.make_async_remote_copy(
        src_ref=src,
        dst_ref=dst,
        send_sem=sems[0],
        recv_sem=sems[1],
        device_id=peer,
        device_id_type=pl.DeviceIdType.MESH,
    )


class Rows:
    def __init__(self, places, shapes, lanes, lines):
        self.p = places
        self.shapes = shapes
        self.lanes = lanes
        self.lines = range(lines)
        grain = places.inner * OUTER * 16
        self.blocks = []
        at = 0
        for m, (rows, columns) in enumerate(shapes):
            share = rows // places.dp
            for block in range(columns // lanes):
                self.blocks.append((m, block, at, share))
                at += share
        self.used = at
        grains = max(-(-at // grain), lines)
        self.total = grains * grain
        cuts = [grains * line // lines * grain for line in range(lines + 1)]
        self.start = cuts[:-1]
        self.span = [b - a for a, b in zip(cuts[:-1], cuts[1:])]
        self.size = [v // places.inner for v in self.span]
        self.small = [v // OUTER for v in self.size]
        self.part_start = [v // places.inner for v in self.start]
        self.part_total = self.total // places.inner

    def line(self, line):
        return pl.ds(self.start[line], self.span[line])

    def part(self, line, x):
        return pl.ds(pl.multiple_of(self.start[line] + x * self.size[line], 16), self.size[line])

    def quarter(self, line, x, z):
        first = self.start[line] + x * self.size[line] + z * self.small[line]
        return pl.ds(pl.multiple_of(first, 16), self.small[line])


def add_to(ref, arrived):
    if len(arrived) == 1:
        ref[...] = ref[...] + arrived[0]
        return
    total = ref[...].astype(F32)
    for a in arrived:
        total = total + a.astype(F32)
    ref[...] = total.astype(BF16)


class Scatter:
    def __init__(self, rows, y_first):
        self.rows = rows
        self.y_first = y_first
        self.count = 5 + 2 * len(rows.lines)

    def scratch(self):
        r, p, dma = self.rows, self.rows.p, pltpu.SemaphoreType.DMA
        g, n, lines = p.groups, p.inner, len(r.lines)
        out = [pltpu.VMEM((g, r.total, r.lanes), BF16), pltpu.VMEM((g, r.total, r.lanes), BF16)]
        for line, y_first in enumerate(self.y_first):
            out.append(pltpu.VMEM((g - 1, r.span[line] if y_first else r.size[line], r.lanes), BF16))
            out.append(pltpu.VMEM((n - 1, 1 if y_first else g, r.size[line], r.lanes), BF16))
        return out + [dma((len(r.blocks), g, 3)), dma((lines, g - 1, 2)), dma((lines, n - 1, g, 2))]

    def bind(self, grads, refs):
        self.grads = grads
        self.held, self.land = refs[:2]
        self.c_sem, self.y_sem, self.x_sem = refs[-3:]
        self.y_land, self.x_land = refs[2:-3:2], refs[3:-3:2]
        dp, seq = lax.axis_index("dp"), lax.axis_index("seq")
        n = self.rows.p.inner
        self.core, self.group = lax.rem(dp, 2), lax.div(dp, 2)
        self.z, self.x = lax.div(seq, n), lax.rem(seq, n)

    def source(self, i, g, core):
        m, block, at, share = self.rows.blocks[i]
        first = pl.multiple_of((g * 2 + core) * share, 16)
        return self.grads[m].at[pl.ds(first, share), pl.ds(block * self.rows.lanes, self.rows.lanes)], pl.ds(at, share)

    def picked(self, chosen):
        return [i for i, b in enumerate(self.rows.blocks) if chosen is None or b[0] in chosen]

    def core_copies(self, chosen=None):
        for i in self.picked(chosen):
            for g in range(self.rows.p.groups):
                src, where = self.source(i, g, 1 - self.core)
                sems = self.c_sem.at[i, g, 0], self.c_sem.at[i, g, 1]
                yield remote(src, self.land.at[g, where], sems, dp=self.group * 2 + 1 - self.core)

    def own_copies(self, chosen=None):
        for i in self.picked(chosen):
            for g in range(self.rows.p.groups):
                src, where = self.source(i, g, self.core)
                yield pltpu.make_async_copy(src, self.held.at[g, where], self.c_sem.at[i, g, 2])

    def y_copies(self, line):
        r = self.rows
        for t in range(1, r.p.groups):
            other = lax.rem(self.group + t, r.p.groups)
            where = r.line(line) if self.y_first[line] else r.part(line, self.x)
            sems = self.y_sem.at[line, t - 1, 0], self.y_sem.at[line, t - 1, 1]
            yield remote(self.held.at[other, where], self.y_land[line].at[t - 1], sems, dp=other * 2 + self.core)

    def x_copies(self, line):
        r = self.rows
        n = r.p.inner
        for s in range(1, n):
            other = lax.rem(self.x + s, n)
            where = r.part(line, other)
            for g in range(1 if self.y_first[line] else r.p.groups):
                sems = self.x_sem.at[line, s - 1, g, 0], self.x_sem.at[line, s - 1, g, 1]
                src = self.held.at[self.group if self.y_first[line] else g, where]
                yield remote(src, self.x_land[line].at[s - 1, g], sems, seq=self.z * n + other)

    def hop(self, line, which):
        return self.y_copies(line) if (which == 0) == self.y_first[line] else self.x_copies(line)


    def step_core(self, chosen=None):
        for c in self.core_copies(chosen):
            c.start()
        for c in self.own_copies(chosen):
            c.start()

    def step_first(self, begin):
        r = self.rows
        for c in self.core_copies():
            c.wait_recv()
        for c in self.own_copies():
            c.wait()
        for line in r.lines:
            end = r.start[line] + r.span[line]
            first, last = r.start[line], min(end, r.used)
            for g in range(r.p.groups):
                where = pl.ds(first, last - first)
                add_to(self.held.at[g, where], [self.land[g, where]])
                if last < end:
                    self.held[g, last:end] = jnp.zeros((end - last, r.lanes), BF16)
            if line in begin:
                self.start_first(line)

    def start_first(self, line):
        for c in self.hop(line, 0):
            c.start()

    def step_second(self, line):
        r = self.rows
        for c in self.hop(line, 0):
            c.wait_recv()
        if self.y_first[line]:
            arrived = [self.y_land[line][t] for t in range(r.p.groups - 1)]
            add_to(self.held.at[self.group, r.line(line)], arrived)
        else:
            for g in range(r.p.groups):
                arrived = [self.x_land[line][s, g] for s in range(r.p.inner - 1)]
                add_to(self.held.at[g, r.part(line, self.x)], arrived)
        for c in self.hop(line, 1):
            c.start()

    def step_third(self, line):
        r = self.rows
        for c in self.hop(line, 1):
            c.wait_recv()
        if self.y_first[line]:
            arrived = [self.x_land[line][s, 0] for s in range(r.p.inner - 1)]
        else:
            arrived = [self.y_land[line][t] for t in range(r.p.groups - 1)]
        add_to(self.held.at[self.group, r.part(line, self.x)], arrived)

    def part(self, line):
        return self.held.at[self.group, self.rows.part(line, self.x)]

    def end(self):
        for c in self.core_copies():
            c.wait_send()
        for line in self.rows.lines:
            for which in range(2):
                for c in self.hop(line, which):
                    c.wait_send()


class Spread:
    def __init__(self, rows, halves=False):
        self.rows = rows
        self.halves = halves

    def scratch(self):
        r, dma = self.rows, pltpu.SemaphoreType.DMA
        lines = len(r.lines)
        land = (lines, 1, max(r.size) // 2, r.lanes) if self.halves else (lines, 3, max(r.small), r.lanes)
        sems = dma((lines, 3, 2))
        return [pltpu.VMEM(land, BF16), sems, sems, dma((lines, OUTER, r.p.inner - 1, 2))]

    count = 4

    def bind(self, piece, target, refs):
        self.piece, self.target = piece, target
        self.land, self.s_sem, self.g_sem, self.x_sem = refs
        seq = lax.axis_index("seq")
        n = self.rows.p.inner
        self.z, self.x = lax.div(seq, n), lax.rem(seq, n)
        self.near, self.two, self.across = around(self.z)

    def copy(self, src, dst, sems, group):
        return remote(src, dst, sems, seq=group * self.rows.p.inner + self.x)

    def sum_copy(self, line, i):
        piece = self.piece(line, (self.near, self.across, self.two)[i])
        sems = self.s_sem.at[line, i, 0], self.s_sem.at[line, i, 1]
        return self.copy(piece, self.landing(line, i), sems, self.two if i == 2 else self.near)

    def landing(self, line, i):
        rows = self.rows.size[line] // 2 if self.halves else self.rows.small[line]
        return self.land.at[line, i, pl.ds(0, rows)]

    def sums(self, line):
        return [self.sum_copy(line, i) for i in range(1 if self.halves else 3)]

    def z_copy(self, line, i):
        where = self.target(line, self.two if i == 2 else self.z)
        sems = self.g_sem.at[line, i, 0], self.g_sem.at[line, i, 1]
        return self.copy(where, where, sems, self.two if i == 0 else self.near)

    def x_copies(self, line, c):
        n = self.rows.p.inner
        where = self.target(line, c)
        for s in range(1, n):
            sems = self.x_sem.at[line, c, s - 1, 0], self.x_sem.at[line, c, s - 1, 1]
            yield remote(where, where, sems, seq=self.z * n + lax.rem(self.x + s, n))

    def spread(self, line, c):
        for s in self.x_copies(line, c):
            s.start()

    def step_pair(self, line):
        self.sum_copy(line, 0).start()
        if not self.halves:
            self.sum_copy(line, 1).start()

    def step_two(self, line):
        for i, c in ((0, self.z), (1, self.two)):
            self.sum_copy(line, i).wait_recv()
            add_to(self.piece(line, c), [self.landing(line, i)[...]])
        self.sum_copy(line, 2).start()

    def step_back(self, line):
        last = 0 if self.halves else 2
        self.sum_copy(line, last).wait_recv()
        self.target(line, self.z)[...] = self.piece(line, self.z)[...] + self.landing(line, last)[...]
        self.z_copy(line, 0).start()
        self.z_copy(line, 1).start()
        self.spread(line, self.z)

    def step_rest(self, line):
        self.z_copy(line, 0).wait_recv()
        self.z_copy(line, 2).start()
        self.spread(line, self.two)
        self.z_copy(line, 1).wait_recv()
        self.spread(line, self.near)

    def step_last(self, line):
        self.z_copy(line, 2).wait_recv()
        self.spread(line, self.across)

    def end(self):
        for line in self.rows.lines:
            for c in range(OUTER):
                for s in self.x_copies(line, c):
                    s.wait_send()
                    s.wait_recv()
            for c in self.sums(line):
                c.wait_send()
            for i in range(3):
                self.z_copy(line, i).wait_send()


class Total:
    def __init__(self, places, rows):
        self.p = places
        self.rows = rows
        self.peers = [1, places.groups - 1, places.inner - 1, 1, 1]
        self.hops = range(5)
        self.count = 8

    def scratch(self):
        dma = pltpu.SemaphoreType.DMA
        out = [pltpu.VMEM((len(self.hops) + 1, self.rows, LANE), F32)]
        out += [pltpu.VMEM((k, self.rows, LANE), F32) for k in self.peers]
        return out + [dma((len(self.hops), max(self.peers))) for _ in range(2)]

    def bind(self, refs):
        self.held, self.land, self.sems = refs[0], refs[1:6], refs[6:]
        dp, seq = lax.axis_index("dp"), lax.axis_index("seq")
        n, groups = self.p.inner, self.p.groups
        core, group, z, x = lax.rem(dp, 2), lax.div(dp, 2), lax.div(seq, n), lax.rem(seq, n)
        near, two, _ = around(z)
        self.targets = [
            [{"dp": group * 2 + 1 - core}],
            [{"dp": lax.rem(group + t, groups) * 2 + core} for t in range(1, groups)],
            [{"seq": z * n + lax.rem(x + s, n)} for s in range(1, n)],
            [{"seq": near * n + x}],
            [{"seq": two * n + x}],
        ]

    def copies(self, hop):
        for i, target in enumerate(self.targets[hop]):
            yield remote(self.held.at[hop], self.land[hop].at[i], (self.sems[0].at[hop, i], self.sems[1].at[hop, i]), **target)

    def send(self, hop):
        for c in self.copies(hop):
            c.start()

    def step(self, hop):
        for c in self.copies(hop):
            c.wait_recv()
        total = self.held[hop]
        for i in range(self.peers[hop]):
            total = total + self.land[hop][i]
        self.held[hop + 1] = total
        if hop + 1 < len(self.hops):
            self.send(hop + 1)

    def end(self):
        for hop in self.hops:
            for c in self.copies(hop):
                c.wait_send()


def greet_all(places):
    dp, seq = lax.axis_index("dp"), lax.axis_index("seq")
    n = places.inner
    core, group = lax.rem(dp, 2), lax.div(dp, 2)
    barrier = pltpu.get_barrier_semaphore()
    mesh = pl.DeviceIdType.MESH
    pl.semaphore_signal(barrier, inc=1, device_id={"dp": group * 2 + 1 - core}, device_id_type=mesh)
    for t in range(1, places.groups):
        other = lax.rem(group + t, places.groups) * 2 + core
        pl.semaphore_signal(barrier, inc=1, device_id={"dp": other}, device_id_type=mesh)
    for peer in peers(n, lax.div(seq, n), lax.rem(seq, n)):
        pl.semaphore_signal(barrier, inc=1, device_id={"seq": peer}, device_id_type=mesh)
    pl.semaphore_wait(barrier, 1 + places.groups - 1 + OUTER - 1 + n - 1)


SMALL = 16


def last_kernel(early, late, *refs):
    count = 13
    sources, (gain_ref, ffn_ref), refs = refs[:count], refs[count : count + 2], refs[count + 2 :]
    grad_in, full_early, full_late, small_out, refs = refs[0], refs[1], refs[2], refs[3], refs[4:]
    slots, load_sem, refs = refs[:count], refs[count], refs[count + 1 :]
    p = late.p
    scatter, spread_early, spread_late = Scatter(late, (True, False)), Spread(early), Spread(late, True)
    (gq, gk, gv, arriving, n_sem), refs = refs[:5], refs[5:]
    scatter.bind((gq, gk, gv), refs[: scatter.count])
    refs = refs[scatter.count :]
    z, x = scatter.z, scatter.x
    columns = half_columns(z)
    loads = []
    for i, (src, dst) in enumerate(zip(sources, slots)):
        loads.append(pltpu.make_async_copy(src.at[:, columns] if 3 <= i < 6 else src, dst, load_sem.at[i]))
    for c in loads:
        c.start()
    held, grads, normed_t, wq_ref, wk_ref, wv_ref, x_ref, mixed_ref, near, far_sum, onehot, other, leaving = slots

    def early_piece(line, c):
        first = pl.multiple_of(early.part_start[line] + c * early.small[line], 16)
        return held.at[pl.ds(first, early.small[line])]

    def late_rows(line, c):
        size = late.size[line] // 2
        first = late.start[line] + x * late.size[line] + lax.rem(c, 2) * size
        return pl.ds(pl.multiple_of(first, 16), size)

    spread_early.bind(early_piece, lambda line, c: full_early.at[early.quarter(line, x, c)], refs[: Spread.count])
    spread_late.bind(
        lambda line, c: scatter.held.at[scatter.group, late_rows(line, c)],
        lambda line, c: full_late.at[lax.div(c, 2), late_rows(line, c)],
        refs[Spread.count : 2 * Spread.count],
    )
    total_small = Total(p, p.dp * SMALL)
    total_small.bind(refs[2 * Spread.count :])
    two = spread_early.two
    n_copy = remote(leaving, arriving, (n_sem.at[0], n_sem.at[1]), seq=two * p.inner + x)
    greet_all(p)
    loads[0].wait()
    loads[-1].wait()
    n_copy.start()
    early_lines, late_lines = list(early.lines), list(late.lines)
    for line in early_lines:
        spread_early.step_pair(line)
    for c in loads[1:-1]:
        c.wait()
    batch, height, width = x_ref.shape

    def weight(i, out):
        total = jnp.zeros((width, HALF), F32)
        for b in range(batch):
            for block in range(2):
                total = total + lax.dot_general(normed_t[block, b], grads[i, b, block], NT, preferred_element_type=F32)
        out[...] = total.astype(BF16)
        scatter.step_core((i,))

    for i, out in enumerate((gq, gk, gv)):
        weight(i, out)
    spread_early.step_two(0)
    scatter.step_first(late.lines)
    spread_early.step_two(1)
    gain = gain_ref[...].reshape(1, -1)
    gain_sums = []

    def positions(b, arrived):
        back = jnp.dot(wq_ref[...], grads[0, b, 0], preferred_element_type=F32)
        back = back + jnp.dot(wk_ref[...], grads[1, b, 0], preferred_element_type=F32)
        back = back + jnp.dot(wv_ref[...], grads[2, b, 0], preferred_element_type=F32)
        back = (back + arrived[...].astype(F32)).T
        values = x_ref[b]
        scale = lax.rsqrt(jnp.mean(values * values, axis=-1, keepdims=True) + epsilon)
        gain_sums.append(jnp.sum(back * values * scale, axis=0, keepdims=True))
        u = back * gain
        along = jnp.mean(u * values, axis=-1, keepdims=True)
        grad_in[b] = mixed_ref[b] + scale * (u - values * (scale * scale * along))

    positions(0, other.at[0])
    spread_early.step_back(0)
    spread_early.step_two(2)
    for line in late_lines:
        scatter.step_second(line)
    for b in range(1, batch - 1):
        positions(b, other.at[b])
    spread_early.step_back(1)
    spread_early.step_two(3)
    for line in late_lines:
        scatter.step_third(line)
        spread_late.step_pair(line)
    n_copy.wait_recv()
    positions(batch - 1, arriving)
    gain_sum = sum(gain_sums)
    spread_early.step_rest(0)
    spread_early.step_back(2)
    for line in late_lines:
        spread_late.step_back(line)
    row = lax.broadcasted_iota(jnp.int32, (BLK, BLK), 0)
    col = lax.broadcasted_iota(jnp.int32, (BLK, BLK), 1)
    flip = (row + col == BLK - 1).astype(F32)
    bucket = lax.broadcasted_iota(jnp.int32, (NB, 1), 0)
    head_lane = lax.broadcasted_iota(jnp.int32, (NB, LANE), 1)
    table = jnp.zeros((NB, LANE), F32)
    for h in range(HEADS):
        line = jnp.zeros((1, SPAN), F32)
        for off in (-1, 0, 1):
            flipped = jnp.dot(flip, near[h, off + 2], preferred_element_type=F32, precision=highest)
            padded = jnp.concatenate([flipped, jnp.zeros((BLK, SPAN - BLK), F32)], axis=1)
            rolled = pltpu.roll(padded, (BLK - off * BLK) % SPAN, 1, stride=1, stride_axis=0)
            line = line + jnp.sum(rolled, axis=0, keepdims=True)
        column = jnp.sum(onehot[...] * line, axis=1, keepdims=True)
        sides = jnp.sum(far_sum[h], axis=1, keepdims=True)
        column = column + jnp.where(bucket == NB // 2 - 1, sides[0:1], 0.0) + jnp.where(bucket == NB - 1, sides[1:2], 0.0)
        table = jnp.where(head_lane == z * HEADS + h, column, table)
    share, buckets = width // p.dp, NB // p.dp
    for i in range(p.dp):
        block = []
        for v in (gain_sum, ffn_ref[...]):
            for first, last in gain_rows(share):
                v_row = v[:, i * share + first : i * share + last]
                if last - first < LANE:
                    v_row = jnp.concatenate([v_row, jnp.zeros((1, LANE - (last - first)), F32)], axis=1)
                block.append(v_row)
        block.append(table[i * buckets : (i + 1) * buckets])
        block.append(jnp.zeros((SMALL - 2 * len(gain_rows(share)) - buckets, LANE), F32))
        total_small.held[0, i * SMALL : (i + 1) * SMALL] = jnp.concatenate(block, axis=0)
    total_small.send(0)
    spread_early.step_rest(1)
    spread_early.step_back(3)
    spread_early.step_last(0)
    total_small.step(0)
    for line in late_lines:
        spread_late.step_rest(line)
    spread_early.step_rest(2)
    spread_early.step_last(1)
    total_small.step(1)
    for line in late_lines:
        spread_late.step_last(line)
    spread_early.step_rest(3)
    total_small.step(2)
    spread_early.step_last(2)
    total_small.step(3)
    spread_early.step_last(3)
    total_small.step(4)
    mine = pl.ds(pl.multiple_of(lax.axis_index("dp") * SMALL, SMALL), SMALL)
    small_out[...] = total_small.held[len(total_small.hops), mine]
    total_small.end()
    n_copy.wait_send()
    spread_early.end()
    spread_late.end()
    scatter.end()


def gain_rows(share):
    return [(at, min(at + LANE, share)) for at in range(0, share, LANE)]


def half_columns(z):
    return pl.ds(pl.multiple_of(lax.div(z, 2) * HALF, LANE), HALF)


def last_grads(early, late, loaded, gain, ffn):
    inputs = loaded[6]
    width = inputs.shape[-1]
    shapes = [(width, HALF) if 3 <= i < 6 else v.shape for i, v in enumerate(loaded)]
    return pl.pallas_call(
        functools.partial(last_kernel, early, late),
        in_specs=[anywhere()] * len(loaded) + [whole()] * 2,
        out_specs=[whole()] * 4,
        out_shape=[
            jax.ShapeDtypeStruct(inputs.shape, F32),
            jax.ShapeDtypeStruct((early.total, early.lanes), BF16),
            jax.ShapeDtypeStruct((2, late.total, late.lanes), BF16),
            jax.ShapeDtypeStruct((SMALL, LANE), F32),
        ],
        scratch_shapes=[pltpu.VMEM(shape, v.dtype) for shape, v in zip(shapes, loaded)]
        + [pltpu.SemaphoreType.DMA((len(loaded),))]
        + [pltpu.VMEM((width, HALF), BF16)] * 3
        + [pltpu.VMEM(loaded[-1].shape, BF16), pltpu.SemaphoreType.DMA((2,))]
        + Scatter(late, (True, False)).scratch()
        + Spread(early).scratch()
        + Spread(late, True).scratch()
        + Total(late.p, late.p.dp * SMALL).scratch(),
        compiler_params=pltpu.CompilerParams(
            vmem_limit_bytes=VMEM_BYTES, collective_id=2, has_side_effects=True
        ),
        name="last_grads",
    )(*loaded, gain, ffn)


def unpack_kernel(early, late, full_early, full_late, small, grad_in, *outs):
    *outs, grad_out, held, sems = outs
    arrive = pltpu.make_async_copy(grad_in, held, sems.at[0])
    leave = pltpu.make_async_copy(held, grad_out, sems.at[1])
    arrive.start()
    for m, block, at, share in early.blocks:
        outs[m][:, block * LANES : (block + 1) * LANES] = full_early[at : at + share].astype(F32)
    arrive.wait()
    leave.start()
    outs = outs[len(early.shapes) :]
    for m, block, at, share in late.blocks:
        for half in range(2):
            first = half * HALF + block * LANE
            outs[m][:, first : first + LANE] = full_late[half, at : at + share].astype(F32)
    d_attn, d_ffn, d_table = outs[len(late.shapes) :]
    at = 0
    for out in (d_attn, d_ffn):
        for begin, end in gain_rows(out.shape[1]):
            out[:, begin:end] = small[at : at + 1, : end - begin]
            at += 1
    buckets, heads = d_table.shape
    d_table[...] = small[at : at + buckets, :heads]
    leave.wait()


def unpack(early, late, full_early, full_late, small, grad_in):
    width = grad_in.shape[-1]
    dp = early.p.dp
    shapes = [(height // dp, columns) for height, columns in early.shapes]
    shapes += [(width // dp, width)] * 3 + [(1, width // dp)] * 2 + [(NB // dp, H)]
    return pl.pallas_call(
        functools.partial(unpack_kernel, early, late),
        in_specs=[whole()] * 3 + [anywhere()],
        out_specs=[whole()] * len(shapes) + [anywhere()],
        out_shape=[jax.ShapeDtypeStruct(s, F32) for s in shapes + [grad_in.shape]],
        scratch_shapes=[pltpu.VMEM(grad_in.shape, F32), pltpu.SemaphoreType.DMA((2,))],
        compiler_params=params(),
        name="unpack",
    )(full_early, full_late, small, grad_in)


def greet(n, z, x):
    barrier = pltpu.get_barrier_semaphore()
    for peer in peers(n, z, x):
        pl.semaphore_signal(barrier, inc=1, device_id={"seq": peer}, device_id_type=pl.DeviceIdType.MESH)
    pl.semaphore_wait(barrier, OUTER - 1 + n - 1)


def far_case(n, j, kb):
    if kb < n * j - 1:
        return 0
    if kb > n * j + n:
        return 2
    return None


def near_case(n, j, kb, x):
    off = kb - (n * j + x)
    near = jnp.logical_and(off >= -1, off <= 1)
    return jnp.where(near, off + 2, 0), jnp.where(off <= -2, 0, jnp.where(off >= 2, 2, 1))


def key_rows(keys, kb, length):
    one = jnp.ones((1, BLK), F32)
    lane = lax.broadcasted_iota(jnp.int32, (1, BLK), 1)
    mask = jnp.where(kb * BLK + lane < length, 0.0, -1e30)
    return jnp.concatenate([keys, tail(BLK, (one, one, one, mask)).astype(BF16)], axis=0).T


def forward_kernel(
    n, len_ref, table_ref, onehot_ref, x_ref, gain_ref, wq_ref, wk_ref, wv_ref,
    normed_out, own_out, pair_out, att, o_ref, lse_ref, tile_out, far_ref,
    normed_ref, own, pair, tile_ref, keep_sem, tile_sem, here, there, send, ka, qa, va,
    n_send, n_recv, z_send, z_recv, x_send, x_recv, o_send, o_recv,
):
    nk = OUTER * n
    batch = x_ref.shape[0]
    units = batch * HEADS
    me = lax.axis_index("seq")
    z, x = lax.div(me, n), lax.rem(me, n)
    greet(n, z, x)

    near, two, across = around(z)
    groups = (z, two, near, across)
    low = lax.rem(z, 2) == 0
    columns = half_columns(z)

    def n_copy(b):
        return remote(here.at[b], there.at[b], (n_send.at[b], n_recv.at[b]), seq=two * n + x)

    def z_copy(u, i):
        sems = z_send.at[u, i], z_recv.at[u, i]
        return remote(send.at[u, i], own.at[u, groups[i]], sems, seq=near * n + x)

    def x_copy(u, s, i):
        rows = pl.ds(DH, 2 * DH)
        sems = x_send.at[s - 1, u, i], x_recv.at[s - 1, u, i]
        peer = z * n + lax.rem(x + s, n)
        return remote(own.at[u, groups[i], rows], pair.at[s - 1, u, groups[i]], sems, seq=peer)

    def o_copy(u, d):
        group = lax.rem(z + d, OUTER)
        b, h = lax.div(u, HEADS), lax.rem(u, HEADS)
        rows = pl.ds(pl.multiple_of((z * HEADS + h) * DH, DH), DH)
        sems = o_send.at[u, d - 1], o_recv.at[u, d - 1]
        return remote(o_ref.at[u, group], att.at[b, rows], sems, seq=group * n + x)

    for b in range(batch):
        values = x_ref[b]
        scale = lax.rsqrt(jnp.mean(values * values, axis=-1, keepdims=True) + epsilon)
        here[b] = (values * scale * gain_ref[...].reshape(1, -1)).astype(BF16)
        if b == 0:
            n_copy(0).start()

    def project(b, i):
        normed = (here, there)[i][b]
        normed_ref[i, b] = normed.T
        for m, (w_ref, factor) in enumerate(((wq_ref, LOG2E), (wk_ref, 1.0), (wv_ref, 1.0))):
            turned = (jnp.dot(normed, w_ref[:, columns], preferred_element_type=F32) * factor).T.astype(BF16)
            for h in range(HEADS):
                first, second = turned[h * DH : (h + 1) * DH], turned[HW + h * DH : HW + (h + 1) * DH]
                rows = slice(m * DH, (m + 1) * DH)
                own[b * HEADS + h, groups[i], rows] = jnp.where(low, first, second)
                send[b * HEADS + h, i, rows] = jnp.where(low, second, first)
        for h in range(HEADS):
            for s in range(1, n):
                x_copy(b * HEADS + h, s, i).start()

    def start_near(b, i):
        for h in range(HEADS):
            z_copy(b * HEADS + h, i).start()

    def keep(u):
        yield pltpu.make_async_copy(own.at[u], own_out.at[u], keep_sem.at[u, 0])
        for s in range(1, n):
            yield pltpu.make_async_copy(pair.at[s - 1, u], pair_out.at[s - 1, u], keep_sem.at[u, s])

    keep_normed = pltpu.make_async_copy(normed_ref, normed_out, tile_sem.at[0])
    keep_tiles = pltpu.make_async_copy(tile_ref, tile_out, tile_sem.at[1])
    for b in range(batch):
        project(b, 0)
        if b == 0:
            start_near(0, 0)

    table_lane = lax.broadcasted_iota(jnp.int32, (1, NB), 1)
    for h in range(HEADS):
        chosen = table_ref[pl.ds(z * HEADS + h, 1), :] * LOG2E
        padded = jnp.broadcast_to(chosen, (8, NB))
        line = jnp.dot(padded, onehot_ref[...], preferred_element_type=F32, precision=highest)[0:1]
        line = jnp.broadcast_to(line, (BLK, SPAN))
        tile_ref[h, 0] = jnp.zeros((BLK, BLK), F32)
        for off in (-1, 0, 1):
            shift = (off * BLK - (2 * BLK - 1)) % SPAN
            tile_ref[h, off + 2] = pltpu.roll(line, shift, 1, stride=1, stride_axis=0)[:, :BLK]
        for side, bucket in enumerate((NB // 2 - 1, NB - 1)):
            value = jnp.sum(jnp.where(table_lane == bucket, chosen, 0.0), axis=1, keepdims=True)
            far_ref[h, side] = jnp.broadcast_to(value, (1, BLK))
    keep_tiles.start()

    def attend(u):
        b, h = lax.div(u, HEADS), lax.rem(u, HEADS)
        length = len_ref[b]
        left, right = far_ref[h, 0], far_ref[h, 1]
        one = jnp.ones((1, BLK), F32)
        vtail = tail(BLK, (one,)).astype(BF16)
        for s in range(1, n):
            for i in range(OUTER):
                x_copy(u, s, i).wait_recv()
        for s in range(n):
            col = lax.rem(x + s, n)
            for j in range(OUTER):
                kb = n * j + col
                if s == 0:
                    keys, vals = own[u, j, DH : 2 * DH], own[u, j, 2 * DH :]
                else:
                    keys, vals = pair[n - s - 1, u, j, :DH], pair[n - s - 1, u, j, DH:]
                ka[kb] = key_rows(keys, kb, length)
                columns = pl.ds(pl.multiple_of(kb * BLK, BLK), BLK)
                va[:DH, columns] = vals
                va[DH:, columns] = vtail

        def scores(kb, j):
            case = far_case(n, j, kb)
            if case is not None:
                return jnp.dot(ka[kb], qa[case, j], preferred_element_type=F32)
            tile, case = near_case(n, j, kb, x)
            return jnp.dot(ka[kb], qa[case, j], preferred_element_type=F32) + tile_ref[h, tile]

        for j in range(OUTER):
            for v, c in enumerate((left, 0.0 * one, right)):
                qa[v, j, :DH] = own[u, j, :DH]
                qa[v, j, DH:] = tail(BLK, split3(c) + (one,)).astype(BF16)
        tops = []
        for j in range(OUTER):
            top = jnp.full((8, BLK), -1e30, F32)
            for kb in range(nk):
                top = jnp.maximum(top, jnp.max(scores(kb, j).reshape(BLK // 8, 8, BLK), axis=0))
            top = jnp.max(top, axis=0, keepdims=True)
            tops.append(top)
            for v, c in enumerate((left, 0.0, right)):
                qa[v, j, DH:] = tail(BLK, split3(c - top) + (one,)).astype(BF16)
        for j in range(OUTER):
            weights = [jnp.exp2(scores(kb, j)).astype(BF16) for kb in range(nk)]
            total = jnp.dot(va[...], jnp.concatenate(weights, axis=0), preferred_element_type=F32)
            weight = total[DH : DH + 1]
            o_ref[u, j] = (total[:DH] / weight).astype(BF16)
            lse_ref[u, j] = tops[j] + jnp.log2(weight)
        for c in keep(u):
            c.start()
        rows = pl.ds(pl.multiple_of((z * HEADS + h) * DH, DH), DH)
        att[b, rows] = o_ref[u, z]
        @pl.when(u >= held_back)
        def _():
            start_o(u)

    held_back = units - HEADS - 1

    def start_o(u):
        for d in (2, 1, 3):
            o_copy(u, d).start()

    def turn(u, carry):
        @pl.when(jnp.logical_and(u < units, lax.rem(u, HEADS) == 0))
        def _():
            b = lax.div(u, HEADS)
            n_copy(b).wait_recv()

            @pl.when(b == batch - 1)
            def _():
                lax.fori_loop(0, held_back, lambda u, c: (start_o(u), c)[1], 0)

            @pl.when(b + 1 < batch)
            def _():
                n_copy(b + 1).start()

            project(b, 1)
            start_near(b, 1)

            @pl.when(b + 1 < batch)
            def _():
                start_near(b + 1, 0)

        @pl.when(u < units)
        def _():
            for i in range(2):
                z_copy(u, i).wait_recv()
                for s in range(1, n):
                    x_copy(u, s, 2 + i).start()

        @pl.when(u > 0)
        def _():
            attend(u - 1)

        return carry

    lax.fori_loop(0, units + 1, turn, 0)
    keep_normed.start()

    def finish(u, carry):
        for c in keep(u):
            c.wait()
        for d in range(1, OUTER):
            o_copy(u, d).wait_send()
            o_copy(u, d).wait_recv()
        for i in range(2):
            z_copy(u, i).wait_send()
        for s in range(1, n):
            for i in range(OUTER):
                x_copy(u, s, i).wait_send()
        return carry

    lax.fori_loop(0, units, finish, 0)
    for b in range(batch):
        n_copy(b).wait_send()
    keep_normed.wait()
    keep_tiles.wait()


def attention_forward(n, lengths, table, onehot, inputs, gain, wq, wk, wv):
    batch, height, width = inputs.shape
    units, nk = batch * HEADS, n * OUTER
    dma = pltpu.SemaphoreType.DMA
    return pl.pallas_call(
        functools.partial(forward_kernel, n),
        in_specs=[smem()] + [whole()] * 7,
        out_specs=[anywhere()] * 3 + [whole()] * 3 + [anywhere(), whole()],
        out_shape=[
            jax.ShapeDtypeStruct((2, batch, width, height), BF16),
            jax.ShapeDtypeStruct((units, OUTER, 3 * DH, BLK), BF16),
            jax.ShapeDtypeStruct((n - 1, units, OUTER, 2 * DH, BLK), BF16),
            jax.ShapeDtypeStruct((batch, width, height), BF16),
            jax.ShapeDtypeStruct((units, OUTER, DH, BLK), BF16),
            jax.ShapeDtypeStruct((units, OUTER, 1, BLK), F32),
            jax.ShapeDtypeStruct((HEADS, TILES, BLK, BLK), F32),
            jax.ShapeDtypeStruct((HEADS, 2, 1, BLK), F32),
        ],
        scratch_shapes=[
            pltpu.VMEM((2, batch, width, height), BF16),
            pltpu.VMEM((units, OUTER, 3 * DH, BLK), BF16),
            pltpu.VMEM((n - 1, units, OUTER, 2 * DH, BLK), BF16),
            pltpu.VMEM((HEADS, TILES, BLK, BLK), F32),
            dma((units, n)),
            dma((2,)),
            pltpu.VMEM((batch, height, width), BF16),
            pltpu.VMEM((batch, height, width), BF16),
            pltpu.VMEM((units, 2, 3 * DH, BLK), BF16),
            pltpu.VMEM((nk, BLK, AUG), BF16),
            pltpu.VMEM((3, OUTER, AUG, BLK), BF16),
            pltpu.VMEM((AUG, nk * BLK), BF16),
            dma((batch,)),
            dma((batch,)),
            dma((units, 2)),
            dma((units, 2)),
            dma((n - 1, units, OUTER)),
            dma((n - 1, units, OUTER)),
            dma((units, OUTER - 1)),
            dma((units, OUTER - 1)),
        ],
        compiler_params=pltpu.CompilerParams(
            vmem_limit_bytes=VMEM_BYTES, collective_id=0, has_side_effects=True
        ),
        cost_estimate=pl.CostEstimate(flops=45 * 10**9, bytes_accessed=24 << 20, transcendentals=0),
        name="attention_forward",
    )(lengths, table, onehot, inputs, gain, wq, wk, wv)


def early_scatter(early):
    return Scatter(early, (True,) * len(early.lines))


def backward_kernel(
    n, early, len_ref, far_ref, lse_ref, tile_in, own, pair, o_in, dout, *refs
):
    scatter = early_scatter(early)
    count = len(early.shapes)
    weights, refs = refs[:count], refs[count:]
    projections, refs = refs[:3], refs[3:]
    (grads_out, near_out, far_sum, parts, other, leaving,
    tile_ref, o_ref, grads, near, first_sem, own_sem, keep_sem, w_half, other_out, w_sem, n_send, n_recv, own_slot, pair_slot, load_sem,
    do_land, x_out, x_land, z_out, kept,
    ka, kt, va, qa, da, dk_all, dv_all,
    d_send, d_recv, x_send, x_recv, z_send, z_recv) = refs[: -scatter.count]
    scatter.bind(weights, refs[-scatter.count :])
    nk = OUTER * n
    batch = dout.shape[0]
    units = batch * HEADS
    x_slots, z_slots = staging(n, units)
    me = lax.axis_index("seq")
    z, x = lax.div(me, n), lax.rem(me, n)
    near_z, two, across = around(z)
    low = lax.rem(z, 2) * HW
    greet_all(early.p)
    scatter.step_core()
    firsts = [
        pltpu.make_async_copy(src, dst, first_sem.at[i]) for i, (src, dst) in enumerate(((tile_in, tile_ref), (o_in, o_ref)))
    ]
    for c in firsts:
        c.start()

    def own_part(u):
        b, h = lax.div(u, HEADS), lax.rem(u, HEADS)
        return pltpu.make_async_copy(dout.at[b, head_rows(z, h)], do_land.at[u, z], own_sem.at[u])

    def keep_grads(b):
        return [pltpu.make_async_copy(grads.at[m, b], grads_out.at[m, b], keep_sem.at[m, b]) for m in range(3)]

    columns = half_columns(z)
    w_loads = [pltpu.make_async_copy(w.at[:, columns], w_half.at[m], w_sem.at[m]) for m, w in enumerate(projections)]
    for c in w_loads:
        c.start()

    def head_rows(group, h):
        return pl.ds(pl.multiple_of((group * HEADS + h) * DH, DH), DH)

    def d_copy(u, d):
        group = lax.rem(z + d, OUTER)
        b, h = lax.div(u, HEADS), lax.rem(u, HEADS)
        sems = d_send.at[u, d - 1], d_recv.at[u, d - 1]
        return remote(dout.at[b, head_rows(group, h)], do_land.at[u, z], sems, seq=group * n + x)

    def x_copy(u, s):
        peer = z * n + lax.rem(x + s, n)
        sems = x_send.at[s - 1, u], x_recv.at[s - 1, u]
        return remote(
            x_out.at[s - 1, lax.rem(u, x_slots)], x_land.at[s - 1, lax.rem(u, X_LAND)], sems, seq=peer
        )

    def half_rows(h):
        return pl.ds(pl.multiple_of(low + h * DH, DH), DH)

    def z_copy(u, i, m):
        b, h = lax.div(u, HEADS), lax.rem(u, HEADS)
        sems = z_send.at[u, i, m], z_recv.at[u, i, m]
        src, dst = z_out.at[lax.rem(u, z_slots), i, pl.ds(m * DH, DH)], grads.at[m, b, i, half_rows(h)]
        return remote(src, dst, sems, seq=near_z * n + x)

    def n_copy(b):
        return remote(other_out.at[b], other.at[b], (n_send.at[b], n_recv.at[b]), seq=two * n + x)

    def loads(u):
        slot = lax.rem(u, 2)
        yield pltpu.make_async_copy(own.at[u], own_slot.at[slot], load_sem.at[slot, 0])
        for s in range(1, n):
            yield pltpu.make_async_copy(pair.at[s - 1, u], pair_slot.at[slot, s - 1], load_sem.at[slot, s])

    for c in loads(0):
        c.start()

    def start_d(u):
        for d in (2, 1, 3):
            d_copy(u, d).start()

    start_d(0)
    start_d(1)

    def begin(u, carry):
        own_part(u).start()
        return carry

    lax.fori_loop(0, units, begin, 0)
    near[...] = jnp.zeros_like(near)
    far_sum[...] = jnp.zeros_like(far_sum)
    one = jnp.ones((1, BLK), F32)
    ones3 = tail(BLK, (one, one, one)).astype(BF16)
    row16 = lax.broadcasted_iota(jnp.int32, (16, BLK), 0)
    marks = [jnp.where(row16 == r, 1.0, 0.0).astype(BF16) for r in range(2)]

    def work(u):
        b, h = lax.div(u, HEADS), lax.rem(u, HEADS)
        length = len_ref[b]
        left, right = far_ref[h, 0], far_ref[h, 1]
        slot = lax.rem(u, 2)
        for c in loads(u):
            c.wait()

        @pl.when(u + 1 < units)
        def _():
            for c in loads(u + 1):
                c.start()

        @pl.when(u + 2 < units)
        def _():
            start_d(u + 2)

        for s in range(n):
            col = lax.rem(x + s, n)
            for j in range(OUTER):
                kb = n * j + col
                if s == 0:
                    keys, vals = own_slot[slot, j, DH : 2 * DH], own_slot[slot, j, 2 * DH :]
                else:
                    keys, vals = pair_slot[slot, n - s - 1, j, :DH], pair_slot[slot, n - s - 1, j, DH:]
                ka[kb] = key_rows(keys, kb, length)
                kt[kb] = keys
                va[kb] = jnp.concatenate([vals, ones3], axis=0).T
        own_part(u).wait()
        for d in range(1, OUTER):
            d_copy(u, d).wait_recv()
        for j in range(OUTER):
            lse = lse_ref[u, j]
            for v, c in enumerate((left, 0.0, right)):
                qa[v, j, :DH] = own_slot[slot, j, :DH]
                qa[v, j, DH:] = tail(BLK, split3(c - lse) + (one,)).astype(BF16)
            arrived = do_land[u, j]
            delta = jnp.sum(arrived.astype(F32) * o_ref[u, j].astype(F32), axis=0, keepdims=True)
            da[j, :DH] = arrived
            da[j, DH:] = tail(BLK, split3(-delta)).astype(BF16)
        dqs = [None] * OUTER
        for g in range(0, nk, GROUP):
            blocks = range(g, g + GROUP)
            ps, dss = {}, {}
            for j in range(OUTER):
                left_side = []
                for kb in blocks:
                    case = far_case(n, j, kb)
                    if case is not None:
                        p = jnp.exp2(jnp.dot(ka[kb], qa[case, j], preferred_element_type=F32))
                        mark = marks[case // 2]
                    else:
                        tile, case = near_case(n, j, kb, x)
                        s = jnp.dot(ka[kb], qa[case, j], preferred_element_type=F32)
                        p = jnp.exp2(s + tile_ref[h, tile])
                        want = jnp.where(case == 1, 2, lax.div(case, 2))
                        mark = jnp.where(row16 == want, 1.0, 0.0).astype(BF16)
                    ds = p * jnp.dot(va[kb], da[j], preferred_element_type=F32)
                    if far_case(n, j, kb) is None:
                        near[h, tile] += ds
                    ps[kb, j], dss[kb, j] = p.astype(BF16), ds.astype(BF16)
                    left_side.append(jnp.concatenate([kt[kb], mark], axis=0))
                right_side = jnp.concatenate([dss[kb, j] for kb in blocks], axis=0)
                dq = jnp.dot(jnp.concatenate(left_side, axis=1), right_side, preferred_element_type=F32)
                dqs[j] = dq if g == 0 else dqs[j] + dq
            for kb in blocks:
                dv, dk = jnp.zeros((DH, BLK), F32), jnp.zeros((DH, BLK), F32)
                for j in range(OUTER):
                    dv = dv + lax.dot_general(da[j, :DH], ps[kb, j], NT, preferred_element_type=F32)
                    dk = dk + lax.dot_general(qa[0, j, :DH], dss[kb, j], NT, preferred_element_type=F32)
                dk_all[kb] = dk * LN2
                dv_all[kb] = dv
        @pl.when(u >= x_slots)
        def _():
            for s in range(1, n):
                x_copy(u - x_slots, s).wait_send()

        far = jnp.zeros((8, BLK), F32)
        for j in range(OUTER):
            far = far + dqs[j][DH : DH + 8]
        far_sum[h] += far
        parity = lax.rem(u, 2)
        for j in range(OUTER):
            kept[parity, j, :DH] = dqs[j][:DH]
            kept[parity, j, DH : 2 * DH] = dk_all[n * j + x]
            kept[parity, j, 2 * DH :] = dv_all[n * j + x]
            for s in range(1, n):
                kb = n * j + lax.rem(x + s, n)
                x_out[s - 1, lax.rem(u, x_slots), j, :DH] = dk_all[kb].astype(BF16)
                x_out[s - 1, lax.rem(u, x_slots), j, DH:] = dv_all[kb].astype(BF16)
        for s in range(1, n):
            x_copy(u, s).start()

    def hand_over(u):
        b, h = lax.div(u, HEADS), lax.rem(u, HEADS)
        parity = lax.rem(u, 2)
        for s in range(1, n):
            x_copy(u, s).wait_recv()

        @pl.when(u >= z_slots)
        def _():
            for i in range(2):
                for m in range(3):
                    z_copy(u - z_slots, i, m).wait_send()

        for i, (mine, theirs) in enumerate(((z, near_z), (two, across))):
            for j, stays in ((mine, True), (theirs, False)):
                rest = kept[parity, j, DH:]
                for s in range(1, n):
                    rest = rest + x_land[s - 1, lax.rem(u, X_LAND), j].astype(F32)
                total = jnp.concatenate([kept[parity, j, :DH], rest], axis=0).astype(BF16)
                if stays:
                    for m in range(3):
                        grads[m, b, i, half_rows(h)] = total[m * DH : (m + 1) * DH]
                else:
                    z_out[lax.rem(u, z_slots), i] = total
            for m in range(3):
                z_copy(u, i, m).start()

    def combine(b):
        for h in range(HEADS):
            for i in range(2):
                for m in range(3):
                    z_copy(b * HEADS + h, i, m).wait_recv()
        for c in keep_grads(b):
            c.start()
        total = jnp.dot(w_half[0], grads[0, b, 1], preferred_element_type=F32)
        total = total + jnp.dot(w_half[1], grads[1, b, 1], preferred_element_type=F32)
        total = total + jnp.dot(w_half[2], grads[2, b, 1], preferred_element_type=F32)
        @pl.when(b < batch - 1)
        def _():
            other_out[b] = total.astype(BF16)
            n_copy(b).start()

        @pl.when(b == batch - 1)
        def _():
            leaving[...] = total.astype(BF16)

    def turn(u, carry):
        @pl.when(u < units)
        def _():
            work(u)

        @pl.when(jnp.logical_and(u > 0, u <= units))
        def _():
            hand_over(u - 1)

        @pl.when(jnp.logical_and(u > HEADS, lax.rem(u - 1, HEADS) == 0))
        def _():
            combine(lax.div(u - 1, HEADS) - 1)

        @pl.when(u == 0)
        def _():
            scatter.step_first((0,))

        for line in early.lines:

            @pl.when(u == 2 * line + 2)
            def _():
                scatter.step_second(line)
                if line + 1 < len(early.lines):
                    scatter.start_first(line + 1)

        return carry

    for c in w_loads + firsts:
        c.wait()
    lax.fori_loop(0, units + 2, turn, 0)
    near_copy = pltpu.make_async_copy(near, near_out, first_sem.at[0])
    near_copy.start()

    def finish(u, carry):
        for d in range(1, OUTER):
            d_copy(u, d).wait_send()

        @pl.when(u >= units - z_slots)
        def _():
            for i in range(2):
                for m in range(3):
                    z_copy(u, i, m).wait_send()

        @pl.when(u >= units - x_slots)
        def _():
            for s in range(1, n):
                x_copy(u, s).wait_send()

        return carry

    lax.fori_loop(0, units, finish, 0)
    for b in range(batch - 1):
        n_copy(b).wait_send()
        n_copy(b).wait_recv()
    for line in early.lines:
        scatter.step_third(line)
        parts[early.part_start[line] : early.part_start[line] + early.size[line]] = scatter.part(line)[...]
    scatter.end()
    for b in range(batch):
        for c in keep_grads(b):
            c.wait()
    near_copy.wait()


def staging(n, units):
    return (units, units) if n <= 2 else (2, 4)


X_LAND = 4


def attention_backward(n, early, lengths, far, tiles, own, pair, out, lse, dout, weights, projections):
    batch, width, height = dout.shape
    units, nk = batch * HEADS, n * OUTER
    dma = pltpu.SemaphoreType.DMA
    x_slots, z_slots = staging(n, units)
    return pl.pallas_call(
        functools.partial(backward_kernel, n, early),
        in_specs=[smem()] + [whole()] * 2 + [anywhere()] * (8 + len(weights)),
        out_specs=[anywhere()] * 2 + [whole()] * 4,
        out_shape=[
            jax.ShapeDtypeStruct((3, batch, 2, HALF, height), BF16),
            jax.ShapeDtypeStruct((HEADS, TILES, BLK, BLK), F32),
            jax.ShapeDtypeStruct((HEADS, 8, BLK), F32),
            jax.ShapeDtypeStruct((early.part_total, LANES), BF16),
            jax.ShapeDtypeStruct((batch - 1, width, height), BF16),
            jax.ShapeDtypeStruct((width, height), BF16),
        ],
        scratch_shapes=[
            pltpu.VMEM(tiles.shape, F32),
            pltpu.VMEM(out.shape, BF16),
            pltpu.VMEM((3, batch, 2, HALF, height), BF16),
            pltpu.VMEM((HEADS, TILES, BLK, BLK), F32),
            dma((2,)),
            dma((units,)),
            dma((3, batch)),
            pltpu.VMEM((3, width, HALF), BF16),
            pltpu.VMEM((batch - 1, width, height), BF16),
            dma((3,)),
            dma((batch - 1,)),
            dma((batch - 1,)),
            pltpu.VMEM((2, OUTER, 3 * DH, BLK), BF16),
            pltpu.VMEM((2, n - 1, OUTER, 2 * DH, BLK), BF16),
            dma((2, n)),
            pltpu.VMEM((units, OUTER, DH, BLK), BF16),
            pltpu.VMEM((n - 1, x_slots, OUTER, 2 * DH, BLK), BF16),
            pltpu.VMEM((n - 1, X_LAND, OUTER, 2 * DH, BLK), BF16),
            pltpu.VMEM((z_slots, 2, 3 * DH, BLK), BF16),
            pltpu.VMEM((2, OUTER, 3 * DH, BLK), F32),
            pltpu.VMEM((nk, BLK, AUG), BF16),
            pltpu.VMEM((nk, DH, BLK), BF16),
            pltpu.VMEM((nk, BLK, AUG), BF16),
            pltpu.VMEM((3, OUTER, AUG, BLK), BF16),
            pltpu.VMEM((OUTER, AUG, BLK), BF16),
            pltpu.VMEM((nk, DH, BLK), F32),
            pltpu.VMEM((nk, DH, BLK), F32),
            dma((units, OUTER - 1)),
            dma((units, OUTER - 1)),
            dma((n - 1, units)),
            dma((n - 1, units)),
            dma((units, 2, 3)),
            dma((units, 2, 3)),
        ]
        + early_scatter(early).scratch(),
        compiler_params=pltpu.CompilerParams(
            vmem_limit_bytes=VMEM_BYTES, collective_id=1, has_side_effects=True
        ),
        cost_estimate=pl.CostEstimate(flops=110 * 10**9, bytes_accessed=24 << 20, transcendentals=0),
        name="attention_backward",
    )(lengths, far, lse, tiles, own, pair, out, dout, *weights, *projections)


FF_STEP = 512


def middle_kernel(
    x_in, att_in, cot_in, gain_ref, w_out, w_gate, w_up, w_down,
    result_out, mixed_out, dout_out, d_gain, d_out, d_gate, d_up, d_down,
    x_ref, att_ref, cot_ref, result, grad_mixed, dout,
    wo, wg, wu, wd, att, low, hidden, g_gate, g_up, s_out, s_gate, s_up, s_down, kept, in_sem, out_sem,
):
    tokens, width = x_ref.shape
    batch = att_ref.shape[0]
    ff = w_gate.shape[1]
    pairs = ((w_out, wo), (w_gate, wg), (w_up, wu), (w_down, wd), (att_in, att_ref), (x_in, x_ref), (cot_in, cot_ref))
    loads = [pltpu.make_async_copy(src, dst, in_sem.at[i]) for i, (src, dst) in enumerate(pairs)]
    pairs = ((s_out, d_out), (s_gate, d_gate), (s_up, d_up), (s_down, d_down))
    pairs += ((result, result_out), (grad_mixed, mixed_out), (dout, dout_out))
    stores = [pltpu.make_async_copy(src, dst, out_sem.at[i]) for i, (src, dst) in enumerate(pairs)]
    loads = loads[4:5] + loads[:1] + loads[5:] + loads[1:4]
    for c in loads:
        c.start()
    height = tokens // batch
    loads[0].wait()
    for b in range(batch):
        att[b * height : (b + 1) * height] = att_ref[b].T
    for c in loads[1:4]:
        c.wait()
    low[...] = cot_ref[...].astype(BF16)
    mixed = x_ref[...] + jnp.dot(att[...], wo[...], preferred_element_type=F32)
    kept[...] = mixed
    result[...] = mixed
    scale = lax.rsqrt(jnp.mean(mixed * mixed, axis=-1, keepdims=True) + epsilon)
    normed = (mixed * scale * gain_ref[...].reshape(1, -1)).astype(BF16)
    att[...] = normed
    for c in loads[4:]:
        c.wait()
    root = 0.7978845608028654
    for at in range(0, ff, FF_STEP):
        part = slice(at, at + FF_STEP)
        gate = jnp.dot(att[...], wg[:, part], preferred_element_type=F32)
        upward = jnp.dot(att[...], wu[:, part], preferred_element_type=F32)
        g_hidden = lax.dot_general(low[...], wd[part], NT, preferred_element_type=F32)
        square = gate * gate
        t = jnp.tanh(root * gate * (1.0 + 0.044715 * square))
        half = 0.5 * (1.0 + t)
        act = gate * half
        slope = half + 0.5 * gate * (1.0 - t * t) * (root * (1.0 + 3.0 * 0.044715 * square))
        hidden[:, part] = (act * upward).astype(BF16)
        g_gate[:, part] = (g_hidden * upward * slope).astype(BF16)
        g_up[:, part] = (g_hidden * act).astype(BF16)
    result[...] += jnp.dot(hidden[...], wd[...], preferred_element_type=F32)
    stores[4].start()
    d_normed = lax.dot_general(g_gate[...], wg[...], NT, preferred_element_type=F32)
    d_normed = d_normed + lax.dot_general(g_up[...], wu[...], NT, preferred_element_type=F32)
    mixed = kept[...]
    scale = lax.rsqrt(jnp.mean(mixed * mixed, axis=-1, keepdims=True) + epsilon)
    d_gain[...] = jnp.sum(d_normed * mixed * scale, axis=0, keepdims=True)
    u = d_normed * gain_ref[...].reshape(1, -1)
    along = jnp.mean(u * mixed, axis=-1, keepdims=True)
    d_mixed = cot_ref[...] + scale * (u - mixed * (scale * scale * along))
    grad_mixed[...] = d_mixed
    stores[5].start()
    d_low = d_mixed.astype(BF16)
    turned = lax.dot_general(wo[...], d_low, NT, preferred_element_type=F32).astype(BF16)
    for b in range(batch):
        dout[b] = turned[:, b * height : (b + 1) * height]
    stores[6].start()
    total = jnp.zeros((width, width), F32)
    for b in range(batch):
        total = total + jnp.dot(att_ref[b], d_low[b * height : (b + 1) * height], preferred_element_type=F32)
    s_out[...] = total.astype(BF16)
    stores[0].start()
    normed_t = att[...].T
    for src, dst, store in ((g_gate, s_gate, stores[1]), (g_up, s_up, stores[2])):
        for at in range(0, ff, FF_STEP):
            part = slice(at, at + FF_STEP)
            dst[:, part] = jnp.dot(normed_t, src[:, part], preferred_element_type=F32).astype(BF16)
        store.start()
    for at in range(0, ff, FF_STEP):
        part = slice(at, at + FF_STEP)
        s_down[part] = jnp.dot(hidden[:, part].T, low[...], preferred_element_type=F32).astype(BF16)
    stores[3].start()
    for c in stores:
        c.wait()


def middle(inputs, att, cotangent, gain, w_out, w_gate, w_up, w_down):
    batch, height, width = inputs.shape
    tokens, ff = batch * height, w_gate.shape[1]
    weights = (w_out, w_gate, w_up, w_down)
    flat = (tokens, width)
    out = pl.pallas_call(
        middle_kernel,
        in_specs=[anywhere()] * 3 + [whole()] + [anywhere()] * 4,
        out_specs=[anywhere()] * 3 + [whole()] + [anywhere()] * 4,
        out_shape=[
            jax.ShapeDtypeStruct(flat, F32),
            jax.ShapeDtypeStruct(flat, F32),
            jax.ShapeDtypeStruct((batch, width, height), BF16),
            jax.ShapeDtypeStruct((1, width), F32),
        ]
        + [jax.ShapeDtypeStruct(w.shape, BF16) for w in weights],
        scratch_shapes=[
            pltpu.VMEM(flat, F32),
            pltpu.VMEM(att.shape, BF16),
            pltpu.VMEM(flat, F32),
            pltpu.VMEM(flat, F32),
            pltpu.VMEM(flat, F32),
            pltpu.VMEM(att.shape, BF16),
        ]
        + [pltpu.VMEM(w.shape, BF16) for w in weights]
        + [pltpu.VMEM(flat, BF16)] * 2
        + [pltpu.VMEM((tokens, ff), BF16)] * 3
        + [pltpu.VMEM(w.shape, BF16) for w in weights]
        + [pltpu.VMEM(flat, F32)]
        + [pltpu.SemaphoreType.DMA((7,))] * 2,
        compiler_params=params(),
        cost_estimate=pl.CostEstimate(flops=25 * 10**9, bytes_accessed=32 << 20, transcendentals=0),
        name="middle",
    )(inputs.reshape(flat), att, cotangent.reshape(flat), gain, *weights)
    return out[0].reshape(inputs.shape), out[1].reshape(inputs.shape), out[2], out[3], out[4:]


def shards(
    places,
    inputs,
    lengths,
    norm_attn,
    w_query,
    w_key,
    w_value,
    w_out,
    norm_ffn,
    w_gate,
    w_up,
    w_down,
    bucket_bias,
    cotangent,
):
    batch, height, width = inputs.shape
    n = places.inner
    onehot = jnp.asarray(ONEHOT)
    normed_t, own, pair, attended_t, out, lse, tiles, far = attention_forward(
        n, lengths, bucket_bias.T, onehot, inputs, norm_attn, w_query, w_key, w_value
    )
    result, grad_mixed, grad_attended_t, grad_norm_ffn, weights = middle(
        inputs, attended_t, cotangent, norm_ffn, w_out, w_gate, w_up, w_down
    )
    early = Rows(places, [g.shape for g in weights], LANES, 4)
    projections = (w_query, w_key, w_value)
    grads, near, far_sum, parts, other, leaving = attention_backward(
        n, early, lengths, far, tiles, own, pair, out, lse, grad_attended_t, weights, projections
    )
    late = Rows(places, [(width, HALF)] * 3, LANE, 2)
    loaded = (
        parts, grads, normed_t, *projections, inputs, grad_mixed, near, far_sum, onehot, other, leaving
    )
    grad_inputs, full_early, full_late, small = last_grads(early, late, loaded, norm_attn, grad_norm_ffn)
    (part_out, part_gate, part_up, part_down, part_query, part_key, part_value, part_attn, part_ffn, part_table,
     grad_inputs) = unpack(early, late, full_early, full_late, small, grad_inputs)
    return (
        result,
        grad_inputs,
        part_attn.reshape(-1),
        part_ffn.reshape(-1),
        part_query,
        part_key,
        part_value,
        part_out,
        part_gate,
        part_up,
        part_down,
        part_table,
    )


def solution(mesh):
    rows = P("dp", "seq", None)
    share = P("dp", None)
    return jax.shard_map(
        functools.partial(shards, Places(mesh)),
        mesh=mesh,
        in_specs=(rows, P("dp")) + (P(),) * 10 + (rows,),
        out_specs=(rows, rows, P("dp"), P("dp")) + (share,) * 8,
        check_vma=False,
    )
```

```python
import functools

import jax
import jax.numpy as jnp
import numpy as np
from jax import lax
from jax.experimental import pallas as pl
from jax.experimental.pallas import tpu as pltpu
from jax.sharding import PartitionSpec as P

H = 12
DH = 64
NB = 32
OUTER = 4
HEADS = H // OUTER
HW = HEADS * DH
HALF = 2 * HW
BLK = 256
AUG = DH + 16
SPAN = 4 * BLK
LANES = 256
LANE = 128
LOG2E = 1.4426950408889634
LN2 = 0.6931471805599453
F32 = jnp.float32
BF16 = jnp.bfloat16
NT = (((1,), (1,)), ((), ()))
VMEM_BYTES = 62 << 20
GROUP = 8
TILES = 4

epsilon = 1e-06
limits = (1, 2, 3, 4, 5, 6, 7, 8, 12, 16, 23, 32, 46, 64, 91)
highest = lax.Precision.HIGHEST


def bucket_lines():
    relative = 2 * BLK - 1 - np.arange(SPAN)
    count = sum((np.abs(relative) >= limit).astype(np.int32) for limit in limits)
    bucket = count + (relative > 0).astype(np.int32) * (NB // 2)
    return (bucket[None, :] == np.arange(NB)[:, None]).astype(np.float32)


ONEHOT = bucket_lines()


def params():
    return pltpu.CompilerParams(vmem_limit_bytes=VMEM_BYTES)


def smem():
    return pl.BlockSpec(memory_space=pltpu.SMEM)


def anywhere():
    return pl.BlockSpec(memory_space=pl.ANY)


def whole():
    return pl.BlockSpec(memory_space=pltpu.VMEM)


def split3(v):
    a = v.astype(BF16)
    r = v - a.astype(F32)
    b = r.astype(BF16)
    c = (r - b.astype(F32)).astype(BF16)
    return a.astype(F32), b.astype(F32), c.astype(F32)


def tail(width, values):
    row = lax.broadcasted_iota(jnp.int32, (16, width), 0)
    out = jnp.zeros((16, width), F32)
    for i, v in enumerate(values):
        out = jnp.where(row == i, v, out)
    return out


def peers(n, z, x):
    return [lax.rem(z + d, OUTER) * n + x for d in range(1, OUTER)] + [z * n + lax.rem(x + s, n) for s in range(1, n)]


def around(z):
    near = z + 1 - 2 * lax.rem(z, 2)
    return near, lax.rem(z + 2, OUTER), lax.rem(near + 2, OUTER)


class Places:
    def __init__(self, mesh):
        self.dp = mesh.shape["dp"]
        self.groups = self.dp // 2
        self.inner = mesh.shape["seq"] // OUTER


def remote(src, dst, sems, **peer):
    return pltpu.make_async_remote_copy(
        src_ref=src,
        dst_ref=dst,
        send_sem=sems[0],
        recv_sem=sems[1],
        device_id=peer,
        device_id_type=pl.DeviceIdType.MESH,
    )


class Rows:
    def __init__(self, places, shapes, lanes, lines):
        self.p = places
        self.shapes = shapes
        self.lanes = lanes
        self.lines = range(lines)
        grain = places.inner * OUTER * 16
        self.blocks = []
        at = 0
        for m, (rows, columns) in enumerate(shapes):
            share = rows // places.dp
            for block in range(columns // lanes):
                self.blocks.append((m, block, at, share))
                at += share
        self.used = at
        grains = max(-(-at // grain), lines)
        self.total = grains * grain
        cuts = [grains * line // lines * grain for line in range(lines + 1)]
        self.start = cuts[:-1]
        self.span = [b - a for a, b in zip(cuts[:-1], cuts[1:])]
        self.size = [v // places.inner for v in self.span]
        self.small = [v // OUTER for v in self.size]
        self.part_start = [v // places.inner for v in self.start]
        self.part_total = self.total // places.inner

    def line(self, line):
        return pl.ds(self.start[line], self.span[line])

    def part(self, line, x):
        return pl.ds(pl.multiple_of(self.start[line] + x * self.size[line], 16), self.size[line])

    def quarter(self, line, x, z):
        first = self.start[line] + x * self.size[line] + z * self.small[line]
        return pl.ds(pl.multiple_of(first, 16), self.small[line])


def add_to(ref, arrived):
    if len(arrived) == 1:
        ref[...] = ref[...] + arrived[0]
        return
    total = ref[...].astype(F32)
    for a in arrived:
        total = total + a.astype(F32)
    ref[...] = total.astype(BF16)


class Scatter:
    def __init__(self, rows, y_first):
        self.rows = rows
        self.y_first = y_first
        self.count = 5 + 2 * len(rows.lines)

    def scratch(self):
        r, p, dma = self.rows, self.rows.p, pltpu.SemaphoreType.DMA
        g, n, lines = p.groups, p.inner, len(r.lines)
        out = [pltpu.VMEM((g, r.total, r.lanes), BF16), pltpu.VMEM((g, r.total, r.lanes), BF16)]
        for line, y_first in enumerate(self.y_first):
            out.append(pltpu.VMEM((g - 1, r.span[line] if y_first else r.size[line], r.lanes), BF16))
            out.append(pltpu.VMEM((n - 1, 1 if y_first else g, r.size[line], r.lanes), BF16))
        return out + [dma((len(r.blocks), g, 3)), dma((lines, g - 1, 2)), dma((lines, n - 1, g, 2))]

    def bind(self, grads, refs):
        self.grads = grads
        self.held, self.land = refs[:2]
        self.c_sem, self.y_sem, self.x_sem = refs[-3:]
        self.y_land, self.x_land = refs[2:-3:2], refs[3:-3:2]
        dp, seq = lax.axis_index("dp"), lax.axis_index("seq")
        n = self.rows.p.inner
        self.core, self.group = lax.rem(dp, 2), lax.div(dp, 2)
        self.z, self.x = lax.div(seq, n), lax.rem(seq, n)

    def source(self, i, g, core):
        m, block, at, share = self.rows.blocks[i]
        first = pl.multiple_of((g * 2 + core) * share, 16)
        return self.grads[m].at[pl.ds(first, share), pl.ds(block * self.rows.lanes, self.rows.lanes)], pl.ds(at, share)

    def picked(self, chosen):
        return [i for i, b in enumerate(self.rows.blocks) if chosen is None or b[0] in chosen]

    def core_copies(self, chosen=None):
        for i in self.picked(chosen):
            for g in range(self.rows.p.groups):
                src, where = self.source(i, g, 1 - self.core)
                sems = self.c_sem.at[i, g, 0], self.c_sem.at[i, g, 1]
                yield remote(src, self.land.at[g, where], sems, dp=self.group * 2 + 1 - self.core)

    def own_copies(self, chosen=None):
        for i in self.picked(chosen):
            for g in range(self.rows.p.groups):
                src, where = self.source(i, g, self.core)
                yield pltpu.make_async_copy(src, self.held.at[g, where], self.c_sem.at[i, g, 2])

    def y_copies(self, line):
        r = self.rows
        for t in range(1, r.p.groups):
            other = lax.rem(self.group + t, r.p.groups)
            where = r.line(line) if self.y_first[line] else r.part(line, self.x)
            sems = self.y_sem.at[line, t - 1, 0], self.y_sem.at[line, t - 1, 1]
            yield remote(self.held.at[other, where], self.y_land[line].at[t - 1], sems, dp=other * 2 + self.core)

    def x_copies(self, line):
        r = self.rows
        n = r.p.inner
        for s in range(1, n):
            other = lax.rem(self.x + s, n)
            where = r.part(line, other)
            for g in range(1 if self.y_first[line] else r.p.groups):
                sems = self.x_sem.at[line, s - 1, g, 0], self.x_sem.at[line, s - 1, g, 1]
                src = self.held.at[self.group if self.y_first[line] else g, where]
                yield remote(src, self.x_land[line].at[s - 1, g], sems, seq=self.z * n + other)

    def hop(self, line, which):
        return self.y_copies(line) if (which == 0) == self.y_first[line] else self.x_copies(line)


    def step_core(self, chosen=None):
        for c in self.core_copies(chosen):
            c.start()
        for c in self.own_copies(chosen):
            c.start()

    def step_first(self, begin):
        r = self.rows
        for c in self.core_copies():
            c.wait_recv()
        for c in self.own_copies():
            c.wait()
        for line in r.lines:
            end = r.start[line] + r.span[line]
            first, last = r.start[line], min(end, r.used)
            for g in range(r.p.groups):
                where = pl.ds(first, last - first)
                add_to(self.held.at[g, where], [self.land[g, where]])
                if last < end:
                    self.held[g, last:end] = jnp.zeros((end - last, r.lanes), BF16)
            if line in begin:
                self.start_first(line)

    def start_first(self, line):
        for c in self.hop(line, 0):
            c.start()

    def step_second(self, line):
        r = self.rows
        for c in self.hop(line, 0):
            c.wait_recv()
        if self.y_first[line]:
            arrived = [self.y_land[line][t] for t in range(r.p.groups - 1)]
            add_to(self.held.at[self.group, r.line(line)], arrived)
        else:
            for g in range(r.p.groups):
                arrived = [self.x_land[line][s, g] for s in range(r.p.inner - 1)]
                add_to(self.held.at[g, r.part(line, self.x)], arrived)
        for c in self.hop(line, 1):
            c.start()

    def step_third(self, line):
        r = self.rows
        for c in self.hop(line, 1):
            c.wait_recv()
        if self.y_first[line]:
            arrived = [self.x_land[line][s, 0] for s in range(r.p.inner - 1)]
        else:
            arrived = [self.y_land[line][t] for t in range(r.p.groups - 1)]
        add_to(self.held.at[self.group, r.part(line, self.x)], arrived)

    def part(self, line):
        return self.held.at[self.group, self.rows.part(line, self.x)]

    def end(self):
        for c in self.core_copies():
            c.wait_send()
        for line in self.rows.lines:
            for which in range(2):
                for c in self.hop(line, which):
                    c.wait_send()


class Spread:
    def __init__(self, rows, halves=False):
        self.rows = rows
        self.halves = halves

    def scratch(self):
        r, dma = self.rows, pltpu.SemaphoreType.DMA
        lines = len(r.lines)
        land = (lines, 1, max(r.size) // 2, r.lanes) if self.halves else (lines, 3, max(r.small), r.lanes)
        sems = dma((lines, 3, 2))
        return [pltpu.VMEM(land, BF16), sems, sems, dma((lines, OUTER, r.p.inner - 1, 2))]

    count = 4

    def bind(self, piece, target, refs):
        self.piece, self.target = piece, target
        self.land, self.s_sem, self.g_sem, self.x_sem = refs
        seq = lax.axis_index("seq")
        n = self.rows.p.inner
        self.z, self.x = lax.div(seq, n), lax.rem(seq, n)
        self.near, self.two, self.across = around(self.z)

    def copy(self, src, dst, sems, group):
        return remote(src, dst, sems, seq=group * self.rows.p.inner + self.x)

    def sum_copy(self, line, i):
        piece = self.piece(line, (self.near, self.across, self.two)[i])
        sems = self.s_sem.at[line, i, 0], self.s_sem.at[line, i, 1]
        return self.copy(piece, self.landing(line, i), sems, self.two if i == 2 else self.near)

    def landing(self, line, i):
        rows = self.rows.size[line] // 2 if self.halves else self.rows.small[line]
        return self.land.at[line, i, pl.ds(0, rows)]

    def sums(self, line):
        return [self.sum_copy(line, i) for i in range(1 if self.halves else 3)]

    def z_copy(self, line, i):
        where = self.target(line, self.two if i == 2 else self.z)
        sems = self.g_sem.at[line, i, 0], self.g_sem.at[line, i, 1]
        return self.copy(where, where, sems, self.two if i == 0 else self.near)

    def x_copies(self, line, c):
        n = self.rows.p.inner
        where = self.target(line, c)
        for s in range(1, n):
            sems = self.x_sem.at[line, c, s - 1, 0], self.x_sem.at[line, c, s - 1, 1]
            yield remote(where, where, sems, seq=self.z * n + lax.rem(self.x + s, n))

    def spread(self, line, c):
        for s in self.x_copies(line, c):
            s.start()

    def step_pair(self, line):
        self.sum_copy(line, 0).start()
        if not self.halves:
            self.sum_copy(line, 1).start()

    def step_two(self, line):
        for i, c in ((0, self.z), (1, self.two)):
            self.sum_copy(line, i).wait_recv()
            add_to(self.piece(line, c), [self.landing(line, i)[...]])
        self.sum_copy(line, 2).start()

    def step_back(self, line):
        last = 0 if self.halves else 2
        self.sum_copy(line, last).wait_recv()
        self.target(line, self.z)[...] = self.piece(line, self.z)[...] + self.landing(line, last)[...]
        self.z_copy(line, 0).start()
        self.z_copy(line, 1).start()
        self.spread(line, self.z)

    def step_rest(self, line):
        self.z_copy(line, 0).wait_recv()
        self.z_copy(line, 2).start()
        self.spread(line, self.two)
        self.z_copy(line, 1).wait_recv()
        self.spread(line, self.near)

    def step_last(self, line):
        self.z_copy(line, 2).wait_recv()
        self.spread(line, self.across)

    def end(self):
        for line in self.rows.lines:
            for c in range(OUTER):
                for s in self.x_copies(line, c):
                    s.wait_send()
                    s.wait_recv()
            for c in self.sums(line):
                c.wait_send()
            for i in range(3):
                self.z_copy(line, i).wait_send()


class Total:
    def __init__(self, places, rows):
        self.p = places
        self.rows = rows
        self.peers = [1, places.groups - 1, places.inner - 1, 1, 1]
        self.hops = range(5)
        self.count = 8

    def scratch(self):
        dma = pltpu.SemaphoreType.DMA
        out = [pltpu.VMEM((len(self.hops) + 1, self.rows, LANE), F32)]
        out += [pltpu.VMEM((k, self.rows, LANE), F32) for k in self.peers]
        return out + [dma((len(self.hops), max(self.peers))) for _ in range(2)]

    def bind(self, refs):
        self.held, self.land, self.sems = refs[0], refs[1:6], refs[6:]
        dp, seq = lax.axis_index("dp"), lax.axis_index("seq")
        n, groups = self.p.inner, self.p.groups
        core, group, z, x = lax.rem(dp, 2), lax.div(dp, 2), lax.div(seq, n), lax.rem(seq, n)
        near, two, _ = around(z)
        self.targets = [
            [{"dp": group * 2 + 1 - core}],
            [{"dp": lax.rem(group + t, groups) * 2 + core} for t in range(1, groups)],
            [{"seq": z * n + lax.rem(x + s, n)} for s in range(1, n)],
            [{"seq": near * n + x}],
            [{"seq": two * n + x}],
        ]

    def copies(self, hop):
        for i, target in enumerate(self.targets[hop]):
            yield remote(self.held.at[hop], self.land[hop].at[i], (self.sems[0].at[hop, i], self.sems[1].at[hop, i]), **target)

    def send(self, hop):
        for c in self.copies(hop):
            c.start()

    def step(self, hop):
        for c in self.copies(hop):
            c.wait_recv()
        total = self.held[hop]
        for i in range(self.peers[hop]):
            total = total + self.land[hop][i]
        self.held[hop + 1] = total
        if hop + 1 < len(self.hops):
            self.send(hop + 1)

    def end(self):
        for hop in self.hops:
            for c in self.copies(hop):
                c.wait_send()


def greet_all(places):
    dp, seq = lax.axis_index("dp"), lax.axis_index("seq")
    n = places.inner
    core, group = lax.rem(dp, 2), lax.div(dp, 2)
    barrier = pltpu.get_barrier_semaphore()
    mesh = pl.DeviceIdType.MESH
    pl.semaphore_signal(barrier, inc=1, device_id={"dp": group * 2 + 1 - core}, device_id_type=mesh)
    for t in range(1, places.groups):
        other = lax.rem(group + t, places.groups) * 2 + core
        pl.semaphore_signal(barrier, inc=1, device_id={"dp": other}, device_id_type=mesh)
    for peer in peers(n, lax.div(seq, n), lax.rem(seq, n)):
        pl.semaphore_signal(barrier, inc=1, device_id={"seq": peer}, device_id_type=mesh)
    pl.semaphore_wait(barrier, 1 + places.groups - 1 + OUTER - 1 + n - 1)


SMALL = 16


def last_kernel(early, late, *refs):
    count = 13
    sources, (gain_ref, ffn_ref), refs = refs[:count], refs[count : count + 2], refs[count + 2 :]
    grad_out, full_early, full_late, small_out, refs = refs[0], refs[1], refs[2], refs[3], refs[4:]
    slots, load_sem, refs = refs[:count], refs[count], refs[count + 1 :]
    p = late.p
    scatter, spread_early, spread_late = Scatter(late, (True, False)), Spread(early), Spread(late, True)
    (gq, gk, gv, arriving, n_sem, grad_in, out_sem), refs = refs[:7], refs[7:]
    scatter.bind((gq, gk, gv), refs[: scatter.count])
    refs = refs[scatter.count :]
    z, x = scatter.z, scatter.x
    columns = half_columns(z)
    loads = []
    for i, (src, dst) in enumerate(zip(sources, slots)):
        loads.append(pltpu.make_async_copy(src.at[:, columns] if 3 <= i < 6 else src, dst, load_sem.at[i]))
    for c in loads:
        c.start()
    held, grads, normed_t, wq_ref, wk_ref, wv_ref, x_ref, mixed_ref, near, far_sum, onehot, other, leaving = slots

    def early_piece(line, c):
        first = pl.multiple_of(early.part_start[line] + c * early.small[line], 16)
        return held.at[pl.ds(first, early.small[line])]

    def late_rows(line, c):
        size = late.size[line] // 2
        first = late.start[line] + x * late.size[line] + lax.rem(c, 2) * size
        return pl.ds(pl.multiple_of(first, 16), size)

    spread_early.bind(early_piece, lambda line, c: full_early.at[early.quarter(line, x, c)], refs[: Spread.count])
    spread_late.bind(
        lambda line, c: scatter.held.at[scatter.group, late_rows(line, c)],
        lambda line, c: full_late.at[lax.div(c, 2), late_rows(line, c)],
        refs[Spread.count : 2 * Spread.count],
    )
    total_small = Total(p, p.dp * SMALL)
    total_small.bind(refs[2 * Spread.count :])
    two = spread_early.two
    n_copy = remote(leaving, arriving, (n_sem.at[0], n_sem.at[1]), seq=two * p.inner + x)
    greet_all(p)
    loads[0].wait()
    loads[-1].wait()
    n_copy.start()
    early_lines, late_lines = list(early.lines), list(late.lines)
    for line in early_lines:
        spread_early.step_pair(line)
    for c in loads[1:-1]:
        c.wait()
    batch, height, width = x_ref.shape

    def weight(i, out):
        total = jnp.zeros((width, HALF), F32)
        for b in range(batch):
            for block in range(2):
                total = total + lax.dot_general(normed_t[block, b], grads[i, b, block], NT, preferred_element_type=F32)
        out[...] = total.astype(BF16)
        scatter.step_core((i,))

    for i, out in enumerate((gq, gk, gv)):
        weight(i, out)
    spread_early.step_two(0)
    scatter.step_first(late.lines)
    spread_early.step_two(1)
    gain = gain_ref[...].reshape(1, -1)
    gain_sums = []

    leaves = [pltpu.make_async_copy(grad_in.at[b], grad_out.at[b], out_sem.at[b]) for b in range(batch)]

    def positions(b, arrived):
        back = jnp.dot(wq_ref[...], grads[0, b, 0], preferred_element_type=F32)
        back = back + jnp.dot(wk_ref[...], grads[1, b, 0], preferred_element_type=F32)
        back = back + jnp.dot(wv_ref[...], grads[2, b, 0], preferred_element_type=F32)
        back = (back + arrived[...].astype(F32)).T
        values = x_ref[b]
        scale = lax.rsqrt(jnp.mean(values * values, axis=-1, keepdims=True) + epsilon)
        gain_sums.append(jnp.sum(back * values * scale, axis=0, keepdims=True))
        u = back * gain
        along = jnp.mean(u * values, axis=-1, keepdims=True)
        grad_in[b] = mixed_ref[b] + scale * (u - values * (scale * scale * along))
        leaves[b].start()

    positions(0, other.at[0])
    spread_early.step_back(0)
    spread_early.step_two(2)
    for line in late_lines:
        scatter.step_second(line)
    for b in range(1, batch - 1):
        positions(b, other.at[b])
    spread_early.step_back(1)
    spread_early.step_two(3)
    for line in late_lines:
        scatter.step_third(line)
        spread_late.step_pair(line)
    n_copy.wait_recv()
    positions(batch - 1, arriving)
    gain_sum = sum(gain_sums)
    spread_early.step_rest(0)
    spread_early.step_back(2)
    for line in late_lines:
        spread_late.step_back(line)
    row = lax.broadcasted_iota(jnp.int32, (BLK, BLK), 0)
    col = lax.broadcasted_iota(jnp.int32, (BLK, BLK), 1)
    flip = (row + col == BLK - 1).astype(F32)
    bucket = lax.broadcasted_iota(jnp.int32, (NB, 1), 0)
    head_lane = lax.broadcasted_iota(jnp.int32, (NB, LANE), 1)
    table = jnp.zeros((NB, LANE), F32)
    for h in range(HEADS):
        line = jnp.zeros((1, SPAN), F32)
        for off in (-1, 0, 1):
            flipped = jnp.dot(flip, near[h, off + 2], preferred_element_type=F32, precision=highest)
            padded = jnp.concatenate([flipped, jnp.zeros((BLK, SPAN - BLK), F32)], axis=1)
            rolled = pltpu.roll(padded, (BLK - off * BLK) % SPAN, 1, stride=1, stride_axis=0)
            line = line + jnp.sum(rolled, axis=0, keepdims=True)
        column = jnp.sum(onehot[...] * line, axis=1, keepdims=True)
        sides = jnp.sum(far_sum[h], axis=1, keepdims=True)
        column = column + jnp.where(bucket == NB // 2 - 1, sides[0:1], 0.0) + jnp.where(bucket == NB - 1, sides[1:2], 0.0)
        table = jnp.where(head_lane == z * HEADS + h, column, table)
    share, buckets = width // p.dp, NB // p.dp
    for i in range(p.dp):
        block = []
        for v in (gain_sum, ffn_ref[...]):
            for first, last in gain_rows(share):
                v_row = v[:, i * share + first : i * share + last]
                if last - first < LANE:
                    v_row = jnp.concatenate([v_row, jnp.zeros((1, LANE - (last - first)), F32)], axis=1)
                block.append(v_row)
        block.append(table[i * buckets : (i + 1) * buckets])
        block.append(jnp.zeros((SMALL - 2 * len(gain_rows(share)) - buckets, LANE), F32))
        total_small.held[0, i * SMALL : (i + 1) * SMALL] = jnp.concatenate(block, axis=0)
    total_small.send(0)
    spread_early.step_rest(1)
    spread_early.step_back(3)
    spread_early.step_last(0)
    total_small.step(0)
    for line in late_lines:
        spread_late.step_rest(line)
    spread_early.step_rest(2)
    spread_early.step_last(1)
    total_small.step(1)
    for line in late_lines:
        spread_late.step_last(line)
    spread_early.step_rest(3)
    total_small.step(2)
    spread_early.step_last(2)
    total_small.step(3)
    spread_early.step_last(3)
    total_small.step(4)
    mine = pl.ds(pl.multiple_of(lax.axis_index("dp") * SMALL, SMALL), SMALL)
    small_out[...] = total_small.held[len(total_small.hops), mine]
    total_small.end()
    n_copy.wait_send()
    for c in leaves:
        c.wait()
    spread_early.end()
    spread_late.end()
    scatter.end()


def gain_rows(share):
    return [(at, min(at + LANE, share)) for at in range(0, share, LANE)]


def half_columns(z):
    return pl.ds(pl.multiple_of(lax.div(z, 2) * HALF, LANE), HALF)


def last_grads(early, late, loaded, gain, ffn):
    inputs = loaded[6]
    width = inputs.shape[-1]
    shapes = [(width, HALF) if 3 <= i < 6 else v.shape for i, v in enumerate(loaded)]
    return pl.pallas_call(
        functools.partial(last_kernel, early, late),
        in_specs=[anywhere()] * len(loaded) + [whole()] * 2,
        out_specs=[anywhere()] + [whole()] * 3,
        out_shape=[
            jax.ShapeDtypeStruct(inputs.shape, F32),
            jax.ShapeDtypeStruct((early.total, early.lanes), BF16),
            jax.ShapeDtypeStruct((2, late.total, late.lanes), BF16),
            jax.ShapeDtypeStruct((SMALL, LANE), F32),
        ],
        scratch_shapes=[pltpu.VMEM(shape, v.dtype) for shape, v in zip(shapes, loaded)]
        + [pltpu.SemaphoreType.DMA((len(loaded),))]
        + [pltpu.VMEM((width, HALF), BF16)] * 3
        + [pltpu.VMEM(loaded[-1].shape, BF16), pltpu.SemaphoreType.DMA((2,))]
        + [pltpu.VMEM(inputs.shape, F32), pltpu.SemaphoreType.DMA((inputs.shape[0],))]
        + Scatter(late, (True, False)).scratch()
        + Spread(early).scratch()
        + Spread(late, True).scratch()
        + Total(late.p, late.p.dp * SMALL).scratch(),
        compiler_params=pltpu.CompilerParams(
            vmem_limit_bytes=VMEM_BYTES, collective_id=2, has_side_effects=True
        ),
        name="last_grads",
    )(*loaded, gain, ffn)


def unpack_kernel(early, late, full_early, full_late, small, grad_in, *refs):
    count = len(early.shapes) + len(late.shapes)
    targets, (d_attn, d_ffn, d_table, grad_out), refs = refs[:count], refs[count : count + 4], refs[count + 4 :]
    outs, (held, taken_early, taken_late, sems) = refs[:count], refs[count:]
    arrive = [
        pltpu.make_async_copy(src, dst, sems.at[i])
        for i, (src, dst) in enumerate(((full_early, taken_early), (full_late, taken_late), (grad_in, held)))
    ]
    leave = [pltpu.make_async_copy(held, grad_out, sems.at[3])]
    leave += [pltpu.make_async_copy(src, dst, sems.at[4 + i]) for i, (src, dst) in enumerate(zip(outs, targets))]
    for c in arrive:
        c.start()
    arrive[0].wait()
    for m in range(len(early.shapes)):
        for i, block, at, share in early.blocks:
            if i == m:
                outs[m][:, block * LANES : (block + 1) * LANES] = taken_early[at : at + share].astype(F32)
        leave[1 + m].start()
    arrive[1].wait()
    for m in range(len(late.shapes)):
        for i, block, at, share in late.blocks:
            for half in range(2):
                first = half * HALF + block * LANE
                if i == m:
                    out = outs[len(early.shapes) + m]
                    out[:, first : first + LANE] = taken_late[half, at : at + share].astype(F32)
        leave[1 + len(early.shapes) + m].start()
    arrive[2].wait()
    leave[0].start()
    at = 0
    for out in (d_attn, d_ffn):
        for begin, end in gain_rows(out.shape[1]):
            out[:, begin:end] = small[at : at + 1, : end - begin]
            at += 1
    buckets, heads = d_table.shape
    d_table[...] = small[at : at + buckets, :heads]
    for c in leave:
        c.wait()


def unpack(early, late, full_early, full_late, small, grad_in):
    width = grad_in.shape[-1]
    dp = early.p.dp
    shapes = [(height // dp, columns) for height, columns in early.shapes] + [(width // dp, width)] * 3
    few = [(1, width // dp)] * 2 + [(NB // dp, H)]
    return pl.pallas_call(
        functools.partial(unpack_kernel, early, late),
        in_specs=[anywhere()] * 2 + [whole(), anywhere()],
        out_specs=[anywhere()] * len(shapes) + [whole()] * len(few) + [anywhere()],
        out_shape=[jax.ShapeDtypeStruct(s, F32) for s in shapes + few + [grad_in.shape]],
        scratch_shapes=[pltpu.VMEM(s, F32) for s in shapes]
        + [
            pltpu.VMEM(grad_in.shape, F32),
            pltpu.VMEM(full_early.shape, BF16),
            pltpu.VMEM(full_late.shape, BF16),
            pltpu.SemaphoreType.DMA((4 + len(shapes),)),
        ],
        compiler_params=params(),
        name="unpack",
    )(full_early, full_late, small, grad_in)


def greet(n, z, x):
    barrier = pltpu.get_barrier_semaphore()
    for peer in peers(n, z, x):
        pl.semaphore_signal(barrier, inc=1, device_id={"seq": peer}, device_id_type=pl.DeviceIdType.MESH)
    pl.semaphore_wait(barrier, OUTER - 1 + n - 1)


def far_case(n, j, kb):
    if kb < n * j - 1:
        return 0
    if kb > n * j + n:
        return 2
    return None


def near_case(n, j, kb, x):
    off = kb - (n * j + x)
    near = jnp.logical_and(off >= -1, off <= 1)
    return jnp.where(near, off + 2, 0), jnp.where(off <= -2, 0, jnp.where(off >= 2, 2, 1))


def key_rows(keys, kb, length):
    one = jnp.ones((1, BLK), F32)
    lane = lax.broadcasted_iota(jnp.int32, (1, BLK), 1)
    mask = jnp.where(kb * BLK + lane < length, 0.0, -1e30)
    return jnp.concatenate([keys, tail(BLK, (one, one, one, mask)).astype(BF16)], axis=0).T


def forward_kernel(
    n, len_ref, table_ref, onehot_ref, x_ref, gain_ref, wq_ref, wk_ref, wv_ref,
    normed_out, own_out, pair_out, att, o_ref, lse_ref, tile_out, far_ref,
    normed_ref, own, pair, tile_ref, keep_sem, tile_sem, here, there, send, ka, qa, va,
    n_send, n_recv, z_send, z_recv, x_send, x_recv, o_send, o_recv,
):
    nk = OUTER * n
    batch = x_ref.shape[0]
    units = batch * HEADS
    me = lax.axis_index("seq")
    z, x = lax.div(me, n), lax.rem(me, n)
    greet(n, z, x)

    near, two, across = around(z)
    groups = (z, two, near, across)
    low = lax.rem(z, 2) == 0
    columns = half_columns(z)

    def n_copy(b):
        return remote(here.at[b], there.at[b], (n_send.at[b], n_recv.at[b]), seq=two * n + x)

    def z_copy(u, i):
        sems = z_send.at[u, i], z_recv.at[u, i]
        return remote(send.at[u, i], own.at[u, groups[i]], sems, seq=near * n + x)

    def x_copy(u, s, i):
        rows = pl.ds(DH, 2 * DH)
        sems = x_send.at[s - 1, u, i], x_recv.at[s - 1, u, i]
        peer = z * n + lax.rem(x + s, n)
        return remote(own.at[u, groups[i], rows], pair.at[s - 1, u, groups[i]], sems, seq=peer)

    def o_copy(u, d):
        group = lax.rem(z + d, OUTER)
        b, h = lax.div(u, HEADS), lax.rem(u, HEADS)
        rows = pl.ds(pl.multiple_of((z * HEADS + h) * DH, DH), DH)
        sems = o_send.at[u, d - 1], o_recv.at[u, d - 1]
        return remote(o_ref.at[u, group], att.at[b, rows], sems, seq=group * n + x)

    for b in range(batch):
        values = x_ref[b]
        scale = lax.rsqrt(jnp.mean(values * values, axis=-1, keepdims=True) + epsilon)
        here[b] = (values * scale * gain_ref[...].reshape(1, -1)).astype(BF16)
        if b == 0:
            n_copy(0).start()

    def project(b, i):
        normed = (here, there)[i][b]
        normed_ref[i, b] = normed.T
        for m, (w_ref, factor) in enumerate(((wq_ref, LOG2E), (wk_ref, 1.0), (wv_ref, 1.0))):
            turned = (jnp.dot(normed, w_ref[:, columns], preferred_element_type=F32) * factor).T.astype(BF16)
            for h in range(HEADS):
                first, second = turned[h * DH : (h + 1) * DH], turned[HW + h * DH : HW + (h + 1) * DH]
                rows = slice(m * DH, (m + 1) * DH)
                own[b * HEADS + h, groups[i], rows] = jnp.where(low, first, second)
                send[b * HEADS + h, i, rows] = jnp.where(low, second, first)
        for h in range(HEADS):
            for s in range(1, n):
                x_copy(b * HEADS + h, s, i).start()

    def start_near(b, i):
        for h in range(HEADS):
            z_copy(b * HEADS + h, i).start()

    def keep(u):
        yield pltpu.make_async_copy(own.at[u], own_out.at[u], keep_sem.at[u, 0])
        for s in range(1, n):
            yield pltpu.make_async_copy(pair.at[s - 1, u], pair_out.at[s - 1, u], keep_sem.at[u, s])

    keep_normed = pltpu.make_async_copy(normed_ref, normed_out, tile_sem.at[0])
    keep_tiles = pltpu.make_async_copy(tile_ref, tile_out, tile_sem.at[1])
    for b in range(batch):
        project(b, 0)
        if b == 0:
            start_near(0, 0)

    table_lane = lax.broadcasted_iota(jnp.int32, (1, NB), 1)
    for h in range(HEADS):
        chosen = table_ref[pl.ds(z * HEADS + h, 1), :] * LOG2E
        padded = jnp.broadcast_to(chosen, (8, NB))
        line = jnp.dot(padded, onehot_ref[...], preferred_element_type=F32, precision=highest)[0:1]
        line = jnp.broadcast_to(line, (BLK, SPAN))
        tile_ref[h, 0] = jnp.zeros((BLK, BLK), F32)
        for off in (-1, 0, 1):
            shift = (off * BLK - (2 * BLK - 1)) % SPAN
            tile_ref[h, off + 2] = pltpu.roll(line, shift, 1, stride=1, stride_axis=0)[:, :BLK]
        for side, bucket in enumerate((NB // 2 - 1, NB - 1)):
            value = jnp.sum(jnp.where(table_lane == bucket, chosen, 0.0), axis=1, keepdims=True)
            far_ref[h, side] = jnp.broadcast_to(value, (1, BLK))
    keep_tiles.start()

    def attend(u):
        b, h = lax.div(u, HEADS), lax.rem(u, HEADS)
        length = len_ref[b]
        left, right = far_ref[h, 0], far_ref[h, 1]
        one = jnp.ones((1, BLK), F32)
        vtail = tail(BLK, (one,)).astype(BF16)
        for s in range(1, n):
            for i in range(OUTER):
                x_copy(u, s, i).wait_recv()
        for s in range(n):
            col = lax.rem(x + s, n)
            for j in range(OUTER):
                kb = n * j + col
                if s == 0:
                    keys, vals = own[u, j, DH : 2 * DH], own[u, j, 2 * DH :]
                else:
                    keys, vals = pair[n - s - 1, u, j, :DH], pair[n - s - 1, u, j, DH:]
                ka[kb] = key_rows(keys, kb, length)
                columns = pl.ds(pl.multiple_of(kb * BLK, BLK), BLK)
                va[:DH, columns] = vals
                va[DH:, columns] = vtail

        def scores(kb, j):
            case = far_case(n, j, kb)
            if case is not None:
                return jnp.dot(ka[kb], qa[case, j], preferred_element_type=F32)
            tile, case = near_case(n, j, kb, x)
            return jnp.dot(ka[kb], qa[case, j], preferred_element_type=F32) + tile_ref[h, tile]

        for j in range(OUTER):
            for v, c in enumerate((left, 0.0 * one, right)):
                qa[v, j, :DH] = own[u, j, :DH]
                qa[v, j, DH:] = tail(BLK, split3(c) + (one,)).astype(BF16)
        tops = []
        for j in range(OUTER):
            top = jnp.full((8, BLK), -1e30, F32)
            for kb in range(nk):
                top = jnp.maximum(top, jnp.max(scores(kb, j).reshape(BLK // 8, 8, BLK), axis=0))
            top = jnp.max(top, axis=0, keepdims=True)
            tops.append(top)
            for v, c in enumerate((left, 0.0, right)):
                qa[v, j, DH:] = tail(BLK, split3(c - top) + (one,)).astype(BF16)
        for j in range(OUTER):
            weights = [jnp.exp2(scores(kb, j)).astype(BF16) for kb in range(nk)]
            total = jnp.dot(va[...], jnp.concatenate(weights, axis=0), preferred_element_type=F32)
            weight = total[DH : DH + 1]
            o_ref[u, j] = (total[:DH] / weight).astype(BF16)
            lse_ref[u, j] = tops[j] + jnp.log2(weight)
        for c in keep(u):
            c.start()
        rows = pl.ds(pl.multiple_of((z * HEADS + h) * DH, DH), DH)
        att[b, rows] = o_ref[u, z]
        for d in (2, 1, 3):
            o_copy(u, d).start()

    def turn(u, carry):
        @pl.when(jnp.logical_and(u < units, lax.rem(u, HEADS) == 0))
        def _():
            b = lax.div(u, HEADS)
            n_copy(b).wait_recv()

            @pl.when(b + 1 < batch)
            def _():
                n_copy(b + 1).start()

            project(b, 1)
            start_near(b, 1)

            @pl.when(b + 1 < batch)
            def _():
                start_near(b + 1, 0)

        @pl.when(u < units)
        def _():
            for i in range(2):
                z_copy(u, i).wait_recv()
                for s in range(1, n):
                    x_copy(u, s, 2 + i).start()

        @pl.when(u > 0)
        def _():
            attend(u - 1)

        return carry

    lax.fori_loop(0, units + 1, turn, 0)
    keep_normed.start()

    def finish(u, carry):
        for c in keep(u):
            c.wait()
        for d in range(1, OUTER):
            o_copy(u, d).wait_send()
            o_copy(u, d).wait_recv()
        for i in range(2):
            z_copy(u, i).wait_send()
        for s in range(1, n):
            for i in range(OUTER):
                x_copy(u, s, i).wait_send()
        return carry

    lax.fori_loop(0, units, finish, 0)
    for b in range(batch):
        n_copy(b).wait_send()
    keep_normed.wait()
    keep_tiles.wait()


def attention_forward(n, lengths, table, onehot, inputs, gain, wq, wk, wv):
    batch, height, width = inputs.shape
    units, nk = batch * HEADS, n * OUTER
    dma = pltpu.SemaphoreType.DMA
    return pl.pallas_call(
        functools.partial(forward_kernel, n),
        in_specs=[smem()] + [whole()] * 7,
        out_specs=[anywhere()] * 3 + [whole()] * 3 + [anywhere(), whole()],
        out_shape=[
            jax.ShapeDtypeStruct((2, batch, width, height), BF16),
            jax.ShapeDtypeStruct((units, OUTER, 3 * DH, BLK), BF16),
            jax.ShapeDtypeStruct((n - 1, units, OUTER, 2 * DH, BLK), BF16),
            jax.ShapeDtypeStruct((batch, width, height), BF16),
            jax.ShapeDtypeStruct((units, OUTER, DH, BLK), BF16),
            jax.ShapeDtypeStruct((units, OUTER, 1, BLK), F32),
            jax.ShapeDtypeStruct((HEADS, TILES, BLK, BLK), F32),
            jax.ShapeDtypeStruct((HEADS, 2, 1, BLK), F32),
        ],
        scratch_shapes=[
            pltpu.VMEM((2, batch, width, height), BF16),
            pltpu.VMEM((units, OUTER, 3 * DH, BLK), BF16),
            pltpu.VMEM((n - 1, units, OUTER, 2 * DH, BLK), BF16),
            pltpu.VMEM((HEADS, TILES, BLK, BLK), F32),
            dma((units, n)),
            dma((2,)),
            pltpu.VMEM((batch, height, width), BF16),
            pltpu.VMEM((batch, height, width), BF16),
            pltpu.VMEM((units, 2, 3 * DH, BLK), BF16),
            pltpu.VMEM((nk, BLK, AUG), BF16),
            pltpu.VMEM((3, OUTER, AUG, BLK), BF16),
            pltpu.VMEM((AUG, nk * BLK), BF16),
            dma((batch,)),
            dma((batch,)),
            dma((units, 2)),
            dma((units, 2)),
            dma((n - 1, units, OUTER)),
            dma((n - 1, units, OUTER)),
            dma((units, OUTER - 1)),
            dma((units, OUTER - 1)),
        ],
        compiler_params=pltpu.CompilerParams(
            vmem_limit_bytes=VMEM_BYTES, collective_id=0, has_side_effects=True
        ),
        cost_estimate=pl.CostEstimate(flops=45 * 10**9, bytes_accessed=24 << 20, transcendentals=0),
        name="attention_forward",
    )(lengths, table, onehot, inputs, gain, wq, wk, wv)


def early_scatter(early):
    return Scatter(early, (True,) * len(early.lines))


def backward_kernel(
    n, early, len_ref, far_ref, lse_ref, tile_in, own, pair, o_in, dout, *refs
):
    scatter = early_scatter(early)
    count = len(early.shapes)
    weights, refs = refs[:count], refs[count:]
    projections, refs = refs[:3], refs[3:]
    (grads_out, near_out, far_sum, parts, other, leaving,
    tile_ref, o_ref, grads, near, first_sem, own_sem, keep_sem, w_half, other_out, w_sem, n_send, n_recv, own_slot, pair_slot, load_sem,
    do_land, x_out, x_land, z_out, kept,
    ka, kt, va, qa, da, dk_all, dv_all,
    d_send, d_recv, x_send, x_recv, z_send, z_recv) = refs[: -scatter.count]
    scatter.bind(weights, refs[-scatter.count :])
    nk = OUTER * n
    batch = dout.shape[0]
    units = batch * HEADS
    x_slots, z_slots = staging(n, units)
    me = lax.axis_index("seq")
    z, x = lax.div(me, n), lax.rem(me, n)
    near_z, two, across = around(z)
    low = lax.rem(z, 2) * HW
    greet_all(early.p)
    scatter.step_core()
    firsts = [
        pltpu.make_async_copy(src, dst, first_sem.at[i]) for i, (src, dst) in enumerate(((tile_in, tile_ref), (o_in, o_ref)))
    ]
    for c in firsts:
        c.start()

    def own_part(u):
        b, h = lax.div(u, HEADS), lax.rem(u, HEADS)
        return pltpu.make_async_copy(dout.at[b, head_rows(z, h)], do_land.at[u, z], own_sem.at[u])

    def keep_grads(b):
        return [pltpu.make_async_copy(grads.at[m, b], grads_out.at[m, b], keep_sem.at[m, b]) for m in range(3)]

    columns = half_columns(z)
    w_loads = [pltpu.make_async_copy(w.at[:, columns], w_half.at[m], w_sem.at[m]) for m, w in enumerate(projections)]
    for c in w_loads:
        c.start()

    def head_rows(group, h):
        return pl.ds(pl.multiple_of((group * HEADS + h) * DH, DH), DH)

    def d_copy(u, d):
        group = lax.rem(z + d, OUTER)
        b, h = lax.div(u, HEADS), lax.rem(u, HEADS)
        sems = d_send.at[u, d - 1], d_recv.at[u, d - 1]
        return remote(dout.at[b, head_rows(group, h)], do_land.at[u, z], sems, seq=group * n + x)

    def x_copy(u, s):
        peer = z * n + lax.rem(x + s, n)
        sems = x_send.at[s - 1, u], x_recv.at[s - 1, u]
        return remote(
            x_out.at[s - 1, lax.rem(u, x_slots)], x_land.at[s - 1, lax.rem(u, X_LAND)], sems, seq=peer
        )

    def half_rows(h):
        return pl.ds(pl.multiple_of(low + h * DH, DH), DH)

    def z_copy(u, i, m):
        b, h = lax.div(u, HEADS), lax.rem(u, HEADS)
        sems = z_send.at[u, i, m], z_recv.at[u, i, m]
        src, dst = z_out.at[lax.rem(u, z_slots), i, pl.ds(m * DH, DH)], grads.at[m, b, i, half_rows(h)]
        return remote(src, dst, sems, seq=near_z * n + x)

    def n_copy(b):
        return remote(other_out.at[b], other.at[b], (n_send.at[b], n_recv.at[b]), seq=two * n + x)

    def loads(u):
        slot = lax.rem(u, 2)
        yield pltpu.make_async_copy(own.at[u], own_slot.at[slot], load_sem.at[slot, 0])
        for s in range(1, n):
            yield pltpu.make_async_copy(pair.at[s - 1, u], pair_slot.at[slot, s - 1], load_sem.at[slot, s])

    for c in loads(0):
        c.start()

    def start_d(u):
        for d in (2, 1, 3):
            d_copy(u, d).start()

    start_d(0)
    start_d(1)

    def begin(u, carry):
        own_part(u).start()
        return carry

    lax.fori_loop(0, units, begin, 0)
    near[...] = jnp.zeros_like(near)
    far_sum[...] = jnp.zeros_like(far_sum)
    one = jnp.ones((1, BLK), F32)
    ones3 = tail(BLK, (one, one, one)).astype(BF16)
    row16 = lax.broadcasted_iota(jnp.int32, (16, BLK), 0)
    marks = [jnp.where(row16 == r, 1.0, 0.0).astype(BF16) for r in range(2)]

    def work(u):
        b, h = lax.div(u, HEADS), lax.rem(u, HEADS)
        length = len_ref[b]
        left, right = far_ref[h, 0], far_ref[h, 1]
        slot = lax.rem(u, 2)
        for c in loads(u):
            c.wait()

        @pl.when(u + 1 < units)
        def _():
            for c in loads(u + 1):
                c.start()

        @pl.when(u + 2 < units)
        def _():
            start_d(u + 2)

        for s in range(n):
            col = lax.rem(x + s, n)
            for j in range(OUTER):
                kb = n * j + col
                if s == 0:
                    keys, vals = own_slot[slot, j, DH : 2 * DH], own_slot[slot, j, 2 * DH :]
                else:
                    keys, vals = pair_slot[slot, n - s - 1, j, :DH], pair_slot[slot, n - s - 1, j, DH:]
                ka[kb] = key_rows(keys, kb, length)
                kt[kb] = keys
                va[kb] = jnp.concatenate([vals, ones3], axis=0).T
        own_part(u).wait()
        for d in range(1, OUTER):
            d_copy(u, d).wait_recv()
        for j in range(OUTER):
            lse = lse_ref[u, j]
            for v, c in enumerate((left, 0.0, right)):
                qa[v, j, :DH] = own_slot[slot, j, :DH]
                qa[v, j, DH:] = tail(BLK, split3(c - lse) + (one,)).astype(BF16)
            arrived = do_land[u, j]
            delta = jnp.sum(arrived.astype(F32) * o_ref[u, j].astype(F32), axis=0, keepdims=True)
            da[j, :DH] = arrived
            da[j, DH:] = tail(BLK, split3(-delta)).astype(BF16)
        dqs = [None] * OUTER
        for g in range(0, nk, GROUP):
            blocks = range(g, g + GROUP)
            ps, dss = {}, {}
            for j in range(OUTER):
                left_side = []
                for kb in blocks:
                    case = far_case(n, j, kb)
                    if case is not None:
                        p = jnp.exp2(jnp.dot(ka[kb], qa[case, j], preferred_element_type=F32))
                        mark = marks[case // 2]
                    else:
                        tile, case = near_case(n, j, kb, x)
                        s = jnp.dot(ka[kb], qa[case, j], preferred_element_type=F32)
                        p = jnp.exp2(s + tile_ref[h, tile])
                        want = jnp.where(case == 1, 2, lax.div(case, 2))
                        mark = jnp.where(row16 == want, 1.0, 0.0).astype(BF16)
                    ds = p * jnp.dot(va[kb], da[j], preferred_element_type=F32)
                    if far_case(n, j, kb) is None:
                        near[h, tile] += ds
                    ps[kb, j], dss[kb, j] = p.astype(BF16), ds.astype(BF16)
                    left_side.append(jnp.concatenate([kt[kb], mark], axis=0))
                right_side = jnp.concatenate([dss[kb, j] for kb in blocks], axis=0)
                dq = jnp.dot(jnp.concatenate(left_side, axis=1), right_side, preferred_element_type=F32)
                dqs[j] = dq if g == 0 else dqs[j] + dq
            for kb in blocks:
                dv, dk = jnp.zeros((DH, BLK), F32), jnp.zeros((DH, BLK), F32)
                for j in range(OUTER):
                    dv = dv + lax.dot_general(da[j, :DH], ps[kb, j], NT, preferred_element_type=F32)
                    dk = dk + lax.dot_general(qa[0, j, :DH], dss[kb, j], NT, preferred_element_type=F32)
                dk_all[kb] = dk * LN2
                dv_all[kb] = dv
        @pl.when(u >= x_slots)
        def _():
            for s in range(1, n):
                x_copy(u - x_slots, s).wait_send()

        far = jnp.zeros((8, BLK), F32)
        for j in range(OUTER):
            far = far + dqs[j][DH : DH + 8]
        far_sum[h] += far
        parity = lax.rem(u, 2)
        for j in range(OUTER):
            kept[parity, j, :DH] = dqs[j][:DH]
            kept[parity, j, DH : 2 * DH] = dk_all[n * j + x]
            kept[parity, j, 2 * DH :] = dv_all[n * j + x]
            for s in range(1, n):
                kb = n * j + lax.rem(x + s, n)
                x_out[s - 1, lax.rem(u, x_slots), j, :DH] = dk_all[kb].astype(BF16)
                x_out[s - 1, lax.rem(u, x_slots), j, DH:] = dv_all[kb].astype(BF16)
        for s in range(1, n):
            x_copy(u, s).start()

    def hand_over(u):
        b, h = lax.div(u, HEADS), lax.rem(u, HEADS)
        parity = lax.rem(u, 2)
        for s in range(1, n):
            x_copy(u, s).wait_recv()

        @pl.when(u >= z_slots)
        def _():
            for i in range(2):
                for m in range(3):
                    z_copy(u - z_slots, i, m).wait_send()

        for i, (mine, theirs) in enumerate(((z, near_z), (two, across))):
            for j, stays in ((mine, True), (theirs, False)):
                rest = kept[parity, j, DH:]
                for s in range(1, n):
                    rest = rest + x_land[s - 1, lax.rem(u, X_LAND), j].astype(F32)
                total = jnp.concatenate([kept[parity, j, :DH], rest], axis=0).astype(BF16)
                if stays:
                    for m in range(3):
                        grads[m, b, i, half_rows(h)] = total[m * DH : (m + 1) * DH]
                else:
                    z_out[lax.rem(u, z_slots), i] = total
            for m in range(3):
                z_copy(u, i, m).start()

    def combine(b):
        for h in range(HEADS):
            for i in range(2):
                for m in range(3):
                    z_copy(b * HEADS + h, i, m).wait_recv()
        for c in keep_grads(b):
            c.start()
        total = jnp.dot(w_half[0], grads[0, b, 1], preferred_element_type=F32)
        total = total + jnp.dot(w_half[1], grads[1, b, 1], preferred_element_type=F32)
        total = total + jnp.dot(w_half[2], grads[2, b, 1], preferred_element_type=F32)
        @pl.when(b < batch - 1)
        def _():
            other_out[b] = total.astype(BF16)
            n_copy(b).start()

        @pl.when(b == batch - 1)
        def _():
            leaving[...] = total.astype(BF16)

    def turn(u, carry):
        @pl.when(u < units)
        def _():
            work(u)

        @pl.when(jnp.logical_and(u > 0, u <= units))
        def _():
            hand_over(u - 1)

        @pl.when(jnp.logical_and(u > HEADS, lax.rem(u - 1, HEADS) == 0))
        def _():
            combine(lax.div(u - 1, HEADS) - 1)

        @pl.when(u == 0)
        def _():
            scatter.step_first((0,))

        for line in early.lines:

            @pl.when(u == 2 * line + 2)
            def _():
                scatter.step_second(line)
                if line + 1 < len(early.lines):
                    scatter.start_first(line + 1)

        return carry

    for c in w_loads + firsts:
        c.wait()
    lax.fori_loop(0, units + 2, turn, 0)
    near_copy = pltpu.make_async_copy(near, near_out, first_sem.at[0])
    near_copy.start()

    def finish(u, carry):
        for d in range(1, OUTER):
            d_copy(u, d).wait_send()

        @pl.when(u >= units - z_slots)
        def _():
            for i in range(2):
                for m in range(3):
                    z_copy(u, i, m).wait_send()

        @pl.when(u >= units - x_slots)
        def _():
            for s in range(1, n):
                x_copy(u, s).wait_send()

        return carry

    lax.fori_loop(0, units, finish, 0)
    for b in range(batch - 1):
        n_copy(b).wait_send()
        n_copy(b).wait_recv()
    for line in early.lines:
        scatter.step_third(line)
        parts[early.part_start[line] : early.part_start[line] + early.size[line]] = scatter.part(line)[...]
    scatter.end()
    for b in range(batch):
        for c in keep_grads(b):
            c.wait()
    near_copy.wait()


def staging(n, units):
    return (units, units) if n <= 2 else (2, 4)


X_LAND = 4


def attention_backward(n, early, lengths, far, tiles, own, pair, out, lse, dout, weights, projections):
    batch, width, height = dout.shape
    units, nk = batch * HEADS, n * OUTER
    dma = pltpu.SemaphoreType.DMA
    x_slots, z_slots = staging(n, units)
    return pl.pallas_call(
        functools.partial(backward_kernel, n, early),
        in_specs=[smem()] + [whole()] * 2 + [anywhere()] * (8 + len(weights)),
        out_specs=[anywhere()] * 2 + [whole()] * 4,
        out_shape=[
            jax.ShapeDtypeStruct((3, batch, 2, HALF, height), BF16),
            jax.ShapeDtypeStruct((HEADS, TILES, BLK, BLK), F32),
            jax.ShapeDtypeStruct((HEADS, 8, BLK), F32),
            jax.ShapeDtypeStruct((early.part_total, LANES), BF16),
            jax.ShapeDtypeStruct((batch - 1, width, height), BF16),
            jax.ShapeDtypeStruct((width, height), BF16),
        ],
        scratch_shapes=[
            pltpu.VMEM(tiles.shape, F32),
            pltpu.VMEM(out.shape, BF16),
            pltpu.VMEM((3, batch, 2, HALF, height), BF16),
            pltpu.VMEM((HEADS, TILES, BLK, BLK), F32),
            dma((2,)),
            dma((units,)),
            dma((3, batch)),
            pltpu.VMEM((3, width, HALF), BF16),
            pltpu.VMEM((batch - 1, width, height), BF16),
            dma((3,)),
            dma((batch - 1,)),
            dma((batch - 1,)),
            pltpu.VMEM((2, OUTER, 3 * DH, BLK), BF16),
            pltpu.VMEM((2, n - 1, OUTER, 2 * DH, BLK), BF16),
            dma((2, n)),
            pltpu.VMEM((units, OUTER, DH, BLK), BF16),
            pltpu.VMEM((n - 1, x_slots, OUTER, 2 * DH, BLK), BF16),
            pltpu.VMEM((n - 1, X_LAND, OUTER, 2 * DH, BLK), BF16),
            pltpu.VMEM((z_slots, 2, 3 * DH, BLK), BF16),
            pltpu.VMEM((2, OUTER, 3 * DH, BLK), F32),
            pltpu.VMEM((nk, BLK, AUG), BF16),
            pltpu.VMEM((nk, DH, BLK), BF16),
            pltpu.VMEM((nk, BLK, AUG), BF16),
            pltpu.VMEM((3, OUTER, AUG, BLK), BF16),
            pltpu.VMEM((OUTER, AUG, BLK), BF16),
            pltpu.VMEM((nk, DH, BLK), F32),
            pltpu.VMEM((nk, DH, BLK), F32),
            dma((units, OUTER - 1)),
            dma((units, OUTER - 1)),
            dma((n - 1, units)),
            dma((n - 1, units)),
            dma((units, 2, 3)),
            dma((units, 2, 3)),
        ]
        + early_scatter(early).scratch(),
        compiler_params=pltpu.CompilerParams(
            vmem_limit_bytes=VMEM_BYTES, collective_id=1, has_side_effects=True
        ),
        cost_estimate=pl.CostEstimate(flops=110 * 10**9, bytes_accessed=24 << 20, transcendentals=0),
        name="attention_backward",
    )(lengths, far, lse, tiles, own, pair, out, dout, *weights, *projections)


FF_STEP = 512


def middle_kernel(
    x_in, att_in, cot_in, gain_ref, w_out, w_gate, w_up, w_down,
    result_out, mixed_out, dout_out, d_gain, d_out, d_gate, d_up, d_down,
    x_ref, att_ref, cot_ref, result, grad_mixed, dout,
    wo, wg, wu, wd, att, low, hidden, g_gate, g_up, s_out, s_gate, s_up, s_down, kept, in_sem, out_sem,
):
    tokens, width = x_ref.shape
    batch = att_ref.shape[0]
    ff = w_gate.shape[1]
    pairs = ((w_out, wo), (w_gate, wg), (w_up, wu), (w_down, wd), (att_in, att_ref), (x_in, x_ref), (cot_in, cot_ref))
    loads = [pltpu.make_async_copy(src, dst, in_sem.at[i]) for i, (src, dst) in enumerate(pairs)]
    pairs = ((s_out, d_out), (s_gate, d_gate), (s_up, d_up), (s_down, d_down))
    pairs += ((result, result_out), (grad_mixed, mixed_out), (dout, dout_out))
    stores = [pltpu.make_async_copy(src, dst, out_sem.at[i]) for i, (src, dst) in enumerate(pairs)]
    loads = loads[4:5] + loads[:1] + loads[5:] + loads[1:4]
    for c in loads:
        c.start()
    height = tokens // batch
    loads[0].wait()
    for b in range(batch):
        att[b * height : (b + 1) * height] = att_ref[b].T
    for c in loads[1:4]:
        c.wait()
    low[...] = cot_ref[...].astype(BF16)
    mixed = x_ref[...] + jnp.dot(att[...], wo[...], preferred_element_type=F32)
    kept[...] = mixed
    result[...] = mixed
    scale = lax.rsqrt(jnp.mean(mixed * mixed, axis=-1, keepdims=True) + epsilon)
    normed = (mixed * scale * gain_ref[...].reshape(1, -1)).astype(BF16)
    att[...] = normed
    for c in loads[4:]:
        c.wait()
    root = 0.7978845608028654
    for at in range(0, ff, FF_STEP):
        part = slice(at, at + FF_STEP)
        gate = jnp.dot(att[...], wg[:, part], preferred_element_type=F32)
        upward = jnp.dot(att[...], wu[:, part], preferred_element_type=F32)
        g_hidden = lax.dot_general(low[...], wd[part], NT, preferred_element_type=F32)
        square = gate * gate
        t = jnp.tanh(root * gate * (1.0 + 0.044715 * square))
        half = 0.5 * (1.0 + t)
        act = gate * half
        slope = half + 0.5 * gate * (1.0 - t * t) * (root * (1.0 + 3.0 * 0.044715 * square))
        hidden[:, part] = (act * upward).astype(BF16)
        g_gate[:, part] = (g_hidden * upward * slope).astype(BF16)
        g_up[:, part] = (g_hidden * act).astype(BF16)
    result[...] += jnp.dot(hidden[...], wd[...], preferred_element_type=F32)
    stores[4].start()
    d_normed = lax.dot_general(g_gate[...], wg[...], NT, preferred_element_type=F32)
    d_normed = d_normed + lax.dot_general(g_up[...], wu[...], NT, preferred_element_type=F32)
    mixed = kept[...]
    scale = lax.rsqrt(jnp.mean(mixed * mixed, axis=-1, keepdims=True) + epsilon)
    d_gain[...] = jnp.sum(d_normed * mixed * scale, axis=0, keepdims=True)
    u = d_normed * gain_ref[...].reshape(1, -1)
    along = jnp.mean(u * mixed, axis=-1, keepdims=True)
    d_mixed = cot_ref[...] + scale * (u - mixed * (scale * scale * along))
    grad_mixed[...] = d_mixed
    stores[5].start()
    d_low = d_mixed.astype(BF16)
    turned = lax.dot_general(wo[...], d_low, NT, preferred_element_type=F32).astype(BF16)
    for b in range(batch):
        dout[b] = turned[:, b * height : (b + 1) * height]
    stores[6].start()
    total = jnp.zeros((width, width), F32)
    for b in range(batch):
        total = total + jnp.dot(att_ref[b], d_low[b * height : (b + 1) * height], preferred_element_type=F32)
    s_out[...] = total.astype(BF16)
    stores[0].start()
    normed_t = att[...].T
    for src, dst, store in ((g_gate, s_gate, stores[1]), (g_up, s_up, stores[2])):
        for at in range(0, ff, FF_STEP):
            part = slice(at, at + FF_STEP)
            dst[:, part] = jnp.dot(normed_t, src[:, part], preferred_element_type=F32).astype(BF16)
        store.start()
    for at in range(0, ff, FF_STEP):
        part = slice(at, at + FF_STEP)
        s_down[part] = jnp.dot(hidden[:, part].T, low[...], preferred_element_type=F32).astype(BF16)
    stores[3].start()
    for c in stores:
        c.wait()


def middle(inputs, att, cotangent, gain, w_out, w_gate, w_up, w_down):
    batch, height, width = inputs.shape
    tokens, ff = batch * height, w_gate.shape[1]
    weights = (w_out, w_gate, w_up, w_down)
    flat = (tokens, width)
    out = pl.pallas_call(
        middle_kernel,
        in_specs=[anywhere()] * 3 + [whole()] + [anywhere()] * 4,
        out_specs=[anywhere()] * 3 + [whole()] + [anywhere()] * 4,
        out_shape=[
            jax.ShapeDtypeStruct(flat, F32),
            jax.ShapeDtypeStruct(flat, F32),
            jax.ShapeDtypeStruct((batch, width, height), BF16),
            jax.ShapeDtypeStruct((1, width), F32),
        ]
        + [jax.ShapeDtypeStruct(w.shape, BF16) for w in weights],
        scratch_shapes=[
            pltpu.VMEM(flat, F32),
            pltpu.VMEM(att.shape, BF16),
            pltpu.VMEM(flat, F32),
            pltpu.VMEM(flat, F32),
            pltpu.VMEM(flat, F32),
            pltpu.VMEM(att.shape, BF16),
        ]
        + [pltpu.VMEM(w.shape, BF16) for w in weights]
        + [pltpu.VMEM(flat, BF16)] * 2
        + [pltpu.VMEM((tokens, ff), BF16)] * 3
        + [pltpu.VMEM(w.shape, BF16) for w in weights]
        + [pltpu.VMEM(flat, F32)]
        + [pltpu.SemaphoreType.DMA((7,))] * 2,
        compiler_params=params(),
        cost_estimate=pl.CostEstimate(flops=25 * 10**9, bytes_accessed=32 << 20, transcendentals=0),
        name="middle",
    )(inputs.reshape(flat), att, cotangent.reshape(flat), gain, *weights)
    return out[0].reshape(inputs.shape), out[1].reshape(inputs.shape), out[2], out[3], out[4:]


def shards(
    places,
    inputs,
    lengths,
    norm_attn,
    w_query,
    w_key,
    w_value,
    w_out,
    norm_ffn,
    w_gate,
    w_up,
    w_down,
    bucket_bias,
    cotangent,
):
    batch, height, width = inputs.shape
    n = places.inner
    onehot = jnp.asarray(ONEHOT)
    normed_t, own, pair, attended_t, out, lse, tiles, far = attention_forward(
        n, lengths, bucket_bias.T, onehot, inputs, norm_attn, w_query, w_key, w_value
    )
    result, grad_mixed, grad_attended_t, grad_norm_ffn, weights = middle(
        inputs, attended_t, cotangent, norm_ffn, w_out, w_gate, w_up, w_down
    )
    early = Rows(places, [g.shape for g in weights], LANES, 4)
    projections = (w_query, w_key, w_value)
    grads, near, far_sum, parts, other, leaving = attention_backward(
        n, early, lengths, far, tiles, own, pair, out, lse, grad_attended_t, weights, projections
    )
    late = Rows(places, [(width, HALF)] * 3, LANE, 2)
    loaded = (
        parts, grads, normed_t, *projections, inputs, grad_mixed, near, far_sum, onehot, other, leaving
    )
    grad_inputs, full_early, full_late, small = last_grads(early, late, loaded, norm_attn, grad_norm_ffn)
    (part_out, part_gate, part_up, part_down, part_query, part_key, part_value, part_attn, part_ffn, part_table,
     grad_inputs) = unpack(early, late, full_early, full_late, small, grad_inputs)
    return (
        result,
        grad_inputs,
        part_attn.reshape(-1),
        part_ffn.reshape(-1),
        part_query,
        part_key,
        part_value,
        part_out,
        part_gate,
        part_up,
        part_down,
        part_table,
    )


def solution(mesh):
    rows = P("dp", "seq", None)
    share = P("dp", None)
    return jax.shard_map(
        functools.partial(shards, Places(mesh)),
        mesh=mesh,
        in_specs=(rows, P("dp")) + (P(),) * 10 + (rows,),
        out_specs=(rows, rows, P("dp"), P("dp")) + (share,) * 8,
        check_vma=False,
    )
```

```python
import functools

import jax
import jax.numpy as jnp
import numpy as np
from jax import lax
from jax.experimental import pallas as pl
from jax.experimental.pallas import tpu as pltpu
from jax.sharding import PartitionSpec as P

H = 12
DH = 64
NB = 32
OUTER = 4
HEADS = H // OUTER
HW = HEADS * DH
HALF = 2 * HW
BLK = 256
AUG = DH + 16
QAUG = 2 * DH + 16
SPAN = 4 * BLK
LANES = 256
LANE = 128
LOG2E = 1.4426950408889634
F32 = jnp.float32
BF16 = jnp.bfloat16
NT = (((1,), (1,)), ((), ()))
VMEM_BYTES = 62 << 20
GROUP = 8
TILES = 4

epsilon = 1e-06
limits = (1, 2, 3, 4, 5, 6, 7, 8, 12, 16, 23, 32, 46, 64, 91)
highest = lax.Precision.HIGHEST


def bucket_lines():
    relative = 2 * BLK - 1 - np.arange(SPAN)
    count = sum((np.abs(relative) >= limit).astype(np.int32) for limit in limits)
    bucket = count + (relative > 0).astype(np.int32) * (NB // 2)
    return (bucket[None, :] == np.arange(NB)[:, None]).astype(np.float32)


ONEHOT = bucket_lines()


def params():
    return pltpu.CompilerParams(vmem_limit_bytes=VMEM_BYTES)


def smem():
    return pl.BlockSpec(memory_space=pltpu.SMEM)


def anywhere():
    return pl.BlockSpec(memory_space=pl.ANY)


def whole():
    return pl.BlockSpec(memory_space=pltpu.VMEM)


def split3(v):
    a = v.astype(BF16)
    r = v - a.astype(F32)
    b = r.astype(BF16)
    c = (r - b.astype(F32)).astype(BF16)
    return a.astype(F32), b.astype(F32), c.astype(F32)


def tail(width, values):
    row = lax.broadcasted_iota(jnp.int32, (16, width), 0)
    out = jnp.zeros((16, width), F32)
    for i, v in enumerate(values):
        out = jnp.where(row == i, v, out)
    return out


def peers(n, z, x):
    return [lax.rem(z + d, OUTER) * n + x for d in range(1, OUTER)] + [z * n + lax.rem(x + s, n) for s in range(1, n)]


def around(z):
    near = z + 1 - 2 * lax.rem(z, 2)
    return near, lax.rem(z + 2, OUTER), lax.rem(near + 2, OUTER)


class Places:
    def __init__(self, mesh):
        self.dp = mesh.shape["dp"]
        self.groups = self.dp // 2
        self.inner = mesh.shape["seq"] // OUTER


def remote(src, dst, sems, **peer):
    return pltpu.make_async_remote_copy(
        src_ref=src,
        dst_ref=dst,
        send_sem=sems[0],
        recv_sem=sems[1],
        device_id=peer,
        device_id_type=pl.DeviceIdType.MESH,
    )


class Rows:
    def __init__(self, places, shapes, lanes, lines):
        self.p = places
        self.shapes = shapes
        self.lanes = lanes
        self.lines = range(lines)
        grain = places.inner * OUTER * 16
        self.blocks = []
        at = 0
        for m, (rows, columns) in enumerate(shapes):
            share = rows // places.dp
            for block in range(columns // lanes):
                self.blocks.append((m, block, at, share))
                at += share
        self.used = at
        grains = max(-(-at // grain), lines)
        self.total = grains * grain
        cuts = [grains * line // lines * grain for line in range(lines + 1)]
        self.start = cuts[:-1]
        self.span = [b - a for a, b in zip(cuts[:-1], cuts[1:])]
        self.size = [v // places.inner for v in self.span]
        self.small = [v // OUTER for v in self.size]
        self.part_start = [v // places.inner for v in self.start]
        self.part_total = self.total // places.inner

    def line(self, line):
        return pl.ds(self.start[line], self.span[line])

    def part(self, line, x):
        return pl.ds(pl.multiple_of(self.start[line] + x * self.size[line], 16), self.size[line])

    def quarter(self, line, x, z):
        first = self.start[line] + x * self.size[line] + z * self.small[line]
        return pl.ds(pl.multiple_of(first, 16), self.small[line])


def add_to(ref, arrived):
    if len(arrived) == 1:
        ref[...] = ref[...] + arrived[0]
        return
    total = ref[...].astype(F32)
    for a in arrived:
        total = total + a.astype(F32)
    ref[...] = total.astype(BF16)


class Scatter:
    def __init__(self, rows, y_first):
        self.rows = rows
        self.y_first = y_first
        self.count = 5 + 2 * len(rows.lines)

    def scratch(self):
        r, p, dma = self.rows, self.rows.p, pltpu.SemaphoreType.DMA
        g, n, lines = p.groups, p.inner, len(r.lines)
        out = [pltpu.VMEM((g, r.total, r.lanes), BF16), pltpu.VMEM((g, r.total, r.lanes), BF16)]
        for line, y_first in enumerate(self.y_first):
            out.append(pltpu.VMEM((g - 1, r.span[line] if y_first else r.size[line], r.lanes), BF16))
            out.append(pltpu.VMEM((n - 1, 1 if y_first else g, r.size[line], r.lanes), BF16))
        return out + [dma((len(r.blocks), g, 3)), dma((lines, g - 1, 2)), dma((lines, n - 1, g, 2))]

    def bind(self, grads, refs):
        self.grads = grads
        self.held, self.land = refs[:2]
        self.c_sem, self.y_sem, self.x_sem = refs[-3:]
        self.y_land, self.x_land = refs[2:-3:2], refs[3:-3:2]
        dp, seq = lax.axis_index("dp"), lax.axis_index("seq")
        n = self.rows.p.inner
        self.core, self.group = lax.rem(dp, 2), lax.div(dp, 2)
        self.z, self.x = lax.div(seq, n), lax.rem(seq, n)

    def source(self, i, g, core):
        m, block, at, share = self.rows.blocks[i]
        first = pl.multiple_of((g * 2 + core) * share, 16)
        return self.grads[m].at[pl.ds(first, share), pl.ds(block * self.rows.lanes, self.rows.lanes)], pl.ds(at, share)

    def picked(self, chosen):
        return [i for i, b in enumerate(self.rows.blocks) if chosen is None or b[0] in chosen]

    def core_copies(self, chosen=None):
        for i in self.picked(chosen):
            for g in range(self.rows.p.groups):
                src, where = self.source(i, g, 1 - self.core)
                sems = self.c_sem.at[i, g, 0], self.c_sem.at[i, g, 1]
                yield remote(src, self.land.at[g, where], sems, dp=self.group * 2 + 1 - self.core)

    def own_copies(self, chosen=None):
        for i in self.picked(chosen):
            for g in range(self.rows.p.groups):
                src, where = self.source(i, g, self.core)
                yield pltpu.make_async_copy(src, self.held.at[g, where], self.c_sem.at[i, g, 2])

    def y_copies(self, line):
        r = self.rows
        for t in range(1, r.p.groups):
            other = lax.rem(self.group + t, r.p.groups)
            where = r.line(line) if self.y_first[line] else r.part(line, self.x)
            sems = self.y_sem.at[line, t - 1, 0], self.y_sem.at[line, t - 1, 1]
            yield remote(self.held.at[other, where], self.y_land[line].at[t - 1], sems, dp=other * 2 + self.core)

    def x_copies(self, line):
        r = self.rows
        n = r.p.inner
        for s in range(1, n):
            other = lax.rem(self.x + s, n)
            where = r.part(line, other)
            for g in range(1 if self.y_first[line] else r.p.groups):
                sems = self.x_sem.at[line, s - 1, g, 0], self.x_sem.at[line, s - 1, g, 1]
                src = self.held.at[self.group if self.y_first[line] else g, where]
                yield remote(src, self.x_land[line].at[s - 1, g], sems, seq=self.z * n + other)

    def hop(self, line, which):
        return self.y_copies(line) if (which == 0) == self.y_first[line] else self.x_copies(line)


    def step_core(self, chosen=None):
        for c in self.core_copies(chosen):
            c.start()
        for c in self.own_copies(chosen):
            c.start()

    def step_first(self, begin):
        r = self.rows
        for c in self.core_copies():
            c.wait_recv()
        for c in self.own_copies():
            c.wait()
        for line in r.lines:
            end = r.start[line] + r.span[line]
            first, last = r.start[line], min(end, r.used)
            for g in range(r.p.groups):
                where = pl.ds(first, last - first)
                add_to(self.held.at[g, where], [self.land[g, where]])
                if last < end:
                    self.held[g, last:end] = jnp.zeros((end - last, r.lanes), BF16)
            if line in begin:
                self.start_first(line)

    def start_first(self, line):
        for c in self.hop(line, 0):
            c.start()

    def step_second(self, line):
        r = self.rows
        for c in self.hop(line, 0):
            c.wait_recv()
        if self.y_first[line]:
            arrived = [self.y_land[line][t] for t in range(r.p.groups - 1)]
            add_to(self.held.at[self.group, r.line(line)], arrived)
        else:
            for g in range(r.p.groups):
                arrived = [self.x_land[line][s, g] for s in range(r.p.inner - 1)]
                add_to(self.held.at[g, r.part(line, self.x)], arrived)
        for c in self.hop(line, 1):
            c.start()

    def step_third(self, line):
        r = self.rows
        for c in self.hop(line, 1):
            c.wait_recv()
        if self.y_first[line]:
            arrived = [self.x_land[line][s, 0] for s in range(r.p.inner - 1)]
        else:
            arrived = [self.y_land[line][t] for t in range(r.p.groups - 1)]
        add_to(self.held.at[self.group, r.part(line, self.x)], arrived)

    def part(self, line):
        return self.held.at[self.group, self.rows.part(line, self.x)]

    def end(self):
        for c in self.core_copies():
            c.wait_send()
        for line in self.rows.lines:
            for which in range(2):
                for c in self.hop(line, which):
                    c.wait_send()


class Spread:
    def __init__(self, rows, halves=False):
        self.rows = rows
        self.halves = halves

    def scratch(self):
        r, dma = self.rows, pltpu.SemaphoreType.DMA
        lines = len(r.lines)
        land = (lines, 1, max(r.size) // 2, r.lanes) if self.halves else (lines, 3, max(r.small), r.lanes)
        sems = dma((lines, 3, 2))
        return [pltpu.VMEM(land, BF16), sems, sems, dma((lines, OUTER, r.p.inner - 1, 2))]

    count = 4

    def bind(self, piece, target, refs):
        self.piece, self.target = piece, target
        self.land, self.s_sem, self.g_sem, self.x_sem = refs
        seq = lax.axis_index("seq")
        n = self.rows.p.inner
        self.z, self.x = lax.div(seq, n), lax.rem(seq, n)
        self.near, self.two, self.across = around(self.z)

    def copy(self, src, dst, sems, group):
        return remote(src, dst, sems, seq=group * self.rows.p.inner + self.x)

    def sum_copy(self, line, i):
        piece = self.piece(line, (self.near, self.across, self.two)[i])
        sems = self.s_sem.at[line, i, 0], self.s_sem.at[line, i, 1]
        return self.copy(piece, self.landing(line, i), sems, self.two if i == 2 else self.near)

    def landing(self, line, i):
        rows = self.rows.size[line] // 2 if self.halves else self.rows.small[line]
        return self.land.at[line, i, pl.ds(0, rows)]

    def sums(self, line):
        return [self.sum_copy(line, i) for i in range(1 if self.halves else 3)]

    def z_copy(self, line, i):
        where = self.target(line, self.two if i == 2 else self.z)
        sems = self.g_sem.at[line, i, 0], self.g_sem.at[line, i, 1]
        return self.copy(where, where, sems, self.two if i == 0 else self.near)

    def x_copies(self, line, c):
        n = self.rows.p.inner
        where = self.target(line, c)
        for s in range(1, n):
            sems = self.x_sem.at[line, c, s - 1, 0], self.x_sem.at[line, c, s - 1, 1]
            yield remote(where, where, sems, seq=self.z * n + lax.rem(self.x + s, n))

    def spread(self, line, c):
        for s in self.x_copies(line, c):
            s.start()

    def step_pair(self, line):
        self.sum_copy(line, 0).start()
        if not self.halves:
            self.sum_copy(line, 1).start()

    def step_two(self, line):
        for i, c in ((0, self.z), (1, self.two)):
            self.sum_copy(line, i).wait_recv()
            add_to(self.piece(line, c), [self.landing(line, i)[...]])
        self.sum_copy(line, 2).start()

    def step_back(self, line):
        last = 0 if self.halves else 2
        self.sum_copy(line, last).wait_recv()
        self.target(line, self.z)[...] = self.piece(line, self.z)[...] + self.landing(line, last)[...]
        self.z_copy(line, 0).start()
        self.z_copy(line, 1).start()
        self.spread(line, self.z)

    def step_rest(self, line):
        self.z_copy(line, 0).wait_recv()
        self.z_copy(line, 2).start()
        self.spread(line, self.two)
        self.z_copy(line, 1).wait_recv()
        self.spread(line, self.near)

    def step_last(self, line):
        self.z_copy(line, 2).wait_recv()
        self.spread(line, self.across)

    def end(self):
        for line in self.rows.lines:
            for c in range(OUTER):
                for s in self.x_copies(line, c):
                    s.wait_send()
                    s.wait_recv()
            for c in self.sums(line):
                c.wait_send()
            for i in range(3):
                self.z_copy(line, i).wait_send()


class Total:
    def __init__(self, places, rows):
        self.p = places
        self.rows = rows
        self.peers = [1, places.groups - 1, places.inner - 1, 1, 1]
        self.hops = range(5)
        self.count = 8

    def scratch(self):
        dma = pltpu.SemaphoreType.DMA
        out = [pltpu.VMEM((len(self.hops) + 1, self.rows, LANE), F32)]
        out += [pltpu.VMEM((k, self.rows, LANE), F32) for k in self.peers]
        return out + [dma((len(self.hops), max(self.peers))) for _ in range(2)]

    def bind(self, refs):
        self.held, self.land, self.sems = refs[0], refs[1:6], refs[6:]
        dp, seq = lax.axis_index("dp"), lax.axis_index("seq")
        n, groups = self.p.inner, self.p.groups
        core, group, z, x = lax.rem(dp, 2), lax.div(dp, 2), lax.div(seq, n), lax.rem(seq, n)
        near, two, _ = around(z)
        self.targets = [
            [{"dp": group * 2 + 1 - core}],
            [{"dp": lax.rem(group + t, groups) * 2 + core} for t in range(1, groups)],
            [{"seq": z * n + lax.rem(x + s, n)} for s in range(1, n)],
            [{"seq": near * n + x}],
            [{"seq": two * n + x}],
        ]

    def copies(self, hop):
        for i, target in enumerate(self.targets[hop]):
            yield remote(self.held.at[hop], self.land[hop].at[i], (self.sems[0].at[hop, i], self.sems[1].at[hop, i]), **target)

    def send(self, hop):
        for c in self.copies(hop):
            c.start()

    def step(self, hop):
        for c in self.copies(hop):
            c.wait_recv()
        total = self.held[hop]
        for i in range(self.peers[hop]):
            total = total + self.land[hop][i]
        self.held[hop + 1] = total
        if hop + 1 < len(self.hops):
            self.send(hop + 1)

    def end(self):
        for hop in self.hops:
            for c in self.copies(hop):
                c.wait_send()


def greet_all(places):
    dp, seq = lax.axis_index("dp"), lax.axis_index("seq")
    n = places.inner
    core, group = lax.rem(dp, 2), lax.div(dp, 2)
    barrier = pltpu.get_barrier_semaphore()
    mesh = pl.DeviceIdType.MESH
    pl.semaphore_signal(barrier, inc=1, device_id={"dp": group * 2 + 1 - core}, device_id_type=mesh)
    for t in range(1, places.groups):
        other = lax.rem(group + t, places.groups) * 2 + core
        pl.semaphore_signal(barrier, inc=1, device_id={"dp": other}, device_id_type=mesh)
    for peer in peers(n, lax.div(seq, n), lax.rem(seq, n)):
        pl.semaphore_signal(barrier, inc=1, device_id={"seq": peer}, device_id_type=mesh)
    pl.semaphore_wait(barrier, 1 + places.groups - 1 + OUTER - 1 + n - 1)


SMALL = 16


def last_kernel(early, late, *refs):
    count = 13
    sources, (gain_ref, ffn_ref), refs = refs[:count], refs[count : count + 2], refs[count + 2 :]
    grad_out, full_early, full_late, small_out, refs = refs[0], refs[1], refs[2], refs[3], refs[4:]
    slots, load_sem, refs = refs[:count], refs[count], refs[count + 1 :]
    p = late.p
    scatter, spread_early, spread_late = Scatter(late, (True, False)), Spread(early), Spread(late, True)
    (gq, gk, gv, arriving, n_sem, grad_in, out_sem), refs = refs[:7], refs[7:]
    scatter.bind((gq, gk, gv), refs[: scatter.count])
    refs = refs[scatter.count :]
    z, x = scatter.z, scatter.x
    columns = half_columns(z)
    loads = []
    for i, (src, dst) in enumerate(zip(sources, slots)):
        loads.append(pltpu.make_async_copy(src.at[:, columns] if 3 <= i < 6 else src, dst, load_sem.at[i]))
    for c in loads:
        c.start()
    held, grads, normed_t, wq_ref, wk_ref, wv_ref, x_ref, mixed_ref, near, far_sum, onehot, other, leaving = slots

    def early_piece(line, c):
        first = pl.multiple_of(early.part_start[line] + c * early.small[line], 16)
        return held.at[pl.ds(first, early.small[line])]

    def late_rows(line, c):
        size = late.size[line] // 2
        first = late.start[line] + x * late.size[line] + lax.rem(c, 2) * size
        return pl.ds(pl.multiple_of(first, 16), size)

    spread_early.bind(early_piece, lambda line, c: full_early.at[early.quarter(line, x, c)], refs[: Spread.count])
    spread_late.bind(
        lambda line, c: scatter.held.at[scatter.group, late_rows(line, c)],
        lambda line, c: full_late.at[lax.div(c, 2), late_rows(line, c)],
        refs[Spread.count : 2 * Spread.count],
    )
    total_small = Total(p, p.dp * SMALL)
    total_small.bind(refs[2 * Spread.count :])
    two = spread_early.two
    n_copy = remote(leaving, arriving, (n_sem.at[0], n_sem.at[1]), seq=two * p.inner + x)
    greet_all(p)
    loads[0].wait()
    loads[-1].wait()
    n_copy.start()
    early_lines, late_lines = list(early.lines), list(late.lines)
    for line in early_lines:
        spread_early.step_pair(line)
    for c in loads[1:-1]:
        c.wait()
    batch, height, width = x_ref.shape

    def weight(i, out):
        total = jnp.zeros((width, HALF), F32)
        for b in range(batch):
            for block in range(2):
                total = total + lax.dot_general(normed_t[block, b], grads[i, b, block], NT, preferred_element_type=F32)
        out[...] = total.astype(BF16)
        scatter.step_core((i,))

    for i, out in enumerate((gq, gk, gv)):
        weight(i, out)
    spread_early.step_two(0)
    scatter.step_first(late.lines)
    spread_early.step_two(1)
    gain = gain_ref[...].reshape(1, -1)
    gain_sums = []

    leaves = [pltpu.make_async_copy(grad_in.at[b], grad_out.at[b], out_sem.at[b]) for b in range(batch)]

    def positions(b, arrived):
        back = jnp.dot(wq_ref[...], grads[0, b, 0], preferred_element_type=F32)
        back = back + jnp.dot(wk_ref[...], grads[1, b, 0], preferred_element_type=F32)
        back = back + jnp.dot(wv_ref[...], grads[2, b, 0], preferred_element_type=F32)
        back = (back + arrived[...].astype(F32)).T
        values = x_ref[b]
        scale = lax.rsqrt(jnp.mean(values * values, axis=-1, keepdims=True) + epsilon)
        gain_sums.append(jnp.sum(back * values * scale, axis=0, keepdims=True))
        u = back * gain
        along = jnp.mean(u * values, axis=-1, keepdims=True)
        grad_in[b] = mixed_ref[b] + scale * (u - values * (scale * scale * along))
        leaves[b].start()

    positions(0, other.at[0])
    spread_early.step_back(0)
    spread_early.step_two(2)
    for line in late_lines:
        scatter.step_second(line)
    for b in range(1, batch - 1):
        positions(b, other.at[b])
    spread_early.step_back(1)
    spread_early.step_two(3)
    for line in late_lines:
        scatter.step_third(line)
        spread_late.step_pair(line)
    n_copy.wait_recv()
    positions(batch - 1, arriving)
    gain_sum = sum(gain_sums)
    spread_early.step_rest(0)
    spread_early.step_back(2)
    for line in late_lines:
        spread_late.step_back(line)
    row = lax.broadcasted_iota(jnp.int32, (BLK, BLK), 0)
    col = lax.broadcasted_iota(jnp.int32, (BLK, BLK), 1)
    flip = (row + col == BLK - 1).astype(F32)
    bucket = lax.broadcasted_iota(jnp.int32, (NB, 1), 0)
    head_lane = lax.broadcasted_iota(jnp.int32, (NB, LANE), 1)
    table = jnp.zeros((NB, LANE), F32)
    for h in range(HEADS):
        line = jnp.zeros((1, SPAN), F32)
        for off in (-1, 0, 1):
            flipped = jnp.dot(flip, near[h, off + 2], preferred_element_type=F32, precision=highest)
            padded = jnp.concatenate([flipped, jnp.zeros((BLK, SPAN - BLK), F32)], axis=1)
            rolled = pltpu.roll(padded, (BLK - off * BLK) % SPAN, 1, stride=1, stride_axis=0)
            line = line + jnp.sum(rolled, axis=0, keepdims=True)
        column = jnp.sum(onehot[...] * line, axis=1, keepdims=True)
        sides = jnp.sum(far_sum[h], axis=1, keepdims=True)
        column = column + jnp.where(bucket == NB // 2 - 1, sides[0:1], 0.0) + jnp.where(bucket == NB - 1, sides[1:2], 0.0)
        table = jnp.where(head_lane == z * HEADS + h, column, table)
    share, buckets = width // p.dp, NB // p.dp
    for i in range(p.dp):
        block = []
        for v in (gain_sum, ffn_ref[...]):
            for first, last in gain_rows(share):
                v_row = v[:, i * share + first : i * share + last]
                if last - first < LANE:
                    v_row = jnp.concatenate([v_row, jnp.zeros((1, LANE - (last - first)), F32)], axis=1)
                block.append(v_row)
        block.append(table[i * buckets : (i + 1) * buckets])
        block.append(jnp.zeros((SMALL - 2 * len(gain_rows(share)) - buckets, LANE), F32))
        total_small.held[0, i * SMALL : (i + 1) * SMALL] = jnp.concatenate(block, axis=0)
    total_small.send(0)
    spread_early.step_rest(1)
    spread_early.step_back(3)
    spread_early.step_last(0)
    total_small.step(0)
    for line in late_lines:
        spread_late.step_rest(line)
    spread_early.step_rest(2)
    spread_early.step_last(1)
    total_small.step(1)
    for line in late_lines:
        spread_late.step_last(line)
    spread_early.step_rest(3)
    total_small.step(2)
    spread_early.step_last(2)
    total_small.step(3)
    spread_early.step_last(3)
    total_small.step(4)
    mine = pl.ds(pl.multiple_of(lax.axis_index("dp") * SMALL, SMALL), SMALL)
    small_out[...] = total_small.held[len(total_small.hops), mine]
    total_small.end()
    n_copy.wait_send()
    for c in leaves:
        c.wait()
    spread_early.end()
    spread_late.end()
    scatter.end()


def gain_rows(share):
    return [(at, min(at + LANE, share)) for at in range(0, share, LANE)]


def half_columns(z):
    return pl.ds(pl.multiple_of(lax.div(z, 2) * HALF, LANE), HALF)


def last_grads(early, late, loaded, gain, ffn):
    inputs = loaded[6]
    width = inputs.shape[-1]
    shapes = [(width, HALF) if 3 <= i < 6 else v.shape for i, v in enumerate(loaded)]
    return pl.pallas_call(
        functools.partial(last_kernel, early, late),
        in_specs=[anywhere()] * len(loaded) + [whole()] * 2,
        out_specs=[anywhere()] + [whole()] * 3,
        out_shape=[
            jax.ShapeDtypeStruct(inputs.shape, F32),
            jax.ShapeDtypeStruct((early.total, early.lanes), BF16),
            jax.ShapeDtypeStruct((2, late.total, late.lanes), BF16),
            jax.ShapeDtypeStruct((SMALL, LANE), F32),
        ],
        scratch_shapes=[pltpu.VMEM(shape, v.dtype) for shape, v in zip(shapes, loaded)]
        + [pltpu.SemaphoreType.DMA((len(loaded),))]
        + [pltpu.VMEM((width, HALF), BF16)] * 3
        + [pltpu.VMEM(loaded[-1].shape, BF16), pltpu.SemaphoreType.DMA((2,))]
        + [pltpu.VMEM(inputs.shape, F32), pltpu.SemaphoreType.DMA((inputs.shape[0],))]
        + Scatter(late, (True, False)).scratch()
        + Spread(early).scratch()
        + Spread(late, True).scratch()
        + Total(late.p, late.p.dp * SMALL).scratch(),
        compiler_params=pltpu.CompilerParams(
            vmem_limit_bytes=VMEM_BYTES, collective_id=2, has_side_effects=True
        ),
        name="last_grads",
    )(*loaded, gain, ffn)


def unpack_kernel(early, late, full_early, full_late, small, grad_in, *refs):
    count = len(early.shapes) + len(late.shapes)
    targets, (d_attn, d_ffn, d_table, grad_out), refs = refs[:count], refs[count : count + 4], refs[count + 4 :]
    outs, (held, taken_early, taken_late, sems) = refs[:count], refs[count:]
    arrive = [
        pltpu.make_async_copy(src, dst, sems.at[i])
        for i, (src, dst) in enumerate(((full_early, taken_early), (full_late, taken_late), (grad_in, held)))
    ]
    leave = [pltpu.make_async_copy(held, grad_out, sems.at[3])]
    leave += [pltpu.make_async_copy(src, dst, sems.at[4 + i]) for i, (src, dst) in enumerate(zip(outs, targets))]
    for c in arrive:
        c.start()
    arrive[0].wait()
    for m in range(len(early.shapes)):
        for i, block, at, share in early.blocks:
            if i == m:
                outs[m][:, block * LANES : (block + 1) * LANES] = taken_early[at : at + share].astype(F32)
        leave[1 + m].start()
    arrive[1].wait()
    for m in range(len(late.shapes)):
        for i, block, at, share in late.blocks:
            for half in range(2):
                first = half * HALF + block * LANE
                if i == m:
                    out = outs[len(early.shapes) + m]
                    out[:, first : first + LANE] = taken_late[half, at : at + share].astype(F32)
        leave[1 + len(early.shapes) + m].start()
    arrive[2].wait()
    leave[0].start()
    at = 0
    for out in (d_attn, d_ffn):
        for begin, end in gain_rows(out.shape[1]):
            out[:, begin:end] = small[at : at + 1, : end - begin]
            at += 1
    buckets, heads = d_table.shape
    d_table[...] = small[at : at + buckets, :heads]
    for c in leave:
        c.wait()


def unpack(early, late, full_early, full_late, small, grad_in):
    width = grad_in.shape[-1]
    dp = early.p.dp
    shapes = [(height // dp, columns) for height, columns in early.shapes] + [(width // dp, width)] * 3
    few = [(1, width // dp)] * 2 + [(NB // dp, H)]
    return pl.pallas_call(
        functools.partial(unpack_kernel, early, late),
        in_specs=[anywhere()] * 2 + [whole(), anywhere()],
        out_specs=[anywhere()] * len(shapes) + [whole()] * len(few) + [anywhere()],
        out_shape=[jax.ShapeDtypeStruct(s, F32) for s in shapes + few + [grad_in.shape]],
        scratch_shapes=[pltpu.VMEM(s, F32) for s in shapes]
        + [
            pltpu.VMEM(grad_in.shape, F32),
            pltpu.VMEM(full_early.shape, BF16),
            pltpu.VMEM(full_late.shape, BF16),
            pltpu.SemaphoreType.DMA((4 + len(shapes),)),
        ],
        compiler_params=params(),
        name="unpack",
    )(full_early, full_late, small, grad_in)


def greet(n, z, x):
    barrier = pltpu.get_barrier_semaphore()
    for peer in peers(n, z, x):
        pl.semaphore_signal(barrier, inc=1, device_id={"seq": peer}, device_id_type=pl.DeviceIdType.MESH)
    pl.semaphore_wait(barrier, OUTER - 1 + n - 1)


def far_case(n, j, kb):
    if kb < n * j - 1:
        return 0
    if kb > n * j + n:
        return 2
    return None


def near_case(n, j, kb, x):
    off = kb - (n * j + x)
    near = jnp.logical_and(off >= -1, off <= 1)
    return jnp.where(near, off + 2, 0), jnp.where(off <= -2, 0, jnp.where(off >= 2, 2, 1))


def key_rows(keys, kb, length):
    one = jnp.ones((1, BLK), F32)
    lane = lax.broadcasted_iota(jnp.int32, (1, BLK), 1)
    mask = jnp.where(kb * BLK + lane < length, 0.0, -1e30)
    return jnp.concatenate([keys, keys, tail(BLK, (one, one, one, mask)).astype(BF16)], axis=0).T


def query_parts(queries):
    scaled = queries.astype(F32) * LOG2E
    high = scaled.astype(BF16)
    return jnp.concatenate([high, (scaled - high.astype(F32)).astype(BF16)], axis=0)


def forward_kernel(
    n, len_ref, table_ref, onehot_ref, x_ref, gain_ref, wq_ref, wk_ref, wv_ref,
    normed_out, own_out, pair_out, att, o_ref, lse_ref, tile_out, far_ref,
    normed_ref, own, pair, tile_ref, keep_sem, tile_sem, here, there, send, ka, qa, va,
    n_send, n_recv, z_send, z_recv, x_send, x_recv, o_send, o_recv,
):
    nk = OUTER * n
    batch = x_ref.shape[0]
    units = batch * HEADS
    me = lax.axis_index("seq")
    z, x = lax.div(me, n), lax.rem(me, n)
    greet(n, z, x)

    near, two, across = around(z)
    groups = (z, two, near, across)
    low = lax.rem(z, 2) == 0
    columns = half_columns(z)

    def n_copy(b):
        return remote(here.at[b], there.at[b], (n_send.at[b], n_recv.at[b]), seq=two * n + x)

    def z_copy(u, i):
        sems = z_send.at[u, i], z_recv.at[u, i]
        return remote(send.at[u, i], own.at[u, groups[i]], sems, seq=near * n + x)

    def x_copy(u, s, i):
        rows = pl.ds(DH, 2 * DH)
        sems = x_send.at[s - 1, u, i], x_recv.at[s - 1, u, i]
        peer = z * n + lax.rem(x + s, n)
        return remote(own.at[u, groups[i], rows], pair.at[s - 1, u, groups[i]], sems, seq=peer)

    def o_copy(u, d):
        group = lax.rem(z + d, OUTER)
        b, h = lax.div(u, HEADS), lax.rem(u, HEADS)
        rows = pl.ds(pl.multiple_of((z * HEADS + h) * DH, DH), DH)
        sems = o_send.at[u, d - 1], o_recv.at[u, d - 1]
        return remote(o_ref.at[u, group], att.at[b, rows], sems, seq=group * n + x)

    for b in range(batch):
        values = x_ref[b]
        scale = lax.rsqrt(jnp.mean(values * values, axis=-1, keepdims=True) + epsilon)
        here[b] = (values * scale * gain_ref[...].reshape(1, -1)).astype(BF16)
        if b == 0:
            n_copy(0).start()

    def project(b, i):
        normed = (here, there)[i][b]
        normed_ref[i, b] = normed.T
        for m, w_ref in enumerate((wq_ref, wk_ref, wv_ref)):
            turned = jnp.dot(normed, w_ref[:, columns], preferred_element_type=F32).T.astype(BF16)
            for h in range(HEADS):
                first, second = turned[h * DH : (h + 1) * DH], turned[HW + h * DH : HW + (h + 1) * DH]
                rows = slice(m * DH, (m + 1) * DH)
                own[b * HEADS + h, groups[i], rows] = jnp.where(low, first, second)
                send[b * HEADS + h, i, rows] = jnp.where(low, second, first)
        for h in range(HEADS):
            for s in range(1, n):
                x_copy(b * HEADS + h, s, i).start()

    def start_near(b, i):
        for h in range(HEADS):
            z_copy(b * HEADS + h, i).start()

    def keep(u):
        yield pltpu.make_async_copy(own.at[u], own_out.at[u], keep_sem.at[u, 0])
        for s in range(1, n):
            yield pltpu.make_async_copy(pair.at[s - 1, u], pair_out.at[s - 1, u], keep_sem.at[u, s])

    keep_normed = pltpu.make_async_copy(normed_ref, normed_out, tile_sem.at[0])
    keep_tiles = pltpu.make_async_copy(tile_ref, tile_out, tile_sem.at[1])
    for b in range(batch):
        project(b, 0)
        if b == 0:
            start_near(0, 0)

    table_lane = lax.broadcasted_iota(jnp.int32, (1, NB), 1)
    for h in range(HEADS):
        chosen = table_ref[pl.ds(z * HEADS + h, 1), :] * LOG2E
        padded = jnp.broadcast_to(chosen, (8, NB))
        line = jnp.dot(padded, onehot_ref[...], preferred_element_type=F32, precision=highest)[0:1]
        line = jnp.broadcast_to(line, (BLK, SPAN))
        tile_ref[h, 0] = jnp.zeros((BLK, BLK), F32)
        for off in (-1, 0, 1):
            shift = (off * BLK - (2 * BLK - 1)) % SPAN
            tile_ref[h, off + 2] = pltpu.roll(line, shift, 1, stride=1, stride_axis=0)[:, :BLK]
        for side, bucket in enumerate((NB // 2 - 1, NB - 1)):
            value = jnp.sum(jnp.where(table_lane == bucket, chosen, 0.0), axis=1, keepdims=True)
            far_ref[h, side] = jnp.broadcast_to(value, (1, BLK))
    keep_tiles.start()

    def attend(u):
        b, h = lax.div(u, HEADS), lax.rem(u, HEADS)
        length = len_ref[b]
        left, right = far_ref[h, 0], far_ref[h, 1]
        one = jnp.ones((1, BLK), F32)
        vtail = tail(BLK, (one,)).astype(BF16)
        for s in range(1, n):
            for i in range(OUTER):
                x_copy(u, s, i).wait_recv()
        for s in range(n):
            col = lax.rem(x + s, n)
            for j in range(OUTER):
                kb = n * j + col
                if s == 0:
                    keys, vals = own[u, j, DH : 2 * DH], own[u, j, 2 * DH :]
                else:
                    keys, vals = pair[n - s - 1, u, j, :DH], pair[n - s - 1, u, j, DH:]
                ka[kb] = key_rows(keys, kb, length)
                columns = pl.ds(pl.multiple_of(kb * BLK, BLK), BLK)
                va[:DH, columns] = vals
                va[DH:, columns] = vtail

        def scores(kb, j):
            case = far_case(n, j, kb)
            if case is not None:
                return jnp.dot(ka[kb], qa[case, j], preferred_element_type=F32)
            tile, case = near_case(n, j, kb, x)
            return jnp.dot(ka[kb], qa[case, j], preferred_element_type=F32) + tile_ref[h, tile]

        for j in range(OUTER):
            both = query_parts(own[u, j, :DH])
            for v, c in enumerate((left, 0.0 * one, right)):
                qa[v, j, : 2 * DH] = both
                qa[v, j, 2 * DH :] = tail(BLK, split3(c) + (one,)).astype(BF16)
        tops = []
        for j in range(OUTER):
            top = jnp.full((8, BLK), -1e30, F32)
            for kb in range(nk):
                top = jnp.maximum(top, jnp.max(scores(kb, j).reshape(BLK // 8, 8, BLK), axis=0))
            top = jnp.max(top, axis=0, keepdims=True)
            tops.append(top)
            for v, c in enumerate((left, 0.0, right)):
                qa[v, j, 2 * DH :] = tail(BLK, split3(c - top) + (one,)).astype(BF16)
        for j in range(OUTER):
            weights = [jnp.exp2(scores(kb, j)).astype(BF16) for kb in range(nk)]
            total = jnp.dot(va[...], jnp.concatenate(weights, axis=0), preferred_element_type=F32)
            weight = total[DH : DH + 1]
            o_ref[u, j] = (total[:DH] / weight).astype(BF16)
            lse_ref[u, j] = tops[j] + jnp.log2(weight)
        for c in keep(u):
            c.start()
        rows = pl.ds(pl.multiple_of((z * HEADS + h) * DH, DH), DH)
        att[b, rows] = o_ref[u, z]
        for d in (2, 1, 3):
            o_copy(u, d).start()

    def turn(u, carry):
        @pl.when(jnp.logical_and(u < units, lax.rem(u, HEADS) == 0))
        def _():
            b = lax.div(u, HEADS)
            n_copy(b).wait_recv()

            @pl.when(b + 1 < batch)
            def _():
                n_copy(b + 1).start()

            project(b, 1)
            start_near(b, 1)

            @pl.when(b + 1 < batch)
            def _():
                start_near(b + 1, 0)

        @pl.when(u < units)
        def _():
            for i in range(2):
                z_copy(u, i).wait_recv()
                for s in range(1, n):
                    x_copy(u, s, 2 + i).start()

        @pl.when(u > 0)
        def _():
            attend(u - 1)

        return carry

    lax.fori_loop(0, units + 1, turn, 0)
    keep_normed.start()

    def finish(u, carry):
        for c in keep(u):
            c.wait()
        for d in range(1, OUTER):
            o_copy(u, d).wait_send()
            o_copy(u, d).wait_recv()
        for i in range(2):
            z_copy(u, i).wait_send()
        for s in range(1, n):
            for i in range(OUTER):
                x_copy(u, s, i).wait_send()
        return carry

    lax.fori_loop(0, units, finish, 0)
    for b in range(batch):
        n_copy(b).wait_send()
    keep_normed.wait()
    keep_tiles.wait()


def attention_forward(n, lengths, table, onehot, inputs, gain, wq, wk, wv):
    batch, height, width = inputs.shape
    units, nk = batch * HEADS, n * OUTER
    dma = pltpu.SemaphoreType.DMA
    return pl.pallas_call(
        functools.partial(forward_kernel, n),
        in_specs=[smem()] + [whole()] * 7,
        out_specs=[anywhere()] * 3 + [whole()] * 3 + [anywhere(), whole()],
        out_shape=[
            jax.ShapeDtypeStruct((2, batch, width, height), BF16),
            jax.ShapeDtypeStruct((units, OUTER, 3 * DH, BLK), BF16),
            jax.ShapeDtypeStruct((n - 1, units, OUTER, 2 * DH, BLK), BF16),
            jax.ShapeDtypeStruct((batch, width, height), BF16),
            jax.ShapeDtypeStruct((units, OUTER, DH, BLK), BF16),
            jax.ShapeDtypeStruct((units, OUTER, 1, BLK), F32),
            jax.ShapeDtypeStruct((HEADS, TILES, BLK, BLK), F32),
            jax.ShapeDtypeStruct((HEADS, 2, 1, BLK), F32),
        ],
        scratch_shapes=[
            pltpu.VMEM((2, batch, width, height), BF16),
            pltpu.VMEM((units, OUTER, 3 * DH, BLK), BF16),
            pltpu.VMEM((n - 1, units, OUTER, 2 * DH, BLK), BF16),
            pltpu.VMEM((HEADS, TILES, BLK, BLK), F32),
            dma((units, n)),
            dma((2,)),
            pltpu.VMEM((batch, height, width), BF16),
            pltpu.VMEM((batch, height, width), BF16),
            pltpu.VMEM((units, 2, 3 * DH, BLK), BF16),
            pltpu.VMEM((nk, BLK, QAUG), BF16),
            pltpu.VMEM((3, OUTER, QAUG, BLK), BF16),
            pltpu.VMEM((AUG, nk * BLK), BF16),
            dma((batch,)),
            dma((batch,)),
            dma((units, 2)),
            dma((units, 2)),
            dma((n - 1, units, OUTER)),
            dma((n - 1, units, OUTER)),
            dma((units, OUTER - 1)),
            dma((units, OUTER - 1)),
        ],
        compiler_params=pltpu.CompilerParams(
            vmem_limit_bytes=VMEM_BYTES, collective_id=0, has_side_effects=True
        ),
        cost_estimate=pl.CostEstimate(flops=45 * 10**9, bytes_accessed=24 << 20, transcendentals=0),
        name="attention_forward",
    )(lengths, table, onehot, inputs, gain, wq, wk, wv)


def early_scatter(early):
    return Scatter(early, (True,) * len(early.lines))


def backward_kernel(
    n, early, len_ref, far_ref, lse_ref, tile_in, own, pair, o_in, dout, *refs
):
    scatter = early_scatter(early)
    count = len(early.shapes)
    weights, refs = refs[:count], refs[count:]
    projections, refs = refs[:3], refs[3:]
    (grads_out, near_out, far_sum, parts, other, leaving,
    tile_ref, o_ref, grads, near, first_sem, own_sem, keep_sem, w_half, other_out, w_sem, n_send, n_recv, own_slot, pair_slot, load_sem,
    do_land, x_out, x_land, z_out, kept,
    ka, kt, va, qa, da, dk_all, dv_all,
    d_send, d_recv, x_send, x_recv, z_send, z_recv) = refs[: -scatter.count]
    scatter.bind(weights, refs[-scatter.count :])
    nk = OUTER * n
    batch = dout.shape[0]
    units = batch * HEADS
    x_slots, z_slots = staging(n, units)
    me = lax.axis_index("seq")
    z, x = lax.div(me, n), lax.rem(me, n)
    near_z, two, across = around(z)
    low = lax.rem(z, 2) * HW
    greet_all(early.p)
    scatter.step_core()
    firsts = [
        pltpu.make_async_copy(src, dst, first_sem.at[i]) for i, (src, dst) in enumerate(((tile_in, tile_ref), (o_in, o_ref)))
    ]
    for c in firsts:
        c.start()

    def own_part(u):
        b, h = lax.div(u, HEADS), lax.rem(u, HEADS)
        return pltpu.make_async_copy(dout.at[b, head_rows(z, h)], do_land.at[u, z], own_sem.at[u])

    def keep_grads(b):
        return [pltpu.make_async_copy(grads.at[m, b], grads_out.at[m, b], keep_sem.at[m, b]) for m in range(3)]

    columns = half_columns(z)
    w_loads = [pltpu.make_async_copy(w.at[:, columns], w_half.at[m], w_sem.at[m]) for m, w in enumerate(projections)]
    for c in w_loads:
        c.start()

    def head_rows(group, h):
        return pl.ds(pl.multiple_of((group * HEADS + h) * DH, DH), DH)

    def d_copy(u, d):
        group = lax.rem(z + d, OUTER)
        b, h = lax.div(u, HEADS), lax.rem(u, HEADS)
        sems = d_send.at[u, d - 1], d_recv.at[u, d - 1]
        return remote(dout.at[b, head_rows(group, h)], do_land.at[u, z], sems, seq=group * n + x)

    def x_copy(u, s):
        peer = z * n + lax.rem(x + s, n)
        sems = x_send.at[s - 1, u], x_recv.at[s - 1, u]
        return remote(
            x_out.at[s - 1, lax.rem(u, x_slots)], x_land.at[s - 1, lax.rem(u, X_LAND)], sems, seq=peer
        )

    def half_rows(h):
        return pl.ds(pl.multiple_of(low + h * DH, DH), DH)

    def z_copy(u, i, m):
        b, h = lax.div(u, HEADS), lax.rem(u, HEADS)
        sems = z_send.at[u, i, m], z_recv.at[u, i, m]
        src, dst = z_out.at[lax.rem(u, z_slots), i, pl.ds(m * DH, DH)], grads.at[m, b, i, half_rows(h)]
        return remote(src, dst, sems, seq=near_z * n + x)

    def n_copy(b):
        return remote(other_out.at[b], other.at[b], (n_send.at[b], n_recv.at[b]), seq=two * n + x)

    def loads(u):
        slot = lax.rem(u, 2)
        yield pltpu.make_async_copy(own.at[u], own_slot.at[slot], load_sem.at[slot, 0])
        for s in range(1, n):
            yield pltpu.make_async_copy(pair.at[s - 1, u], pair_slot.at[slot, s - 1], load_sem.at[slot, s])

    for c in loads(0):
        c.start()

    def start_d(u):
        for d in (2, 1, 3):
            d_copy(u, d).start()

    start_d(0)
    start_d(1)

    def begin(u, carry):
        own_part(u).start()
        return carry

    lax.fori_loop(0, units, begin, 0)
    near[...] = jnp.zeros_like(near)
    far_sum[...] = jnp.zeros_like(far_sum)
    one = jnp.ones((1, BLK), F32)
    ones3 = tail(BLK, (one, one, one)).astype(BF16)
    row16 = lax.broadcasted_iota(jnp.int32, (16, BLK), 0)
    marks = [jnp.where(row16 == r, 1.0, 0.0).astype(BF16) for r in range(2)]

    def work(u):
        b, h = lax.div(u, HEADS), lax.rem(u, HEADS)
        length = len_ref[b]
        left, right = far_ref[h, 0], far_ref[h, 1]
        slot = lax.rem(u, 2)
        for c in loads(u):
            c.wait()

        @pl.when(u + 1 < units)
        def _():
            for c in loads(u + 1):
                c.start()

        @pl.when(u + 2 < units)
        def _():
            start_d(u + 2)

        for s in range(n):
            col = lax.rem(x + s, n)
            for j in range(OUTER):
                kb = n * j + col
                if s == 0:
                    keys, vals = own_slot[slot, j, DH : 2 * DH], own_slot[slot, j, 2 * DH :]
                else:
                    keys, vals = pair_slot[slot, n - s - 1, j, :DH], pair_slot[slot, n - s - 1, j, DH:]
                ka[kb] = key_rows(keys, kb, length)
                kt[kb] = keys
                va[kb] = jnp.concatenate([vals, ones3], axis=0).T
        own_part(u).wait()
        for d in range(1, OUTER):
            d_copy(u, d).wait_recv()
        for j in range(OUTER):
            lse = lse_ref[u, j]
            both = query_parts(own_slot[slot, j, :DH])
            for v, c in enumerate((left, 0.0, right)):
                qa[v, j, : 2 * DH] = both
                qa[v, j, 2 * DH :] = tail(BLK, split3(c - lse) + (one,)).astype(BF16)
            arrived = do_land[u, j]
            delta = jnp.sum(arrived.astype(F32) * o_ref[u, j].astype(F32), axis=0, keepdims=True)
            da[j, :DH] = arrived
            da[j, DH:] = tail(BLK, split3(-delta)).astype(BF16)
        dqs = [None] * OUTER
        for g in range(0, nk, GROUP):
            blocks = range(g, g + GROUP)
            ps, dss = {}, {}
            for j in range(OUTER):
                left_side = []
                for kb in blocks:
                    case = far_case(n, j, kb)
                    if case is not None:
                        p = jnp.exp2(jnp.dot(ka[kb], qa[case, j], preferred_element_type=F32))
                        mark = marks[case // 2]
                    else:
                        tile, case = near_case(n, j, kb, x)
                        s = jnp.dot(ka[kb], qa[case, j], preferred_element_type=F32)
                        p = jnp.exp2(s + tile_ref[h, tile])
                        want = jnp.where(case == 1, 2, lax.div(case, 2))
                        mark = jnp.where(row16 == want, 1.0, 0.0).astype(BF16)
                    ds = p * jnp.dot(va[kb], da[j], preferred_element_type=F32)
                    if far_case(n, j, kb) is None:
                        near[h, tile] += ds
                    ps[kb, j], dss[kb, j] = p.astype(BF16), ds.astype(BF16)
                    left_side.append(jnp.concatenate([kt[kb], mark], axis=0))
                right_side = jnp.concatenate([dss[kb, j] for kb in blocks], axis=0)
                dq = jnp.dot(jnp.concatenate(left_side, axis=1), right_side, preferred_element_type=F32)
                dqs[j] = dq if g == 0 else dqs[j] + dq
            for kb in blocks:
                dv, dk = jnp.zeros((DH, BLK), F32), jnp.zeros((DH, BLK), F32)
                for j in range(OUTER):
                    dv = dv + lax.dot_general(da[j, :DH], ps[kb, j], NT, preferred_element_type=F32)
                    dk = dk + lax.dot_general(own_slot[slot, j, :DH], dss[kb, j], NT, preferred_element_type=F32)
                dk_all[kb] = dk
                dv_all[kb] = dv
        @pl.when(u >= x_slots)
        def _():
            for s in range(1, n):
                x_copy(u - x_slots, s).wait_send()

        far = jnp.zeros((8, BLK), F32)
        for j in range(OUTER):
            far = far + dqs[j][DH : DH + 8]
        far_sum[h] += far
        parity = lax.rem(u, 2)
        for j in range(OUTER):
            kept[parity, j, :DH] = dqs[j][:DH]
            kept[parity, j, DH : 2 * DH] = dk_all[n * j + x]
            kept[parity, j, 2 * DH :] = dv_all[n * j + x]
            for s in range(1, n):
                kb = n * j + lax.rem(x + s, n)
                x_out[s - 1, lax.rem(u, x_slots), j, :DH] = dk_all[kb].astype(BF16)
                x_out[s - 1, lax.rem(u, x_slots), j, DH:] = dv_all[kb].astype(BF16)
        for s in range(1, n):
            x_copy(u, s).start()

    def hand_over(u):
        b, h = lax.div(u, HEADS), lax.rem(u, HEADS)
        parity = lax.rem(u, 2)
        for s in range(1, n):
            x_copy(u, s).wait_recv()

        @pl.when(u >= z_slots)
        def _():
            for i in range(2):
                for m in range(3):
                    z_copy(u - z_slots, i, m).wait_send()

        for i, (mine, theirs) in enumerate(((z, near_z), (two, across))):
            for j, stays in ((mine, True), (theirs, False)):
                rest = kept[parity, j, DH:]
                for s in range(1, n):
                    rest = rest + x_land[s - 1, lax.rem(u, X_LAND), j].astype(F32)
                total = jnp.concatenate([kept[parity, j, :DH], rest], axis=0).astype(BF16)
                if stays:
                    for m in range(3):
                        grads[m, b, i, half_rows(h)] = total[m * DH : (m + 1) * DH]
                else:
                    z_out[lax.rem(u, z_slots), i] = total
            for m in range(3):
                z_copy(u, i, m).start()

    def combine(b):
        for h in range(HEADS):
            for i in range(2):
                for m in range(3):
                    z_copy(b * HEADS + h, i, m).wait_recv()
        for c in keep_grads(b):
            c.start()
        total = jnp.dot(w_half[0], grads[0, b, 1], preferred_element_type=F32)
        total = total + jnp.dot(w_half[1], grads[1, b, 1], preferred_element_type=F32)
        total = total + jnp.dot(w_half[2], grads[2, b, 1], preferred_element_type=F32)
        @pl.when(b < batch - 1)
        def _():
            other_out[b] = total.astype(BF16)
            n_copy(b).start()

        @pl.when(b == batch - 1)
        def _():
            leaving[...] = total.astype(BF16)

    def turn(u, carry):
        @pl.when(u < units)
        def _():
            work(u)

        @pl.when(jnp.logical_and(u > 0, u <= units))
        def _():
            hand_over(u - 1)

        @pl.when(jnp.logical_and(u > HEADS, lax.rem(u - 1, HEADS) == 0))
        def _():
            combine(lax.div(u - 1, HEADS) - 1)

        @pl.when(u == 0)
        def _():
            scatter.step_first((0,))

        for line in early.lines:

            @pl.when(u == 2 * line + 2)
            def _():
                scatter.step_second(line)
                if line + 1 < len(early.lines):
                    scatter.start_first(line + 1)

        return carry

    for c in w_loads + firsts:
        c.wait()
    lax.fori_loop(0, units + 2, turn, 0)
    near_copy = pltpu.make_async_copy(near, near_out, first_sem.at[0])
    near_copy.start()

    def finish(u, carry):
        for d in range(1, OUTER):
            d_copy(u, d).wait_send()

        @pl.when(u >= units - z_slots)
        def _():
            for i in range(2):
                for m in range(3):
                    z_copy(u, i, m).wait_send()

        @pl.when(u >= units - x_slots)
        def _():
            for s in range(1, n):
                x_copy(u, s).wait_send()

        return carry

    lax.fori_loop(0, units, finish, 0)
    for b in range(batch - 1):
        n_copy(b).wait_send()
        n_copy(b).wait_recv()
    for line in early.lines:
        scatter.step_third(line)
        parts[early.part_start[line] : early.part_start[line] + early.size[line]] = scatter.part(line)[...]
    scatter.end()
    for b in range(batch):
        for c in keep_grads(b):
            c.wait()
    near_copy.wait()


def staging(n, units):
    return (units, units) if n <= 2 else (2, 4)


X_LAND = 4


def attention_backward(n, early, lengths, far, tiles, own, pair, out, lse, dout, weights, projections):
    batch, width, height = dout.shape
    units, nk = batch * HEADS, n * OUTER
    dma = pltpu.SemaphoreType.DMA
    x_slots, z_slots = staging(n, units)
    return pl.pallas_call(
        functools.partial(backward_kernel, n, early),
        in_specs=[smem()] + [whole()] * 2 + [anywhere()] * (8 + len(weights)),
        out_specs=[anywhere()] * 2 + [whole()] * 4,
        out_shape=[
            jax.ShapeDtypeStruct((3, batch, 2, HALF, height), BF16),
            jax.ShapeDtypeStruct((HEADS, TILES, BLK, BLK), F32),
            jax.ShapeDtypeStruct((HEADS, 8, BLK), F32),
            jax.ShapeDtypeStruct((early.part_total, LANES), BF16),
            jax.ShapeDtypeStruct((batch - 1, width, height), BF16),
            jax.ShapeDtypeStruct((width, height), BF16),
        ],
        scratch_shapes=[
            pltpu.VMEM(tiles.shape, F32),
            pltpu.VMEM(out.shape, BF16),
            pltpu.VMEM((3, batch, 2, HALF, height), BF16),
            pltpu.VMEM((HEADS, TILES, BLK, BLK), F32),
            dma((2,)),
            dma((units,)),
            dma((3, batch)),
            pltpu.VMEM((3, width, HALF), BF16),
            pltpu.VMEM((batch - 1, width, height), BF16),
            dma((3,)),
            dma((batch - 1,)),
            dma((batch - 1,)),
            pltpu.VMEM((2, OUTER, 3 * DH, BLK), BF16),
            pltpu.VMEM((2, n - 1, OUTER, 2 * DH, BLK), BF16),
            dma((2, n)),
            pltpu.VMEM((units, OUTER, DH, BLK), BF16),
            pltpu.VMEM((n - 1, x_slots, OUTER, 2 * DH, BLK), BF16),
            pltpu.VMEM((n - 1, X_LAND, OUTER, 2 * DH, BLK), BF16),
            pltpu.VMEM((z_slots, 2, 3 * DH, BLK), BF16),
            pltpu.VMEM((2, OUTER, 3 * DH, BLK), F32),
            pltpu.VMEM((nk, BLK, QAUG), BF16),
            pltpu.VMEM((nk, DH, BLK), BF16),
            pltpu.VMEM((nk, BLK, AUG), BF16),
            pltpu.VMEM((3, OUTER, QAUG, BLK), BF16),
            pltpu.VMEM((OUTER, AUG, BLK), BF16),
            pltpu.VMEM((nk, DH, BLK), F32),
            pltpu.VMEM((nk, DH, BLK), F32),
            dma((units, OUTER - 1)),
            dma((units, OUTER - 1)),
            dma((n - 1, units)),
            dma((n - 1, units)),
            dma((units, 2, 3)),
            dma((units, 2, 3)),
        ]
        + early_scatter(early).scratch(),
        compiler_params=pltpu.CompilerParams(
            vmem_limit_bytes=VMEM_BYTES, collective_id=1, has_side_effects=True
        ),
        cost_estimate=pl.CostEstimate(flops=110 * 10**9, bytes_accessed=24 << 20, transcendentals=0),
        name="attention_backward",
    )(lengths, far, lse, tiles, own, pair, out, dout, *weights, *projections)


FF_STEP = 512


def middle_kernel(
    x_in, att_in, cot_in, gain_ref, w_out, w_gate, w_up, w_down,
    result_out, mixed_out, dout_out, d_gain, d_out, d_gate, d_up, d_down,
    x_ref, att_ref, cot_ref, result, grad_mixed, dout,
    wo, wg, wu, wd, att, low, hidden, g_gate, g_up, s_out, s_gate, s_up, s_down, kept, in_sem, out_sem,
):
    tokens, width = x_ref.shape
    batch = att_ref.shape[0]
    ff = w_gate.shape[1]
    pairs = ((w_out, wo), (w_gate, wg), (w_up, wu), (w_down, wd), (att_in, att_ref), (x_in, x_ref), (cot_in, cot_ref))
    loads = [pltpu.make_async_copy(src, dst, in_sem.at[i]) for i, (src, dst) in enumerate(pairs)]
    pairs = ((s_out, d_out), (s_gate, d_gate), (s_up, d_up), (s_down, d_down))
    pairs += ((result, result_out), (grad_mixed, mixed_out), (dout, dout_out))
    stores = [pltpu.make_async_copy(src, dst, out_sem.at[i]) for i, (src, dst) in enumerate(pairs)]
    loads = loads[4:5] + loads[:1] + loads[5:] + loads[1:4]
    for c in loads:
        c.start()
    height = tokens // batch
    loads[0].wait()
    for b in range(batch):
        att[b * height : (b + 1) * height] = att_ref[b].T
    for c in loads[1:4]:
        c.wait()
    low[...] = cot_ref[...].astype(BF16)
    mixed = x_ref[...] + jnp.dot(att[...], wo[...], preferred_element_type=F32)
    kept[...] = mixed
    result[...] = mixed
    scale = lax.rsqrt(jnp.mean(mixed * mixed, axis=-1, keepdims=True) + epsilon)
    normed = (mixed * scale * gain_ref[...].reshape(1, -1)).astype(BF16)
    att[...] = normed
    for c in loads[4:]:
        c.wait()
    root = 0.7978845608028654
    for at in range(0, ff, FF_STEP):
        part = slice(at, at + FF_STEP)
        gate = jnp.dot(att[...], wg[:, part], preferred_element_type=F32)
        upward = jnp.dot(att[...], wu[:, part], preferred_element_type=F32)
        g_hidden = lax.dot_general(low[...], wd[part], NT, preferred_element_type=F32)
        square = gate * gate
        t = jnp.tanh(root * gate * (1.0 + 0.044715 * square))
        half = 0.5 * (1.0 + t)
        act = gate * half
        slope = half + 0.5 * gate * (1.0 - t * t) * (root * (1.0 + 3.0 * 0.044715 * square))
        hidden[:, part] = (act * upward).astype(BF16)
        g_gate[:, part] = (g_hidden * upward * slope).astype(BF16)
        g_up[:, part] = (g_hidden * act).astype(BF16)
    result[...] += jnp.dot(hidden[...], wd[...], preferred_element_type=F32)
    stores[4].start()
    d_normed = lax.dot_general(g_gate[...], wg[...], NT, preferred_element_type=F32)
    d_normed = d_normed + lax.dot_general(g_up[...], wu[...], NT, preferred_element_type=F32)
    mixed = kept[...]
    scale = lax.rsqrt(jnp.mean(mixed * mixed, axis=-1, keepdims=True) + epsilon)
    d_gain[...] = jnp.sum(d_normed * mixed * scale, axis=0, keepdims=True)
    u = d_normed * gain_ref[...].reshape(1, -1)
    along = jnp.mean(u * mixed, axis=-1, keepdims=True)
    d_mixed = cot_ref[...] + scale * (u - mixed * (scale * scale * along))
    grad_mixed[...] = d_mixed
    stores[5].start()
    d_low = d_mixed.astype(BF16)
    turned = lax.dot_general(wo[...], d_low, NT, preferred_element_type=F32).astype(BF16)
    for b in range(batch):
        dout[b] = turned[:, b * height : (b + 1) * height]
    stores[6].start()
    total = jnp.zeros((width, width), F32)
    for b in range(batch):
        total = total + jnp.dot(att_ref[b], d_low[b * height : (b + 1) * height], preferred_element_type=F32)
    s_out[...] = total.astype(BF16)
    stores[0].start()
    normed_t = att[...].T
    for src, dst, store in ((g_gate, s_gate, stores[1]), (g_up, s_up, stores[2])):
        for at in range(0, ff, FF_STEP):
            part = slice(at, at + FF_STEP)
            dst[:, part] = jnp.dot(normed_t, src[:, part], preferred_element_type=F32).astype(BF16)
        store.start()
    for at in range(0, ff, FF_STEP):
        part = slice(at, at + FF_STEP)
        s_down[part] = jnp.dot(hidden[:, part].T, low[...], preferred_element_type=F32).astype(BF16)
    stores[3].start()
    for c in stores:
        c.wait()


def middle(inputs, att, cotangent, gain, w_out, w_gate, w_up, w_down):
    batch, height, width = inputs.shape
    tokens, ff = batch * height, w_gate.shape[1]
    weights = (w_out, w_gate, w_up, w_down)
    flat = (tokens, width)
    out = pl.pallas_call(
        middle_kernel,
        in_specs=[anywhere()] * 3 + [whole()] + [anywhere()] * 4,
        out_specs=[anywhere()] * 3 + [whole()] + [anywhere()] * 4,
        out_shape=[
            jax.ShapeDtypeStruct(flat, F32),
            jax.ShapeDtypeStruct(flat, F32),
            jax.ShapeDtypeStruct((batch, width, height), BF16),
            jax.ShapeDtypeStruct((1, width), F32),
        ]
        + [jax.ShapeDtypeStruct(w.shape, BF16) for w in weights],
        scratch_shapes=[
            pltpu.VMEM(flat, F32),
            pltpu.VMEM(att.shape, BF16),
            pltpu.VMEM(flat, F32),
            pltpu.VMEM(flat, F32),
            pltpu.VMEM(flat, F32),
            pltpu.VMEM(att.shape, BF16),
        ]
        + [pltpu.VMEM(w.shape, BF16) for w in weights]
        + [pltpu.VMEM(flat, BF16)] * 2
        + [pltpu.VMEM((tokens, ff), BF16)] * 3
        + [pltpu.VMEM(w.shape, BF16) for w in weights]
        + [pltpu.VMEM(flat, F32)]
        + [pltpu.SemaphoreType.DMA((7,))] * 2,
        compiler_params=params(),
        cost_estimate=pl.CostEstimate(flops=25 * 10**9, bytes_accessed=32 << 20, transcendentals=0),
        name="middle",
    )(inputs.reshape(flat), att, cotangent.reshape(flat), gain, *weights)
    return out[0].reshape(inputs.shape), out[1].reshape(inputs.shape), out[2], out[3], out[4:]


def shards(
    places,
    inputs,
    lengths,
    norm_attn,
    w_query,
    w_key,
    w_value,
    w_out,
    norm_ffn,
    w_gate,
    w_up,
    w_down,
    bucket_bias,
    cotangent,
):
    batch, height, width = inputs.shape
    n = places.inner
    onehot = jnp.asarray(ONEHOT)
    normed_t, own, pair, attended_t, out, lse, tiles, far = attention_forward(
        n, lengths, bucket_bias.T, onehot, inputs, norm_attn, w_query, w_key, w_value
    )
    result, grad_mixed, grad_attended_t, grad_norm_ffn, weights = middle(
        inputs, attended_t, cotangent, norm_ffn, w_out, w_gate, w_up, w_down
    )
    early = Rows(places, [g.shape for g in weights], LANES, 4)
    projections = (w_query, w_key, w_value)
    grads, near, far_sum, parts, other, leaving = attention_backward(
        n, early, lengths, far, tiles, own, pair, out, lse, grad_attended_t, weights, projections
    )
    late = Rows(places, [(width, HALF)] * 3, LANE, 2)
    loaded = (
        parts, grads, normed_t, *projections, inputs, grad_mixed, near, far_sum, onehot, other, leaving
    )
    grad_inputs, full_early, full_late, small = last_grads(early, late, loaded, norm_attn, grad_norm_ffn)
    (part_out, part_gate, part_up, part_down, part_query, part_key, part_value, part_attn, part_ffn, part_table,
     grad_inputs) = unpack(early, late, full_early, full_late, small, grad_inputs)
    return (
        result,
        grad_inputs,
        part_attn.reshape(-1),
        part_ffn.reshape(-1),
        part_query,
        part_key,
        part_value,
        part_out,
        part_gate,
        part_up,
        part_down,
        part_table,
    )


def solution(mesh):
    rows = P("dp", "seq", None)
    share = P("dp", None)
    return jax.shard_map(
        functools.partial(shards, Places(mesh)),
        mesh=mesh,
        in_specs=(rows, P("dp")) + (P(),) * 10 + (rows,),
        out_specs=(rows, rows, P("dp"), P("dp")) + (share,) * 8,
        check_vma=False,
    )
```

```python
import functools

import jax
import jax.numpy as jnp
import numpy as np
from jax import lax
from jax.experimental import pallas as pl
from jax.experimental.pallas import tpu as pltpu
from jax.sharding import PartitionSpec as P

H = 12
DH = 64
NB = 32
OUTER = 4
HEADS = H // OUTER
HW = HEADS * DH
HALF = 2 * HW
BLK = 256
AUG = DH + 16
QAUG = 2 * DH + 16
SPAN = 4 * BLK
LANES = 256
LANE = 128
LOG2E = 1.4426950408889634
F32 = jnp.float32
BF16 = jnp.bfloat16
NT = (((1,), (1,)), ((), ()))
VMEM_BYTES = 62 << 20
GROUP = 8
TILES = 4

epsilon = 1e-06
limits = (1, 2, 3, 4, 5, 6, 7, 8, 12, 16, 23, 32, 46, 64, 91)
highest = lax.Precision.HIGHEST


def bucket_lines():
    relative = 2 * BLK - 1 - np.arange(SPAN)
    count = sum((np.abs(relative) >= limit).astype(np.int32) for limit in limits)
    bucket = count + (relative > 0).astype(np.int32) * (NB // 2)
    return (bucket[None, :] == np.arange(NB)[:, None]).astype(np.float32)


ONEHOT = bucket_lines()


def params():
    return pltpu.CompilerParams(vmem_limit_bytes=VMEM_BYTES)


def smem():
    return pl.BlockSpec(memory_space=pltpu.SMEM)


def anywhere():
    return pl.BlockSpec(memory_space=pl.ANY)


def whole():
    return pl.BlockSpec(memory_space=pltpu.VMEM)


def split3(v):
    a = v.astype(BF16)
    r = v - a.astype(F32)
    b = r.astype(BF16)
    c = (r - b.astype(F32)).astype(BF16)
    return a.astype(F32), b.astype(F32), c.astype(F32)


def tail(width, values):
    row = lax.broadcasted_iota(jnp.int32, (16, width), 0)
    out = jnp.zeros((16, width), F32)
    for i, v in enumerate(values):
        out = jnp.where(row == i, v, out)
    return out


def peers(n, z, x):
    return [lax.rem(z + d, OUTER) * n + x for d in range(1, OUTER)] + [z * n + lax.rem(x + s, n) for s in range(1, n)]


def around(z):
    near = z + 1 - 2 * lax.rem(z, 2)
    return near, lax.rem(z + 2, OUTER), lax.rem(near + 2, OUTER)


class Places:
    def __init__(self, mesh):
        self.dp = mesh.shape["dp"]
        self.groups = self.dp // 2
        self.inner = mesh.shape["seq"] // OUTER


def remote(src, dst, sems, **peer):
    return pltpu.make_async_remote_copy(
        src_ref=src,
        dst_ref=dst,
        send_sem=sems[0],
        recv_sem=sems[1],
        device_id=peer,
        device_id_type=pl.DeviceIdType.MESH,
    )


class Rows:
    def __init__(self, places, shapes, lanes, lines):
        self.p = places
        self.shapes = shapes
        self.lanes = lanes
        self.lines = range(lines)
        grain = places.inner * OUTER * 16
        self.blocks = []
        at = 0
        for m, (rows, columns) in enumerate(shapes):
            share = rows // places.dp
            for block in range(columns // lanes):
                self.blocks.append((m, block, at, share))
                at += share
        self.used = at
        grains = max(-(-at // grain), lines)
        self.total = grains * grain
        cuts = [grains * line // lines * grain for line in range(lines + 1)]
        self.start = cuts[:-1]
        self.span = [b - a for a, b in zip(cuts[:-1], cuts[1:])]
        self.size = [v // places.inner for v in self.span]
        self.small = [v // OUTER for v in self.size]
        self.part_start = [v // places.inner for v in self.start]
        self.part_total = self.total // places.inner

    def line(self, line):
        return pl.ds(self.start[line], self.span[line])

    def part(self, line, x):
        return pl.ds(pl.multiple_of(self.start[line] + x * self.size[line], 16), self.size[line])

    def quarter(self, line, x, z):
        first = self.start[line] + x * self.size[line] + z * self.small[line]
        return pl.ds(pl.multiple_of(first, 16), self.small[line])


def add_to(ref, arrived):
    if len(arrived) == 1:
        ref[...] = ref[...] + arrived[0]
        return
    total = ref[...].astype(F32)
    for a in arrived:
        total = total + a.astype(F32)
    ref[...] = total.astype(BF16)


class Scatter:
    def __init__(self, rows, y_first):
        self.rows = rows
        self.y_first = y_first
        self.count = 5 + 2 * len(rows.lines)

    def scratch(self):
        r, p, dma = self.rows, self.rows.p, pltpu.SemaphoreType.DMA
        g, n, lines = p.groups, p.inner, len(r.lines)
        out = [pltpu.VMEM((g, r.total, r.lanes), BF16), pltpu.VMEM((g, r.total, r.lanes), BF16)]
        for line, y_first in enumerate(self.y_first):
            out.append(pltpu.VMEM((g - 1, r.span[line] if y_first else r.size[line], r.lanes), BF16))
            out.append(pltpu.VMEM((n - 1, 1 if y_first else g, r.size[line], r.lanes), BF16))
        return out + [dma((len(r.blocks), g, 3)), dma((lines, g - 1, 2)), dma((lines, n - 1, g, 2))]

    def bind(self, grads, refs):
        self.grads = grads
        self.held, self.land = refs[:2]
        self.c_sem, self.y_sem, self.x_sem = refs[-3:]
        self.y_land, self.x_land = refs[2:-3:2], refs[3:-3:2]
        dp, seq = lax.axis_index("dp"), lax.axis_index("seq")
        n = self.rows.p.inner
        self.core, self.group = lax.rem(dp, 2), lax.div(dp, 2)
        self.z, self.x = lax.div(seq, n), lax.rem(seq, n)

    def source(self, i, g, core):
        m, block, at, share = self.rows.blocks[i]
        first = pl.multiple_of((g * 2 + core) * share, 16)
        return self.grads[m].at[pl.ds(first, share), pl.ds(block * self.rows.lanes, self.rows.lanes)], pl.ds(at, share)

    def picked(self, chosen):
        return [i for i, b in enumerate(self.rows.blocks) if chosen is None or b[0] in chosen]

    def core_copies(self, chosen=None):
        for i in self.picked(chosen):
            for g in range(self.rows.p.groups):
                src, where = self.source(i, g, 1 - self.core)
                sems = self.c_sem.at[i, g, 0], self.c_sem.at[i, g, 1]
                yield remote(src, self.land.at[g, where], sems, dp=self.group * 2 + 1 - self.core)

    def own_copies(self, chosen=None):
        for i in self.picked(chosen):
            for g in range(self.rows.p.groups):
                src, where = self.source(i, g, self.core)
                yield pltpu.make_async_copy(src, self.held.at[g, where], self.c_sem.at[i, g, 2])

    def y_copies(self, line):
        r = self.rows
        for t in range(1, r.p.groups):
            other = lax.rem(self.group + t, r.p.groups)
            where = r.line(line) if self.y_first[line] else r.part(line, self.x)
            sems = self.y_sem.at[line, t - 1, 0], self.y_sem.at[line, t - 1, 1]
            yield remote(self.held.at[other, where], self.y_land[line].at[t - 1], sems, dp=other * 2 + self.core)

    def x_copies(self, line):
        r = self.rows
        n = r.p.inner
        for s in range(1, n):
            other = lax.rem(self.x + s, n)
            where = r.part(line, other)
            for g in range(1 if self.y_first[line] else r.p.groups):
                sems = self.x_sem.at[line, s - 1, g, 0], self.x_sem.at[line, s - 1, g, 1]
                src = self.held.at[self.group if self.y_first[line] else g, where]
                yield remote(src, self.x_land[line].at[s - 1, g], sems, seq=self.z * n + other)

    def hop(self, line, which):
        return self.y_copies(line) if (which == 0) == self.y_first[line] else self.x_copies(line)


    def step_core(self, chosen=None):
        for c in self.core_copies(chosen):
            c.start()
        for c in self.own_copies(chosen):
            c.start()

    def step_first(self, begin):
        r = self.rows
        for c in self.core_copies():
            c.wait_recv()
        for c in self.own_copies():
            c.wait()
        for line in r.lines:
            end = r.start[line] + r.span[line]
            first, last = r.start[line], min(end, r.used)
            for g in range(r.p.groups):
                where = pl.ds(first, last - first)
                add_to(self.held.at[g, where], [self.land[g, where]])
                if last < end:
                    self.held[g, last:end] = jnp.zeros((end - last, r.lanes), BF16)
            if line in begin:
                self.start_first(line)

    def start_first(self, line):
        for c in self.hop(line, 0):
            c.start()

    def step_second(self, line):
        r = self.rows
        for c in self.hop(line, 0):
            c.wait_recv()
        if self.y_first[line]:
            arrived = [self.y_land[line][t] for t in range(r.p.groups - 1)]
            add_to(self.held.at[self.group, r.line(line)], arrived)
        else:
            for g in range(r.p.groups):
                arrived = [self.x_land[line][s, g] for s in range(r.p.inner - 1)]
                add_to(self.held.at[g, r.part(line, self.x)], arrived)
        for c in self.hop(line, 1):
            c.start()

    def step_third(self, line):
        r = self.rows
        for c in self.hop(line, 1):
            c.wait_recv()
        if self.y_first[line]:
            arrived = [self.x_land[line][s, 0] for s in range(r.p.inner - 1)]
        else:
            arrived = [self.y_land[line][t] for t in range(r.p.groups - 1)]
        add_to(self.held.at[self.group, r.part(line, self.x)], arrived)

    def part(self, line):
        return self.held.at[self.group, self.rows.part(line, self.x)]

    def end(self):
        for c in self.core_copies():
            c.wait_send()
        for line in self.rows.lines:
            for which in range(2):
                for c in self.hop(line, which):
                    c.wait_send()


class Spread:
    def __init__(self, rows, halves=False):
        self.rows = rows
        self.halves = halves

    def scratch(self):
        r, dma = self.rows, pltpu.SemaphoreType.DMA
        lines = len(r.lines)
        land = (lines, 1, max(r.size) // 2, r.lanes) if self.halves else (lines, 3, max(r.small), r.lanes)
        sems = dma((lines, 3, 2))
        return [pltpu.VMEM(land, BF16), sems, sems, dma((lines, OUTER, r.p.inner - 1, 2))]

    count = 4

    def bind(self, piece, target, refs):
        self.piece, self.target = piece, target
        self.land, self.s_sem, self.g_sem, self.x_sem = refs
        seq = lax.axis_index("seq")
        n = self.rows.p.inner
        self.z, self.x = lax.div(seq, n), lax.rem(seq, n)
        self.near, self.two, self.across = around(self.z)

    def copy(self, src, dst, sems, group):
        return remote(src, dst, sems, seq=group * self.rows.p.inner + self.x)

    def sum_copy(self, line, i):
        piece = self.piece(line, (self.near, self.across, self.two)[i])
        sems = self.s_sem.at[line, i, 0], self.s_sem.at[line, i, 1]
        return self.copy(piece, self.landing(line, i), sems, self.two if i == 2 else self.near)

    def landing(self, line, i):
        rows = self.rows.size[line] // 2 if self.halves else self.rows.small[line]
        return self.land.at[line, i, pl.ds(0, rows)]

    def sums(self, line):
        return [self.sum_copy(line, i) for i in range(1 if self.halves else 3)]

    def z_copy(self, line, i):
        where = self.target(line, self.two if i == 2 else self.z)
        sems = self.g_sem.at[line, i, 0], self.g_sem.at[line, i, 1]
        return self.copy(where, where, sems, self.two if i == 0 else self.near)

    def x_copies(self, line, c):
        n = self.rows.p.inner
        where = self.target(line, c)
        for s in range(1, n):
            sems = self.x_sem.at[line, c, s - 1, 0], self.x_sem.at[line, c, s - 1, 1]
            yield remote(where, where, sems, seq=self.z * n + lax.rem(self.x + s, n))

    def spread(self, line, c):
        for s in self.x_copies(line, c):
            s.start()

    def step_pair(self, line):
        self.sum_copy(line, 0).start()
        if not self.halves:
            self.sum_copy(line, 1).start()

    def step_two(self, line):
        for i, c in ((0, self.z), (1, self.two)):
            self.sum_copy(line, i).wait_recv()
            add_to(self.piece(line, c), [self.landing(line, i)[...]])
        self.sum_copy(line, 2).start()

    def step_back(self, line):
        last = 0 if self.halves else 2
        self.sum_copy(line, last).wait_recv()
        self.target(line, self.z)[...] = self.piece(line, self.z)[...] + self.landing(line, last)[...]
        self.z_copy(line, 0).start()
        self.z_copy(line, 1).start()
        self.spread(line, self.z)

    def step_rest(self, line):
        self.z_copy(line, 0).wait_recv()
        self.z_copy(line, 2).start()
        self.spread(line, self.two)
        self.z_copy(line, 1).wait_recv()
        self.spread(line, self.near)

    def step_last(self, line):
        self.z_copy(line, 2).wait_recv()
        self.spread(line, self.across)

    def end(self):
        for line in self.rows.lines:
            for c in range(OUTER):
                for s in self.x_copies(line, c):
                    s.wait_send()
                    s.wait_recv()
            for c in self.sums(line):
                c.wait_send()
            for i in range(3):
                self.z_copy(line, i).wait_send()


class Total:
    def __init__(self, places, rows):
        self.p = places
        self.rows = rows
        self.peers = [1, places.groups - 1, places.inner - 1, 1, 1]
        self.hops = range(5)
        self.count = 8

    def scratch(self):
        dma = pltpu.SemaphoreType.DMA
        out = [pltpu.VMEM((len(self.hops) + 1, self.rows, LANE), F32)]
        out += [pltpu.VMEM((k, self.rows, LANE), F32) for k in self.peers]
        return out + [dma((len(self.hops), max(self.peers))) for _ in range(2)]

    def bind(self, refs):
        self.held, self.land, self.sems = refs[0], refs[1:6], refs[6:]
        dp, seq = lax.axis_index("dp"), lax.axis_index("seq")
        n, groups = self.p.inner, self.p.groups
        core, group, z, x = lax.rem(dp, 2), lax.div(dp, 2), lax.div(seq, n), lax.rem(seq, n)
        near, two, _ = around(z)
        self.targets = [
            [{"dp": group * 2 + 1 - core}],
            [{"dp": lax.rem(group + t, groups) * 2 + core} for t in range(1, groups)],
            [{"seq": z * n + lax.rem(x + s, n)} for s in range(1, n)],
            [{"seq": near * n + x}],
            [{"seq": two * n + x}],
        ]

    def copies(self, hop):
        for i, target in enumerate(self.targets[hop]):
            yield remote(self.held.at[hop], self.land[hop].at[i], (self.sems[0].at[hop, i], self.sems[1].at[hop, i]), **target)

    def send(self, hop):
        for c in self.copies(hop):
            c.start()

    def step(self, hop):
        for c in self.copies(hop):
            c.wait_recv()
        total = self.held[hop]
        for i in range(self.peers[hop]):
            total = total + self.land[hop][i]
        self.held[hop + 1] = total
        if hop + 1 < len(self.hops):
            self.send(hop + 1)

    def end(self):
        for hop in self.hops:
            for c in self.copies(hop):
                c.wait_send()


def greet_all(places):
    dp, seq = lax.axis_index("dp"), lax.axis_index("seq")
    n = places.inner
    core, group = lax.rem(dp, 2), lax.div(dp, 2)
    barrier = pltpu.get_barrier_semaphore()
    mesh = pl.DeviceIdType.MESH
    pl.semaphore_signal(barrier, inc=1, device_id={"dp": group * 2 + 1 - core}, device_id_type=mesh)
    for t in range(1, places.groups):
        other = lax.rem(group + t, places.groups) * 2 + core
        pl.semaphore_signal(barrier, inc=1, device_id={"dp": other}, device_id_type=mesh)
    for peer in peers(n, lax.div(seq, n), lax.rem(seq, n)):
        pl.semaphore_signal(barrier, inc=1, device_id={"seq": peer}, device_id_type=mesh)
    pl.semaphore_wait(barrier, 1 + places.groups - 1 + OUTER - 1 + n - 1)


SMALL = 16


def last_kernel(early, late, *refs):
    count = 13
    sources, (gain_ref, ffn_ref), refs = refs[:count], refs[count : count + 2], refs[count + 2 :]
    grad_out, full_early, full_late, small_out, refs = refs[0], refs[1], refs[2], refs[3], refs[4:]
    slots, load_sem, refs = refs[:count], refs[count], refs[count + 1 :]
    p = late.p
    scatter, spread_early, spread_late = Scatter(late, (True, False)), Spread(early), Spread(late, True)
    (gq, gk, gv, arriving, n_sem, grad_in, out_sem), refs = refs[:7], refs[7:]
    scatter.bind((gq, gk, gv), refs[: scatter.count])
    refs = refs[scatter.count :]
    z, x = scatter.z, scatter.x
    columns = half_columns(z)
    loads = []
    for i, (src, dst) in enumerate(zip(sources, slots)):
        loads.append(pltpu.make_async_copy(src.at[:, columns] if 3 <= i < 6 else src, dst, load_sem.at[i]))
    for c in loads:
        c.start()
    held, grads, normed_t, wq_ref, wk_ref, wv_ref, x_ref, mixed_ref, near, far_sum, onehot, other, leaving = slots

    def early_piece(line, c):
        first = pl.multiple_of(early.part_start[line] + c * early.small[line], 16)
        return held.at[pl.ds(first, early.small[line])]

    def late_rows(line, c):
        size = late.size[line] // 2
        first = late.start[line] + x * late.size[line] + lax.rem(c, 2) * size
        return pl.ds(pl.multiple_of(first, 16), size)

    spread_early.bind(early_piece, lambda line, c: full_early.at[early.quarter(line, x, c)], refs[: Spread.count])
    spread_late.bind(
        lambda line, c: scatter.held.at[scatter.group, late_rows(line, c)],
        lambda line, c: full_late.at[lax.div(c, 2), late_rows(line, c)],
        refs[Spread.count : 2 * Spread.count],
    )
    total_small = Total(p, p.dp * SMALL)
    total_small.bind(refs[2 * Spread.count :])
    two = spread_early.two
    n_copy = remote(leaving, arriving, (n_sem.at[0], n_sem.at[1]), seq=two * p.inner + x)
    greet_all(p)
    loads[0].wait()
    loads[-1].wait()
    n_copy.start()
    early_lines, late_lines = list(early.lines), list(late.lines)
    for line in early_lines:
        spread_early.step_pair(line)
    for c in loads[1:-1]:
        c.wait()
    batch, height, width = x_ref.shape

    def weight(i, out):
        total = jnp.zeros((width, HALF), F32)
        for b in range(batch):
            for block in range(2):
                total = total + lax.dot_general(normed_t[block, b], grads[i, b, block], NT, preferred_element_type=F32)
        out[...] = total.astype(BF16)
        scatter.step_core((i,))

    for i, out in enumerate((gq, gk, gv)):
        weight(i, out)
    spread_early.step_two(0)
    scatter.step_first(late.lines)
    spread_early.step_two(1)
    gain = gain_ref[...].reshape(1, -1)
    gain_sums = []

    leaves = [pltpu.make_async_copy(grad_in.at[b], grad_out.at[b], out_sem.at[b]) for b in range(batch)]

    def positions(b, arrived):
        back = jnp.dot(wq_ref[...], grads[0, b, 0], preferred_element_type=F32)
        back = back + jnp.dot(wk_ref[...], grads[1, b, 0], preferred_element_type=F32)
        back = back + jnp.dot(wv_ref[...], grads[2, b, 0], preferred_element_type=F32)
        back = (back + arrived[...].astype(F32)).T
        values = x_ref[b]
        scale = lax.rsqrt(jnp.mean(values * values, axis=-1, keepdims=True) + epsilon)
        gain_sums.append(jnp.sum(back * values * scale, axis=0, keepdims=True))
        u = back * gain
        along = jnp.mean(u * values, axis=-1, keepdims=True)
        grad_in[b] = mixed_ref[b] + scale * (u - values * (scale * scale * along))
        leaves[b].start()

    positions(0, other.at[0])
    spread_early.step_back(0)
    spread_early.step_two(2)
    for line in late_lines:
        scatter.step_second(line)
    for b in range(1, batch - 1):
        positions(b, other.at[b])
    spread_early.step_back(1)
    spread_early.step_two(3)
    for line in late_lines:
        scatter.step_third(line)
        spread_late.step_pair(line)
    n_copy.wait_recv()
    positions(batch - 1, arriving)
    gain_sum = sum(gain_sums)
    spread_early.step_rest(0)
    spread_early.step_back(2)
    for line in late_lines:
        spread_late.step_back(line)
    row = lax.broadcasted_iota(jnp.int32, (BLK, BLK), 0)
    col = lax.broadcasted_iota(jnp.int32, (BLK, BLK), 1)
    flip = (row + col == BLK - 1).astype(F32)
    bucket = lax.broadcasted_iota(jnp.int32, (NB, 1), 0)
    head_lane = lax.broadcasted_iota(jnp.int32, (NB, LANE), 1)
    table = jnp.zeros((NB, LANE), F32)
    for h in range(HEADS):
        line = jnp.zeros((1, SPAN), F32)
        for off in (-1, 0, 1):
            flipped = jnp.dot(flip, near[h, off + 2], preferred_element_type=F32, precision=highest)
            padded = jnp.concatenate([flipped, jnp.zeros((BLK, SPAN - BLK), F32)], axis=1)
            rolled = pltpu.roll(padded, (BLK - off * BLK) % SPAN, 1, stride=1, stride_axis=0)
            line = line + jnp.sum(rolled, axis=0, keepdims=True)
        column = jnp.sum(onehot[...] * line, axis=1, keepdims=True)
        sides = jnp.sum(far_sum[h], axis=1, keepdims=True)
        column = column + jnp.where(bucket == NB // 2 - 1, sides[0:1], 0.0) + jnp.where(bucket == NB - 1, sides[1:2], 0.0)
        table = jnp.where(head_lane == z * HEADS + h, column, table)
    share, buckets = width // p.dp, NB // p.dp
    for i in range(p.dp):
        block = []
        for v in (gain_sum, ffn_ref[...]):
            for first, last in gain_rows(share):
                v_row = v[:, i * share + first : i * share + last]
                if last - first < LANE:
                    v_row = jnp.concatenate([v_row, jnp.zeros((1, LANE - (last - first)), F32)], axis=1)
                block.append(v_row)
        block.append(table[i * buckets : (i + 1) * buckets])
        block.append(jnp.zeros((SMALL - 2 * len(gain_rows(share)) - buckets, LANE), F32))
        total_small.held[0, i * SMALL : (i + 1) * SMALL] = jnp.concatenate(block, axis=0)
    total_small.send(0)
    spread_early.step_rest(1)
    spread_early.step_back(3)
    spread_early.step_last(0)
    total_small.step(0)
    for line in late_lines:
        spread_late.step_rest(line)
    spread_early.step_rest(2)
    spread_early.step_last(1)
    total_small.step(1)
    for line in late_lines:
        spread_late.step_last(line)
    spread_early.step_rest(3)
    total_small.step(2)
    spread_early.step_last(2)
    total_small.step(3)
    spread_early.step_last(3)
    total_small.step(4)
    mine = pl.ds(pl.multiple_of(lax.axis_index("dp") * SMALL, SMALL), SMALL)
    small_out[...] = total_small.held[len(total_small.hops), mine]
    total_small.end()
    n_copy.wait_send()
    for c in leaves:
        c.wait()
    spread_early.end()
    spread_late.end()
    scatter.end()


def gain_rows(share):
    return [(at, min(at + LANE, share)) for at in range(0, share, LANE)]


def half_columns(z):
    return pl.ds(pl.multiple_of(lax.div(z, 2) * HALF, LANE), HALF)


def last_grads(early, late, loaded, gain, ffn):
    inputs = loaded[6]
    width = inputs.shape[-1]
    shapes = [(width, HALF) if 3 <= i < 6 else v.shape for i, v in enumerate(loaded)]
    return pl.pallas_call(
        functools.partial(last_kernel, early, late),
        in_specs=[anywhere()] * len(loaded) + [whole()] * 2,
        out_specs=[anywhere()] + [whole()] * 3,
        out_shape=[
            jax.ShapeDtypeStruct(inputs.shape, F32),
            jax.ShapeDtypeStruct((early.total, early.lanes), BF16),
            jax.ShapeDtypeStruct((2, late.total, late.lanes), BF16),
            jax.ShapeDtypeStruct((SMALL, LANE), F32),
        ],
        scratch_shapes=[pltpu.VMEM(shape, v.dtype) for shape, v in zip(shapes, loaded)]
        + [pltpu.SemaphoreType.DMA((len(loaded),))]
        + [pltpu.VMEM((width, HALF), BF16)] * 3
        + [pltpu.VMEM(loaded[-1].shape, BF16), pltpu.SemaphoreType.DMA((2,))]
        + [pltpu.VMEM(inputs.shape, F32), pltpu.SemaphoreType.DMA((inputs.shape[0],))]
        + Scatter(late, (True, False)).scratch()
        + Spread(early).scratch()
        + Spread(late, True).scratch()
        + Total(late.p, late.p.dp * SMALL).scratch(),
        compiler_params=pltpu.CompilerParams(
            vmem_limit_bytes=VMEM_BYTES, collective_id=2, has_side_effects=True
        ),
        name="last_grads",
    )(*loaded, gain, ffn)


def unpack_kernel(early, late, full_early, full_late, small, grad_in, *refs):
    count = len(early.shapes) + len(late.shapes)
    targets, (d_attn, d_ffn, d_table, grad_out), refs = refs[:count], refs[count : count + 4], refs[count + 4 :]
    outs, (held, taken_early, taken_late, sems) = refs[:count], refs[count:]
    arrive = [
        pltpu.make_async_copy(src, dst, sems.at[i])
        for i, (src, dst) in enumerate(((full_early, taken_early), (full_late, taken_late), (grad_in, held)))
    ]
    leave = [pltpu.make_async_copy(held, grad_out, sems.at[3])]
    leave += [pltpu.make_async_copy(src, dst, sems.at[4 + i]) for i, (src, dst) in enumerate(zip(outs, targets))]
    for c in arrive:
        c.start()
    arrive[0].wait()
    for m in range(len(early.shapes)):
        for i, block, at, share in early.blocks:
            if i == m:
                outs[m][:, block * LANES : (block + 1) * LANES] = taken_early[at : at + share].astype(F32)
        leave[1 + m].start()
    arrive[1].wait()
    for m in range(len(late.shapes)):
        for i, block, at, share in late.blocks:
            for half in range(2):
                first = half * HALF + block * LANE
                if i == m:
                    out = outs[len(early.shapes) + m]
                    out[:, first : first + LANE] = taken_late[half, at : at + share].astype(F32)
        leave[1 + len(early.shapes) + m].start()
    arrive[2].wait()
    leave[0].start()
    at = 0
    for out in (d_attn, d_ffn):
        for begin, end in gain_rows(out.shape[1]):
            out[:, begin:end] = small[at : at + 1, : end - begin]
            at += 1
    buckets, heads = d_table.shape
    d_table[...] = small[at : at + buckets, :heads]
    for c in leave:
        c.wait()


def unpack(early, late, full_early, full_late, small, grad_in):
    width = grad_in.shape[-1]
    dp = early.p.dp
    shapes = [(height // dp, columns) for height, columns in early.shapes] + [(width // dp, width)] * 3
    few = [(1, width // dp)] * 2 + [(NB // dp, H)]
    return pl.pallas_call(
        functools.partial(unpack_kernel, early, late),
        in_specs=[anywhere()] * 2 + [whole(), anywhere()],
        out_specs=[anywhere()] * len(shapes) + [whole()] * len(few) + [anywhere()],
        out_shape=[jax.ShapeDtypeStruct(s, F32) for s in shapes + few + [grad_in.shape]],
        scratch_shapes=[pltpu.VMEM(s, F32) for s in shapes]
        + [
            pltpu.VMEM(grad_in.shape, F32),
            pltpu.VMEM(full_early.shape, BF16),
            pltpu.VMEM(full_late.shape, BF16),
            pltpu.SemaphoreType.DMA((4 + len(shapes),)),
        ],
        compiler_params=params(),
        name="unpack",
    )(full_early, full_late, small, grad_in)


def greet(n, z, x):
    barrier = pltpu.get_barrier_semaphore()
    for peer in peers(n, z, x):
        pl.semaphore_signal(barrier, inc=1, device_id={"seq": peer}, device_id_type=pl.DeviceIdType.MESH)
    pl.semaphore_wait(barrier, OUTER - 1 + n - 1)


def far_case(n, j, kb):
    if kb < n * j - 1:
        return 0
    if kb > n * j + n:
        return 2
    return None


def near_case(n, j, kb, x):
    off = kb - (n * j + x)
    near = jnp.logical_and(off >= -1, off <= 1)
    return jnp.where(near, off + 2, 0), jnp.where(off <= -2, 0, jnp.where(off >= 2, 2, 1))


def key_rows(keys, kb, length):
    one = jnp.ones((1, BLK), F32)
    lane = lax.broadcasted_iota(jnp.int32, (1, BLK), 1)
    mask = jnp.where(kb * BLK + lane < length, 0.0, -1e30)
    return jnp.concatenate([keys, keys, tail(BLK, (one, one, one, mask)).astype(BF16)], axis=0).T


def query_parts(queries):
    scaled = queries.astype(F32) * LOG2E
    high = scaled.astype(BF16)
    return jnp.concatenate([high, (scaled - high.astype(F32)).astype(BF16)], axis=0)


def forward_kernel(
    n, len_ref, table_ref, onehot_ref, x_ref, gain_ref, wq_ref, wk_ref, wv_ref,
    normed_out, own_out, pair_out, att, o_ref, lse_ref, tile_out, far_ref,
    normed_ref, own, pair, tile_ref, keep_sem, tile_sem, here, there, send, ka, qa, va,
    n_send, n_recv, z_send, z_recv, x_send, x_recv, o_send, o_recv,
):
    nk = OUTER * n
    batch = x_ref.shape[0]
    units = batch * HEADS
    me = lax.axis_index("seq")
    z, x = lax.div(me, n), lax.rem(me, n)
    greet(n, z, x)

    near, two, across = around(z)
    groups = (z, two, near, across)
    low = lax.rem(z, 2) == 0
    columns = half_columns(z)

    def n_copy(b):
        return remote(here.at[b], there.at[b], (n_send.at[b], n_recv.at[b]), seq=two * n + x)

    def z_copy(u, i):
        sems = z_send.at[u, i], z_recv.at[u, i]
        return remote(send.at[u, i], own.at[u, groups[i]], sems, seq=near * n + x)

    def x_copy(u, s, i):
        rows = pl.ds(DH, 2 * DH)
        sems = x_send.at[s - 1, u, i], x_recv.at[s - 1, u, i]
        peer = z * n + lax.rem(x + s, n)
        return remote(own.at[u, groups[i], rows], pair.at[s - 1, u, groups[i]], sems, seq=peer)

    def o_copy(u, d):
        group = lax.rem(z + d, OUTER)
        b, h = lax.div(u, HEADS), lax.rem(u, HEADS)
        rows = pl.ds(pl.multiple_of((z * HEADS + h) * DH, DH), DH)
        sems = o_send.at[u, d - 1], o_recv.at[u, d - 1]
        return remote(o_ref.at[u, group], att.at[b, rows], sems, seq=group * n + x)

    for b in range(batch):
        values = x_ref[b]
        scale = lax.rsqrt(jnp.mean(values * values, axis=-1, keepdims=True) + epsilon)
        here[b] = (values * scale * gain_ref[...].reshape(1, -1)).astype(BF16)
        if b == 0:
            n_copy(0).start()

    def project(b, i):
        normed = (here, there)[i][b]
        normed_ref[i, b] = normed.T
        for m, w_ref in enumerate((wq_ref, wk_ref, wv_ref)):
            turned = jnp.dot(normed, w_ref[:, columns], preferred_element_type=F32).T.astype(BF16)
            for h in range(HEADS):
                first, second = turned[h * DH : (h + 1) * DH], turned[HW + h * DH : HW + (h + 1) * DH]
                rows = slice(m * DH, (m + 1) * DH)
                own[b * HEADS + h, groups[i], rows] = jnp.where(low, first, second)
                send[b * HEADS + h, i, rows] = jnp.where(low, second, first)
        for h in range(HEADS):
            for s in range(1, n):
                x_copy(b * HEADS + h, s, i).start()

    def start_near(b, i):
        for h in range(HEADS):
            z_copy(b * HEADS + h, i).start()

    def keep(u):
        yield pltpu.make_async_copy(own.at[u], own_out.at[u], keep_sem.at[u, 0])
        for s in range(1, n):
            yield pltpu.make_async_copy(pair.at[s - 1, u], pair_out.at[s - 1, u], keep_sem.at[u, s])

    keep_normed = pltpu.make_async_copy(normed_ref, normed_out, tile_sem.at[0])
    keep_tiles = pltpu.make_async_copy(tile_ref, tile_out, tile_sem.at[1])
    for b in range(batch):
        project(b, 0)
        if b == 0:
            start_near(0, 0)

    table_lane = lax.broadcasted_iota(jnp.int32, (1, NB), 1)
    for h in range(HEADS):
        chosen = table_ref[pl.ds(z * HEADS + h, 1), :] * LOG2E
        padded = jnp.broadcast_to(chosen, (8, NB))
        line = jnp.dot(padded, onehot_ref[...], preferred_element_type=F32, precision=highest)[0:1]
        line = jnp.broadcast_to(line, (BLK, SPAN))
        tile_ref[h, 0] = jnp.zeros((BLK, BLK), F32)
        for off in (-1, 0, 1):
            shift = (off * BLK - (2 * BLK - 1)) % SPAN
            tile_ref[h, off + 2] = pltpu.roll(line, shift, 1, stride=1, stride_axis=0)[:, :BLK]
        for side, bucket in enumerate((NB // 2 - 1, NB - 1)):
            value = jnp.sum(jnp.where(table_lane == bucket, chosen, 0.0), axis=1, keepdims=True)
            far_ref[h, side] = jnp.broadcast_to(value, (1, BLK))
    keep_tiles.start()

    def attend(u):
        b, h = lax.div(u, HEADS), lax.rem(u, HEADS)
        length = len_ref[b]
        left, right = far_ref[h, 0], far_ref[h, 1]
        one = jnp.ones((1, BLK), F32)
        vtail = tail(BLK, (one,)).astype(BF16)
        for s in range(1, n):
            for i in range(OUTER):
                x_copy(u, s, i).wait_recv()
        for s in range(n):
            col = lax.rem(x + s, n)
            for j in range(OUTER):
                kb = n * j + col
                if s == 0:
                    keys, vals = own[u, j, DH : 2 * DH], own[u, j, 2 * DH :]
                else:
                    keys, vals = pair[n - s - 1, u, j, :DH], pair[n - s - 1, u, j, DH:]
                ka[kb] = key_rows(keys, kb, length)
                columns = pl.ds(pl.multiple_of(kb * BLK, BLK), BLK)
                va[:DH, columns] = vals
                va[DH:, columns] = vtail

        def scores(kb, j):
            case = far_case(n, j, kb)
            if case is not None:
                return jnp.dot(ka[kb], qa[case, j], preferred_element_type=F32)
            tile, case = near_case(n, j, kb, x)
            return jnp.dot(ka[kb], qa[case, j], preferred_element_type=F32) + tile_ref[h, tile]

        for j in range(OUTER):
            both = query_parts(own[u, j, :DH])
            for v, c in enumerate((left, 0.0 * one, right)):
                qa[v, j, : 2 * DH] = both
                qa[v, j, 2 * DH :] = tail(BLK, split3(c) + (one,)).astype(BF16)
        tops = []
        for j in range(OUTER):
            top = jnp.full((8, BLK), -1e30, F32)
            for kb in range(nk):
                top = jnp.maximum(top, jnp.max(scores(kb, j).reshape(BLK // 8, 8, BLK), axis=0))
            top = jnp.max(top, axis=0, keepdims=True)
            tops.append(top)
            for v, c in enumerate((left, 0.0, right)):
                qa[v, j, 2 * DH :] = tail(BLK, split3(c - top) + (one,)).astype(BF16)
        for j in range(OUTER):
            weights = [jnp.exp2(scores(kb, j)).astype(BF16) for kb in range(nk)]
            total = jnp.dot(va[...], jnp.concatenate(weights, axis=0), preferred_element_type=F32)
            weight = total[DH : DH + 1]
            o_ref[u, j] = (total[:DH] / weight).astype(BF16)
            lse_ref[u, j] = tops[j] + jnp.log2(weight)
        for c in keep(u):
            c.start()
        rows = pl.ds(pl.multiple_of((z * HEADS + h) * DH, DH), DH)
        att[b, rows] = o_ref[u, z]
        for d in (2, 1, 3):
            o_copy(u, d).start()

    def turn(u, carry):
        @pl.when(jnp.logical_and(u < units, lax.rem(u, HEADS) == 0))
        def _():
            b = lax.div(u, HEADS)
            n_copy(b).wait_recv()

            @pl.when(b + 1 < batch)
            def _():
                n_copy(b + 1).start()

            project(b, 1)
            start_near(b, 1)

            @pl.when(b + 1 < batch)
            def _():
                start_near(b + 1, 0)

        @pl.when(u < units)
        def _():
            for i in range(2):
                z_copy(u, i).wait_recv()
                for s in range(1, n):
                    x_copy(u, s, 2 + i).start()

        @pl.when(u > 0)
        def _():
            attend(u - 1)

        return carry

    lax.fori_loop(0, units + 1, turn, 0)
    keep_normed.start()

    def finish(u, carry):
        for c in keep(u):
            c.wait()
        for d in range(1, OUTER):
            o_copy(u, d).wait_send()
            o_copy(u, d).wait_recv()
        for i in range(2):
            z_copy(u, i).wait_send()
        for s in range(1, n):
            for i in range(OUTER):
                x_copy(u, s, i).wait_send()
        return carry

    lax.fori_loop(0, units, finish, 0)
    for b in range(batch):
        n_copy(b).wait_send()
    keep_normed.wait()
    keep_tiles.wait()


def attention_forward(n, lengths, table, onehot, inputs, gain, wq, wk, wv):
    batch, height, width = inputs.shape
    units, nk = batch * HEADS, n * OUTER
    dma = pltpu.SemaphoreType.DMA
    return pl.pallas_call(
        functools.partial(forward_kernel, n),
        in_specs=[smem()] + [whole()] * 7,
        out_specs=[anywhere()] * 3 + [whole()] * 3 + [anywhere(), whole()],
        out_shape=[
            jax.ShapeDtypeStruct((2, batch, width, height), BF16),
            jax.ShapeDtypeStruct((units, OUTER, 3 * DH, BLK), BF16),
            jax.ShapeDtypeStruct((n - 1, units, OUTER, 2 * DH, BLK), BF16),
            jax.ShapeDtypeStruct((batch, width, height), BF16),
            jax.ShapeDtypeStruct((units, OUTER, DH, BLK), BF16),
            jax.ShapeDtypeStruct((units, OUTER, 1, BLK), F32),
            jax.ShapeDtypeStruct((HEADS, TILES, BLK, BLK), F32),
            jax.ShapeDtypeStruct((HEADS, 2, 1, BLK), F32),
        ],
        scratch_shapes=[
            pltpu.VMEM((2, batch, width, height), BF16),
            pltpu.VMEM((units, OUTER, 3 * DH, BLK), BF16),
            pltpu.VMEM((n - 1, units, OUTER, 2 * DH, BLK), BF16),
            pltpu.VMEM((HEADS, TILES, BLK, BLK), F32),
            dma((units, n)),
            dma((2,)),
            pltpu.VMEM((batch, height, width), BF16),
            pltpu.VMEM((batch, height, width), BF16),
            pltpu.VMEM((units, 2, 3 * DH, BLK), BF16),
            pltpu.VMEM((nk, BLK, QAUG), BF16),
            pltpu.VMEM((3, OUTER, QAUG, BLK), BF16),
            pltpu.VMEM((AUG, nk * BLK), BF16),
            dma((batch,)),
            dma((batch,)),
            dma((units, 2)),
            dma((units, 2)),
            dma((n - 1, units, OUTER)),
            dma((n - 1, units, OUTER)),
            dma((units, OUTER - 1)),
            dma((units, OUTER - 1)),
        ],
        compiler_params=pltpu.CompilerParams(
            vmem_limit_bytes=VMEM_BYTES, collective_id=0, has_side_effects=True
        ),
        cost_estimate=pl.CostEstimate(flops=45 * 10**9, bytes_accessed=24 << 20, transcendentals=0),
        name="attention_forward",
    )(lengths, table, onehot, inputs, gain, wq, wk, wv)


def early_scatter(early):
    return Scatter(early, (True,) * (len(early.lines) - 1) + (False,))


def backward_kernel(
    n, early, len_ref, far_ref, lse_ref, tile_in, own, pair, o_in, dout, *refs
):
    scatter = early_scatter(early)
    count = len(early.shapes)
    weights, refs = refs[:count], refs[count:]
    projections, refs = refs[:3], refs[3:]
    (grads_out, near_out, far_sum, parts, other, leaving,
    tile_ref, o_ref, grads, near, first_sem, own_sem, keep_sem, w_half, other_out, w_sem, n_send, n_recv, own_slot, pair_slot, load_sem,
    do_land, x_out, x_land, z_out, kept,
    ka, kt, va, qa, da, dk_all, dv_all,
    d_send, d_recv, x_send, x_recv, z_send, z_recv) = refs[: -scatter.count]
    scatter.bind(weights, refs[-scatter.count :])
    nk = OUTER * n
    batch = dout.shape[0]
    units = batch * HEADS
    x_slots, z_slots = staging(n, units)
    me = lax.axis_index("seq")
    z, x = lax.div(me, n), lax.rem(me, n)
    near_z, two, across = around(z)
    low = lax.rem(z, 2) * HW
    greet_all(early.p)
    scatter.step_core()
    firsts = [
        pltpu.make_async_copy(src, dst, first_sem.at[i]) for i, (src, dst) in enumerate(((tile_in, tile_ref), (o_in, o_ref)))
    ]
    for c in firsts:
        c.start()

    def own_part(u):
        b, h = lax.div(u, HEADS), lax.rem(u, HEADS)
        return pltpu.make_async_copy(dout.at[b, head_rows(z, h)], do_land.at[u, z], own_sem.at[u])

    def keep_grads(b):
        return [pltpu.make_async_copy(grads.at[m, b], grads_out.at[m, b], keep_sem.at[m, b]) for m in range(3)]

    columns = half_columns(z)
    w_loads = [pltpu.make_async_copy(w.at[:, columns], w_half.at[m], w_sem.at[m]) for m, w in enumerate(projections)]
    for c in w_loads:
        c.start()

    def head_rows(group, h):
        return pl.ds(pl.multiple_of((group * HEADS + h) * DH, DH), DH)

    def d_copy(u, d):
        group = lax.rem(z + d, OUTER)
        b, h = lax.div(u, HEADS), lax.rem(u, HEADS)
        sems = d_send.at[u, d - 1], d_recv.at[u, d - 1]
        return remote(dout.at[b, head_rows(group, h)], do_land.at[u, z], sems, seq=group * n + x)

    def x_copy(u, s):
        peer = z * n + lax.rem(x + s, n)
        sems = x_send.at[s - 1, u], x_recv.at[s - 1, u]
        return remote(
            x_out.at[s - 1, lax.rem(u, x_slots)], x_land.at[s - 1, lax.rem(u, X_LAND)], sems, seq=peer
        )

    def half_rows(h):
        return pl.ds(pl.multiple_of(low + h * DH, DH), DH)

    def z_copy(u, i, m):
        b, h = lax.div(u, HEADS), lax.rem(u, HEADS)
        sems = z_send.at[u, i, m], z_recv.at[u, i, m]
        src, dst = z_out.at[lax.rem(u, z_slots), i, pl.ds(m * DH, DH)], grads.at[m, b, i, half_rows(h)]
        return remote(src, dst, sems, seq=near_z * n + x)

    def n_copy(b):
        return remote(other_out.at[b], other.at[b], (n_send.at[b], n_recv.at[b]), seq=two * n + x)

    def loads(u):
        slot = lax.rem(u, 2)
        yield pltpu.make_async_copy(own.at[u], own_slot.at[slot], load_sem.at[slot, 0])
        for s in range(1, n):
            yield pltpu.make_async_copy(pair.at[s - 1, u], pair_slot.at[slot, s - 1], load_sem.at[slot, s])

    for c in loads(0):
        c.start()

    def start_d(u):
        for d in (2, 1, 3):
            d_copy(u, d).start()

    start_d(0)
    start_d(1)

    def begin(u, carry):
        own_part(u).start()
        return carry

    lax.fori_loop(0, units, begin, 0)
    near[...] = jnp.zeros_like(near)
    far_sum[...] = jnp.zeros_like(far_sum)
    one = jnp.ones((1, BLK), F32)
    ones3 = tail(BLK, (one, one, one)).astype(BF16)
    row16 = lax.broadcasted_iota(jnp.int32, (16, BLK), 0)
    marks = [jnp.where(row16 == r, 1.0, 0.0).astype(BF16) for r in range(2)]

    def work(u):
        b, h = lax.div(u, HEADS), lax.rem(u, HEADS)
        length = len_ref[b]
        left, right = far_ref[h, 0], far_ref[h, 1]
        slot = lax.rem(u, 2)
        for c in loads(u):
            c.wait()

        @pl.when(u + 1 < units)
        def _():
            for c in loads(u + 1):
                c.start()

        @pl.when(u + 2 < units)
        def _():
            start_d(u + 2)

        for s in range(n):
            col = lax.rem(x + s, n)
            for j in range(OUTER):
                kb = n * j + col
                if s == 0:
                    keys, vals = own_slot[slot, j, DH : 2 * DH], own_slot[slot, j, 2 * DH :]
                else:
                    keys, vals = pair_slot[slot, n - s - 1, j, :DH], pair_slot[slot, n - s - 1, j, DH:]
                ka[kb] = key_rows(keys, kb, length)
                kt[kb] = keys
                va[kb] = jnp.concatenate([vals, ones3], axis=0).T
        own_part(u).wait()
        for d in range(1, OUTER):
            d_copy(u, d).wait_recv()
        for j in range(OUTER):
            lse = lse_ref[u, j]
            both = query_parts(own_slot[slot, j, :DH])
            for v, c in enumerate((left, 0.0, right)):
                qa[v, j, : 2 * DH] = both
                qa[v, j, 2 * DH :] = tail(BLK, split3(c - lse) + (one,)).astype(BF16)
            arrived = do_land[u, j]
            delta = jnp.sum(arrived.astype(F32) * o_ref[u, j].astype(F32), axis=0, keepdims=True)
            da[j, :DH] = arrived
            da[j, DH:] = tail(BLK, split3(-delta)).astype(BF16)
        dqs = [None] * OUTER
        for g in range(0, nk, GROUP):
            blocks = range(g, g + GROUP)
            ps, dss = {}, {}
            for j in range(OUTER):
                left_side = []
                for kb in blocks:
                    case = far_case(n, j, kb)
                    if case is not None:
                        p = jnp.exp2(jnp.dot(ka[kb], qa[case, j], preferred_element_type=F32))
                        mark = marks[case // 2]
                    else:
                        tile, case = near_case(n, j, kb, x)
                        s = jnp.dot(ka[kb], qa[case, j], preferred_element_type=F32)
                        p = jnp.exp2(s + tile_ref[h, tile])
                        want = jnp.where(case == 1, 2, lax.div(case, 2))
                        mark = jnp.where(row16 == want, 1.0, 0.0).astype(BF16)
                    ds = p * jnp.dot(va[kb], da[j], preferred_element_type=F32)
                    if far_case(n, j, kb) is None:
                        near[h, tile] += ds
                    ps[kb, j], dss[kb, j] = p.astype(BF16), ds.astype(BF16)
                    left_side.append(jnp.concatenate([kt[kb], mark], axis=0))
                right_side = jnp.concatenate([dss[kb, j] for kb in blocks], axis=0)
                dq = jnp.dot(jnp.concatenate(left_side, axis=1), right_side, preferred_element_type=F32)
                dqs[j] = dq if g == 0 else dqs[j] + dq
            for kb in blocks:
                dv, dk = jnp.zeros((DH, BLK), F32), jnp.zeros((DH, BLK), F32)
                for j in range(OUTER):
                    dv = dv + lax.dot_general(da[j, :DH], ps[kb, j], NT, preferred_element_type=F32)
                    dk = dk + lax.dot_general(own_slot[slot, j, :DH], dss[kb, j], NT, preferred_element_type=F32)
                dk_all[kb] = dk
                dv_all[kb] = dv
        @pl.when(u >= x_slots)
        def _():
            for s in range(1, n):
                x_copy(u - x_slots, s).wait_send()

        far = jnp.zeros((8, BLK), F32)
        for j in range(OUTER):
            far = far + dqs[j][DH : DH + 8]
        far_sum[h] += far
        parity = lax.rem(u, 2)
        for j in range(OUTER):
            kept[parity, j, :DH] = dqs[j][:DH]
            kept[parity, j, DH : 2 * DH] = dk_all[n * j + x]
            kept[parity, j, 2 * DH :] = dv_all[n * j + x]
            for s in range(1, n):
                kb = n * j + lax.rem(x + s, n)
                x_out[s - 1, lax.rem(u, x_slots), j, :DH] = dk_all[kb].astype(BF16)
                x_out[s - 1, lax.rem(u, x_slots), j, DH:] = dv_all[kb].astype(BF16)
        for s in range(1, n):
            x_copy(u, s).start()

    def hand_over(u):
        b, h = lax.div(u, HEADS), lax.rem(u, HEADS)
        parity = lax.rem(u, 2)
        for s in range(1, n):
            x_copy(u, s).wait_recv()

        @pl.when(u >= z_slots)
        def _():
            for i in range(2):
                for m in range(3):
                    z_copy(u - z_slots, i, m).wait_send()

        for i, (mine, theirs) in enumerate(((z, near_z), (two, across))):
            for j, stays in ((mine, True), (theirs, False)):
                rest = kept[parity, j, DH:]
                for s in range(1, n):
                    rest = rest + x_land[s - 1, lax.rem(u, X_LAND), j].astype(F32)
                total = jnp.concatenate([kept[parity, j, :DH], rest], axis=0).astype(BF16)
                if stays:
                    for m in range(3):
                        grads[m, b, i, half_rows(h)] = total[m * DH : (m + 1) * DH]
                else:
                    z_out[lax.rem(u, z_slots), i] = total
            for m in range(3):
                z_copy(u, i, m).start()

    def combine(b):
        for h in range(HEADS):
            for i in range(2):
                for m in range(3):
                    z_copy(b * HEADS + h, i, m).wait_recv()
        for c in keep_grads(b):
            c.start()
        total = jnp.dot(w_half[0], grads[0, b, 1], preferred_element_type=F32)
        total = total + jnp.dot(w_half[1], grads[1, b, 1], preferred_element_type=F32)
        total = total + jnp.dot(w_half[2], grads[2, b, 1], preferred_element_type=F32)
        @pl.when(b < batch - 1)
        def _():
            other_out[b] = total.astype(BF16)
            n_copy(b).start()

        @pl.when(b == batch - 1)
        def _():
            leaving[...] = total.astype(BF16)

    def turn(u, carry):
        @pl.when(u < units)
        def _():
            work(u)

        @pl.when(jnp.logical_and(u > 0, u <= units))
        def _():
            hand_over(u - 1)

        @pl.when(jnp.logical_and(u > HEADS, lax.rem(u - 1, HEADS) == 0))
        def _():
            combine(lax.div(u - 1, HEADS) - 1)

        @pl.when(u == 0)
        def _():
            scatter.step_first((0, early.lines[-1]))

        for line in early.lines:

            @pl.when(u == (2 * line + 2 if line < early.lines[-1] else 7))
            def _():
                scatter.step_second(line)
                if line + 1 < early.lines[-1]:
                    scatter.start_first(line + 1)

        return carry

    for c in w_loads + firsts:
        c.wait()
    lax.fori_loop(0, units + 2, turn, 0)
    near_copy = pltpu.make_async_copy(near, near_out, first_sem.at[0])
    near_copy.start()

    def finish(u, carry):
        for d in range(1, OUTER):
            d_copy(u, d).wait_send()

        @pl.when(u >= units - z_slots)
        def _():
            for i in range(2):
                for m in range(3):
                    z_copy(u, i, m).wait_send()

        @pl.when(u >= units - x_slots)
        def _():
            for s in range(1, n):
                x_copy(u, s).wait_send()

        return carry

    lax.fori_loop(0, units, finish, 0)
    for b in range(batch - 1):
        n_copy(b).wait_send()
        n_copy(b).wait_recv()
    for line in early.lines:
        scatter.step_third(line)
        parts[early.part_start[line] : early.part_start[line] + early.size[line]] = scatter.part(line)[...]
    scatter.end()
    for b in range(batch):
        for c in keep_grads(b):
            c.wait()
    near_copy.wait()


def staging(n, units):
    return (units, units) if n <= 2 else (2, 4)


X_LAND = 4


def attention_backward(n, early, lengths, far, tiles, own, pair, out, lse, dout, weights, projections):
    batch, width, height = dout.shape
    units, nk = batch * HEADS, n * OUTER
    dma = pltpu.SemaphoreType.DMA
    x_slots, z_slots = staging(n, units)
    return pl.pallas_call(
        functools.partial(backward_kernel, n, early),
        in_specs=[smem()] + [whole()] * 2 + [anywhere()] * (8 + len(weights)),
        out_specs=[anywhere()] * 2 + [whole()] * 4,
        out_shape=[
            jax.ShapeDtypeStruct((3, batch, 2, HALF, height), BF16),
            jax.ShapeDtypeStruct((HEADS, TILES, BLK, BLK), F32),
            jax.ShapeDtypeStruct((HEADS, 8, BLK), F32),
            jax.ShapeDtypeStruct((early.part_total, LANES), BF16),
            jax.ShapeDtypeStruct((batch - 1, width, height), BF16),
            jax.ShapeDtypeStruct((width, height), BF16),
        ],
        scratch_shapes=[
            pltpu.VMEM(tiles.shape, F32),
            pltpu.VMEM(out.shape, BF16),
            pltpu.VMEM((3, batch, 2, HALF, height), BF16),
            pltpu.VMEM((HEADS, TILES, BLK, BLK), F32),
            dma((2,)),
            dma((units,)),
            dma((3, batch)),
            pltpu.VMEM((3, width, HALF), BF16),
            pltpu.VMEM((batch - 1, width, height), BF16),
            dma((3,)),
            dma((batch - 1,)),
            dma((batch - 1,)),
            pltpu.VMEM((2, OUTER, 3 * DH, BLK), BF16),
            pltpu.VMEM((2, n - 1, OUTER, 2 * DH, BLK), BF16),
            dma((2, n)),
            pltpu.VMEM((units, OUTER, DH, BLK), BF16),
            pltpu.VMEM((n - 1, x_slots, OUTER, 2 * DH, BLK), BF16),
            pltpu.VMEM((n - 1, X_LAND, OUTER, 2 * DH, BLK), BF16),
            pltpu.VMEM((z_slots, 2, 3 * DH, BLK), BF16),
            pltpu.VMEM((2, OUTER, 3 * DH, BLK), F32),
            pltpu.VMEM((nk, BLK, QAUG), BF16),
            pltpu.VMEM((nk, DH, BLK), BF16),
            pltpu.VMEM((nk, BLK, AUG), BF16),
            pltpu.VMEM((3, OUTER, QAUG, BLK), BF16),
            pltpu.VMEM((OUTER, AUG, BLK), BF16),
            pltpu.VMEM((nk, DH, BLK), F32),
            pltpu.VMEM((nk, DH, BLK), F32),
            dma((units, OUTER - 1)),
            dma((units, OUTER - 1)),
            dma((n - 1, units)),
            dma((n - 1, units)),
            dma((units, 2, 3)),
            dma((units, 2, 3)),
        ]
        + early_scatter(early).scratch(),
        compiler_params=pltpu.CompilerParams(
            vmem_limit_bytes=VMEM_BYTES, collective_id=1, has_side_effects=True
        ),
        cost_estimate=pl.CostEstimate(flops=110 * 10**9, bytes_accessed=24 << 20, transcendentals=0),
        name="attention_backward",
    )(lengths, far, lse, tiles, own, pair, out, dout, *weights, *projections)


FF_STEP = 512


def middle_kernel(
    x_in, att_in, cot_in, gain_ref, w_out, w_gate, w_up, w_down,
    result_out, mixed_out, dout_out, d_gain, d_out, d_gate, d_up, d_down,
    x_ref, att_ref, cot_ref, result, grad_mixed, dout,
    wo, wg, wu, wd, att, low, hidden, g_gate, g_up, s_out, s_gate, s_up, s_down, kept, in_sem, out_sem,
):
    tokens, width = x_ref.shape
    batch = att_ref.shape[0]
    ff = w_gate.shape[1]
    pairs = ((w_out, wo), (w_gate, wg), (w_up, wu), (w_down, wd), (att_in, att_ref), (x_in, x_ref), (cot_in, cot_ref))
    loads = [pltpu.make_async_copy(src, dst, in_sem.at[i]) for i, (src, dst) in enumerate(pairs)]
    pairs = ((s_out, d_out), (s_gate, d_gate), (s_up, d_up), (s_down, d_down))
    pairs += ((result, result_out), (grad_mixed, mixed_out), (dout, dout_out))
    stores = [pltpu.make_async_copy(src, dst, out_sem.at[i]) for i, (src, dst) in enumerate(pairs)]
    loads = loads[4:5] + loads[:1] + loads[5:] + loads[1:4]
    for c in loads:
        c.start()
    height = tokens // batch
    loads[0].wait()
    for b in range(batch):
        att[b * height : (b + 1) * height] = att_ref[b].T
    for c in loads[1:4]:
        c.wait()
    low[...] = cot_ref[...].astype(BF16)
    mixed = x_ref[...] + jnp.dot(att[...], wo[...], preferred_element_type=F32)
    kept[...] = mixed
    result[...] = mixed
    scale = lax.rsqrt(jnp.mean(mixed * mixed, axis=-1, keepdims=True) + epsilon)
    normed = (mixed * scale * gain_ref[...].reshape(1, -1)).astype(BF16)
    att[...] = normed
    for c in loads[4:]:
        c.wait()
    root = 0.7978845608028654
    for at in range(0, ff, FF_STEP):
        part = slice(at, at + FF_STEP)
        gate = jnp.dot(att[...], wg[:, part], preferred_element_type=F32)
        upward = jnp.dot(att[...], wu[:, part], preferred_element_type=F32)
        g_hidden = lax.dot_general(low[...], wd[part], NT, preferred_element_type=F32)
        square = gate * gate
        t = jnp.tanh(root * gate * (1.0 + 0.044715 * square))
        half = 0.5 * (1.0 + t)
        act = gate * half
        slope = half + 0.5 * gate * (1.0 - t * t) * (root * (1.0 + 3.0 * 0.044715 * square))
        hidden[:, part] = (act * upward).astype(BF16)
        g_gate[:, part] = (g_hidden * upward * slope).astype(BF16)
        g_up[:, part] = (g_hidden * act).astype(BF16)
    result[...] += jnp.dot(hidden[...], wd[...], preferred_element_type=F32)
    stores[4].start()
    d_normed = lax.dot_general(g_gate[...], wg[...], NT, preferred_element_type=F32)
    d_normed = d_normed + lax.dot_general(g_up[...], wu[...], NT, preferred_element_type=F32)
    mixed = kept[...]
    scale = lax.rsqrt(jnp.mean(mixed * mixed, axis=-1, keepdims=True) + epsilon)
    d_gain[...] = jnp.sum(d_normed * mixed * scale, axis=0, keepdims=True)
    u = d_normed * gain_ref[...].reshape(1, -1)
    along = jnp.mean(u * mixed, axis=-1, keepdims=True)
    d_mixed = cot_ref[...] + scale * (u - mixed * (scale * scale * along))
    grad_mixed[...] = d_mixed
    stores[5].start()
    d_low = d_mixed.astype(BF16)
    turned = lax.dot_general(wo[...], d_low, NT, preferred_element_type=F32).astype(BF16)
    for b in range(batch):
        dout[b] = turned[:, b * height : (b + 1) * height]
    stores[6].start()
    total = jnp.zeros((width, width), F32)
    for b in range(batch):
        total = total + jnp.dot(att_ref[b], d_low[b * height : (b + 1) * height], preferred_element_type=F32)
    s_out[...] = total.astype(BF16)
    stores[0].start()
    normed_t = att[...].T
    for src, dst, store in ((g_gate, s_gate, stores[1]), (g_up, s_up, stores[2])):
        for at in range(0, ff, FF_STEP):
            part = slice(at, at + FF_STEP)
            dst[:, part] = jnp.dot(normed_t, src[:, part], preferred_element_type=F32).astype(BF16)
        store.start()
    for at in range(0, ff, FF_STEP):
        part = slice(at, at + FF_STEP)
        s_down[part] = jnp.dot(hidden[:, part].T, low[...], preferred_element_type=F32).astype(BF16)
    stores[3].start()
    for c in stores:
        c.wait()


def middle(inputs, att, cotangent, gain, w_out, w_gate, w_up, w_down):
    batch, height, width = inputs.shape
    tokens, ff = batch * height, w_gate.shape[1]
    weights = (w_out, w_gate, w_up, w_down)
    flat = (tokens, width)
    out = pl.pallas_call(
        middle_kernel,
        in_specs=[anywhere()] * 3 + [whole()] + [anywhere()] * 4,
        out_specs=[anywhere()] * 3 + [whole()] + [anywhere()] * 4,
        out_shape=[
            jax.ShapeDtypeStruct(flat, F32),
            jax.ShapeDtypeStruct(flat, F32),
            jax.ShapeDtypeStruct((batch, width, height), BF16),
            jax.ShapeDtypeStruct((1, width), F32),
        ]
        + [jax.ShapeDtypeStruct(w.shape, BF16) for w in weights],
        scratch_shapes=[
            pltpu.VMEM(flat, F32),
            pltpu.VMEM(att.shape, BF16),
            pltpu.VMEM(flat, F32),
            pltpu.VMEM(flat, F32),
            pltpu.VMEM(flat, F32),
            pltpu.VMEM(att.shape, BF16),
        ]
        + [pltpu.VMEM(w.shape, BF16) for w in weights]
        + [pltpu.VMEM(flat, BF16)] * 2
        + [pltpu.VMEM((tokens, ff), BF16)] * 3
        + [pltpu.VMEM(w.shape, BF16) for w in weights]
        + [pltpu.VMEM(flat, F32)]
        + [pltpu.SemaphoreType.DMA((7,))] * 2,
        compiler_params=params(),
        cost_estimate=pl.CostEstimate(flops=25 * 10**9, bytes_accessed=32 << 20, transcendentals=0),
        name="middle",
    )(inputs.reshape(flat), att, cotangent.reshape(flat), gain, *weights)
    return out[0].reshape(inputs.shape), out[1].reshape(inputs.shape), out[2], out[3], out[4:]


def shards(
    places,
    inputs,
    lengths,
    norm_attn,
    w_query,
    w_key,
    w_value,
    w_out,
    norm_ffn,
    w_gate,
    w_up,
    w_down,
    bucket_bias,
    cotangent,
):
    batch, height, width = inputs.shape
    n = places.inner
    onehot = jnp.asarray(ONEHOT)
    normed_t, own, pair, attended_t, out, lse, tiles, far = attention_forward(
        n, lengths, bucket_bias.T, onehot, inputs, norm_attn, w_query, w_key, w_value
    )
    result, grad_mixed, grad_attended_t, grad_norm_ffn, weights = middle(
        inputs, attended_t, cotangent, norm_ffn, w_out, w_gate, w_up, w_down
    )
    early = Rows(places, [g.shape for g in weights], LANES, 4)
    projections = (w_query, w_key, w_value)
    grads, near, far_sum, parts, other, leaving = attention_backward(
        n, early, lengths, far, tiles, own, pair, out, lse, grad_attended_t, weights, projections
    )
    late = Rows(places, [(width, HALF)] * 3, LANE, 2)
    loaded = (
        parts, grads, normed_t, *projections, inputs, grad_mixed, near, far_sum, onehot, other, leaving
    )
    grad_inputs, full_early, full_late, small = last_grads(early, late, loaded, norm_attn, grad_norm_ffn)
    (part_out, part_gate, part_up, part_down, part_query, part_key, part_value, part_attn, part_ffn, part_table,
     grad_inputs) = unpack(early, late, full_early, full_late, small, grad_inputs)
    return (
        result,
        grad_inputs,
        part_attn.reshape(-1),
        part_ffn.reshape(-1),
        part_query,
        part_key,
        part_value,
        part_out,
        part_gate,
        part_up,
        part_down,
        part_table,
    )


def solution(mesh):
    rows = P("dp", "seq", None)
    share = P("dp", None)
    return jax.shard_map(
        functools.partial(shards, Places(mesh)),
        mesh=mesh,
        in_specs=(rows, P("dp")) + (P(),) * 10 + (rows,),
        out_specs=(rows, rows, P("dp"), P("dp")) + (share,) * 8,
        check_vma=False,
    )
```
